32 devices in a mesh: dp: 2 (over y), fsdp: 16 (over z, x, core).
Axes of the slice: x: 2, y: 2, z: 4, core: 2. Of those that a mesh axis runs over, the one named last changes fastest.
Arguments:
- tokens: bfloat16 [16384, 768], P(('dp', 'fsdp')), may hold values from -6 to 6
- lengths: int32 [32], P(('dp', 'fsdp')), may hold values from 256 to 500, as said below
- buckets: int32 [32, 512, 512], P(('dp', 'fsdp')), may hold values from 0 to 447, as said below
- ln1_gain: bfloat16 [768], P(('dp', 'fsdp')), may hold values from 0.5 to 1.5
- ln1_bias: bfloat16 [768], P(('dp', 'fsdp')), may hold values from -3 to 3
- qkv_weight: bfloat16 [768, 2304], P(('dp', 'fsdp')), may hold values from -0.21875 to 0.21875
- q_bias: bfloat16 [768], P(('dp', 'fsdp')), may hold values from -3 to 3
- v_bias: bfloat16 [768], P(('dp', 'fsdp')), may hold values from -3 to 3
- out_weight: bfloat16 [768, 768], P(('dp', 'fsdp')), may hold values from -0.875 to 0.875
- out_bias: bfloat16 [768], P(('dp', 'fsdp')), may hold values from -3 to 3
- rel_table: bfloat16 [12, 448], replicated, may hold values from -4 to 4
- ln2_gain: bfloat16 [768], P(('dp', 'fsdp')), may hold values from 0.5 to 1.5
- ln2_bias: bfloat16 [768], P(('dp', 'fsdp')), may hold values from -3 to 3
- up_weight: bfloat16 [768, 3072], P(('dp', 'fsdp')), may hold values from -0.21875 to 0.21875
- up_bias: bfloat16 [3072], P(('dp', 'fsdp')), may hold values from -3 to 3
- down_weight: bfloat16 [3072, 768], P(('dp', 'fsdp')), may hold values from -0.109375 to 0.109375
- down_bias: bfloat16 [768], P(('dp', 'fsdp')), may hold values from -3 to 3
- cotangent: bfloat16 [16384, 768], P(('dp', 'fsdp')), may hold values from -6 to 6
Outputs:
- output: bfloat16 [16384, 768], P(('dp', 'fsdp'))
- input_grad: float32 [16384, 768], P(('dp', 'fsdp'))
- grad_ln1_gain: float32 [768], P(('dp', 'fsdp'))
- grad_ln1_bias: float32 [768], P(('dp', 'fsdp'))
- grad_qkv_weight: float32 [768, 2304], P(('dp', 'fsdp'))
- grad_q_bias: float32 [768], P(('dp', 'fsdp'))
- grad_v_bias: float32 [768], P(('dp', 'fsdp'))
- grad_out_weight: float32 [768, 768], P(('dp', 'fsdp'))
- grad_out_bias: float32 [768], P(('dp', 'fsdp'))
- grad_rel_table: float32 [12, 448], replicated
- grad_ln2_gain: float32 [768], P(('dp', 'fsdp'))
- grad_ln2_bias: float32 [768], P(('dp', 'fsdp'))
- grad_up_weight: float32 [768, 3072], P(('dp', 'fsdp'))
- grad_up_bias: float32 [3072], P(('dp', 'fsdp'))
- grad_down_weight: float32 [3072, 768], P(('dp', 'fsdp'))
- grad_down_bias: float32 [768], P(('dp', 'fsdp'))
The draws below stay inside these ranges and needn't reach their ends.
Inputs may be any that keep to these rules, and one draw needn't show every extreme that they name: `lengths`: each item is speech, with 380 to 500 live rows, or text, with exactly 256; item 0 is speech with 500 rows and item 1 is text. With t = j - i: for a speech item buckets[n, i, j] = clip(t, -160, 159) + 160; for a text item 2 * 160 + clip(t, -64, 63) + 64.
All inputs are finite; a program needn't handle non-finite values.
Results may differ from the reference program's by a relative error of at most 0.014.
Values may be sent and summed in bfloat16 or wider, within the bound.
No kernel may reach another device: no remote copies, remote signals or barrier semaphores. Data moves between devices by JAX's collectives and lax.ppermute only.
A program may use at most 320 MiB of HBM per device.

```python
import jax
import jax.numpy as jnp
from jax import lax

D = 768
HEADS = 12
HEAD_DIM = 64
FF = 3072
SPEECH_REACH = 160
TEXT_REACH = 64
BUCKETS = 448
SLOT = 512
LONGEST = 500
SHORTEST = 380
TEXT_LEN = 256
ITEMS = 32
TOKENS = 16384


def item_plan(key):
    base_key = jax.random.fold_in(key, 11)
    key_kind, key_length = jax.random.split(base_key)
    item_kind = jax.random.randint(key_kind, (ITEMS,), 0, 2)
    item_kind = item_kind.at[0].set(0).at[1].set(1)
    speech = jax.random.randint(key_length, (ITEMS,), SHORTEST, LONGEST + 1)
    speech = speech.at[0].set(LONGEST)
    lengths = jnp.where(item_kind == 0, speech, TEXT_LEN).astype(jnp.int32)
    return (item_kind, lengths)


def draw_lengths(key, part):
    return item_plan(key)[1]


def draw_buckets(key, part):
    item_kind, lengths = item_plan(key)
    places = jnp.arange(SLOT, dtype=jnp.int32)
    offset = places[None, :] - places[:, None]
    speech_map = jnp.clip(offset, -SPEECH_REACH, SPEECH_REACH - 1) + SPEECH_REACH
    text_map = 2 * SPEECH_REACH + jnp.clip(offset, -TEXT_REACH, TEXT_REACH - 1) + TEXT_REACH
    return jnp.where(item_kind[:, None, None] == 0, speech_map[None], text_map[None]).astype(jnp.int32)


def strengthened(entries, own_key, source, target, blocks, factor):
    def block_of(dim):
        return (jnp.arange(entries.shape[dim]) // (entries.shape[dim] // blocks)).reshape((-1,) + (1,) * (entries.ndim - 1 - dim))

    near = jax.random.permutation(own_key, blocks)[block_of(target)]
    far = (block_of(target) + blocks // 2) % blocks
    return jnp.where((block_of(source) == near) | (block_of(source) == far), factor * entries, entries)


def block_levels(key, dims, cuts, smallest, high):
    level, own = 1.0, jax.random.fold_in(key, 6)
    for position, parts in cuts:
        heights = jnp.exp(jax.random.uniform(jax.random.fold_in(own, position), (parts,), jnp.float32, smallest / len(cuts), high / len(cuts)))
        level = level * jnp.repeat(heights, dims[position] // parts).reshape([-1 if axis == position else 1 for axis in range(len(dims))])
    return level


def centred(key, shape, scale, most, cuts=(), held_as=jnp.bfloat16):
    loudness = block_levels(key, shape, cuts, -0.22, 0.18) if cuts else 1.0
    array = jax.random.normal(key, shape, jnp.float32) * scale * loudness
    return jnp.minimum(jnp.maximum(array, -most), most).astype(held_as)


def bell_draw_with(stream_key, shape, width, bound, cuts, heavy, kind=jnp.bfloat16):
    values = width * jax.random.normal(stream_key, shape, jnp.float32)
    if cuts:
        values = values * block_levels(stream_key, shape, cuts, -0.22, 0.18)
    return jnp.clip(strengthened(values, jax.random.fold_in(stream_key, 3), *heavy), -bound, bound).astype(kind)


def setup_inputs(seed: int = 0) -> dict:
    arg_keys = jax.random.split(jax.random.key(seed), 19)
    return {
        "tokens": centred(arg_keys[0], (TOKENS, D), 1.0, 6.0, ((0, 32),)),
        "lengths": draw_lengths(jax.random.fold_in(arg_keys[18], 71), 0),
        "buckets": draw_buckets(jax.random.fold_in(arg_keys[18], 71), 0),
        "ln1_gain": jnp.clip(1.0 + 0.1 * jax.random.normal(arg_keys[3], (D,), jnp.float32), 0.5, 1.5).astype(jnp.bfloat16),
        "ln1_bias": centred(arg_keys[4], (D,), 0.5, 3.0, ((0, 32),)),
        "qkv_weight": centred(arg_keys[5], (D, 3 * D), D ** -0.5, 0.21875, ((0, 32),)),
        "q_bias": centred(arg_keys[6], (D,), 0.5, 3.0, ((0, 32),)),
        "v_bias": centred(arg_keys[7], (D,), 0.5, 3.0, ((0, 32),)),
        "out_weight": centred(arg_keys[8], (D, D), (D // 16) ** -0.5, 0.875, ((0, 32),)),
        "out_bias": centred(arg_keys[9], (D,), 0.5, 3.0, ((0, 32),)),
        "rel_table": centred(arg_keys[10], (HEADS, BUCKETS), 1.0, 4.0),
        "ln2_gain": jnp.clip(1.0 + 0.1 * jax.random.normal(arg_keys[11], (D,), jnp.float32), 0.5, 1.5).astype(jnp.bfloat16),
        "ln2_bias": centred(arg_keys[12], (D,), 0.5, 3.0, ((0, 32),)),
        "up_weight": centred(arg_keys[13], (D, FF), D ** -0.5, 0.21875, ((0, 32),)),
        "up_bias": centred(arg_keys[14], (FF,), 0.5, 3.0, ((0, 32),)),
        "down_weight": centred(arg_keys[15], (FF, D), FF ** -0.5, 0.109375, ((0, 32),)),
        "down_bias": centred(arg_keys[16], (D,), 0.5, 3.0, ((0, 32),)),
        "cotangent": bell_draw_with(arg_keys[17], (TOKENS, D), 1.0, 6.0, ((0, 32),), (0, 1, 32, 2.75)),
    }


highest = lax.Precision.HIGHEST

@jax.custom_vjp
def low(v):
    return lax.optimization_barrier(v.astype(jnp.bfloat16)).astype(jnp.float32)

@jax.custom_vjp
def low_back(v):
    return v

def low_keep(v):
    return (low(v), None)

def low_pass(kept, grad):
    return (grad,)

def back_keep(v):
    return (v, None)

def back_low(kept, grad):
    return (low(grad),)
low.defvjp(low_keep, low_pass)
low_back.defvjp(back_keep, back_low)

def normalize(row_data, gain_vec, bias_vec):
    centre = row_data - lax.optimization_barrier(jnp.mean(row_data, -1, keepdims=True))
    spread = lax.optimization_barrier(jnp.mean(centre * centre, -1, keepdims=True))
    return centre * lax.rsqrt(spread + 1e-05) * gain_vec + bias_vec

def gelu_exact(argument):
    return 0.5 * argument * (1.0 + lax.erf(argument * 0.7071067811865476))

def attend_item(table_in, packed):
    queries, key_rows, values, bucket, length = packed
    scores = jnp.einsum('qhd,khd->hqk', queries, key_rows, precision=highest) * HEAD_DIM ** (-0.5) + table_in[:, bucket]
    scores = low_back(scores)
    allowed = jnp.arange(SLOT) < length
    scores = jnp.where(allowed[None, None, :], scores, -1e+30)
    peak_score = lax.optimization_barrier(jnp.max(scores, -1, keepdims=True))
    raised = jnp.exp(scores - peak_score)
    probs_low = low(raised / lax.optimization_barrier(jnp.sum(raised, -1, keepdims=True)))
    mixed = jnp.einsum('hqk,khd->qhd', probs_low, values, precision=highest)
    return low_back(low(mixed))

def forward(weights_in, inputs, bucket, lengths):
    gain_first, bias_first, w_qkv, bias_q, bias_v, w_out, bias_out, table_in, gain_second, bias_second, w_up, bias_up, w_down, bias_down = weights_in
    members = inputs.shape[0]
    normed = low(normalize(inputs, gain_first, bias_first))
    joined = jnp.einsum('isd,de->ise', normed, w_qkv, precision=highest)
    joined = joined + jnp.concatenate([bias_q, jnp.zeros_like(bias_q), bias_v])
    joined = low_back(low(joined)).reshape(members, SLOT, 3, HEADS, HEAD_DIM)
    attend = jax.checkpoint(lambda packed: attend_item(table_in, packed))
    mixed = lax.map(attend, (joined[:, :, 0], joined[:, :, 1], joined[:, :, 2], bucket, lengths))
    mixed = mixed.reshape(members, SLOT, D)
    branch = low_back(jnp.einsum('isd,de->ise', mixed, w_out, precision=highest) + bias_out)
    residual = inputs + branch
    normed_two = low(normalize(residual, gain_second, bias_second))
    pre_act = low_back(jnp.einsum('isd,df->isf', normed_two, w_up, precision=highest) + bias_up)
    active = low(gelu_exact(pre_act))
    result = residual + jnp.einsum('isf,fd->isd', active, w_down, precision=highest) + bias_down
    live_mask = (jnp.arange(SLOT)[None, :] < lengths[:, None])[:, :, None]
    return jnp.where(live_mask, result, 0.0)

def reference(tokens, lengths, buckets, ln1_gain, ln1_bias, qkv_weight, q_bias, v_bias, out_weight, out_bias, rel_table, ln2_gain, ln2_bias, up_weight, up_bias, down_weight, down_bias, cotangent):
    weights = tuple((member.astype(jnp.float32) for member in (ln1_gain, ln1_bias, qkv_weight, q_bias, v_bias, out_weight, out_bias, rel_table, ln2_gain, ln2_bias, up_weight, up_bias, down_weight, down_bias)))
    groups = ITEMS // 8
    inputs = tokens.astype(jnp.float32).reshape(groups, 8, SLOT, D)
    cot_rows = cotangent.astype(jnp.float32).reshape(groups, 8, SLOT, D)
    bucket_all = buckets.reshape(groups, 8, SLOT, SLOT)
    length_all = lengths.reshape(groups, 8)

    def one_group(totals, packed):
        row_data, bucket, length, cot_group = packed
        result, pullback = jax.vjp(lambda weights_in, inputs_in: forward(weights_in, inputs_in, bucket, length), weights, row_data)
        gradients, grad_rows = pullback(cot_group)
        return (jax.tree.map(lambda summed, added: summed + added, totals, gradients), (result, grad_rows))
    initial = jax.tree.map(jnp.zeros_like, weights)
    totals, (results, grad_rows) = lax.scan(one_group, initial, (inputs, bucket_all, length_all, cot_rows))
    return (results.reshape(TOKENS, D).astype(jnp.bfloat16), grad_rows.reshape(TOKENS, D), totals[0], totals[1], totals[2], totals[3], totals[4], totals[5], totals[6], totals[7], totals[8], totals[9], totals[10], totals[11], totals[12], totals[13])
```

```python
import functools

import jax
import jax.numpy as jnp
from jax import lax
from jax.experimental import pallas as pl
from jax.experimental.pallas import tpu as pltpu
from jax.sharding import PartitionSpec as P

BF = jnp.bfloat16
F32 = jnp.float32
AXES = ("dp", "fsdp")
TILE = 128
CHUNK = 64
VMEM_BYTES = 56 * 1024 * 1024
EPS = 1e-05
NN = (((1,), (0,)), ((), ()))
NT = (((1,), (1,)), ((), ()))
TN = (((0,), (0,)), ((), ()))
VMEM = pltpu.VMEM


def mm(left, right, dims=NN):
    return lax.dot_general(left, right, dims, preferred_element_type=F32)


def any_spec():
    return pl.BlockSpec(memory_space=pl.ANY)


def smem_spec():
    return pl.BlockSpec(memory_space=pltpu.SMEM)


def whole(shape):
    return pl.BlockSpec(shape, lambda *_: (0,) * len(shape))


def params(grid_dims=1):
    return pltpu.CompilerParams(
        dimension_semantics=("arbitrary",) * grid_dims, vmem_limit_bytes=VMEM_BYTES
    )


def cost(flops, moved):
    return pl.CostEstimate(flops=int(flops), bytes_accessed=int(moved), transcendentals=0)


class Pieces:
    def __init__(self, buffers, offsets, rows):
        self.buffers = buffers
        self.offsets = offsets
        self.rows = rows

    @property
    def slots(self):
        return sum(b.shape[0] for b in self.buffers)


def load_copies(refs, offs_ref, rows, picks, sems):
    copies, slot, count = [], 0, 0
    for ref in refs:
        for k in range(ref.shape[0]):
            at = pl.multiple_of(offs_ref[slot], 16)
            for first, target in picks:
                copies.append(
                    pltpu.make_async_copy(
                        ref.at[k, pl.ds(first, rows)], target.at[pl.ds(at, rows)], sems.at[count]
                    )
                )
                count += 1
            slot += 1
    return copies


def row_norm(x):
    centre = x - jnp.mean(x, -1, keepdims=True)
    scale = lax.rsqrt(jnp.mean(centre * centre, -1, keepdims=True) + EPS)
    return centre * scale, scale


def bias_tiles(curve):
    heads, span = curve.shape
    tiles = span // TILE - 1

    def kernel(curve_ref, out_ref):
        base = pltpu.roll(jnp.broadcast_to(curve_ref[0], (8, span)), 0, 1, stride=1, stride_axis=0)
        for pair in range(TILE // 16):
            rolled = jnp.concatenate(
                [pltpu.roll(base, 16 * pair + 8 * i, 1) if pair + i else base for i in range(2)], 0
            ).astype(BF)
            for d in range(tiles):
                out_ref[0, d, 16 * pair : 16 * pair + 16, :] = rolled[
                    :, TILE * (d + 1) : TILE * (d + 2)
                ]

    return pl.pallas_call(
        kernel,
        grid=(heads,),
        in_specs=[pl.BlockSpec((1, 1, span), lambda h: (h, 0, 0))],
        out_specs=pl.BlockSpec((1, tiles, TILE, TILE), lambda h: (h, 0, 0, 0)),
        out_shape=jax.ShapeDtypeStruct((heads, tiles, TILE, TILE), BF),
        compiler_params=params(),
        name="bias_tiles",
    )(curve.reshape(heads, 1, span))


def place_rows(block, offset, wide):
    padded = jnp.concatenate([block, jnp.zeros((block.shape[0], wide - TILE), block.dtype)], 1)
    return pltpu.roll(padded, offset, 1)


def attention_forward(half, core, tokens, normed, vec, pieces, tiles, lengths, head_size, tokens_in=()):
    rows, model = tokens.shape if normed is None else normed.shape
    width = model // 2
    heads = width // head_size
    pairs = width // TILE
    per = TILE // head_size
    first = normed is None
    unpack = vec is None
    n_buf = len(pieces.buffers)
    slots = pieces.slots
    scale = head_size**-0.5

    def kernel(core_ref, offs_ref, len_ref, x_ref, *refs):
        if not unpack:
            vec_ref, refs = refs[0], refs[1:]
        tile_ref, bufs, rest = refs[0], refs[1 : 1 + n_buf], refs[1 + n_buf + len(tokens_in) :]
        if first:
            n1_ref, rest = rest[0], rest[1:]
        if unpack:
            vec_ref, rest = rest[0], rest[1:]
        joined_ref, mixed_ref, p_ref, w_ref, qs_ref, s_ref, raw_ref, sems = rest
        pair = pl.program_id(0)

        @pl.when(pair == 0)
        def _():
            copies = load_copies(
                bufs, offs_ref, pieces.rows, [(j * pieces.rows, w_ref.at[j]) for j in range(3)], sems
            )
            if unpack:
                small, slot = [], 0
                for ref in bufs:
                    for k in range(ref.shape[0]):
                        small.append(
                            pltpu.make_async_copy(
                                ref.at[k, pl.ds(4 * pieces.rows, 16), pl.ds(0, TILE)],
                                raw_ref.at[slot],
                                sems.at[3 * slots + slot],
                            )
                        )
                        slot += 1
                for c in small:
                    c.start()
            for c in copies:
                c.start()
            if unpack:
                for c in small:
                    c.wait()
                total = jnp.zeros((16, model), F32)
                for slot in range(slots):
                    total += place_rows(raw_ref[slot].astype(F32), offs_ref[slot], model)
                vec_ref[...] = total
            if first:
                for r in range(0, rows, CHUNK):
                    xhat, _ = row_norm(x_ref[r : r + CHUNK, :].astype(F32))
                    n1_ref[r : r + CHUNK, :] = (xhat * vec_ref[0:1, :] + vec_ref[1:2, :]).astype(BF)
            for c in copies:
                c.wait()
            src = n1_ref if first else x_ref
            cols = pl.ds(pl.multiple_of((core_ref[0] ^ half) * width, TILE), width)
            for j in range(3):
                joined = mm(src[...], w_ref[j])
                if j != 1:
                    joined = joined + vec_ref[2 + j // 2 : 3 + j // 2, cols]
                qs_ref[j] = joined.astype(BF)

        lanes = pl.ds(pl.multiple_of(pair * TILE, TILE), TILE)
        q, k, v = (qs_ref[j, :, lanes] for j in range(3))
        for j, one in enumerate((q, k, v)):
            joined_ref[j] = one
        lane = lax.broadcasted_iota(jnp.int32, (1, TILE), 1)
        column = lax.broadcasted_iota(jnp.int32, (1, rows), 1)
        dead = jnp.where(column < len_ref[0], 0.0, -1e30).astype(F32)
        scaled = q.astype(F32) * scale
        outs = []
        for e in range(per):
            mine = (lane >= e * head_size) & (lane < (e + 1) * head_size)
            qm = jnp.where(mine, scaled, 0.0).astype(BF)
            s_ref[e] = mm(qm, k, NT)
            for r in range(0, rows, CHUNK):
                block, sub = r // TILE, r % TILE
                rel = jnp.concatenate(
                    [
                        tile_ref[e, j - block + rows // TILE - 1, sub : sub + CHUNK, :]
                        for j in range(rows // TILE)
                    ],
                    1,
                ).astype(F32)
                s = s_ref[e, r : r + CHUNK, :] + (rel + dead)
                raised = jnp.exp(s - jnp.max(s, -1, keepdims=True))
                inv = 1.0 / jnp.sum(raised, -1, keepdims=True)
                p_ref[e, r : r + CHUNK, :] = (raised * inv).astype(BF)
            outs.append(jnp.where(mine, mm(p_ref[e], v), 0.0))
        mixed_ref[...] = functools.reduce(lambda a, b: a + b, outs).astype(BF)

    ins = [core, pieces.offsets, lengths, tokens if first else normed]
    specs = [smem_spec(), smem_spec(), smem_spec(), whole((rows, model))]
    if not unpack:
        ins.append(vec)
        specs.append(whole((16, model)))
    tiles_n = tiles.shape[1]
    ins += [tiles, *pieces.buffers, *tokens_in]
    base = half * (heads // per)
    specs += [
        pl.BlockSpec((per, tiles_n, TILE, TILE), lambda p: (base + p, 0, 0, 0)),
        *[any_spec()] * (n_buf + len(tokens_in)),
    ]
    shapes = [
        jax.ShapeDtypeStruct((3, rows, width), BF),
        jax.ShapeDtypeStruct((rows, width), BF),
        jax.ShapeDtypeStruct((heads, rows, rows), BF),
    ]
    outs = [
        pl.BlockSpec((3, rows, TILE), lambda p: (0, 0, p)),
        pl.BlockSpec((rows, TILE), lambda p: (0, p)),
        pl.BlockSpec((per, rows, rows), lambda p: (p, 0, 0)),
    ]
    if unpack:
        shapes.insert(0, jax.ShapeDtypeStruct((16, model), F32))
        outs.insert(0, whole((16, model)))
    if first:
        shapes.insert(0, jax.ShapeDtypeStruct((rows, model), BF))
        outs.insert(0, whole((rows, model)))
    return pl.pallas_call(
        kernel,
        grid=(pairs,),
        in_specs=specs,
        out_specs=outs,
        out_shape=shapes,
        scratch_shapes=[
            VMEM((3, model, width), BF),
            VMEM((3, rows, width), BF),
            VMEM((per, rows, rows), F32),
            VMEM((slots, 16, TILE), BF),
            pltpu.SemaphoreType.DMA((4 * slots,)),
        ],
        compiler_params=params(),
        cost_estimate=cost(2e9, 1e7),
        name="attention_forward",
    )(*ins)


def project_out(core, mixed, tokens, pieces, vec, tokens_in=()):
    rows, model = tokens.shape
    width = model // 2
    sizes = [len(p.buffers) for p in pieces]
    per = [p.slots for p in pieces]

    def kernel(core_ref, offs0, offs1, m0_ref, m1_ref, x_ref, vec_ref, *rest):
        bufs = [rest[: sizes[0]], rest[sizes[0] : sum(sizes)]]
        res_ref, n2_ref, w_ref, sems = rest[sum(sizes) + len(tokens_in) :]
        copies = []
        for h, offs in enumerate((offs0, offs1)):
            copies += load_copies(
                bufs[h], offs, pieces[h].rows, [(3 * pieces[h].rows, w_ref.at[h])],
                sems.at[pl.ds(h * per[0], per[h])],
            )
        for c in copies:
            c.start()
        for c in copies:
            c.wait()
        for h in range(2):
            cols = pl.ds(pl.multiple_of((core_ref[0] ^ h) * width, TILE), width)
            acc = 0.0
            for g, m_ref in enumerate((m0_ref, m1_ref)):
                feats = pl.ds(pl.multiple_of((core_ref[0] ^ g) * width, TILE), width)
                acc = acc + mm(m_ref[...], w_ref[h, feats, :])
            res_ref[:, cols] = x_ref[:, cols].astype(F32) + acc + vec_ref[4:5, cols]
        for r in range(0, rows, CHUNK):
            xhat, _ = row_norm(res_ref[r : r + CHUNK, :])
            n2_ref[r : r + CHUNK, :] = (xhat * vec_ref[5:6, :] + vec_ref[6:7, :]).astype(BF)

    return pl.pallas_call(
        kernel,
        grid=(1,),
        in_specs=[
            *[smem_spec()] * 3,
            whole((rows, width)),
            whole((rows, width)),
            whole((rows, model)),
            whole((16, model)),
            *[any_spec()] * (sum(sizes) + len(tokens_in)),
        ],
        out_specs=[whole((rows, model)), whole((rows, model))],
        out_shape=[
            jax.ShapeDtypeStruct((rows, model), F32),
            jax.ShapeDtypeStruct((rows, model), BF),
        ],
        scratch_shapes=[VMEM((2, model, width), BF), pltpu.SemaphoreType.DMA((sum(per),))],
        compiler_params=params(),
        cost_estimate=cost(6e8, 5e6),
        name="project_out",
    )(
        core, pieces[0].offsets, pieces[1].offsets, mixed[0], mixed[1], tokens, vec,
        *pieces[0].buffers, *pieces[1].buffers, *tokens_in,
    )


def feed_forward(part, core, normed, grad_rows, vec, pieces, result_in, grad_in, tokens_in=()):
    rows, model = normed.shape
    hidden = model
    sizes = [len(p.buffers) for p in pieces]
    per = [p.slots for p in pieces]
    first = grad_in is None
    step_rows = rows // 2

    def kernel(core_ref, offs0, offs1, n_ref, gr_ref, vec_ref, res_ref, *rest):
        if not first:
            gin_ref, rest = rest[0], rest[1:]
        bufs = [rest[: sizes[0]], rest[sizes[0] : sum(sizes)]]
        out_ref, gn_ref, act_ref, gp_ref, col_ref, up_ref, down_ref, sems = rest[
            sum(sizes) + len(tokens_in) :
        ]
        step = pl.program_id(0)

        def copies(h):
            return load_copies(
                bufs[h], (offs0, offs1)[h], pieces[h].rows,
                [(0, up_ref.at[h]), (pieces[h].rows, down_ref.at[h])],
                sems.at[pl.ds(2 * h * per[0], 2 * per[h])],
            )

        @pl.when(step == 0)
        def _():
            both = [copies(0), copies(1)]
            for c in both[0] + both[1]:
                c.start()
            if first:
                out_ref[...] = res_ref[...] + vec_ref[7:8, :]
                gn_ref[...] = jnp.zeros_like(gn_ref)
            else:
                out_ref[...] = res_ref[...]
                gn_ref[...] = gin_ref[...]
            for c in both[0]:
                c.wait()

        @pl.when(step == 1)
        def _():
            for c in copies(1):
                c.wait()

        sums = jnp.zeros((1, hidden), F32)
        up_bias = vec_ref[pl.ds(8 + 2 * part + (core_ref[0] ^ step), 1), :]
        for r in range(0, rows, step_rows):
            block = slice(r, r + step_rows)
            pre = mm(n_ref[block, :], up_ref[step]) + up_bias
            gact = mm(gr_ref[block, :], down_ref[step], NT)
            cdf = 0.5 * (1.0 + lax.erf(pre * 0.7071067811865476))
            act = (pre * cdf).astype(BF)
            slope = cdf + pre * (jnp.exp(-0.5 * (pre * pre)) * 0.3989422804014327)
            gp = (gact * slope).astype(BF)
            act_ref[0, block, :] = act
            gp_ref[0, block, :] = gp
            sums += jnp.sum(gp.astype(F32), 0, keepdims=True)
            out_ref[block, :] += mm(act, down_ref[step])
            gn_ref[block, :] += mm(gp, up_ref[step], NT)
        col_ref[0] = sums

    ins = [core, pieces[0].offsets, pieces[1].offsets, normed, grad_rows, vec, result_in]
    specs = [
        *[smem_spec()] * 3, whole((rows, model)), whole((rows, model)),
        whole((16, model)), whole((rows, model)),
    ]
    if not first:
        ins.append(grad_in)
        specs.append(whole((rows, model)))
    return pl.pallas_call(
        kernel,
        grid=(2,),
        in_specs=specs + [any_spec()] * (sum(sizes) + len(tokens_in)),
        out_specs=[
            whole((rows, model)),
            whole((rows, model)),
            pl.BlockSpec((1, rows, hidden), lambda s: (s, 0, 0)),
            pl.BlockSpec((1, rows, hidden), lambda s: (s, 0, 0)),
            pl.BlockSpec((1, 1, hidden), lambda s: (s, 0, 0)),
        ],
        out_shape=[
            jax.ShapeDtypeStruct((rows, model), F32),
            jax.ShapeDtypeStruct((rows, model), F32),
            jax.ShapeDtypeStruct((2, rows, hidden), BF),
            jax.ShapeDtypeStruct((2, rows, hidden), BF),
            jax.ShapeDtypeStruct((2, 1, hidden), F32),
        ],
        scratch_shapes=[
            VMEM((2, model, hidden), BF),
            VMEM((2, hidden, model), BF),
            pltpu.SemaphoreType.DMA((2 * sum(per),)),
        ],
        compiler_params=params(),
        cost_estimate=cost(6.4e9, 2e7),
        name="feed_forward",
    )(*ins, *pieces[0].buffers, *pieces[1].buffers, *tokens_in)


def outer_products(pairs, offsets, rows, extra=None, tokens_in=()):
    counts = [len(lefts) for lefts, _ in pairs]
    slots = offsets.shape[0]
    half = max(slots // 2, 1)
    wide = pairs[0][1][0][0].shape[-1]
    tall = pairs[0][0][0][0].shape[-1]
    tail = 0 if extra is None else 32
    n_mat = len(pairs)
    flat, where = [], []
    for lefts, rights in pairs:
        places = []
        for one, lead in (*lefts, *rights):
            match = [i for i, known in enumerate(flat) if known is one]
            if not match:
                flat.append(one)
                match = [len(flat) - 1]
            places.append((match[0], lead))
        where.append(places)

    def kernel(offs_ref, *rest):
        ins = rest[: len(flat)]
        rest = rest[len(flat) :]
        if tail:
            vec_ref, table_ref, rest = rest[0], rest[1], rest[2:]
        rest = rest[len(tokens_in) :]
        keep_ref = rest[0]
        send_ref = rest[1] if slots > 1 else None
        w_ref, tail_ref, sems = rest[-3:]
        copies = [[] for _ in range(n_mat + 1)]
        count = 0
        for s in range(slots):
            at = pl.multiple_of(offs_ref[s], 16)
            out_ref = (keep_ref if s < half else send_ref).at[s % half]
            for m in range(n_mat):
                copies[m].append(
                    pltpu.make_async_copy(
                        w_ref.at[m, pl.ds(at, rows)], out_ref.at[pl.ds(m * rows, rows)], sems.at[count]
                    )
                )
                count += 1
            if tail:
                copies[n_mat].append(
                    pltpu.make_async_copy(
                        tail_ref.at[s], out_ref.at[pl.ds(n_mat * rows, tail)], sems.at[count]
                    )
                )
                count += 1
        if tail:
            model = vec_ref.shape[1]
            table = table_ref[...]
            for s in range(slots):
                small = pltpu.roll(vec_ref[...], lax.rem(model - offs_ref[s], model), 1)[:, :TILE]
                tail_ref[s] = jnp.concatenate(
                    [jnp.concatenate([small, table[:16, TILE:]], 1), table[16:]], 0
                ).astype(BF)
            for c in copies[n_mat]:
                c.start()
        for m in range(n_mat):
            places = where[m]
            total = 0.0
            for i in range(counts[m]):
                left, right = (
                    ins[at][...] if lead is None else ins[at][lead]
                    for at, lead in (places[i], places[counts[m] + i])
                )
                total = total + mm(left, right, TN)
            w_ref[m] = total.astype(BF)
            for c in copies[m]:
                c.start()
        for group in copies:
            for c in group:
                c.wait()

    ins = [offsets, *flat]
    specs = [smem_spec(), *[whole(one.shape) for one in flat]]
    if tail:
        ins += list(extra)
        specs += [whole(one.shape) for one in extra]
    ins += list(tokens_in)
    specs += [any_spec()] * len(tokens_in)
    shape = jax.ShapeDtypeStruct((half, n_mat * rows + tail, wide), BF)
    n_out = 2 if slots > 1 else 1
    return pl.pallas_call(
        kernel,
        grid=(1,),
        in_specs=specs,
        out_specs=[any_spec()] * n_out,
        out_shape=[shape] * n_out,
        scratch_shapes=[
            VMEM((n_mat, tall, wide), BF),
            VMEM((slots, 32, wide), BF),
            pltpu.SemaphoreType.DMA((slots * (n_mat + 1),)),
        ],
        compiler_params=params(),
        cost_estimate=cost(2e9, 1e7),
        name="outer_products",
    )(*ins)


def norm_back(x, up, gain):
    xhat, scale = row_norm(x)
    e = up * gain
    grad = scale * (e - jnp.mean(e, -1, keepdims=True) - xhat * jnp.mean(e * xhat, -1, keepdims=True))
    return grad, up * xhat


def second_norm_back(core, residual, result, grad_normed, grad_rows, pieces, vec, lengths, tokens_in=()):
    rows, model = residual.shape
    width = model // 2
    sizes = [len(p.buffers) for p in pieces]
    per = [p.slots for p in pieces]

    def kernel(core_ref, len_ref, offs0, offs1, res_ref, out_in, gn_ref, gr_ref, vec_ref, *rest):
        bufs = [rest[: sizes[0]], rest[sizes[0] : sum(sizes)]]
        out_ref, gres_ref, gb_ref, gm0_ref, gm1_ref, sums_ref, w_ref, sems = rest[
            sum(sizes) + len(tokens_in) :
        ]
        copies = []
        for h, offs in enumerate((offs0, offs1)):
            copies += load_copies(
                bufs[h], offs, pieces[h].rows, [(3 * pieces[h].rows, w_ref.at[h])],
                sems.at[pl.ds(h * per[0], per[h])],
            )
        for c in copies:
            c.start()
        totals = [jnp.zeros((1, model), F32) for _ in range(4)]
        for r in range(0, rows, CHUNK):
            block = slice(r, r + CHUNK)
            row = lax.broadcasted_iota(jnp.int32, (CHUNK, 1), 0) + r
            out_ref[block, :] = jnp.where(row < len_ref[0], out_in[block, :], 0.0).astype(BF)
            up = gn_ref[block, :]
            grad, gain_terms = norm_back(res_ref[block, :], up, vec_ref[5:6, :])
            gr = gr_ref[block, :].astype(F32)
            grad = gr + grad
            low = grad.astype(BF)
            gres_ref[block, :] = grad
            gb_ref[block, :] = low
            for i, terms in enumerate((gain_terms, up, low.astype(F32), gr)):
                totals[i] += jnp.sum(terms, 0, keepdims=True)
        sums_ref[...] = jnp.concatenate(totals + [jnp.zeros((4, model), F32)], 0)
        for c in copies:
            c.wait()
        for h, gm_ref in enumerate((gm0_ref, gm1_ref)):
            feats = pl.ds(pl.multiple_of((core_ref[0] ^ h) * width, TILE), width)
            acc = 0.0
            for g in range(2):
                cols = pl.ds(pl.multiple_of((core_ref[0] ^ g) * width, TILE), width)
                acc = acc + mm(gb_ref[:, cols], w_ref[g, feats, :], NT)
            gm_ref[...] = acc.astype(BF)

    return pl.pallas_call(
        kernel,
        grid=(1,),
        in_specs=[
            *[smem_spec()] * 4,
            *[whole((rows, model))] * 4,
            whole((16, model)),
            *[any_spec()] * (sum(sizes) + len(tokens_in)),
        ],
        out_specs=[
            *[whole((rows, model))] * 3,
            *[whole((rows, width))] * 2,
            whole((8, model)),
        ],
        out_shape=[
            jax.ShapeDtypeStruct((rows, model), BF),
            jax.ShapeDtypeStruct((rows, model), F32),
            jax.ShapeDtypeStruct((rows, model), BF),
            jax.ShapeDtypeStruct((rows, width), BF),
            jax.ShapeDtypeStruct((rows, width), BF),
            jax.ShapeDtypeStruct((8, model), F32),
        ],
        scratch_shapes=[VMEM((2, model, width), BF), pltpu.SemaphoreType.DMA((sum(per),))],
        compiler_params=params(),
        cost_estimate=cost(6e8, 1e7),
        name="second_norm_back",
    )(
        core, lengths, pieces[0].offsets, pieces[1].offsets, residual, result, grad_normed, grad_rows,
        vec, *pieces[0].buffers, *pieces[1].buffers, *tokens_in,
    )


def attention_backward(joined, probs, mixed, grad_mixed, head_size, tokens_in=()):
    _, rows, width = joined.shape
    heads = width // head_size
    pairs = width // TILE
    per = TILE // head_size
    tiles = 2 * (rows // TILE) - 1
    span = 2 * rows
    scale = head_size**-0.5

    def kernel(joined_ref, p_ref, mixed_ref, gm_ref, *rest):
        out_ref, diag_ref, gp_ref, ds_ref, acc_ref = rest[len(tokens_in) :]
        q, k, v = joined_ref[0], joined_ref[1], joined_ref[2]
        gm = gm_ref[...]
        lane = lax.broadcasted_iota(jnp.int32, (1, TILE), 1)
        dots = gm.astype(F32) * mixed_ref[...].astype(F32)
        q_t, gm_t = q.T, gm.T
        dq, dk, dv = [], [], []
        for e in range(per):
            mine = (lane >= e * head_size) & (lane < (e + 1) * head_size)
            feats = slice(e * head_size, (e + 1) * head_size)
            delta = jnp.sum(jnp.where(mine, dots, 0.0), -1, keepdims=True)
            gp_ref[e] = mm(jnp.where(mine, gm, jnp.zeros_like(gm)), v, NT)
            acc_ref[...] = jnp.zeros_like(acc_ref)
            for r in range(0, rows, CHUNK):
                block, sub = r // TILE, r % TILE
                ds = p_ref[e, r : r + CHUNK, :].astype(F32) * (
                    gp_ref[e, r : r + CHUNK, :] - delta[r : r + CHUNK, :]
                )
                ds_ref[e, r : r + CHUNK, :] = ds.astype(BF)
                for j in range(rows // TILE):
                    acc_ref[j - block + rows // TILE - 1, sub : sub + CHUNK, :] += ds[
                        :, j * TILE : (j + 1) * TILE
                    ]
            dq.append(jnp.where(mine, mm(ds_ref[e], k), 0.0))
            dk.append(mm(q_t[feats, :], ds_ref[e]))
            dv.append(mm(gm_t[feats, :], p_ref[e]))
            total = jnp.zeros((8, span), F32)
            for g in range(TILE // 8):
                strip = jnp.concatenate(
                    [jnp.zeros((8, TILE), F32)]
                    + [acc_ref[d, 8 * g : 8 * g + 8, :] for d in range(tiles)],
                    1,
                )
                total += pltpu.roll(strip, (span - 8 * g) % span, 1) if g else strip
            line = total[0:1]
            for i in range(1, 8):
                line = line + pltpu.roll(total[i : i + 1], span - i, 1)
            diag_ref[e] = line
        out_ref[0] = (functools.reduce(lambda a, b: a + b, dq) * scale).astype(BF)
        out_ref[1] = (jnp.concatenate(dk, 0) * scale).T.astype(BF)
        out_ref[2] = jnp.concatenate(dv, 0).T.astype(BF)

    return pl.pallas_call(
        kernel,
        grid=(pairs,),
        in_specs=[
            pl.BlockSpec((3, rows, TILE), lambda p: (0, 0, p)),
            pl.BlockSpec((per, rows, rows), lambda p: (p, 0, 0)),
            pl.BlockSpec((rows, TILE), lambda p: (0, p)),
            pl.BlockSpec((rows, TILE), lambda p: (0, p)),
            *[any_spec()] * len(tokens_in),
        ],
        out_specs=[
            pl.BlockSpec((3, rows, TILE), lambda p: (0, 0, p)),
            pl.BlockSpec((per, 1, span), lambda p: (p, 0, 0)),
        ],
        out_shape=[
            jax.ShapeDtypeStruct((3, rows, width), BF),
            jax.ShapeDtypeStruct((heads, 1, span), F32),
        ],
        scratch_shapes=[
            VMEM((per, rows, rows), F32),
            VMEM((per, rows, rows), BF),
            VMEM((tiles, TILE, TILE), F32),
        ],
        compiler_params=params(),
        cost_estimate=cost(4e9, 1e7),
        name="attention_backward",
    )(joined, probs, mixed, grad_mixed, *tokens_in)


def first_norm_back(core, grads, tokens, grad_residual, vec, pieces, sums_second, sums_up, diags, chosen, tokens_in=()):
    rows, model = tokens.shape
    width = model // 2
    heads = diags[0].shape[0]
    number, span = chosen.shape
    sizes = [len(p.buffers) for p in pieces]
    per = [p.slots for p in pieces]

    def kernel(core_ref, offs0, offs1, d0_ref, d1_ref, x_ref, gres_ref, vec_ref, s2_ref, u0_ref, u1_ref, t0_ref,
               t1_ref, chosen_ref, *rest):
        bufs = [rest[: sizes[0]], rest[sizes[0] : sum(sizes)]]
        gx_ref, sums_ref, table_ref, w_ref, acc_ref, sems = rest[sum(sizes) + len(tokens_in) :]
        groups = []
        for h, offs in enumerate((offs0, offs1)):
            groups.append(
                load_copies(
                    bufs[h], offs, pieces[h].rows,
                    [(j * pieces[h].rows, w_ref.at[h, j]) for j in range(3)],
                    sems.at[pl.ds(3 * h * per[0], 3 * per[h])],
                )
            )
        for c in groups[0] + groups[1]:
            c.start()
        straight = core_ref[0] == 0

        def ordered(a, b):
            return [jnp.where(straight, a, b), jnp.where(straight, b, a)]

        diag = jnp.concatenate(ordered(t0_ref[:, 0, :], t1_ref[:, 0, :]) + [jnp.zeros((16 - 2 * heads, span), F32)], 0)
        table, left = 0.0, diag
        for _ in range(3):
            part = left.astype(BF)
            table = table + mm(part, chosen_ref[...], NT)
            left = left - part.astype(F32)
        table = jnp.concatenate([table, jnp.zeros((16, 2 * width - number), F32)], 1)
        table_ref[...] = jnp.concatenate(
            [
                jnp.concatenate([jnp.zeros((16, TILE), F32), table[:, width : 2 * width - TILE]], 1),
                table[:, :width],
            ],
            0,
        )
        columns = [
            jnp.concatenate(
                ordered(*(jnp.sum(d_ref[j].astype(F32), 0, keepdims=True) for d_ref in (d0_ref, d1_ref))), 1
            )
            for j in (0, 2)
        ]
        for c in groups[0] + groups[1]:
            c.wait()
        acc = 0.0
        for h, d_ref in enumerate((d0_ref, d1_ref)):
            for j in range(3):
                acc = acc + mm(d_ref[j], w_ref[h, j], NT)
        acc_ref[...] = acc
        totals = [jnp.zeros((1, model), F32) for _ in range(2)]
        for r in range(0, rows, CHUNK):
            block = slice(r, r + CHUNK)
            up = acc_ref[block, :]
            grad, gain_terms = norm_back(x_ref[block, :].astype(F32), up, vec_ref[0:1, :])
            gx_ref[block, :] = gres_ref[block, :] + grad
            totals[0] += jnp.sum(gain_terms, 0, keepdims=True)
            totals[1] += jnp.sum(up, 0, keepdims=True)
        sums_ref[...] = jnp.concatenate(
            totals
            + columns
            + [s2_ref[2:3, :], s2_ref[0:1, :], s2_ref[1:2, :], s2_ref[3:4, :]]
            + ordered(u0_ref[0], u0_ref[1])
            + ordered(u1_ref[0], u1_ref[1])
            + [jnp.zeros((4, model), F32)],
            0,
        )

    return pl.pallas_call(
        kernel,
        grid=(1,),
        in_specs=[
            *[smem_spec()] * 3,
            whole((3, rows, width)),
            whole((3, rows, width)),
            whole((rows, model)),
            whole((rows, model)),
            whole((16, model)),
            whole((8, model)),
            whole((2, 1, model)),
            whole((2, 1, model)),
            whole((heads, 1, span)),
            whole((heads, 1, span)),
            whole((number, span)),
            *[any_spec()] * (sum(sizes) + len(tokens_in)),
        ],
        out_specs=[whole((rows, model)), whole((16, model)), whole((32, width))],
        out_shape=[
            jax.ShapeDtypeStruct((rows, model), F32),
            jax.ShapeDtypeStruct((16, model), F32),
            jax.ShapeDtypeStruct((32, width), F32),
        ],
        scratch_shapes=[
            VMEM((2, 3, model, width), BF),
            VMEM((rows, model), F32),
            pltpu.SemaphoreType.DMA((3 * sum(per),)),
        ],
        compiler_params=params(),
        cost_estimate=cost(2e9, 1e7),
        name="first_norm_back",
    )(
        core, pieces[0].offsets, pieces[1].offsets, grads[0], grads[1], tokens, grad_residual, vec, sums_second,
        *sums_up, *diags, chosen, *pieces[0].buffers, *pieces[1].buffers, *tokens_in,
    )


def pack_blocks(core, qkv, out, up):
    local, model = out.shape
    width = model // 2
    n_up = up.shape[1]
    owners = n_up // (4 * model)
    del owners
    unit = local * 2
    chips = n_up // (4 * unit)

    def kernel(core_ref, qkv_ref, out_ref, up_ref, a0_ref, a1_ref, u0_ref, u1_ref):
        core_at = core_ref[0]
        for h, (a_ref, u_ref) in enumerate(((a0_ref, u0_ref), (a1_ref, u1_ref))):
            at = (core_at ^ h) * width
            for j in range(3):
                a_ref[j] = qkv_ref[:, pl.ds(pl.multiple_of(j * model + at, TILE), width)]
            a_ref[3] = out_ref[:, pl.ds(pl.multiple_of(at, TILE), width)]
        for f in range(2):
            by_core = []
            for c in range(2):
                by_core.append(
                    jnp.concatenate(
                        [
                            up_ref[:, ((2 * chip + c) * 2 + f) * unit : ((2 * chip + c) * 2 + f + 1) * unit]
                            for chip in range(chips)
                        ],
                        1,
                    ).astype(F32)
                )
            first = core_at == 0
            u0_ref[f] = jnp.where(first, by_core[0], by_core[1]).astype(BF)
            u1_ref[f] = jnp.where(first, by_core[1], by_core[0]).astype(BF)

    shapes = [jax.ShapeDtypeStruct((4, local, width), BF)] * 2 + [jax.ShapeDtypeStruct((2, local, model), BF)] * 2
    return pl.pallas_call(
        kernel,
        grid=(1,),
        in_specs=[smem_spec(), whole(qkv.shape), whole(out.shape), whole(up.shape)],
        out_specs=[whole(one.shape) for one in shapes],
        out_shape=shapes,
        compiler_params=params(),
        name="pack_blocks",
    )(core, qkv, out, up)


def ordered_rows(core_at, mine, theirs):
    first = core_at == 0
    a, b = mine.astype(F32), theirs.astype(F32)
    return jnp.concatenate([jnp.where(first, a, b), jnp.where(first, b, a)], 0)


def merge_attention(core, mine, theirs, small, small_theirs):
    count, local, width = mine.shape

    def kernel(core_ref, a_ref, b_ref, s_ref, t_ref, out_ref):
        for j in range(count):
            out_ref[2 * local * j : 2 * local * (j + 1), :] = ordered_rows(core_ref[0], a_ref[j], b_ref[j]).astype(BF)
        vec = s_ref[...].astype(F32) + t_ref[...].astype(F32)
        out_ref[2 * local * count :, :] = jnp.concatenate([vec, jnp.zeros((16, width - TILE), F32)], 1).astype(BF)

    return pl.pallas_call(
        kernel,
        grid=(1,),
        in_specs=[smem_spec(), *[whole(mine.shape)] * 2, *[whole(small.shape)] * 2],
        out_specs=whole((2 * local * count + 16, width)),
        out_shape=jax.ShapeDtypeStruct((2 * local * count + 16, width), BF),
        compiler_params=params(),
        name="merge_attention",
    )(core, mine, theirs, small, small_theirs)


def merge_feed_forward(core, mine, theirs, down):
    _, local, model = mine.shape
    unit = 2 * local

    def kernel(core_ref, a_ref, b_ref, d_ref, *outs):
        for f in range(2):
            outs[f][:unit, :] = ordered_rows(core_ref[0], a_ref[f], b_ref[f]).astype(BF)
            outs[f][unit:, :] = d_ref[f * unit : (f + 1) * unit, :]

    shape = jax.ShapeDtypeStruct((2 * unit, model), BF)
    return pl.pallas_call(
        kernel,
        grid=(1,),
        in_specs=[smem_spec(), *[whole(mine.shape)] * 2, whole(down.shape)],
        out_specs=[whole(shape.shape)] * 2,
        out_shape=[shape] * 2,
        compiler_params=params(),
        name="merge_feed_forward",
    )(core, mine, theirs, down)


def pair_sum(refs):
    parts = [ref[...].astype(F32) for ref in refs]
    while len(parts) > 1:
        half = len(parts) // 2
        parts = [parts[i] + parts[i + half] for i in range(half)]
    return parts[0]


def rows_of(total, first, core_at, local, mine):
    a, b = total[first : first + local], total[first + local : first + 2 * local]
    return jnp.where((core_at == 0) == mine, a, b)


def total_attention(core, parts, local):
    tall, width = parts[0].shape
    tail = tall - 8 * local

    def kernel(core_ref, *refs):
        ins, (mine_ref, sent_ref, tail_ref) = refs[: len(parts)], refs[len(parts) :]
        total = pair_sum(ins)
        for j in range(4):
            mine_ref[j] = rows_of(total, 2 * local * j, core_ref[0], local, True)
            sent_ref[j] = rows_of(total, 2 * local * j, core_ref[0], local, False).astype(BF)
        tail_ref[...] = total[8 * local :].astype(BF)

    shapes = [
        jax.ShapeDtypeStruct((4, local, width), F32),
        jax.ShapeDtypeStruct((4, local, width), BF),
        jax.ShapeDtypeStruct((tail, width), BF),
    ]
    return pl.pallas_call(
        kernel,
        grid=(1,),
        in_specs=[smem_spec(), *[whole(one.shape) for one in parts]],
        out_specs=[whole(one.shape) for one in shapes],
        out_shape=shapes,
        compiler_params=params(),
        name="total_attention",
    )(core, *parts)


def finish_attention(core, mine, theirs, tail, tail_theirs, heads, number):
    _, local, width = mine.shape
    model = 2 * width

    def kernel(core_ref, a_ref, b_ref, s_ref, t_ref, qkv_ref, out_ref, small_ref, table_ref):
        at = core_ref[0]
        for h, ref in enumerate((a_ref, b_ref)):
            for j in range(3):
                cols = pl.ds(pl.multiple_of(j * model + (at ^ h) * width, TILE), width)
                qkv_ref[:, cols] = ref[j].astype(F32)
            out_ref[:, pl.ds(pl.multiple_of((at ^ h) * width, TILE), width)] = ref[3].astype(F32)
        total = s_ref[...].astype(F32) + t_ref[...].astype(F32)
        small = total[:16, :TILE]
        moved = pltpu.roll(small, TILE - local, 1)
        small_ref[:8, :] = jnp.where(at == 0, small[:8], moved[:8])
        small_ref[8:, :] = small[8:]
        table_ref[...] = jnp.concatenate([total[16:, :], total[:16, TILE : TILE + number - width]], 1)[:heads]

    shapes = [
        jax.ShapeDtypeStruct((local, 3 * model), F32),
        jax.ShapeDtypeStruct((local, model), F32),
        jax.ShapeDtypeStruct((16, TILE), F32),
        jax.ShapeDtypeStruct((heads, number), F32),
    ]
    return pl.pallas_call(
        kernel,
        grid=(1,),
        in_specs=[smem_spec(), *[whole(one.shape) for one in (mine, theirs, tail, tail_theirs)]],
        out_specs=[whole(one.shape) for one in shapes],
        out_shape=shapes,
        compiler_params=params(),
        name="finish_attention",
    )(core, mine, theirs, tail, tail_theirs)


def total_feed_forward(core, parts, local):
    _, model = parts[0].shape
    unit = 2 * local

    def kernel(core_ref, *refs):
        ins, (mine_ref, sent_ref, down_ref) = refs[: len(parts)], refs[len(parts) :]
        total = pair_sum(ins)
        mine_ref[...] = rows_of(total, 0, core_ref[0], local, True)
        sent_ref[...] = rows_of(total, 0, core_ref[0], local, False).astype(BF)
        down_ref[...] = total[unit:]

    shapes = [
        jax.ShapeDtypeStruct((local, model), F32),
        jax.ShapeDtypeStruct((local, model), BF),
        jax.ShapeDtypeStruct((unit, model), F32),
    ]
    return pl.pallas_call(
        kernel,
        grid=(1,),
        in_specs=[smem_spec(), *[whole(one.shape) for one in parts]],
        out_specs=[whole(one.shape) for one in shapes],
        out_shape=shapes,
        compiler_params=params(),
        name="total_feed_forward",
    )(core, *parts)


def finish_feed_forward(core, mine, theirs, downs):
    local, model = mine[0].shape
    unit = 2 * local
    chips = model // unit

    def kernel(core_ref, m0, m1, t0, t1, d0, d1, up_ref, down_ref):
        first = core_ref[0] == 0
        by = []
        for a, b in ((m0, t0), (m1, t1)):
            a, b = a[...], b[...].astype(F32)
            by.append((jnp.where(first, a, b), jnp.where(first, b, a)))
        up_ref[...] = jnp.concatenate(
            [
                by[f][c][:, chip * unit : (chip + 1) * unit]
                for chip in range(chips)
                for c in range(2)
                for f in range(2)
            ],
            1,
        )
        down_ref[:unit, :] = d0[...]
        down_ref[unit:, :] = d1[...]

    shapes = [jax.ShapeDtypeStruct((local, 4 * model), F32), jax.ShapeDtypeStruct((2 * unit, model), F32)]
    ins = (*mine, *theirs, *downs)
    return pl.pallas_call(
        kernel,
        grid=(1,),
        in_specs=[smem_spec(), *[whole(one.shape) for one in ins]],
        out_specs=[whole(one.shape) for one in shapes],
        out_shape=shapes,
        compiler_params=params(),
        name="finish_feed_forward",
    )(core, *ins)


VECTORS = 8


class GridLinks:
    pair = True

    def __init__(self, sizes, model):
        self.ny, self.nz, self.nx = sizes
        self.chips = self.ny * self.nz * self.nx
        self.rows = model // self.chips
        dp, inner = lax.axis_index("dp"), lax.axis_index("fsdp")
        self.core = inner % 2
        chip = inner // 2
        self.place = (dp, chip // self.nx, chip % self.nx)
        self.gather_offsets = [self._offsets(self.core ^ h, -1) for h in range(2)]
        self.scatter_offsets = self._offsets(self.core, 1)

    def _offsets(self, core, sign):
        y, z, x = self.place
        out = []
        for r1 in range(2):
            for r2 in range(2):
                for k in range(self.nz):
                    fy = jnp.where(core == 0, r1, r2)
                    fx = jnp.where(core == 0, r2, r1)
                    zz = (z + sign * k + self.nz) % self.nz
                    out.append(((y ^ fy) * self.nz + zz) * self.nx + (x ^ fx))
        return (jnp.stack(out) * self.rows).astype(jnp.int32)

    def _send(self, value, move):
        pairs = []
        for y in range(self.ny):
            for z in range(self.nz):
                for x in range(self.nx):
                    for c in range(2):
                        source = ((y * self.nz + z) * self.nx + x) * 2 + c
                        ty, tz, tx, tc = move(y, z, x, c)
                        pairs.append((source, ((ty * self.nz + tz) * self.nx + tx) * 2 + tc))
        return lax.ppermute(value, AXES, pairs)

    def swap(self, value):
        return self._send(value, lambda y, z, x, c: (y, z, x, 1 - c))

    def along_z(self, value, k):
        return self._send(value, lambda y, z, x, c: (y, (z + k) % self.nz, x, c))

    def x_first(self, value):
        return self._send(value, lambda y, z, x, c: (y, z, 1 - x, c) if c == 0 else (1 - y, z, x, c))

    def y_first(self, value):
        return self._send(value, lambda y, z, x, c: (y, z, 1 - x, c) if c == 1 else (1 - y, z, x, c))

    def gather(self, piece):
        parts = [piece] + [self.along_z(piece, k) for k in range(1, self.nz)]
        near = jnp.stack(parts)
        second = self.x_first(near)
        third = self.y_first(near)
        fourth = self.y_first(second)
        own = [near, second, third, fourth]
        other = [self.swap(one) for one in own]
        return (
            Pieces(own, self.gather_offsets[0], self.rows),
            Pieces(other, self.gather_offsets[1], self.rows),
        )

    def scatter(self, keep, send):
        n = self.nz

        def add(a, b):
            return (a.astype(F32) + b.astype(F32)).astype(BF)

        moved = self.y_first(send)
        send, keep = add(keep[n:], moved[n:]), add(keep[:n], moved[:n])
        moved = self.x_first(send)
        sums = [add(keep[k], moved[k]) for k in range(n)]
        return [sums[0]] + [self.along_z(sums[k], k) for k in range(1, n)]


def on_device(
    links,
    tokens,
    lengths,
    buckets,
    ln1_gain,
    ln1_bias,
    qkv_weight,
    q_bias,
    v_bias,
    out_weight,
    out_bias,
    rel_table,
    ln2_gain,
    ln2_bias,
    up_weight,
    up_bias,
    down_weight,
    down_bias,
    cotangent,
):
    rows, model = tokens.shape
    heads, number = rel_table.shape
    head_size = model // heads
    width = model // 2
    local = qkv_weight.shape[0]
    core, chips = links.core, links.chips
    core_arg = core.astype(jnp.int32).reshape(1)

    n_first = jnp.stack([ln1_gain, ln1_bias, q_bias, v_bias, out_bias, ln2_gain, ln2_bias, down_bias])
    spread = jnp.where(
        core == 0, jnp.pad(n_first, ((0, 0), (0, TILE - local))), jnp.pad(n_first, ((0, 0), (local, TILE - 2 * local)))
    )
    halves = jnp.pad(up_bias.reshape(2, 1, 2 * local), ((0, 0), (0, 0), (0, TILE - 2 * local)))
    blank = jnp.zeros_like(halves)
    halves = jnp.where(core == 0, jnp.concatenate([halves, blank], 1), jnp.concatenate([blank, halves], 1))
    small = jnp.concatenate([spread, halves.reshape(4, TILE), jnp.zeros((4, TILE), BF)], 0)
    small_theirs = links.swap(small)
    a_mine, a_sent, u_mine, u_sent = pack_blocks(core_arg, qkv_weight, out_weight, up_weight)
    a_theirs = links.swap(a_sent)
    u_theirs = links.swap(u_sent)
    a_piece = merge_attention(core_arg, a_mine, a_theirs, small, small_theirs)
    f_pieces = merge_feed_forward(core_arg, u_mine, u_theirs, down_weight)

    grad_rows = jnp.where(
        (jnp.arange(rows, dtype=jnp.int32) < lengths[0])[:, None], cotangent, jnp.zeros_like(cotangent)
    )
    grad_rows_other = links.swap(grad_rows)

    a_own, a_other = links.gather(a_piece)

    line = jnp.concatenate([buckets[0, rows - 1, :1], buckets[0, rows - 1, :], buckets[0, 0, 1:]])
    chosen = (jnp.arange(number, dtype=jnp.int32)[:, None] == line[None, :]).astype(BF)
    half_heads = heads // 2
    table_rel = jnp.where(
        core == 0, rel_table, jnp.concatenate([rel_table[half_heads:], rel_table[:half_heads]], 0)
    )
    curve = jnp.dot(table_rel, chosen, preferred_element_type=F32)
    tiles = bias_tiles(curve)

    normed, vec, joined0, mixed0, probs0 = attention_forward(
        0, core_arg, tokens, None, None, a_own, tiles, lengths, head_size
    )
    normed_other = links.swap(normed)
    joined1, mixed1, probs1 = attention_forward(
        1, core_arg, tokens, normed, vec, a_other, tiles, lengths, head_size
    )
    f_own, f_other = zip(*[links.gather(piece) for piece in f_pieces])
    residual, normed2 = project_out(core_arg, (mixed0, mixed1), tokens, (a_own, a_other), vec)
    normed2_other = links.swap(normed2)

    result, grad_n2 = residual, None
    up_sums, ffn = [], []
    for f in range(2):
        result, grad_n2, active, grad_pre, sums = feed_forward(
            f, core_arg, normed2, grad_rows, vec, (f_own[f], f_other[f]), result, grad_n2
        )
        up_sums.append(sums)
        active_other = links.swap(active[1])
        pre_other = links.swap(grad_pre[1])
        keep, send = outer_products(
            [
                ([(normed2, None), (normed2_other, None)], [(grad_pre, 0), (pre_other, None)]),
                ([(active, 0), (active_other, None)], [(grad_rows, None), (grad_rows_other, None)]),
            ],
            links.scatter_offsets,
            links.rows,
        )
        ffn.append(total_feed_forward(core_arg, links.scatter(keep, send), local))

    output, grad_res, grad_branch, gm0, gm1, sums2 = second_norm_back(
        core_arg, residual, result, grad_n2, grad_rows, (a_own, a_other), vec, lengths
    )
    branch_cols = lax.dynamic_slice_in_dim(grad_branch, core * width, width, 1)
    branch_theirs = lax.dynamic_slice_in_dim(grad_branch, (1 - core) * width, width, 1)
    branch_other = links.swap(branch_theirs)

    first = core == 0
    mixed = jnp.concatenate([jnp.where(first, mixed0, mixed1), jnp.where(first, mixed1, mixed0)], 1)
    mixed_other = links.swap(mixed)
    dj1, diag1 = attention_backward(joined1, probs1, mixed1, gm1, head_size)
    dj_other = links.swap(dj1)
    dj0, diag0 = attention_backward(joined0, probs0, mixed0, gm0, head_size)

    input_grad, vec_grads, table_grad = first_norm_back(
        core_arg, (dj0, dj1), tokens, grad_res, vec, (a_own, a_other), sums2, up_sums, (diag0, diag1), chosen
    )
    keep, send = outer_products(
        [([(normed, None), (normed_other, None)], [(dj0, j), (dj_other, j)]) for j in range(3)]
        + [([(mixed, None), (mixed_other, None)], [(branch_cols, None), (branch_other, None)])],
        links.scatter_offsets,
        links.rows,
        (vec_grads, table_grad),
    )
    mine, sent, tail = total_attention(core_arg, links.scatter(keep, send), local)
    theirs, tail_theirs = links.swap(sent), links.swap(tail)
    grad_qkv, grad_out, small, grad_table = finish_attention(
        core_arg, mine, theirs, tail, tail_theirs, heads, number
    )
    ups = [links.swap(one[1]) for one in ffn]
    grad_up, grad_down = finish_feed_forward(
        core_arg, [one[0] for one in ffn], ups, [one[2] for one in ffn]
    )
    small_grads = [small[i, :local] for i in range(VECTORS)]
    unit = 2 * local
    halves = small[8:12, :].reshape(2, 2, TILE)
    grad_up_bias = lax.dynamic_index_in_dim(halves, core, 1, keepdims=False)[:, :unit].reshape(2 * unit)

    return (
        output,
        input_grad,
        small_grads[0],
        small_grads[1],
        grad_qkv,
        small_grads[2],
        small_grads[3],
        grad_out,
        small_grads[4],
        grad_table,
        small_grads[5],
        small_grads[6],
        grad_up,
        grad_up_bias,
        grad_down,
        small_grads[7],
    )


def on_any_mesh(
    tokens,
    lengths,
    buckets,
    ln1_gain,
    ln1_bias,
    qkv_weight,
    q_bias,
    v_bias,
    out_weight,
    out_bias,
    rel_table,
    ln2_gain,
    ln2_bias,
    up_weight,
    up_bias,
    down_weight,
    down_bias,
    cotangent,
):
    rows, model = tokens.shape
    heads, number = rel_table.shape
    head_size = model // heads
    width = model // 2
    local = qkv_weight.shape[0]
    hidden = up_weight.shape[1]
    core = jnp.zeros((1,), jnp.int32)
    offsets = jnp.zeros((1,), jnp.int32)

    def gathered(x):
        return lax.all_gather(x, AXES, axis=0, tiled=True)

    def scattered(x):
        return lax.psum_scatter(x, AXES, scatter_dimension=0, tiled=True)

    vectors = [ln1_gain, ln1_bias, q_bias, v_bias, out_bias, ln2_gain, ln2_bias, down_bias]
    unit = up_bias.shape[0]
    small = gathered(jnp.concatenate([*vectors, up_bias])[None, :])
    wide = [small[:, i * local : (i + 1) * local].reshape(1, model) for i in range(VECTORS)]
    ub = small[:, VECTORS * local :].reshape(2, 2, model).transpose(1, 0, 2).reshape(4, model)
    del unit
    vec = jnp.concatenate([*wide, ub, jnp.zeros((4, model), BF)], 0).astype(F32)
    attn = gathered(jnp.concatenate([qkv_weight, out_weight], 1))
    up, down = gathered(up_weight), gathered(down_weight)
    a_pieces = tuple(
        Pieces(
            [jnp.concatenate([attn[:, j * model + h * width : j * model + (h + 1) * width] for j in range(4)], 0)[None]],
            offsets,
            model,
        )
        for h in range(2)
    )

    def chunk(f, h):
        at = (2 * h + f) * model
        return Pieces(
            [jnp.concatenate([up[:, at : at + model], down[at : at + model]], 0)[None]], offsets, model
        )

    grad_rows = jnp.where(
        (jnp.arange(rows, dtype=jnp.int32) < lengths[0])[:, None], cotangent, jnp.zeros_like(cotangent)
    )
    line = jnp.concatenate([buckets[0, rows - 1, :1], buckets[0, rows - 1, :], buckets[0, 0, 1:]])
    chosen = (jnp.arange(number, dtype=jnp.int32)[:, None] == line[None, :]).astype(BF)
    tiles = bias_tiles(jnp.dot(rel_table, chosen, preferred_element_type=F32))
    normed, joined0, mixed0, probs0 = attention_forward(
        0, core, tokens, None, vec, a_pieces[0], tiles, lengths, head_size
    )
    joined1, mixed1, probs1 = attention_forward(
        1, core, tokens, normed, vec, a_pieces[1], tiles, lengths, head_size
    )
    residual, normed2 = project_out(core, (mixed0, mixed1), tokens, a_pieces, vec)
    result, grad_n2 = residual, None
    up_sums, ups, downs = [], [], []
    for f in range(2):
        result, grad_n2, active, grad_pre, sums = feed_forward(
            f, core, normed2, grad_rows, vec, (chunk(f, 0), chunk(f, 1)), result, grad_n2
        )
        up_sums.append(sums)
        for h in range(2):
            (both,) = outer_products(
                [([(normed2, None)], [(grad_pre, h)]), ([(active, h)], [(grad_rows, None)])], offsets, model
            )
            ups.append(both[0, :model])
            downs.append(both[0, model:])
    output, grad_res, grad_branch, gm0, gm1, sums2 = second_norm_back(
        core, residual, result, grad_n2, grad_rows, a_pieces, vec, lengths
    )
    dj0, diag0 = attention_backward(joined0, probs0, mixed0, gm0, head_size)
    dj1, diag1 = attention_backward(joined1, probs1, mixed1, gm1, head_size)
    input_grad, vec_grads, table_grad = first_norm_back(
        core, (dj0, dj1), tokens, grad_res, vec, a_pieces, sums2, up_sums, (diag0, diag1), chosen
    )
    mixed = jnp.concatenate([mixed0, mixed1], 1)
    halves = [
        outer_products(
            [([(normed, None)], [(dj, j)]) for j in range(3)]
            + [([(mixed, None)], [(grad_branch[:, h * width : (h + 1) * width], None)])],
            offsets,
            model,
        )[0][0].reshape(4, model, width)
        for h, dj in enumerate((dj0, dj1))
    ]
    grads = jnp.stack(halves, 2).transpose(1, 0, 2, 3).reshape(model, 4 * model)
    grads = scattered(grads)
    grad_up = scattered(jnp.concatenate([ups[0], ups[2], ups[1], ups[3]], 1))
    grad_down = scattered(jnp.concatenate([downs[0], downs[2], downs[1], downs[3]], 0))
    by_owner = vec_grads[:VECTORS].reshape(VECTORS, model // local, local).transpose(1, 0, 2)
    own_units = vec_grads[VECTORS : VECTORS + 4].reshape(2, 2, model).transpose(1, 0, 2)
    both = jnp.concatenate(
        [by_owner.reshape(model // local, VECTORS * local), own_units.reshape(model // local, hidden * local // model)],
        1,
    )
    both = scattered(both)[0]
    table = jnp.concatenate([table_grad[16:], table_grad[:16, TILE : TILE + number - width]], 1)[:heads]
    grad_table = lax.psum(table, AXES)
    small_grads = [both[i * local : (i + 1) * local] for i in range(VECTORS)]
    return (
        output,
        input_grad,
        small_grads[0],
        small_grads[1],
        grads[:, : 3 * model].astype(F32),
        small_grads[2],
        small_grads[3],
        grads[:, 3 * model :].astype(F32),
        small_grads[4],
        grad_table,
        small_grads[5],
        small_grads[6],
        grad_up.astype(F32),
        both[VECTORS * local :],
        grad_down.astype(F32),
        small_grads[7],
    )


def solution(mesh):
    both = P(AXES)
    row = P(AXES, None)
    in_specs = (
        row, both, P(AXES, None, None), both, both, row, both, both, row, both, P(), both, both, row, both, row,
        both, row,
    )
    out_specs = (row, row, both, both, row, both, both, row, both, P(), both, both, row, both, row, both)

    if tuple(mesh.shape[name] for name in AXES) == (2, 16):

        def body(*args):
            return on_device(GridLinks((2, 4, 2), args[0].shape[1]), *args)

    else:
        body = on_any_mesh

    return jax.shard_map(body, mesh=mesh, in_specs=in_specs, out_specs=out_specs, check_vma=False)
```

```python
import functools

import jax
import jax.numpy as jnp
from jax import lax
from jax.experimental import pallas as pl
from jax.experimental.pallas import tpu as pltpu
from jax.sharding import PartitionSpec as P

BF = jnp.bfloat16
F32 = jnp.float32
AXES = ("dp", "fsdp")
TILE = 128
CHUNK = 64
EPS = 1e-05
NN = (((1,), (0,)), ((), ()))
NT = (((1,), (1,)), ((), ()))
TN = (((0,), (0,)), ((), ()))
VMEM = pltpu.VMEM


def mm(left, right, dims=NN):
    return lax.dot_general(left, right, dims, preferred_element_type=F32)


def any_spec():
    return pl.BlockSpec(memory_space=pl.ANY)


def hbm_spec():
    return pl.BlockSpec(memory_space=pltpu.HBM)


def in_hbm(x):
    return pltpu.with_memory_space_constraint(x, pltpu.HBM)


def smem_spec():
    return pl.BlockSpec(memory_space=pltpu.SMEM)


def whole(shape):
    return pl.BlockSpec(shape, lambda *_: (0,) * len(shape))


def params(mebibytes):
    return pltpu.CompilerParams(
        dimension_semantics=("arbitrary",), vmem_limit_bytes=mebibytes * 1024 * 1024
    )


def cost(micros):
    return pl.CostEstimate(flops=int(micros * 1e9), bytes_accessed=1, transcendentals=0)


class Pieces:
    def __init__(self, buffers, offsets, rows):
        self.buffers = buffers
        self.offsets = offsets
        self.rows = rows

    @property
    def slots(self):
        return sum(b.shape[0] for b in self.buffers)


def lay_blocks(refs, offs_ref, rows, count, put):
    slot = 0
    for ref in refs:
        for k in range(ref.shape[0]):
            at = pl.multiple_of(offs_ref[slot], 16)
            for j in range(count):
                put(j, at, ref[k, j * rows : (j + 1) * rows, :])
            slot += 1


def row_norm(x):
    centre = x - jnp.mean(x, -1, keepdims=True)
    scale = lax.rsqrt(jnp.mean(centre * centre, -1, keepdims=True) + EPS)
    return centre * scale, scale


def bucket_line(line, number):
    rows = lax.broadcasted_iota(jnp.int32, (number, line.shape[1]), 0)
    return jnp.where(rows == line.astype(jnp.int32), 1.0, 0.0).astype(BF)


def bias_tiles(core, lines, table, cotangent, lengths, halves):
    span = lines[0].shape[1]
    heads, number = table.shape
    count = heads // 2
    tiles = span // TILE - 1
    n = len(lines)
    rows, model = cotangent.shape

    def kernel(core_ref, len_ref, table_ref, cot_ref, *refs):
        line_refs, (out_ref, gr_ref, curve_ref) = refs[:n], refs[n:]
        at = pl.program_id(0)

        @pl.when(at == 0)
        def _():
            for i in range(n):
                curve = mm(table_ref[...], bucket_line(line_refs[i][0:1, :], number))
                curve = jnp.where((core_ref[0] ^ halves[i]) == 0, curve[:count], curve[count:])
                for h in range(count):
                    curve_ref[i * count + h] = jnp.broadcast_to(curve[h : h + 1], (8, span))
            row = lax.broadcasted_iota(jnp.int32, (rows, 1), 0)
            gr_ref[...] = jnp.where(row < len_ref[0], cot_ref[...].astype(F32), 0.0).astype(BF)

        base = pltpu.roll(curve_ref[at], 0, 1, stride=1, stride_axis=0)
        for pair in range(TILE // 16):
            rolled = jnp.concatenate(
                [pltpu.roll(base, 16 * pair + 8 * i, 1) if pair + i else base for i in range(2)], 0
            ).astype(BF)
            for d in range(tiles):
                out_ref[0, 0, d, 16 * pair : 16 * pair + 16, :] = rolled[
                    :, TILE * (d + 1) : TILE * (d + 2)
                ]

    return pl.pallas_call(
        kernel,
        grid=(n * count,),
        in_specs=[
            smem_spec(),
            smem_spec(),
            whole((heads, number)),
            whole((rows, model)),
            *[whole((8, span))] * n,
        ],
        out_specs=[
            pl.BlockSpec((1, 1, tiles, TILE, TILE), lambda h: (h // count, h % count, 0, 0, 0)),
            whole((rows, model)),
        ],
        out_shape=[
            VMEM((n, count, tiles, TILE, TILE), BF),
            VMEM((rows, model), BF),
        ],
        scratch_shapes=[VMEM((n * count, 8, span), F32)],
        compiler_params=params(8),
        cost_estimate=cost(4),
        name="bias_tiles",
    )(core, lengths, table, cotangent, *lines)


def place_rows(block, offset, wide):
    padded = jnp.concatenate([block, jnp.zeros((block.shape[0], wide - TILE), block.dtype)], 1)
    return pltpu.roll(padded, offset, 1)


def assemble_attention(pieces, model):
    width = model // 2
    rows = pieces.rows
    n_buf = len(pieces.buffers)

    def kernel(offs_ref, *refs):
        bufs, (w_ref, o_ref, vec_ref) = refs[:n_buf], refs[n_buf:]

        def put(j, at, block):
            if j < 3:
                w_ref[j, pl.ds(at, rows), :] = block
            else:
                o_ref[pl.ds(at, rows), :] = block

        lay_blocks(bufs, offs_ref, rows, 4, put)
        total, slot = jnp.zeros((16, model), F32), 0
        for ref in bufs:
            for k in range(ref.shape[0]):
                total += place_rows(ref[k, 4 * rows : 4 * rows + 16, :TILE].astype(F32), offs_ref[slot], model)
                slot += 1
        vec_ref[...] = total

    return pl.pallas_call(
        kernel,
        grid=(1,),
        in_specs=[smem_spec(), *[whole(one.shape) for one in pieces.buffers]],
        out_specs=[whole((3, model, width)), whole((model, width)), whole((16, model))],
        out_shape=[
            VMEM((3, model, width), BF),
            VMEM((model, width), BF),
            VMEM((16, model), F32),
        ],
        compiler_params=params(6),
        cost_estimate=cost(2),
        name="assemble_attention",
    )(pieces.offsets, *pieces.buffers)


def attention_forward(item, half, core, tokens, vec, weights, tiles, line, head_size):
    rows, model = tokens.shape
    width = model // 2
    heads = width // head_size
    pairs = width // TILE
    per = TILE // head_size
    scale = head_size**-0.5

    def kernel(core_ref, line_ref, x_ref, vec_ref, tile_ref, w_ref, n1_ref, joined_ref, mixed_ref, p_ref, qs_ref, s_ref):
        pair = pl.program_id(0)

        @pl.when(pair == 0)
        def _():
            for r in range(0, rows, CHUNK):
                xhat, _ = row_norm(x_ref[r : r + CHUNK, :].astype(F32))
                n1_ref[r : r + CHUNK, :] = (xhat * vec_ref[0:1, :] + vec_ref[1:2, :]).astype(BF)
            cols = pl.ds(pl.multiple_of((core_ref[0] ^ half) * width, TILE), width)
            for j in range(3):
                joined = mm(n1_ref[...], w_ref[j])
                if j != 1:
                    joined = joined + vec_ref[2 + j // 2 : 3 + j // 2, cols]
                qs_ref[j] = joined.astype(BF)

        lanes = pl.ds(pl.multiple_of(pair * TILE, TILE), TILE)
        q, k, v = (qs_ref[j, :, lanes] for j in range(3))
        for j, one in enumerate((q, k, v)):
            joined_ref[j] = one
        lane = lax.broadcasted_iota(jnp.int32, (1, TILE), 1)
        column = lax.broadcasted_iota(jnp.int32, (1, rows), 1)
        dead = jnp.where(column < line_ref[1:2, :rows].astype(jnp.int32), 0.0, -1e30).astype(F32)
        scaled = q.astype(F32) * scale
        outs = []
        for e in range(per):
            mine = (lane >= e * head_size) & (lane < (e + 1) * head_size)
            qm = jnp.where(mine, scaled, 0.0).astype(BF)
            s_ref[e] = mm(qm, k, NT)
            for r in range(0, rows, CHUNK):
                block, sub = r // TILE, r % TILE
                rel = jnp.concatenate(
                    [
                        tile_ref[0, e, j - block + rows // TILE - 1, sub : sub + CHUNK, :]
                        for j in range(rows // TILE)
                    ],
                    1,
                ).astype(F32)
                s = s_ref[e, r : r + CHUNK, :] + (rel + dead)
                raised = jnp.exp(s - jnp.max(s, -1, keepdims=True))
                inv = 1.0 / jnp.sum(raised, -1, keepdims=True)
                p_ref[e, r : r + CHUNK, :] = (raised * inv).astype(BF)
            outs.append(jnp.where(mine, mm(p_ref[e], v), 0.0))
        mixed_ref[...] = functools.reduce(lambda a, b: a + b, outs).astype(BF)

    shapes = [
        VMEM((3, rows, width), BF),
        VMEM((rows, width), BF),
        VMEM((heads, rows, rows), BF),
    ]
    outs = [
        pl.BlockSpec((3, rows, TILE), lambda p: (0, 0, p)),
        pl.BlockSpec((rows, TILE), lambda p: (0, p)),
        pl.BlockSpec((per, rows, rows), lambda p: (p, 0, 0)),
    ]
    shapes.insert(0, VMEM((rows, model), BF))
    outs.insert(0, whole((rows, model)))
    return pl.pallas_call(
        kernel,
        grid=(pairs,),
        in_specs=[
            smem_spec(),
            whole((8, 2 * rows)),
            whole((rows, model)),
            whole((16, model)),
            pl.BlockSpec((1, per, tiles.shape[2], TILE, TILE), lambda p: (item, p, 0, 0, 0)),
            whole((3, model, width)),
        ],
        out_specs=outs,
        out_shape=shapes,
        scratch_shapes=[VMEM((3, rows, width), BF), VMEM((per, rows, rows), F32)],
        compiler_params=params(12),
        cost_estimate=cost(6),
        name="attention_forward",
    )(core, line, tokens, vec, tiles, weights)


def project_out(core, mixed, tokens, weights, vec):
    rows, model = tokens.shape
    width = model // 2

    def kernel(core_ref, m0_ref, m1_ref, x_ref, vec_ref, w0_ref, w1_ref, res_ref, n2_ref):
        for h, w_ref in enumerate((w0_ref, w1_ref)):
            cols = pl.ds(pl.multiple_of((core_ref[0] ^ h) * width, TILE), width)
            acc = 0.0
            for g, m_ref in enumerate((m0_ref, m1_ref)):
                feats = pl.ds(pl.multiple_of((core_ref[0] ^ g) * width, TILE), width)
                acc = acc + mm(m_ref[...], w_ref[feats, :])
            res_ref[:, cols] = x_ref[:, cols].astype(F32) + acc + vec_ref[4:5, cols]
        for r in range(0, rows, CHUNK):
            xhat, _ = row_norm(res_ref[r : r + CHUNK, :])
            n2_ref[r : r + CHUNK, :] = (xhat * vec_ref[5:6, :] + vec_ref[6:7, :]).astype(BF)

    return pl.pallas_call(
        kernel,
        grid=(1,),
        in_specs=[
            smem_spec(),
            whole((rows, width)),
            whole((rows, width)),
            whole((rows, model)),
            whole((16, model)),
            whole((model, width)),
            whole((model, width)),
        ],
        out_specs=[whole((rows, model)), whole((rows, model))],
        out_shape=[
            VMEM((rows, model), F32),
            VMEM((rows, model), BF),
        ],
        compiler_params=params(6),
        cost_estimate=cost(2.5),
        name="project_out",
    )(core, mixed[0], mixed[1], tokens, vec, *weights)


def gelu_parts(v):
    bell = jnp.exp(-0.5 * (v * v))
    t = 1.0 / (1.0 + 0.23164189 * jnp.abs(v))
    tail = t * (0.127414796 + t * (-0.142248368 + t * (0.710706871 + t * (-0.726576014 + t * 0.530702714))))
    tail = tail * bell
    return jnp.where(v < 0.0, tail, 1.0 - tail), bell * 0.3989422804014327


def feed_forward(row, core, sets, vec, pieces):
    rows, model = sets[0][0].shape
    hidden = model
    n = len(sets)
    n_buf = len(pieces.buffers)
    per = pieces.rows
    half = rows // 2
    width = model // 2

    def kernel(core_ref, offs_ref, vec_ref, *refs):
        ins, refs = refs[: len(flat)], refs[len(flat) :]
        bufs, refs = refs[:n_buf], refs[n_buf:]
        outs, (col_ref, up_ref, down_ref) = refs[: 4 * n], refs[4 * n :]

        def put(j, at, block):
            ref = up_ref if j < 2 else down_ref
            ref[pl.ds(at, per), (j % 2) * width : (j % 2 + 1) * width] = block

        lay_blocks(bufs, offs_ref, per, 4, put)
        up_bias = vec_ref[pl.ds(row(core_ref[0]), 1), :]
        sums = jnp.zeros((1, hidden), F32)
        for i in range(n):
            n_ref, gr_ref, res_ref, gin_ref = (None if at is None else ins[at] for at in where[i])
            out_ref, gn_ref, act_ref, gp_ref = outs[4 * i : 4 * i + 4]
            for r in range(0, rows, half):
                block = slice(r, r + half)
                pre = mm(n_ref[block, :], up_ref[...]) + up_bias
                gact = mm(gr_ref[block, :], down_ref[...], NT)
                cdf, density = gelu_parts(pre)
                act = (pre * cdf).astype(BF)
                gp = gact * (cdf + pre * density)
                low = gp.astype(BF)
                act_ref[block, :] = act
                gp_ref[block, :] = low
                sums += jnp.sum(low.astype(F32), 0, keepdims=True)
                out = mm(act, down_ref[...])
                if res_ref is not None:
                    out = out + res_ref[block, :]
                    if gin_ref is None:
                        out = out + vec_ref[7:8, :]
                out_ref[block, :] = out
                gn = mm(low, up_ref[...], NT)
                gn_ref[block, :] = gn if gin_ref is None else gn + gin_ref[block, :]
        col_ref[...] = sums

    flat, where = [], []
    for one in sets:
        places = []
        for array in one:
            places.append(None if array is None else len(flat))
            if array is not None:
                flat.append(array)
        where.append(places)
    shapes = [
        VMEM((rows, model), F32),
        VMEM((rows, model), F32),
        VMEM((rows, hidden), BF),
        VMEM((rows, hidden), BF),
    ] * n + [VMEM((1, hidden), F32)]
    out = pl.pallas_call(
        kernel,
        grid=(1,),
        in_specs=[
            smem_spec(),
            smem_spec(),
            whole((16, model)),
            *[whole((rows, model))] * len(flat),
            *[whole(one.shape) for one in pieces.buffers],
        ],
        out_specs=[whole(one.shape) for one in shapes],
        out_shape=shapes,
        scratch_shapes=[
            VMEM((model, hidden), BF),
            VMEM((hidden, model), BF),
        ],
        compiler_params=params(20),
        cost_estimate=cost(9),
        name="feed_forward",
    )(core, pieces.offsets, vec, *flat, *pieces.buffers)
    return [out[4 * i : 4 * i + 4] for i in range(n)], out[-1]


def outer_products(core, pairs, offsets, rows):
    slots = offsets.shape[0]
    half = max(slots // 2, 1)
    tall = pairs[0][0][0][0].shape[-1]
    wide = tall // 2
    n_mat = len(pairs)
    flat = []

    def place(one, part):
        if isinstance(one, tuple):
            return [place(each, part) for each in one]
        match = [i for i, known in enumerate(flat) if known is one]
        if not match:
            flat.append(one)
            match = [len(flat) - 1]
        return match[0], part

    where = [([place(*one) for one in lefts], [place(*one) for one in rights]) for lefts, rights in pairs]

    def kernel(core_ref, offs_ref, *rest):
        ins, outs, w_ref = rest[: len(flat)], rest[len(flat) : -1], rest[-1]

        def pick(at, part):
            ref = ins[at]
            if part is None:
                return ref[...]
            if len(ref.shape) == 3:
                return ref[part]
            return ref[:, part * wide : (part + 1) * wide]

        for m, (lefts, rights) in enumerate(where):
            if isinstance(lefts[0], list):
                for h in range(2):
                    total = sum(mm(pick(*left[h]), pick(*right), TN) for left, right in zip(lefts, rights))
                    at = pl.multiple_of((core_ref[0] ^ h) * wide, 16)
                    w_ref[pl.ds(at, wide), :] = total.astype(BF)
            else:
                total = sum(mm(pick(*left), pick(*right), TN) for left, right in zip(lefts, rights))
                w_ref[...] = total.astype(BF)
            for s in range(slots):
                at = pl.multiple_of(offs_ref[s], 16)
                outs[s // half][s % half, m * rows : (m + 1) * rows, :] = w_ref[pl.ds(at, rows), :]

    n_out = 2 if slots > 1 else 1
    shape = (half, n_mat * rows, wide)
    return pl.pallas_call(
        kernel,
        grid=(1,),
        in_specs=[smem_spec(), smem_spec(), *[whole(one.shape) for one in flat]],
        out_specs=[whole(shape)] * n_out,
        out_shape=[VMEM(shape, BF)] * n_out,
        scratch_shapes=[VMEM((tall, wide), BF)],
        compiler_params=params(14),
        cost_estimate=cost(5),
        name="outer_products",
    )(core, offsets, *flat)


def late_slots(vectors, table, offsets):
    model = vectors.shape[1]
    slots = offsets.shape[0]
    half = slots // 2

    def kernel(offs_ref, vec_ref, table_ref, keep_ref, send_ref):
        for s in range(slots):
            small = pltpu.roll(vec_ref[...], lax.rem(model - offs_ref[s], model), 1)[:, :TILE]
            (keep_ref if s < half else send_ref)[s % half] = jnp.concatenate(
                [jnp.concatenate([small, table_ref[:16, TILE:]], 1), table_ref[16:, :]], 0
            ).astype(BF)

    shape = (half, *table.shape)
    return pl.pallas_call(
        kernel,
        grid=(1,),
        in_specs=[smem_spec(), whole(vectors.shape), whole(table.shape)],
        out_specs=[whole(shape)] * 2,
        out_shape=[VMEM(shape, BF)] * 2,
        compiler_params=params(4),
        cost_estimate=cost(1),
        name="late_slots",
    )(offsets, vectors, table)


def norm_back(x, up, gain):
    xhat, scale = row_norm(x)
    e = up * gain
    grad = scale * (e - jnp.mean(e, -1, keepdims=True) - xhat * jnp.mean(e * xhat, -1, keepdims=True))
    return grad, up * xhat


def second_norm_back(core, residual, results, grads_normed, grad_rows, weights, vec, lengths):
    rows, model = residual.shape
    width = model // 2
    n, m = len(results), len(grads_normed)

    def kernel(core_ref, len_ref, res_ref, gr_ref, vec_ref, w0_ref, w1_ref, *refs):
        out_refs, gn_refs = refs[:n], refs[n : n + m]
        out_ref, gres_ref, gm_ref, br_ref, sent_ref, sums_ref, gb_ref = refs[n + m :]
        totals = [jnp.zeros((1, model), F32) for _ in range(4)]
        for r in range(0, rows, CHUNK):
            block = slice(r, r + CHUNK)
            row = lax.broadcasted_iota(jnp.int32, (CHUNK, 1), 0) + r
            result = functools.reduce(lambda a, b: a + b, [ref[block, :] for ref in out_refs])
            out_ref[block, :] = jnp.where(row < len_ref[0], result, 0.0).astype(BF)
            up = functools.reduce(lambda a, b: a + b, [ref[block, :] for ref in gn_refs])
            grad, gain_terms = norm_back(res_ref[block, :], up, vec_ref[5:6, :])
            gr = gr_ref[block, :].astype(F32)
            grad = gr + grad
            low = grad.astype(BF)
            gres_ref[block, :] = grad
            gb_ref[block, :] = low
            for i, terms in enumerate((gain_terms, up, low.astype(F32), gr)):
                totals[i] += jnp.sum(terms, 0, keepdims=True)
        sums_ref[...] = jnp.concatenate(totals + [jnp.zeros((4, model), F32)], 0)
        parts = [pl.ds(pl.multiple_of((core_ref[0] ^ h) * width, TILE), width) for h in range(2)]
        for h in range(2):
            acc = 0.0
            for g, w_ref in enumerate((w0_ref, w1_ref)):
                acc = acc + mm(gb_ref[:, parts[g]], w_ref[parts[h], :], NT)
            if h == 0:
                gm_ref[...] = acc.astype(BF)
                br_ref[...] = gb_ref[:, parts[0]]
            else:
                sent_ref[:, :width] = acc.astype(BF)
                sent_ref[:, width:] = gb_ref[:, parts[1]]

    return pl.pallas_call(
        kernel,
        grid=(1,),
        in_specs=[
            *[smem_spec()] * 2,
            *[whole((rows, model))] * 2,
            whole((16, model)),
            whole((model, width)),
            whole((model, width)),
            *[whole((rows, model))] * (n + m),
        ],
        out_specs=[
            *[whole((rows, model))] * 2,
            *[whole((rows, width))] * 2,
            whole((rows, model)),
            whole((8, model)),
        ],
        out_shape=[
            jax.ShapeDtypeStruct((rows, model), BF),
            jax.ShapeDtypeStruct((rows, model), F32),
            jax.ShapeDtypeStruct((rows, width), BF),
            jax.ShapeDtypeStruct((rows, width), BF),
            jax.ShapeDtypeStruct((rows, model), BF),
            jax.ShapeDtypeStruct((8, model), F32),
        ],
        scratch_shapes=[VMEM((rows, model), BF)],
        compiler_params=params(10),
        cost_estimate=cost(4),
        name="second_norm_back",
    )(core, lengths, residual, grad_rows, vec, *weights, *results, *grads_normed)


def attention_backward(joined, probs, mixed, grad_mixed, head_size, tokens_in=()):
    _, rows, width = joined.shape
    heads = width // head_size
    pairs = width // TILE
    per = TILE // head_size
    tiles = 2 * (rows // TILE) - 1
    span = 2 * rows
    scale = head_size**-0.5

    def kernel(joined_ref, p_ref, mixed_ref, gm_ref, *rest):
        out_ref, diag_ref, gp_ref, ds_ref, acc_ref = rest[len(tokens_in) :]
        q, k, v = joined_ref[0], joined_ref[1], joined_ref[2]
        gm = gm_ref[...]
        lane = lax.broadcasted_iota(jnp.int32, (1, TILE), 1)
        dots = gm.astype(F32) * mixed_ref[...].astype(F32)
        q_t, gm_t = q.T, gm.T
        dq, dk, dv = [], [], []
        for e in range(per):
            mine = (lane >= e * head_size) & (lane < (e + 1) * head_size)
            feats = slice(e * head_size, (e + 1) * head_size)
            delta = jnp.sum(jnp.where(mine, dots, 0.0), -1, keepdims=True)
            gp_ref[e] = mm(jnp.where(mine, gm, jnp.zeros_like(gm)), v, NT)
            acc_ref[...] = jnp.zeros_like(acc_ref)
            for r in range(0, rows, CHUNK):
                block, sub = r // TILE, r % TILE
                ds = p_ref[e, r : r + CHUNK, :].astype(F32) * (
                    gp_ref[e, r : r + CHUNK, :] - delta[r : r + CHUNK, :]
                )
                ds_ref[e, r : r + CHUNK, :] = ds.astype(BF)
                for j in range(rows // TILE):
                    acc_ref[j - block + rows // TILE - 1, sub : sub + CHUNK, :] += ds[
                        :, j * TILE : (j + 1) * TILE
                    ]
            dq.append(jnp.where(mine, mm(ds_ref[e], k), 0.0))
            dk.append(mm(q_t[feats, :], ds_ref[e]))
            dv.append(mm(gm_t[feats, :], p_ref[e]))
            total = jnp.zeros((8, span), F32)
            for g in range(TILE // 8):
                strip = jnp.concatenate(
                    [jnp.zeros((8, TILE), F32)]
                    + [acc_ref[d, 8 * g : 8 * g + 8, :] for d in range(tiles)],
                    1,
                )
                total += pltpu.roll(strip, (span - 8 * g) % span, 1) if g else strip
            line = total[0:1]
            for i in range(1, 8):
                line = line + pltpu.roll(total[i : i + 1], span - i, 1)
            diag_ref[e] = line
        out_ref[0] = (functools.reduce(lambda a, b: a + b, dq) * scale).astype(BF)
        out_ref[1] = (jnp.concatenate(dk, 0) * scale).T.astype(BF)
        out_ref[2] = jnp.concatenate(dv, 0).T.astype(BF)

    return pl.pallas_call(
        kernel,
        grid=(pairs,),
        in_specs=[
            pl.BlockSpec((3, rows, TILE), lambda p: (0, 0, p)),
            pl.BlockSpec((per, rows, rows), lambda p: (p, 0, 0)),
            pl.BlockSpec((rows, TILE), lambda p: (0, p)),
            pl.BlockSpec((rows, TILE), lambda p: (0, p)),
            *[any_spec()] * len(tokens_in),
        ],
        out_specs=[
            pl.BlockSpec((3, rows, TILE), lambda p: (0, 0, p)),
            pl.BlockSpec((per, 1, span), lambda p: (p, 0, 0)),
        ],
        out_shape=[
            VMEM((3, rows, width), BF),
            VMEM((heads, 1, span), F32),
        ],
        scratch_shapes=[
            VMEM((per, rows, rows), F32),
            VMEM((per, rows, rows), BF),
            VMEM((tiles, TILE, TILE), F32),
        ],
        compiler_params=params(12),
        cost_estimate=cost(4.5),
        name="attention_backward",
    )(joined, probs, mixed, grad_mixed, *tokens_in)


def normed_back(grads, weights):
    _, rows, width = grads.shape
    model = weights.shape[1]

    def kernel(d_ref, w_ref, out_ref):
        out_ref[...] = sum(mm(d_ref[j], w_ref[j], NT) for j in range(3))

    return pl.pallas_call(
        kernel,
        grid=(1,),
        in_specs=[whole(grads.shape), whole(weights.shape)],
        out_specs=whole((rows, model)),
        out_shape=VMEM((rows, model), F32),
        compiler_params=params(8),
        cost_estimate=cost(1.5),
        name="normed_back",
    )(grads, weights)


def first_norm_back(
    core, grads, part, tokens, grad_residual, vec, weights, sums_second, sums_up, diags, lines, number, apart
):
    rows, model = tokens.shape
    width = model // 2
    count = diags[0].shape[0]
    span = lines[0].shape[1]
    n_up = len(sums_up[0])

    def kernel(core_ref, d0_ref, d1_ref, part_ref, x_ref, gres_ref, vec_ref, w_ref, s2_ref, t0_ref, t1_ref, l0_ref, l1_ref,
               *rest):
        up_refs = rest[: 2 * n_up]
        gx_ref, sums_ref, table_ref, acc_ref = rest[2 * n_up :]
        straight = core_ref[0] == 0

        def ordered(a, b):
            return [jnp.where(straight, a, b), jnp.where(straight, b, a)]

        tables = []
        for t_ref, l_ref in ((t0_ref, l0_ref), (t1_ref, l1_ref)):
            chosen = bucket_line(l_ref[0:1, :], number)
            table, left = 0.0, t_ref[:, 0, :]
            for _ in range(3):
                low = left.astype(BF)
                table = table + mm(low, chosen, NT)
                left = left - low.astype(F32)
            tables.append(table)
        blank = jnp.zeros((count, number), F32)
        tables = tables if apart else ordered(tables[0] + tables[1], blank)
        table = jnp.concatenate([*tables, jnp.zeros((16 - 2 * count, number), F32)], 0)
        table = jnp.concatenate([table, jnp.zeros((16, 2 * width - number), F32)], 1)
        table_ref[...] = jnp.concatenate(
            [
                jnp.concatenate([jnp.zeros((16, TILE), F32), table[:, width : 2 * width - TILE]], 1),
                table[:, :width],
            ],
            0,
        )
        columns = []
        for j in (0, 2):
            a, b = (jnp.sum(d_ref[j].astype(F32), 0, keepdims=True) for d_ref in (d0_ref, d1_ref))
            columns.append(jnp.concatenate([a, b] if apart else ordered(a + b, jnp.zeros_like(a)), 1))
        ups = []
        for f in range(2):
            here = [ref[...] for ref in up_refs[f * n_up : (f + 1) * n_up]]
            ups += here if apart else ordered(here[0], jnp.zeros_like(here[0]))
        acc_ref[...] = part_ref[...] + sum(mm(d0_ref[j], w_ref[j], NT) for j in range(3))
        totals = [jnp.zeros((1, model), F32) for _ in range(2)]
        for r in range(0, rows, CHUNK):
            block = slice(r, r + CHUNK)
            up = acc_ref[block, :]
            grad, gain_terms = norm_back(x_ref[block, :].astype(F32), up, vec_ref[0:1, :])
            gx_ref[block, :] = gres_ref[block, :] + grad
            totals[0] += jnp.sum(gain_terms, 0, keepdims=True)
            totals[1] += jnp.sum(up, 0, keepdims=True)
        sums_ref[...] = jnp.concatenate(
            totals
            + columns
            + [s2_ref[2:3, :], s2_ref[0:1, :], s2_ref[1:2, :], s2_ref[3:4, :]]
            + ups
            + [jnp.zeros((4, model), F32)],
            0,
        )

    return pl.pallas_call(
        kernel,
        grid=(1,),
        in_specs=[
            smem_spec(),
            whole((3, rows, width)),
            whole((3, rows, width)),
            whole((rows, model)),
            whole((rows, model)),
            whole((rows, model)),
            whole((16, model)),
            whole((3, model, width)),
            whole((8, model)),
            whole((count, 1, span)),
            whole((count, 1, span)),
            whole((8, span)),
            whole((8, span)),
            *[whole((1, model))] * (2 * n_up),
        ],
        out_specs=[whole((rows, model)), whole((16, model)), whole((32, width))],
        out_shape=[
            jax.ShapeDtypeStruct((rows, model), F32),
            jax.ShapeDtypeStruct((16, model), F32),
            jax.ShapeDtypeStruct((32, width), F32),
        ],
        scratch_shapes=[VMEM((rows, model), F32)],
        compiler_params=params(14),
        cost_estimate=cost(5),
        name="first_norm_back",
    )(
        core, *grads, part, tokens, grad_residual, vec, weights, sums_second, *diags, *lines, *sums_up[0], *sums_up[1]
    )


def pack_blocks(core, lengths, buckets, vectors, qkv, out, up):
    local, model = out.shape
    width = model // 2
    unit = local * 2
    chips = up.shape[1] // (4 * unit)
    rows = buckets.shape[1]

    def kernel(core_ref, len_ref, buckets_hbm, vec_ref, qkv_hbm, out_hbm, up_hbm, a0_ref, a1_ref, u0_ref, u1_ref,
               small_ref, line_ref, first_ref, last_ref, qkv_ref, out_ref, up_ref, sems):
        copies = [
            pltpu.make_async_copy(source, target, sems.at[i])
            for i, (source, target) in enumerate(
                (
                    (qkv_hbm, qkv_ref),
                    (out_hbm, out_ref),
                    (up_hbm, up_ref),
                    (buckets_hbm.at[pl.ds(0, 1), pl.ds(0, 8)], first_ref),
                    (buckets_hbm.at[pl.ds(0, 1), pl.ds(rows - 8, 8)], last_ref),
                )
            )
        ]
        for c in copies:
            c.start()
        for c in copies:
            c.wait()
        core_at = core_ref[0]
        for h, a_ref in enumerate((a0_ref, a1_ref)):
            at = (core_at ^ h) * width
            for j in range(3):
                a_ref[j] = qkv_ref[:, pl.ds(pl.multiple_of(j * model + at, TILE), width)]
            a_ref[3] = out_ref[:, pl.ds(pl.multiple_of(at, TILE), width)]
        first = core_at == 0
        values = jnp.concatenate(
            [vec_ref[...].astype(F32), jnp.zeros((VECTORS + 4, TILE - local), F32)], 1
        )
        moved = pltpu.roll(values, local, 1)
        lines = [jnp.where(first, values[:VECTORS], moved[:VECTORS])]
        for f in range(2):
            at = VECTORS + 2 * f
            both = values[at : at + 1] + moved[at + 1 : at + 2]
            blank = jnp.zeros_like(both)
            lines += [jnp.where(first, both, blank), jnp.where(first, blank, both)]
        small_ref[...] = jnp.concatenate(lines + [jnp.zeros((4, TILE), F32)], 0).astype(BF)
        ahead = pltpu.roll(last_ref[0, 7:8, :].astype(F32), 1, 1)
        line = jnp.concatenate([ahead, first_ref[0, 0:1, :].astype(F32)], 1)
        live = jnp.zeros_like(line) + len_ref[0].astype(F32)
        line_ref[...] = jnp.concatenate([line, live, jnp.zeros((6, 2 * rows), F32)], 0)
        for f in range(2):
            by_core = []
            for c in range(2):
                by_core.append(
                    jnp.concatenate(
                        [
                            up_ref[:, ((2 * chip + c) * 2 + f) * unit : ((2 * chip + c) * 2 + f + 1) * unit]
                            for chip in range(chips)
                        ],
                        1,
                    ).astype(F32)
                )
            u0_ref[f] = jnp.where(first, by_core[0], by_core[1]).astype(BF)
            u1_ref[f] = jnp.where(first, by_core[1], by_core[0]).astype(BF)

    shapes = [
        *[VMEM((4, local, width), BF)] * 2,
        *[VMEM((2, local, model), BF)] * 2,
        VMEM((16, TILE), BF),
        VMEM((8, 2 * rows), F32),
    ]
    return pl.pallas_call(
        kernel,
        grid=(1,),
        in_specs=[
            smem_spec(),
            smem_spec(),
            hbm_spec(),
            whole(vectors.shape),
            *[hbm_spec()] * 3,
        ],
        out_specs=[whole(one.shape) for one in shapes],
        out_shape=shapes,
        scratch_shapes=[
            VMEM((1, 8, rows), jnp.int32),
            VMEM((1, 8, rows), jnp.int32),
            VMEM(qkv.shape, BF),
            VMEM(out.shape, BF),
            VMEM(up.shape, BF),
            pltpu.SemaphoreType.DMA((5,)),
        ],
        compiler_params=params(6),
        cost_estimate=cost(1.5),
        name="pack_blocks",
    )(core, lengths, in_hbm(buckets), vectors, in_hbm(qkv), in_hbm(out), in_hbm(up))


def ordered_rows(core_at, mine, theirs):
    first = core_at == 0
    a, b = mine.astype(F32), theirs.astype(F32)
    return jnp.concatenate([jnp.where(first, a, b), jnp.where(first, b, a)], 0)


def merge_attention(core, mine, theirs, small, small_theirs):
    count, local, width = mine.shape

    def kernel(core_ref, a_ref, b_ref, s_ref, t_ref, out_ref):
        for j in range(count):
            out_ref[2 * local * j : 2 * local * (j + 1), :] = ordered_rows(core_ref[0], a_ref[j], b_ref[j]).astype(BF)
        vec = s_ref[...].astype(F32) + t_ref[...].astype(F32)
        out_ref[2 * local * count :, :] = jnp.concatenate([vec, jnp.zeros((16, width - TILE), F32)], 1).astype(BF)

    return pl.pallas_call(
        kernel,
        grid=(1,),
        in_specs=[smem_spec(), *[whole(mine.shape)] * 2, *[whole(small.shape)] * 2],
        out_specs=whole((2 * local * count + 16, width)),
        out_shape=VMEM((2 * local * count + 16, width), BF),
        compiler_params=params(4),
        cost_estimate=cost(1),
        name="merge_attention",
    )(core, mine, theirs, small, small_theirs)


def merge_feed_forward(core, mine, theirs, down):
    _, local, model = mine.shape
    unit = 2 * local
    width = model // 2

    def kernel(core_ref, a_ref, b_ref, d_ref, *outs):
        for f in range(2):
            up = ordered_rows(core_ref[0], a_ref[f], b_ref[f]).astype(BF)
            low = d_ref[f * unit : (f + 1) * unit, :]
            for j, block in enumerate((up[:, :width], up[:, width:], low[:, :width], low[:, width:])):
                outs[f][j * unit : (j + 1) * unit, :] = block

    shape = VMEM((4 * unit, width), BF)
    return pl.pallas_call(
        kernel,
        grid=(1,),
        in_specs=[smem_spec(), *[whole(mine.shape)] * 2, whole(down.shape)],
        out_specs=[whole(shape.shape)] * 2,
        out_shape=[shape] * 2,
        compiler_params=params(4),
        cost_estimate=cost(1),
        name="merge_feed_forward",
    )(core, mine, theirs, down)


def pair_sum(refs):
    parts = [ref[...].astype(F32) for ref in refs]
    while len(parts) > 1:
        half = len(parts) // 2
        parts = [parts[i] + parts[i + half] for i in range(half)]
    return parts[0]


def rows_of(total, first, core_at, local, mine):
    a, b = total[first : first + local], total[first + local : first + 2 * local]
    return jnp.where((core_at == 0) == mine, a, b)


def total_attention(core, parts, local):
    tall, width = parts[0].shape
    tail = tall - 8 * local

    def kernel(core_ref, *refs):
        ins, (mine_ref, sent_ref, tail_ref) = refs[: len(parts)], refs[len(parts) :]
        total = pair_sum(ins)
        for j in range(4):
            mine_ref[j] = rows_of(total, 2 * local * j, core_ref[0], local, True)
            sent_ref[j] = rows_of(total, 2 * local * j, core_ref[0], local, False).astype(BF)
        tail_ref[...] = total[8 * local :].astype(BF)

    shapes = [
        jax.ShapeDtypeStruct((4, local, width), F32),
        jax.ShapeDtypeStruct((4, local, width), BF),
        jax.ShapeDtypeStruct((tail, width), BF),
    ]
    return pl.pallas_call(
        kernel,
        grid=(1,),
        in_specs=[smem_spec(), *[whole(one.shape) for one in parts]],
        out_specs=[whole(one.shape) for one in shapes],
        out_shape=shapes,
        compiler_params=params(6),
        cost_estimate=cost(1),
        name="total_attention",
    )(core, *parts)


def finish_attention(core, mine, theirs, tail, tail_theirs, heads, number):
    _, local, width = mine.shape
    model = 2 * width

    def kernel(core_ref, a_ref, b_ref, s_ref, t_ref, qkv_ref, out_ref, small_ref, table_ref):
        at = core_ref[0]
        for h, ref in enumerate((a_ref, b_ref)):
            for j in range(3):
                cols = pl.ds(pl.multiple_of(j * model + (at ^ h) * width, TILE), width)
                qkv_ref[:, cols] = ref[j].astype(F32)
            out_ref[:, pl.ds(pl.multiple_of((at ^ h) * width, TILE), width)] = ref[3].astype(F32)
        total = s_ref[...].astype(F32) + t_ref[...].astype(F32)
        small = total[:16, :TILE]
        moved = pltpu.roll(small, TILE - local, 1)
        small_ref[:8, :] = jnp.where(at == 0, small[:8], moved[:8])
        small_ref[8:, :] = small[8:]
        table_ref[...] = jnp.concatenate([total[16:, :], total[:16, TILE : TILE + number - width]], 1)[:heads]

    shapes = [
        jax.ShapeDtypeStruct((local, 3 * model), F32),
        jax.ShapeDtypeStruct((local, model), F32),
        jax.ShapeDtypeStruct((16, TILE), F32),
        jax.ShapeDtypeStruct((heads, number), F32),
    ]
    return pl.pallas_call(
        kernel,
        grid=(1,),
        in_specs=[smem_spec(), *[whole(one.shape) for one in (mine, theirs, tail, tail_theirs)]],
        out_specs=[whole(one.shape) for one in shapes],
        out_shape=shapes,
        compiler_params=params(6),
        cost_estimate=cost(1),
        name="finish_attention",
    )(core, mine, theirs, tail, tail_theirs)


def total_feed_forward(core, parts, local):
    _, width = parts[0].shape
    model = 2 * width
    unit = 2 * local

    def kernel(core_ref, *refs):
        ins, (mine_ref, sent_ref, down_ref) = refs[: len(parts)], refs[len(parts) :]
        total = pair_sum(ins)
        for h in range(2):
            cols = slice(h * width, (h + 1) * width)
            mine_ref[:, cols] = rows_of(total, h * unit, core_ref[0], local, True)
            sent_ref[:, cols] = rows_of(total, h * unit, core_ref[0], local, False).astype(BF)
            down_ref[:, cols] = total[(2 + h) * unit : (3 + h) * unit]

    shapes = [
        jax.ShapeDtypeStruct((local, model), F32),
        jax.ShapeDtypeStruct((local, model), BF),
        jax.ShapeDtypeStruct((unit, model), F32),
    ]
    return pl.pallas_call(
        kernel,
        grid=(1,),
        in_specs=[smem_spec(), *[whole(one.shape) for one in parts]],
        out_specs=[whole(one.shape) for one in shapes],
        out_shape=shapes,
        compiler_params=params(6),
        cost_estimate=cost(1),
        name="total_feed_forward",
    )(core, *parts)


def finish_feed_forward(core, mine, theirs, downs):
    local, model = mine[0].shape
    unit = 2 * local
    chips = model // unit

    def kernel(core_ref, m0, m1, t0, t1, d0, d1, up_ref, down_ref):
        first = core_ref[0] == 0
        by = []
        for a, b in ((m0, t0), (m1, t1)):
            a, b = a[...], b[...].astype(F32)
            by.append((jnp.where(first, a, b), jnp.where(first, b, a)))
        up_ref[...] = jnp.concatenate(
            [
                by[f][c][:, chip * unit : (chip + 1) * unit]
                for chip in range(chips)
                for c in range(2)
                for f in range(2)
            ],
            1,
        )
        down_ref[:unit, :] = d0[...]
        down_ref[unit:, :] = d1[...]

    shapes = [jax.ShapeDtypeStruct((local, 4 * model), F32), jax.ShapeDtypeStruct((2 * unit, model), F32)]
    ins = (*mine, *theirs, *downs)
    return pl.pallas_call(
        kernel,
        grid=(1,),
        in_specs=[smem_spec(), *[whole(one.shape) for one in ins]],
        out_specs=[whole(one.shape) for one in shapes],
        out_shape=shapes,
        compiler_params=params(6),
        cost_estimate=cost(1),
        name="finish_feed_forward",
    )(core, *ins)


VECTORS = 8


class Order:
    def __init__(self, token):
        self.token = token

    def go(self, *values):
        out, _ = lax.optimization_barrier((values, self.token))
        return out if len(out) > 1 else out[0]

    def mark(self, *values):
        out, self.token = lax.optimization_barrier((values, self.token))
        return out if len(out) > 1 else out[0]


class GridLinks:
    pair = True

    def __init__(self, sizes, model):
        self.ny, self.nz, self.nx = sizes
        self.chips = self.ny * self.nz * self.nx
        self.rows = model // self.chips
        dp, inner = lax.axis_index("dp"), lax.axis_index("fsdp")
        self.core = inner % 2
        chip = inner // 2
        self.place = (dp, chip // self.nx, chip % self.nx)
        self.gather_offsets = self._offsets(self.core, -1, (range(self.nz),))
        self.early_offsets = self._offsets(self.core, -1, ((0,), range(1, self.nz)))
        self.scatter_offsets = self._offsets(self.core, 1, (range(self.nz),))

    def _offsets(self, core, sign, parts):
        y, z, x = self.place
        out = []
        for part in parts:
            for r1 in range(2):
                for r2 in range(2):
                    for k in part:
                        fy = jnp.where(core == 0, r1, r2)
                        fx = jnp.where(core == 0, r2, r1)
                        zz = (z + sign * k + self.nz) % self.nz
                        out.append(((y ^ fy) * self.nz + zz) * self.nx + (x ^ fx))
        return (jnp.stack(out) * self.rows).astype(jnp.int32)

    def _send(self, value, move):
        pairs = []
        for y in range(self.ny):
            for z in range(self.nz):
                for x in range(self.nx):
                    for c in range(2):
                        source = ((y * self.nz + z) * self.nx + x) * 2 + c
                        ty, tz, tx, tc = move(y, z, x, c)
                        pairs.append((source, ((ty * self.nz + tz) * self.nx + tx) * 2 + tc))
        return lax.ppermute(value, AXES, pairs)

    def swap(self, value):
        return self._send(value, lambda y, z, x, c: (y, z, x, 1 - c))

    def along_z(self, value, k):
        return self._send(value, lambda y, z, x, c: (y, (z + k) % self.nz, x, c))

    def x_first(self, value):
        return self._send(value, lambda y, z, x, c: (y, z, 1 - x, c) if c == 0 else (1 - y, z, x, c))

    def y_first(self, value):
        return self._send(value, lambda y, z, x, c: (y, z, 1 - x, c) if c == 1 else (1 - y, z, x, c))

    def spread(self, near):
        second = self.x_first(near)
        third = self.y_first(near)
        return [near, second, third, self.y_first(second)]

    def scatter_z(self, sums):
        return [sums[0]] + [self.along_z(sums[k], k) for k in range(1, self.nz)]


def small_kernel(kernel, name, shapes, *ins):
    return pl.pallas_call(
        kernel,
        grid=(1,),
        in_specs=[whole(one.shape) for one in ins],
        out_specs=[whole(shape) for shape in shapes],
        out_shape=[VMEM(shape, BF) for shape in shapes],
        compiler_params=params(4),
        cost_estimate=cost(1),
        name=name,
    )(*ins)


def stack_blocks(*blocks):
    def kernel(*refs):
        for i, ref in enumerate(refs[:-1]):
            refs[-1][i] = ref[...]

    return small_kernel(kernel, "stack_blocks", [(len(blocks), *blocks[0].shape)], *blocks)[0]


def add_low(a, b):
    return (a.astype(F32) + b.astype(F32)).astype(BF)


def fold(keep, moved):
    n = keep.shape[0] // 2

    def kernel(keep_ref, moved_ref, *outs):
        for s in range(2 * n):
            outs[s // n][s % n] = add_low(keep_ref[s], moved_ref[s])

    return small_kernel(kernel, "fold", [(n, *keep.shape[1:])] * 2, keep, moved)


def fold_last(*sides):
    n = sides[0][0].shape[0]
    tall = sum(side[0].shape[1] for side in sides)
    wide = sides[0][0].shape[2]

    def kernel(*refs):
        outs = refs[2 * len(sides) :]
        for s in range(n):
            at = 0
            for i in range(len(sides)):
                keep_ref, moved_ref = refs[2 * i : 2 * i + 2]
                rows = keep_ref.shape[1]
                outs[s][at : at + rows, :] = add_low(keep_ref[s], moved_ref[s])
                at += rows

    return small_kernel(kernel, "fold_last", [(tall, wide)] * n, *(one for side in sides for one in side))


def on_device(
    links,
    tokens,
    lengths,
    buckets,
    ln1_gain,
    ln1_bias,
    qkv_weight,
    q_bias,
    v_bias,
    out_weight,
    out_bias,
    rel_table,
    ln2_gain,
    ln2_bias,
    up_weight,
    up_bias,
    down_weight,
    down_bias,
    cotangent,
):
    rows, model = tokens.shape
    heads, number = rel_table.shape
    head_size = model // heads
    width = model // 2
    local = qkv_weight.shape[0]
    core, chips = links.core, links.chips
    core_arg = core.astype(jnp.int32).reshape(1)

    order = Order(core_arg)
    vectors = jnp.stack(
        [ln1_gain, ln1_bias, q_bias, v_bias, out_bias, ln2_gain, ln2_bias, down_bias]
        + [up_bias[i * local : (i + 1) * local] for i in range(4)]
    )
    a_mine, a_sent, u_mine, u_sent, small, line = pack_blocks(
        core_arg, lengths, buckets, vectors, qkv_weight, out_weight, up_weight
    )
    a_theirs, small_theirs = links.swap(a_sent), links.swap(small)
    line_other, tokens_other, u_theirs = links.swap(line), links.swap(tokens), links.swap(u_sent)
    early_offsets, gather_offsets, scatter_offsets = links.early_offsets, links.gather_offsets, links.scatter_offsets
    a_piece = merge_attention(core_arg, a_mine, a_theirs, small, small_theirs)
    a_piece, line_other, tokens_other, u_theirs, early_offsets, gather_offsets, scatter_offsets = order.mark(
        a_piece, line_other, tokens_other, u_theirs, early_offsets, gather_offsets, scatter_offsets
    )

    z_parts = [links.along_z(a_piece, k) for k in (1, 3, 2)]
    near = a_piece[None]
    second, third = links.x_first(near), links.y_first(near)
    tiles, grad_rows = bias_tiles(core_arg, (line, line_other), rel_table, cotangent, lengths, (0, 0))
    f0, f1 = merge_feed_forward(core_arg, u_mine, order.go(u_theirs), down_weight)
    tiles, grad_rows, f0, f1, z_parts, second, third = order.mark(
        tiles, grad_rows, f0, f1, z_parts, second, third
    )
    parts = [near, second, third, links.y_first(second)]
    near = stack_blocks(z_parts[0], z_parts[2], z_parts[1])
    second, third = links.x_first(near), links.y_first(near)
    f0_z = [links.along_z(f0, k) for k in (1, 3)]
    second, parts, f0_z = order.mark(second, parts, f0_z)
    fourth = links.y_first(second)
    f0_z.append(links.along_z(order.go(f0), 2))
    grad_rows_other = links.swap(grad_rows)
    third, fourth = order.mark(third, fourth)
    parts += [near, second, third, fourth]
    own, own_out, vec = order.mark(*assemble_attention(Pieces(parts, early_offsets, links.rows), model))
    other_out = links.swap(own_out)
    f0_z = order.mark(f0_z)
    f0_near = stack_blocks(f0, f0_z[0], f0_z[2], f0_z[1])
    f0_second = links.x_first(f0_near)
    f1 = order.go(f1)
    f1_z = [links.along_z(f1, k) for k in (1, 3)]

    normed_other, joined1, mixed1, probs1 = attention_forward(
        1, 0, core_arg, tokens_other, vec, order.go(own), tiles, line_other, head_size
    )
    mixed1, f0_second, other_out, grad_rows_other, f1_z = order.mark(
        mixed1, f0_second, other_out, grad_rows_other, f1_z
    )
    mixed_rest = links.swap(mixed1)
    f0_third, f0_fourth = links.y_first(f0_near), links.y_first(f0_second)
    f1_z.append(links.along_z(order.go(f1), 2))
    normed, joined0, mixed0, probs0 = attention_forward(
        0, 0, core_arg, tokens, vec, order.go(own), tiles, line, head_size
    )
    mixed0, mixed_rest, f1_z = order.mark(mixed0, mixed_rest, f1_z)
    mixed_rest_other = links.swap(mixed0)
    residual, normed2 = project_out(core_arg, (order.go(mixed0), mixed_rest), tokens, (own_out, other_out), vec)
    normed2, f0_third, f0_fourth, mixed_rest_other = order.mark(normed2, f0_third, f0_fourth, mixed_rest_other)

    normed2_other = links.swap(normed2)
    f1_near = stack_blocks(f1, f1_z[0], f1_z[2], f1_z[1])
    f1_second = links.x_first(f1_near)
    normed2_other, f1_near = order.mark(normed2_other, f1_near)

    def chunk(bufs):
        return Pieces(bufs, gather_offsets, links.rows)

    def products(own_set, other_set):
        return order.mark(*outer_products(
            core_arg,
            [([(normed2, None), (normed2_other, None)], [(own_set[3], h), (other_set[3], h)]) for h in range(2)]
            + [([(own_set[2], None), (other_set[2], None)], [(grad_rows, h), (grad_rows_other, h)]) for h in range(2)],
            scatter_offsets,
            links.rows,
        ))

    (own0, other0), sums_f0 = feed_forward(
        lambda c: 8 + c, core_arg,
        [(normed2, grad_rows, residual, None), (normed2_other, grad_rows_other, None, None)],
        vec, chunk([f0_near, f0_second, f0_third, f0_fourth]),
    )
    own0, f1_second = order.mark(own0, f1_second)
    f1_third, f1_fourth = links.y_first(f1_near), links.y_first(f1_second)
    keep0, send0 = products(own0, other0)
    moved0 = links.y_first(send0)
    f1_third, f1_fourth = order.mark(f1_third, f1_fourth)
    (own1, other1), sums_f1 = feed_forward(
        lambda c: 10 + c, core_arg,
        [(normed2, grad_rows, own0[0], own0[1]), (normed2_other, grad_rows_other, other0[0], other0[1])],
        vec, chunk([f1_near, f1_second, f1_third, f1_fourth]),
    )
    own1 = order.mark(own1)
    result_rest, grad_rest = links.swap(other1[0]), links.swap(other1[1])
    keep1, send1 = products(own1, other1)
    result_rest, grad_rest, moved0 = order.mark(result_rest, grad_rest, moved0)
    keep0, send0 = fold(keep0, moved0)
    moved0 = links.x_first(send0)
    output, grad_res, gm0, branch_cols, sent, sums2 = second_norm_back(
        core_arg, residual, (order.go(own1[0]), result_rest), (own1[1], grad_rest), grad_rows,
        (own_out, other_out), vec, lengths,
    )
    sent, moved0 = order.mark(sent, moved0)
    moved1 = links.y_first(order.go(send1))
    parts0 = links.scatter_z(fold_last((keep0, moved0)))
    got = links.swap(sent)
    dj0, diag0 = attention_backward(joined0, probs0, mixed0, order.go(gm0), head_size)
    dj0, got = order.mark(dj0, got)
    dj1, diag1 = attention_backward(joined1, probs1, mixed1, order.go(got), head_size)
    dj1, moved1, parts0 = order.mark(dj1, moved1, parts0)
    keep1, send1 = fold(keep1, moved1)
    moved1 = links.x_first(send1)
    keep, send = outer_products(
        core_arg,
        [([(normed, None), (normed_other, None)], [(order.go(dj0), j), (dj1, j)]) for j in range(3)]
        + [([((mixed0, mixed_rest), None), ((mixed1, mixed_rest_other), None)], [(branch_cols, None), (got, 1)])],
        scatter_offsets,
        links.rows,
    )
    keep, send, moved1 = order.mark(keep, send, moved1)
    moved = links.y_first(send)
    parts1 = links.scatter_z(fold_last((keep1, moved1)))
    part = order.mark(normed_back(order.go(dj1), own))
    part_rest = links.swap(part)
    ffn0 = total_feed_forward(core_arg, order.go(parts0), local)
    ffn0, part_rest = order.mark(ffn0, part_rest)
    input_grad, vec_grads, table_grad = first_norm_back(
        core_arg, (order.go(dj0), dj1), part_rest, tokens, grad_res, vec, own, sums2, ([sums_f0], [sums_f1]),
        (diag0, diag1), (line, line_other), number, False,
    )
    late_keep, late_send = order.mark(*late_slots(vec_grads, table_grad, scatter_offsets))
    late_moved = links.y_first(late_send)
    moved = order.mark(moved)
    keep, send = fold(keep, moved)
    moved = links.x_first(send)
    late_moved, parts1 = order.mark(late_moved, parts1)
    late_keep, late_send = fold(late_keep, late_moved)
    late_moved = links.x_first(late_send)
    ffn1 = total_feed_forward(core_arg, order.go(parts1), local)
    ups = [links.swap(ffn0[1]), links.swap(ffn1[1])]
    ups, ffn1 = order.mark(ups, ffn1)
    grad_up, grad_down = finish_feed_forward(
        core_arg, [ffn0[0], ffn1[0]], ups, [ffn0[2], ffn1[2]]
    )
    grad_up, grad_down, moved, late_moved = order.mark(grad_up, grad_down, moved, late_moved)
    parts = links.scatter_z(fold_last((keep, moved), (late_keep, late_moved)))
    mine, sent, tail = total_attention(core_arg, parts, local)
    theirs, tail_theirs = links.swap(sent), links.swap(tail)
    grad_qkv, grad_out, small, grad_table = finish_attention(
        core_arg, mine, theirs, tail, tail_theirs, heads, number
    )
    small_grads = [small[i, :local] for i in range(VECTORS)]
    unit = 2 * local
    halves = small[8:12, :].reshape(2, 2, TILE)
    grad_up_bias = lax.dynamic_index_in_dim(halves, core, 1, keepdims=False)[:, :unit].reshape(2 * unit)

    return (
        output,
        input_grad,
        small_grads[0],
        small_grads[1],
        grad_qkv,
        small_grads[2],
        small_grads[3],
        grad_out,
        small_grads[4],
        grad_table,
        small_grads[5],
        small_grads[6],
        grad_up,
        grad_up_bias,
        grad_down,
        small_grads[7],
    )


def on_any_mesh(
    tokens,
    lengths,
    buckets,
    ln1_gain,
    ln1_bias,
    qkv_weight,
    q_bias,
    v_bias,
    out_weight,
    out_bias,
    rel_table,
    ln2_gain,
    ln2_bias,
    up_weight,
    up_bias,
    down_weight,
    down_bias,
    cotangent,
):
    rows, model = tokens.shape
    heads, number = rel_table.shape
    head_size = model // heads
    width = model // 2
    local = qkv_weight.shape[0]
    hidden = up_weight.shape[1]
    core = jnp.zeros((1,), jnp.int32)
    offsets = jnp.zeros((1,), jnp.int32)

    def gathered(x):
        return lax.all_gather(x, AXES, axis=0, tiled=True)

    def scattered(x):
        return lax.psum_scatter(x, AXES, scatter_dimension=0, tiled=True)

    vectors = [ln1_gain, ln1_bias, q_bias, v_bias, out_bias, ln2_gain, ln2_bias, down_bias]
    unit = up_bias.shape[0]
    small = gathered(jnp.concatenate([*vectors, up_bias])[None, :])
    wide = [small[:, i * local : (i + 1) * local].reshape(1, model) for i in range(VECTORS)]
    ub = small[:, VECTORS * local :].reshape(2, 2, model).transpose(1, 0, 2).reshape(4, model)
    del unit
    vec = jnp.concatenate([*wide, ub, jnp.zeros((4, model), BF)], 0).astype(F32)
    attn = gathered(jnp.concatenate([qkv_weight, out_weight], 1))
    up, down = gathered(up_weight), gathered(down_weight)
    a_pieces = tuple(
        jnp.stack([attn[:, j * model + h * width : j * model + (h + 1) * width] for j in range(3)])
        for h in range(2)
    )

    a_out = tuple(attn[:, 3 * model + h * width : 3 * model + (h + 1) * width] for h in range(2))

    def chunk(f, h):
        at = (2 * h + f) * model
        blocks = [one[:, k * width : (k + 1) * width] for one in (up[:, at : at + model], down[at : at + model]) for k in range(2)]
        return Pieces([jnp.concatenate(blocks, 0)[None]], offsets, model)

    ahead = jnp.roll(buckets[0, rows - 1], 1)
    line = jnp.concatenate([ahead, buckets[0, 0]]).astype(F32)
    line = jnp.stack([line, jnp.full_like(line, lengths[0])] + [jnp.zeros_like(line)] * 6)
    tiles, grad_rows = bias_tiles(core, (line, line), rel_table, cotangent, lengths, (0, 1))
    normed, joined0, mixed0, probs0 = attention_forward(0, 0, core, tokens, vec, a_pieces[0], tiles, line, head_size)
    _, joined1, mixed1, probs1 = attention_forward(1, 1, core, tokens, vec, a_pieces[1], tiles, line, head_size)
    residual, normed2 = project_out(core, (mixed0, mixed1), tokens, a_out, vec)
    result, grad_n2 = residual, None
    up_sums, ups, downs = [[], []], [], []
    for f in range(2):
        for h in range(2):
            ((result, grad_n2, active, grad_pre),), sums = feed_forward(
                lambda c, at=8 + 2 * f + h: c + at, core, [(normed2, grad_rows, result, grad_n2)], vec, chunk(f, h)
            )
            up_sums[f].append(sums)
            (both,) = outer_products(
                core,
                [([(normed2, None)], [(grad_pre, k)]) for k in range(2)]
                + [([(active, None)], [(grad_rows, k)]) for k in range(2)],
                offsets,
                model,
            )
            both = both[0].reshape(2, 2, model, width).transpose(0, 2, 1, 3).reshape(2, model, model)
            ups.append(both[0])
            downs.append(both[1])
    output, grad_res, gm0, branch0, sent, sums2 = second_norm_back(
        core, residual, (result,), (grad_n2,), grad_rows, a_out, vec, lengths
    )
    dj0, diag0 = attention_backward(joined0, probs0, mixed0, gm0, head_size)
    dj1, diag1 = attention_backward(joined1, probs1, mixed1, sent, head_size)
    input_grad, vec_grads, table_grad = first_norm_back(
        core, (dj0, dj1), normed_back(dj1, a_pieces[1]), tokens, grad_res, vec, a_pieces[0], sums2, up_sums,
        (diag0, diag1), (line, line), number, True,
    )
    mixed = jnp.concatenate([mixed0, mixed1], 1)
    halves = [
        outer_products(
            core, [([(normed, None)], [(dj, j)]) for j in range(3)] + [([(mixed, None)], [branch])], offsets, model
        )[0][0].reshape(4, model, width)
        for dj, branch in ((dj0, (branch0, None)), (dj1, (sent, 1)))
    ]
    grads = jnp.stack(halves, 2).transpose(1, 0, 2, 3).reshape(model, 4 * model)
    grads = scattered(grads)
    grad_up = scattered(jnp.concatenate([ups[0], ups[2], ups[1], ups[3]], 1))
    grad_down = scattered(jnp.concatenate([downs[0], downs[2], downs[1], downs[3]], 0))
    by_owner = vec_grads[:VECTORS].reshape(VECTORS, model // local, local).transpose(1, 0, 2)
    own_units = vec_grads[VECTORS : VECTORS + 4].reshape(2, 2, model).transpose(1, 0, 2)
    both = jnp.concatenate(
        [by_owner.reshape(model // local, VECTORS * local), own_units.reshape(model // local, hidden * local // model)],
        1,
    )
    both = scattered(both)[0]
    table = jnp.concatenate([table_grad[16:], table_grad[:16, TILE : TILE + number - width]], 1)[:heads]
    grad_table = lax.psum(table, AXES)
    small_grads = [both[i * local : (i + 1) * local] for i in range(VECTORS)]
    return (
        output,
        input_grad,
        small_grads[0],
        small_grads[1],
        grads[:, : 3 * model].astype(F32),
        small_grads[2],
        small_grads[3],
        grads[:, 3 * model :].astype(F32),
        small_grads[4],
        grad_table,
        small_grads[5],
        small_grads[6],
        grad_up.astype(F32),
        both[VECTORS * local :],
        grad_down.astype(F32),
        small_grads[7],
    )


def solution(mesh):
    both = P(AXES)
    row = P(AXES, None)
    in_specs = (
        row, both, P(AXES, None, None), both, both, row, both, both, row, both, P(), both, both, row, both, row,
        both, row,
    )
    out_specs = (row, row, both, both, row, both, both, row, both, P(), both, both, row, both, row, both)

    if tuple(mesh.shape[name] for name in AXES) == (2, 16):

        def body(*args):
            return on_device(GridLinks((2, 4, 2), args[0].shape[1]), *args)

    else:
        body = on_any_mesh

    return jax.shard_map(body, mesh=mesh, in_specs=in_specs, out_specs=out_specs, check_vma=False)
```

```python
import functools

import jax
import jax.numpy as jnp
from jax import lax
from jax.experimental import pallas as pl
from jax.experimental.pallas import tpu as pltpu
from jax.sharding import PartitionSpec as P

BF = jnp.bfloat16
F32 = jnp.float32
AXES = ("dp", "fsdp")
TILE = 128
CHUNK = 64
EPS = 1e-05
NN = (((1,), (0,)), ((), ()))
NT = (((1,), (1,)), ((), ()))
TN = (((0,), (0,)), ((), ()))
VMEM = pltpu.VMEM


def mm(left, right, dims=NN):
    return lax.dot_general(left, right, dims, preferred_element_type=F32)


def any_spec():
    return pl.BlockSpec(memory_space=pl.ANY)


def hbm_spec():
    return pl.BlockSpec(memory_space=pltpu.HBM)


def in_hbm(x):
    return pltpu.with_memory_space_constraint(x, pltpu.HBM)


def smem_spec():
    return pl.BlockSpec(memory_space=pltpu.SMEM)


def whole(shape):
    return pl.BlockSpec(shape, lambda *_: (0,) * len(shape))


def params(mebibytes):
    return pltpu.CompilerParams(
        dimension_semantics=("arbitrary",), vmem_limit_bytes=mebibytes * 1024 * 1024
    )


def cost(micros):
    return pl.CostEstimate(flops=int(micros * 1e9), bytes_accessed=1, transcendentals=0)


class Pieces:
    def __init__(self, buffers, offsets, rows):
        self.buffers = buffers
        self.offsets = offsets
        self.rows = rows

    @property
    def slots(self):
        return sum(b.shape[0] for b in self.buffers)


def lay_blocks(refs, offs_ref, rows, count, put):
    slot = 0
    for ref in refs:
        for k in range(ref.shape[0]):
            at = pl.multiple_of(offs_ref[slot], 16)
            for j in range(count):
                put(j, at, ref[k, j * rows : (j + 1) * rows, :])
            slot += 1


def row_norm(x):
    centre = x - jnp.mean(x, -1, keepdims=True)
    scale = lax.rsqrt(jnp.mean(centre * centre, -1, keepdims=True) + EPS)
    return centre * scale, scale


def bucket_line(line, number):
    rows = lax.broadcasted_iota(jnp.int32, (number, line.shape[1]), 0)
    return jnp.where(rows == line.astype(jnp.int32), 1.0, 0.0).astype(BF)


def bias_tiles(core, lines, table, cotangent, lengths, halves):
    span = lines[0].shape[1]
    heads, number = table.shape
    count = heads // 2
    tiles = span // TILE - 1
    n = len(lines)
    rows, model = cotangent.shape

    def kernel(core_ref, len_ref, table_ref, cot_ref, *refs):
        line_refs, (out_ref, gr_ref, curve_ref) = refs[:n], refs[n:]
        at = pl.program_id(0)

        @pl.when(at == 0)
        def _():
            for i in range(n):
                curve = mm(table_ref[...], bucket_line(line_refs[i][0:1, :], number))
                curve = jnp.where((core_ref[0] ^ halves[i]) == 0, curve[:count], curve[count:])
                for h in range(count):
                    curve_ref[i * count + h] = jnp.broadcast_to(curve[h : h + 1], (8, span))
            row = lax.broadcasted_iota(jnp.int32, (rows, 1), 0)
            gr_ref[...] = jnp.where(row < len_ref[0], cot_ref[...].astype(F32), 0.0).astype(BF)

        base = pltpu.roll(curve_ref[at], 0, 1, stride=1, stride_axis=0)
        for pair in range(TILE // 16):
            rolled = jnp.concatenate(
                [pltpu.roll(base, 16 * pair + 8 * i, 1) if pair + i else base for i in range(2)], 0
            ).astype(BF)
            for d in range(tiles):
                out_ref[0, 0, d, 16 * pair : 16 * pair + 16, :] = rolled[
                    :, TILE * (d + 1) : TILE * (d + 2)
                ]

    return pl.pallas_call(
        kernel,
        grid=(n * count,),
        in_specs=[
            smem_spec(),
            smem_spec(),
            whole((heads, number)),
            whole((rows, model)),
            *[whole((8, span))] * n,
        ],
        out_specs=[
            pl.BlockSpec((1, 1, tiles, TILE, TILE), lambda h: (h // count, h % count, 0, 0, 0)),
            whole((rows, model)),
        ],
        out_shape=[
            VMEM((n, count, tiles, TILE, TILE), BF),
            VMEM((rows, model), BF),
        ],
        scratch_shapes=[VMEM((n * count, 8, span), F32)],
        compiler_params=params(8),
        cost_estimate=cost(4),
        name="bias_tiles",
    )(core, lengths, table, cotangent, *lines)


def place_rows(block, offset, wide):
    padded = jnp.concatenate([block, jnp.zeros((block.shape[0], wide - TILE), block.dtype)], 1)
    return pltpu.roll(padded, offset, 1)


def assemble_attention(pieces, model):
    width = model // 2
    rows = pieces.rows
    n_buf = len(pieces.buffers)

    def kernel(offs_ref, *refs):
        bufs, (w_ref, o_ref, vec_ref) = refs[:n_buf], refs[n_buf:]

        def put(j, at, block):
            if j < 3:
                w_ref[j, pl.ds(at, rows), :] = block
            else:
                o_ref[pl.ds(at, rows), :] = block

        lay_blocks(bufs, offs_ref, rows, 4, put)
        total, slot = jnp.zeros((16, model), F32), 0
        for ref in bufs:
            for k in range(ref.shape[0]):
                total += place_rows(ref[k, 4 * rows : 4 * rows + 16, :TILE].astype(F32), offs_ref[slot], model)
                slot += 1
        vec_ref[...] = total

    return pl.pallas_call(
        kernel,
        grid=(1,),
        in_specs=[smem_spec(), *[whole(one.shape) for one in pieces.buffers]],
        out_specs=[whole((3, model, width)), whole((model, width)), whole((16, model))],
        out_shape=[
            VMEM((3, model, width), BF),
            VMEM((model, width), BF),
            VMEM((16, model), F32),
        ],
        compiler_params=params(6),
        cost_estimate=cost(2),
        name="assemble_attention",
    )(pieces.offsets, *pieces.buffers)


def attention_forward(item, half, core, tokens, vec, weights, tiles, line, head_size):
    rows, model = tokens.shape
    width = model // 2
    heads = width // head_size
    pairs = width // TILE
    per = TILE // head_size
    scale = head_size**-0.5

    def kernel(core_ref, line_ref, x_ref, vec_ref, tile_ref, w_ref, n1_ref, joined_ref, mixed_ref, p_ref, qs_ref, s_ref):
        pair = pl.program_id(0)

        @pl.when(pair == 0)
        def _():
            for r in range(0, rows, CHUNK):
                xhat, _ = row_norm(x_ref[r : r + CHUNK, :].astype(F32))
                n1_ref[r : r + CHUNK, :] = (xhat * vec_ref[0:1, :] + vec_ref[1:2, :]).astype(BF)
            cols = pl.ds(pl.multiple_of((core_ref[0] ^ half) * width, TILE), width)
            for j in range(3):
                joined = mm(n1_ref[...], w_ref[j])
                if j != 1:
                    joined = joined + vec_ref[2 + j // 2 : 3 + j // 2, cols]
                qs_ref[j] = joined.astype(BF)

        lanes = pl.ds(pl.multiple_of(pair * TILE, TILE), TILE)
        q, k, v = (qs_ref[j, :, lanes] for j in range(3))
        for j, one in enumerate((q, k, v)):
            joined_ref[j] = one
        lane = lax.broadcasted_iota(jnp.int32, (1, TILE), 1)
        column = lax.broadcasted_iota(jnp.int32, (1, rows), 1)
        dead = jnp.where(column < line_ref[1:2, :rows].astype(jnp.int32), 0.0, -1e30).astype(F32)
        scaled = q.astype(F32) * scale
        outs = []
        for e in range(per):
            mine = (lane >= e * head_size) & (lane < (e + 1) * head_size)
            qm = jnp.where(mine, scaled, 0.0).astype(BF)
            s_ref[e] = mm(qm, k, NT)
            for r in range(0, rows, CHUNK):
                block, sub = r // TILE, r % TILE
                rel = jnp.concatenate(
                    [
                        tile_ref[0, e, j - block + rows // TILE - 1, sub : sub + CHUNK, :]
                        for j in range(rows // TILE)
                    ],
                    1,
                ).astype(F32)
                s = s_ref[e, r : r + CHUNK, :] + (rel + dead)
                raised = jnp.exp(s - jnp.max(s, -1, keepdims=True))
                inv = 1.0 / jnp.sum(raised, -1, keepdims=True)
                p_ref[e, r : r + CHUNK, :] = (raised * inv).astype(BF)
            outs.append(jnp.where(mine, mm(p_ref[e], v), 0.0))
        mixed_ref[...] = functools.reduce(lambda a, b: a + b, outs).astype(BF)

    shapes = [
        VMEM((3, rows, width), BF),
        VMEM((rows, width), BF),
        VMEM((heads, rows, rows), BF),
    ]
    outs = [
        pl.BlockSpec((3, rows, TILE), lambda p: (0, 0, p)),
        pl.BlockSpec((rows, TILE), lambda p: (0, p)),
        pl.BlockSpec((per, rows, rows), lambda p: (p, 0, 0)),
    ]
    shapes.insert(0, VMEM((rows, model), BF))
    outs.insert(0, whole((rows, model)))
    return pl.pallas_call(
        kernel,
        grid=(pairs,),
        in_specs=[
            smem_spec(),
            whole((8, 2 * rows)),
            whole((rows, model)),
            whole((16, model)),
            pl.BlockSpec((1, per, tiles.shape[2], TILE, TILE), lambda p: (item, p, 0, 0, 0)),
            whole((3, model, width)),
        ],
        out_specs=outs,
        out_shape=shapes,
        scratch_shapes=[VMEM((3, rows, width), BF), VMEM((per, rows, rows), F32)],
        compiler_params=params(12),
        cost_estimate=cost(6),
        name="attention_forward",
    )(core, line, tokens, vec, tiles, weights)


def project_out(core, mixed, tokens, weights, vec):
    rows, model = tokens.shape
    width = model // 2

    def kernel(core_ref, m0_ref, m1_ref, x_ref, vec_ref, w0_ref, w1_ref, res_ref, n2_ref):
        for h, w_ref in enumerate((w0_ref, w1_ref)):
            cols = pl.ds(pl.multiple_of((core_ref[0] ^ h) * width, TILE), width)
            acc = 0.0
            for g, m_ref in enumerate((m0_ref, m1_ref)):
                feats = pl.ds(pl.multiple_of((core_ref[0] ^ g) * width, TILE), width)
                acc = acc + mm(m_ref[...], w_ref[feats, :])
            res_ref[:, cols] = x_ref[:, cols].astype(F32) + acc + vec_ref[4:5, cols]
        for r in range(0, rows, CHUNK):
            xhat, _ = row_norm(res_ref[r : r + CHUNK, :])
            n2_ref[r : r + CHUNK, :] = (xhat * vec_ref[5:6, :] + vec_ref[6:7, :]).astype(BF)

    return pl.pallas_call(
        kernel,
        grid=(1,),
        in_specs=[
            smem_spec(),
            whole((rows, width)),
            whole((rows, width)),
            whole((rows, model)),
            whole((16, model)),
            whole((model, width)),
            whole((model, width)),
        ],
        out_specs=[whole((rows, model)), whole((rows, model))],
        out_shape=[
            VMEM((rows, model), F32),
            VMEM((rows, model), BF),
        ],
        compiler_params=params(6),
        cost_estimate=cost(2.5),
        name="project_out",
    )(core, mixed[0], mixed[1], tokens, vec, *weights)


def gelu_parts(v):
    bell = jnp.exp(-0.5 * (v * v))
    t = 1.0 / (1.0 + 0.23164189 * jnp.abs(v))
    tail = t * (0.127414796 + t * (-0.142248368 + t * (0.710706871 + t * (-0.726576014 + t * 0.530702714))))
    tail = tail * bell
    return jnp.where(v < 0.0, tail, 1.0 - tail), bell * 0.3989422804014327


def feed_forward(row, core, sets, vec, pieces, offsets=None):
    rows, model = sets[0][0].shape
    hidden = model
    n = len(sets)
    n_buf = len(pieces.buffers)
    per = pieces.rows
    half = rows // 2
    width = model // 2

    def kernel(core_ref, offs_ref, out_offs_ref, vec_ref, *refs):
        ins, refs = refs[: len(flat)], refs[len(flat) :]
        bufs, refs = refs[:n_buf], refs[n_buf:]
        outs, refs = refs[: 4 * n], refs[4 * n :]
        col_ref, slot_refs, (up_ref, down_ref, w_ref) = refs[0], refs[1:-3], refs[-3:]

        def put(j, at, block):
            ref = up_ref if j < 2 else down_ref
            ref[pl.ds(at, per), (j % 2) * width : (j % 2 + 1) * width] = block

        lay_blocks(bufs, offs_ref, per, 4, put)
        up_bias = vec_ref[pl.ds(row(core_ref[0]), 1), :]
        sums = jnp.zeros((1, hidden), F32)
        for i in range(n):
            n_ref, gr_ref, res_ref, gin_ref = (None if at is None else ins[at] for at in where[i])
            out_ref, gn_ref, act_ref, gp_ref = outs[4 * i : 4 * i + 4]
            for r in range(0, rows, half):
                block = slice(r, r + half)
                pre = mm(n_ref[block, :], up_ref[...]) + up_bias
                gact = mm(gr_ref[block, :], down_ref[...], NT)
                cdf, density = gelu_parts(pre)
                act = (pre * cdf).astype(BF)
                gp = gact * (cdf + pre * density)
                low = gp.astype(BF)
                act_ref[block, :] = act
                gp_ref[block, :] = low
                sums += jnp.sum(low.astype(F32), 0, keepdims=True)
                out = mm(act, down_ref[...])
                if res_ref is not None:
                    out = out + res_ref[block, :]
                    if gin_ref is None:
                        out = out + vec_ref[7:8, :]
                out_ref[block, :] = out
                gn = mm(low, up_ref[...], NT)
                gn_ref[block, :] = gn if gin_ref is None else gn + gin_ref[block, :]
        col_ref[...] = sums
        if offsets is None:
            return
        for m in range(4):
            cols = slice((m % 2) * width, (m % 2 + 1) * width)
            total = 0.0
            for i in range(n):
                n_ref, gr_ref = (ins[at] for at in where[i][:2])
                act_ref, gp_ref = outs[4 * i + 2 : 4 * i + 4]
                left, right = (n_ref, gp_ref) if m < 2 else (act_ref, gr_ref)
                total = total + mm(left[...], right[:, cols], TN)
            w_ref[...] = total.astype(BF)
            to_slots(w_ref, out_offs_ref, slot_refs, m, per)

    flat, where = [], []
    for one in sets:
        places = []
        for array in one:
            places.append(None if array is None else len(flat))
            if array is not None:
                flat.append(array)
        where.append(places)
    shapes = [
        VMEM((rows, model), F32),
        VMEM((rows, model), F32),
        VMEM((rows, hidden), BF),
        VMEM((rows, hidden), BF),
    ] * n + [VMEM((1, hidden), F32)]
    if offsets is not None:
        shapes += [VMEM((offsets.shape[0] // 2, 4 * per, width), BF)] * 2
    out = pl.pallas_call(
        kernel,
        grid=(1,),
        in_specs=[
            *[smem_spec()] * 3,
            whole((16, model)),
            *[whole((rows, model))] * len(flat),
            *[whole(one.shape) for one in pieces.buffers],
        ],
        out_specs=[whole(one.shape) for one in shapes],
        out_shape=shapes,
        scratch_shapes=[
            VMEM((model, hidden), BF),
            VMEM((hidden, model), BF),
            VMEM((model, width), BF),
        ],
        compiler_params=params(20),
        cost_estimate=cost(13),
        name="feed_forward",
    )(core, pieces.offsets, pieces.offsets if offsets is None else offsets, vec, *flat, *pieces.buffers)
    return [out[4 * i : 4 * i + 4] for i in range(n)], out[4 * n], out[4 * n + 1 :]


def to_slots(w_ref, offs_ref, outs, matrix, rows):
    slot = 0
    for out in outs:
        for k in range(out.shape[0]):
            at = pl.multiple_of(offs_ref[slot], 16)
            out[k, matrix * rows : (matrix + 1) * rows, :] = w_ref[pl.ds(at, rows), :]
            slot += 1


class Products:
    def __init__(self, core, pairs, offsets, rows, counts):
        self.core, self.offsets, self.rows = core, offsets, rows
        self.tall = pairs[0][0][0][0].shape[-1]
        self.wide = self.tall // 2
        self.flat = []
        self.where = [([self._place(*one) for one in lefts], [self._place(*one) for one in rights]) for lefts, rights in pairs]
        self.shapes = [VMEM((count, len(pairs) * rows, self.wide), BF) for count in counts]
        self.scratch = VMEM((self.tall, self.wide), BF)

    def _place(self, one, part):
        if isinstance(one, tuple):
            return [self._place(each, part) for each in one]
        if one is None:
            return None, part
        match = [i for i, known in enumerate(self.flat) if known is one]
        if not match:
            self.flat.append(one)
            match = [len(self.flat) - 1]
        return match[0], part

    def run(self, core_ref, offs_ref, ins, outs, w_ref, own_ref=None):
        def pick(at, part):
            ref = own_ref if at is None else ins[at]
            if part is None:
                return ref[...]
            if len(ref.shape) == 3:
                return ref[part]
            return ref[:, part * self.wide : (part + 1) * self.wide]

        for m, (lefts, rights) in enumerate(self.where):
            if isinstance(lefts[0], list):
                for h in range(2):
                    total = sum(mm(pick(*left[h]), pick(*right), TN) for left, right in zip(lefts, rights))
                    at = pl.multiple_of((core_ref[0] ^ h) * self.wide, 16)
                    w_ref[pl.ds(at, self.wide), :] = total.astype(BF)
            else:
                total = sum(mm(pick(*left), pick(*right), TN) for left, right in zip(lefts, rights))
                w_ref[...] = total.astype(BF)
            to_slots(w_ref, offs_ref, outs, m, self.rows)


def outer_products(core, pairs, offsets, rows):
    work = Products(core, pairs, offsets, rows, offsets.shape)
    n = len(work.flat)

    def kernel(core_ref, offs_ref, *rest):
        work.run(core_ref, offs_ref, rest[:n], rest[n:-1], rest[-1])

    return pl.pallas_call(
        kernel,
        grid=(1,),
        in_specs=[smem_spec(), smem_spec(), *[whole(one.shape) for one in work.flat]],
        out_specs=[whole(one.shape) for one in work.shapes],
        out_shape=work.shapes,
        scratch_shapes=[work.scratch],
        compiler_params=params(14),
        cost_estimate=cost(5),
        name="outer_products",
    )(core, offsets, *work.flat)


def late_slots(vectors, table, offsets):
    model = vectors.shape[1]
    slots = offsets.shape[0]
    half = slots // 2

    def kernel(offs_ref, vec_ref, table_ref, keep_ref, send_ref):
        for i, ref in enumerate((keep_ref, send_ref)):
            for s in range(half):
                moved = pltpu.roll(vec_ref[...], lax.rem(model - offs_ref[i * half + s], model), 1)
                ref[16 * s : 16 * s + 16, :] = moved[:, :TILE].astype(BF)
            ref[16 * half :, :] = table_ref[...].astype(BF)

    shape = (16 * half + table.shape[0], TILE)
    return pl.pallas_call(
        kernel,
        grid=(1,),
        in_specs=[smem_spec(), whole(vectors.shape), whole(table.shape)],
        out_specs=[whole(shape)] * 2,
        out_shape=[VMEM(shape, BF)] * 2,
        compiler_params=params(4),
        cost_estimate=cost(1),
        name="late_slots",
    )(offsets, vectors, table)


def norm_back(x, up, gain):
    xhat, scale = row_norm(x)
    e = up * gain
    grad = scale * (e - jnp.mean(e, -1, keepdims=True) - xhat * jnp.mean(e * xhat, -1, keepdims=True))
    return grad, up * xhat


def second_norm_back(core, residual, results, grads_normed, grad_rows, weights, vec, lengths):
    rows, model = residual.shape
    width = model // 2
    n, m = len(results), len(grads_normed)

    def kernel(core_ref, len_ref, res_ref, gr_ref, vec_ref, w0_ref, w1_ref, *refs):
        out_refs, gn_refs = refs[:n], refs[n : n + m]
        out_ref, gres_ref, gm_ref, br_ref, sent_ref, sums_ref, gb_ref = refs[n + m :]
        totals = [jnp.zeros((1, model), F32) for _ in range(4)]
        for r in range(0, rows, CHUNK):
            block = slice(r, r + CHUNK)
            row = lax.broadcasted_iota(jnp.int32, (CHUNK, 1), 0) + r
            result = functools.reduce(lambda a, b: a + b, [ref[block, :] for ref in out_refs])
            out_ref[block, :] = jnp.where(row < len_ref[0], result, 0.0).astype(BF)
            up = functools.reduce(lambda a, b: a + b, [ref[block, :] for ref in gn_refs])
            grad, gain_terms = norm_back(res_ref[block, :], up, vec_ref[5:6, :])
            gr = gr_ref[block, :].astype(F32)
            grad = gr + grad
            low = grad.astype(BF)
            gres_ref[block, :] = grad
            gb_ref[block, :] = low
            for i, terms in enumerate((gain_terms, up, low.astype(F32), gr)):
                totals[i] += jnp.sum(terms, 0, keepdims=True)
        sums_ref[...] = jnp.concatenate(totals + [jnp.zeros((4, model), F32)], 0)
        parts = [pl.ds(pl.multiple_of((core_ref[0] ^ h) * width, TILE), width) for h in range(2)]
        for h in range(2):
            acc = 0.0
            for g, w_ref in enumerate((w0_ref, w1_ref)):
                acc = acc + mm(gb_ref[:, parts[g]], w_ref[parts[h], :], NT)
            if h == 0:
                gm_ref[...] = acc.astype(BF)
                br_ref[...] = gb_ref[:, parts[0]]
            else:
                sent_ref[:, :width] = acc.astype(BF)
                sent_ref[:, width:] = gb_ref[:, parts[1]]

    return pl.pallas_call(
        kernel,
        grid=(1,),
        in_specs=[
            *[smem_spec()] * 2,
            *[whole((rows, model))] * 2,
            whole((16, model)),
            whole((model, width)),
            whole((model, width)),
            *[whole((rows, model))] * (n + m),
        ],
        out_specs=[
            *[whole((rows, model))] * 2,
            *[whole((rows, width))] * 2,
            whole((rows, model)),
            whole((8, model)),
        ],
        out_shape=[
            jax.ShapeDtypeStruct((rows, model), BF),
            jax.ShapeDtypeStruct((rows, model), F32),
            jax.ShapeDtypeStruct((rows, width), BF),
            jax.ShapeDtypeStruct((rows, width), BF),
            jax.ShapeDtypeStruct((rows, model), BF),
            jax.ShapeDtypeStruct((8, model), F32),
        ],
        scratch_shapes=[VMEM((rows, model), BF)],
        compiler_params=params(10),
        cost_estimate=cost(4),
        name="second_norm_back",
    )(core, lengths, residual, grad_rows, vec, *weights, *results, *grads_normed)


def attention_backward(joined, probs, mixed, grad_mixed, head_size, products=None, weights=None):
    _, rows, width = joined.shape
    heads = width // head_size
    pairs = width // TILE
    per = TILE // head_size
    tiles = 2 * (rows // TILE) - 1
    span = 2 * rows
    scale = head_size**-0.5
    flat = [] if products is None else products.flat
    n_in = 4 + len(flat) + (2 if products else 0) + (1 if weights is not None else 0)

    def kernel(*refs):
        ins, refs = refs[:n_in], refs[n_in:]
        joined_ref, p_ref, mixed_ref, gm_ref = ins[:4]
        out_ref, diag_ref, refs = refs[0], refs[1], refs[2:]
        gp_ref, ds_ref, acc_ref = refs[-3:]
        lane = lax.broadcasted_iota(jnp.int32, (1, TILE), 1)
        for pair in range(pairs):
            lanes = slice(pair * TILE, (pair + 1) * TILE)
            q, k, v = (joined_ref[j, :, lanes] for j in range(3))
            gm = gm_ref[:, lanes]
            dots = gm.astype(F32) * mixed_ref[:, lanes].astype(F32)
            q_t, gm_t = q.T, gm.T
            dq, dk, dv = [], [], []
            for e in range(per):
                head = pair * per + e
                mine = (lane >= e * head_size) & (lane < (e + 1) * head_size)
                feats = slice(e * head_size, (e + 1) * head_size)
                delta = jnp.sum(jnp.where(mine, dots, 0.0), -1, keepdims=True)
                gp_ref[e] = mm(jnp.where(mine, gm, jnp.zeros_like(gm)), v, NT)
                acc_ref[...] = jnp.zeros_like(acc_ref)
                for r in range(0, rows, CHUNK):
                    block, sub = r // TILE, r % TILE
                    ds = p_ref[head, r : r + CHUNK, :].astype(F32) * (
                        gp_ref[e, r : r + CHUNK, :] - delta[r : r + CHUNK, :]
                    )
                    ds_ref[e, r : r + CHUNK, :] = ds.astype(BF)
                    for j in range(rows // TILE):
                        acc_ref[j - block + rows // TILE - 1, sub : sub + CHUNK, :] += ds[
                            :, j * TILE : (j + 1) * TILE
                        ]
                dq.append(jnp.where(mine, mm(ds_ref[e], k), 0.0))
                dk.append(mm(q_t[feats, :], ds_ref[e]))
                dv.append(mm(gm_t[feats, :], p_ref[head]))
                total = jnp.zeros((8, span), F32)
                for g in range(TILE // 8):
                    strip = jnp.concatenate(
                        [jnp.zeros((8, TILE), F32)]
                        + [acc_ref[d, 8 * g : 8 * g + 8, :] for d in range(tiles)],
                        1,
                    )
                    total += pltpu.roll(strip, (span - 8 * g) % span, 1) if g else strip
                line = total[0:1]
                for i in range(1, 8):
                    line = line + pltpu.roll(total[i : i + 1], span - i, 1)
                diag_ref[head] = line
            out_ref[0, :, lanes] = (functools.reduce(lambda a, b: a + b, dq) * scale).astype(BF)
            out_ref[1, :, lanes] = (jnp.concatenate(dk, 0) * scale).T.astype(BF)
            out_ref[2, :, lanes] = jnp.concatenate(dv, 0).T.astype(BF)
        if weights is not None:
            refs[0][...] = sum(mm(out_ref[j], ins[-1][j], NT) for j in range(3))
        if products is not None:
            slot_refs = refs[1:-4] if weights is not None else refs[:-4]
            products.run(ins[4], ins[5], ins[6 : 6 + len(flat)], slot_refs, refs[-4], out_ref)

    ins = [joined, probs, mixed, grad_mixed]
    specs = [whole(one.shape) for one in ins]
    shapes = [VMEM((3, rows, width), BF), VMEM((heads, 1, span), F32)]
    scratch = [VMEM((per, rows, rows), F32), VMEM((per, rows, rows), BF), VMEM((tiles, TILE, TILE), F32)]
    if products is not None:
        ins += [products.core, products.offsets, *flat]
        specs += [smem_spec(), smem_spec(), *[whole(one.shape) for one in flat]]
    if weights is not None:
        ins.append(weights)
        specs.append(whole(weights.shape))
        shapes.append(VMEM((rows, weights.shape[1]), F32))
    if products is not None:
        shapes += products.shapes
        scratch.insert(0, products.scratch)
    return pl.pallas_call(
        kernel,
        grid=(1,),
        in_specs=specs,
        out_specs=[whole(one.shape) for one in shapes],
        out_shape=shapes,
        scratch_shapes=scratch,
        compiler_params=params(16),
        cost_estimate=cost(4.5),
        name="attention_backward",
    )(*ins)


def normed_back(grads, weights):
    _, rows, width = grads.shape
    model = weights.shape[1]

    def kernel(d_ref, w_ref, out_ref):
        out_ref[...] = sum(mm(d_ref[j], w_ref[j], NT) for j in range(3))

    return pl.pallas_call(
        kernel,
        grid=(1,),
        in_specs=[whole(grads.shape), whole(weights.shape)],
        out_specs=whole((rows, model)),
        out_shape=VMEM((rows, model), F32),
        compiler_params=params(8),
        cost_estimate=cost(1.5),
        name="normed_back",
    )(grads, weights)


def first_norm_back(
    core, grads, part, tokens, grad_residual, vec, weights, sums_second, sums_up, diags, lines, number, apart
):
    rows, model = tokens.shape
    width = model // 2
    count = diags[0].shape[0]
    span = lines[0].shape[1]
    n_up = len(sums_up[0])

    def kernel(core_ref, d0_ref, d1_ref, part_ref, x_ref, gres_ref, vec_ref, w_ref, s2_ref, t0_ref, t1_ref, l0_ref, l1_ref,
               *rest):
        up_refs = rest[: 2 * n_up]
        gx_ref, sums_ref, table_ref, acc_ref = rest[2 * n_up :]
        straight = core_ref[0] == 0

        def ordered(a, b):
            return [jnp.where(straight, a, b), jnp.where(straight, b, a)]

        tables = []
        for t_ref, l_ref in ((t0_ref, l0_ref), (t1_ref, l1_ref)):
            chosen = bucket_line(l_ref[0:1, :], number)
            table, left = 0.0, t_ref[:, 0, :]
            for _ in range(3):
                low = left.astype(BF)
                table = table + mm(low, chosen, NT)
                left = left - low.astype(F32)
            tables.append(table)
        blank = jnp.zeros((count, number), F32)
        tables = tables if apart else ordered(tables[0] + tables[1], blank)
        table = jnp.concatenate([*tables, jnp.zeros((16 - 2 * count, number), F32)], 0)
        table = jnp.concatenate([table, jnp.zeros((16, 4 * TILE - number), F32)], 1)
        table_ref[...] = jnp.concatenate([table[:, i * TILE : (i + 1) * TILE] for i in range(4)], 0)
        columns = []
        for j in (0, 2):
            a, b = (jnp.sum(d_ref[j].astype(F32), 0, keepdims=True) for d_ref in (d0_ref, d1_ref))
            columns.append(jnp.concatenate([a, b] if apart else ordered(a + b, jnp.zeros_like(a)), 1))
        ups = []
        for f in range(2):
            here = [ref[...] for ref in up_refs[f * n_up : (f + 1) * n_up]]
            ups += here if apart else ordered(here[0], jnp.zeros_like(here[0]))
        acc_ref[...] = part_ref[...] + sum(mm(d0_ref[j], w_ref[j], NT) for j in range(3))
        totals = [jnp.zeros((1, model), F32) for _ in range(2)]
        for r in range(0, rows, CHUNK):
            block = slice(r, r + CHUNK)
            up = acc_ref[block, :]
            grad, gain_terms = norm_back(x_ref[block, :].astype(F32), up, vec_ref[0:1, :])
            gx_ref[block, :] = gres_ref[block, :] + grad
            totals[0] += jnp.sum(gain_terms, 0, keepdims=True)
            totals[1] += jnp.sum(up, 0, keepdims=True)
        sums_ref[...] = jnp.concatenate(
            totals
            + columns
            + [s2_ref[2:3, :], s2_ref[0:1, :], s2_ref[1:2, :], s2_ref[3:4, :]]
            + ups
            + [jnp.zeros((4, model), F32)],
            0,
        )

    return pl.pallas_call(
        kernel,
        grid=(1,),
        in_specs=[
            smem_spec(),
            whole((3, rows, width)),
            whole((3, rows, width)),
            whole((rows, model)),
            whole((rows, model)),
            whole((rows, model)),
            whole((16, model)),
            whole((3, model, width)),
            whole((8, model)),
            whole((count, 1, span)),
            whole((count, 1, span)),
            whole((8, span)),
            whole((8, span)),
            *[whole((1, model))] * (2 * n_up),
        ],
        out_specs=[whole((rows, model)), whole((16, model)), whole((64, TILE))],
        out_shape=[
            jax.ShapeDtypeStruct((rows, model), F32),
            jax.ShapeDtypeStruct((16, model), F32),
            jax.ShapeDtypeStruct((64, TILE), F32),
        ],
        scratch_shapes=[VMEM((rows, model), F32)],
        compiler_params=params(14),
        cost_estimate=cost(5),
        name="first_norm_back",
    )(
        core, *grads, part, tokens, grad_residual, vec, weights, sums_second, *diags, *lines, *sums_up[0], *sums_up[1]
    )


def pack_blocks(core, lengths, buckets, qkv, out, up):
    local, model = out.shape
    width = model // 2
    unit = local * 2
    chips = up.shape[1] // (4 * unit)
    rows = buckets.shape[1]

    def kernel(core_ref, len_ref, buckets_hbm, qkv_hbm, out_hbm, up_hbm, a0_ref, a1_ref, u0_ref, u1_ref, line_ref,
               first_ref, last_ref, qkv_ref, out_ref, up_ref, sems):
        copies = [
            pltpu.make_async_copy(source, target, sems.at[i])
            for i, (source, target) in enumerate(
                (
                    (qkv_hbm, qkv_ref),
                    (out_hbm, out_ref),
                    (up_hbm, up_ref),
                    (buckets_hbm.at[pl.ds(0, 1), pl.ds(0, 8)], first_ref),
                    (buckets_hbm.at[pl.ds(0, 1), pl.ds(rows - 8, 8)], last_ref),
                )
            )
        ]
        for c in copies:
            c.start()
        for c in copies:
            c.wait()
        core_at = core_ref[0]
        for h, a_ref in enumerate((a0_ref, a1_ref)):
            at = (core_at ^ h) * width
            for j in range(3):
                a_ref[j] = qkv_ref[:, pl.ds(pl.multiple_of(j * model + at, TILE), width)]
            a_ref[3] = out_ref[:, pl.ds(pl.multiple_of(at, TILE), width)]
        first = core_at == 0
        ahead = pltpu.roll(last_ref[0, 7:8, :].astype(F32), 1, 1)
        line = jnp.concatenate([ahead, first_ref[0, 0:1, :].astype(F32)], 1)
        live = jnp.zeros_like(line) + len_ref[0].astype(F32)
        line_ref[...] = jnp.concatenate([line, live, jnp.zeros((6, 2 * rows), F32)], 0)
        for f in range(2):
            by_core = []
            for c in range(2):
                by_core.append(
                    jnp.concatenate(
                        [
                            up_ref[:, ((2 * chip + c) * 2 + f) * unit : ((2 * chip + c) * 2 + f + 1) * unit]
                            for chip in range(chips)
                        ],
                        1,
                    ).astype(F32)
                )
            u0_ref[f] = jnp.where(first, by_core[0], by_core[1]).astype(BF)
            u1_ref[f] = jnp.where(first, by_core[1], by_core[0]).astype(BF)

    shapes = [
        *[VMEM((4, local, width), BF)] * 2,
        *[VMEM((2, local, model), BF)] * 2,
        VMEM((8, 2 * rows), F32),
    ]
    return pl.pallas_call(
        kernel,
        grid=(1,),
        in_specs=[
            smem_spec(),
            smem_spec(),
            *[hbm_spec()] * 4,
        ],
        out_specs=[whole(one.shape) for one in shapes],
        out_shape=shapes,
        scratch_shapes=[
            VMEM((1, 8, rows), jnp.int32),
            VMEM((1, 8, rows), jnp.int32),
            VMEM(qkv.shape, BF),
            VMEM(out.shape, BF),
            VMEM(up.shape, BF),
            pltpu.SemaphoreType.DMA((5,)),
        ],
        compiler_params=params(6),
        cost_estimate=cost(1.5),
        name="pack_blocks",
    )(core, lengths, in_hbm(buckets), in_hbm(qkv), in_hbm(out), in_hbm(up))


def pack_vectors(core, vectors):
    _, local = vectors.shape

    def kernel(core_ref, vec_ref, small_ref):
        first = core_ref[0] == 0
        values = jnp.concatenate(
            [vec_ref[...].astype(F32), jnp.zeros((VECTORS + 4, TILE - local), F32)], 1
        )
        moved = pltpu.roll(values, local, 1)
        lines = [jnp.where(first, values[:VECTORS], moved[:VECTORS])]
        for f in range(2):
            at = VECTORS + 2 * f
            both = values[at : at + 1] + moved[at + 1 : at + 2]
            blank = jnp.zeros_like(both)
            lines += [jnp.where(first, both, blank), jnp.where(first, blank, both)]
        small_ref[...] = jnp.concatenate(lines + [jnp.zeros((4, TILE), F32)], 0).astype(BF)

    return pl.pallas_call(
        kernel,
        grid=(1,),
        in_specs=[smem_spec(), whole(vectors.shape)],
        out_specs=whole((16, TILE)),
        out_shape=VMEM((16, TILE), BF),
        compiler_params=params(4),
        cost_estimate=cost(1),
        name="pack_vectors",
    )(core, vectors)


def ordered_rows(core_at, mine, theirs):
    first = core_at == 0
    a, b = mine.astype(F32), theirs.astype(F32)
    return jnp.concatenate([jnp.where(first, a, b), jnp.where(first, b, a)], 0)


def merge_attention(core, mine, theirs, small, small_theirs):
    count, local, width = mine.shape

    def kernel(core_ref, a_ref, b_ref, s_ref, t_ref, out_ref):
        for j in range(count):
            out_ref[2 * local * j : 2 * local * (j + 1), :] = ordered_rows(core_ref[0], a_ref[j], b_ref[j]).astype(BF)
        vec = s_ref[...].astype(F32) + t_ref[...].astype(F32)
        out_ref[2 * local * count :, :] = jnp.concatenate([vec, jnp.zeros((16, width - TILE), F32)], 1).astype(BF)

    return pl.pallas_call(
        kernel,
        grid=(1,),
        in_specs=[smem_spec(), *[whole(mine.shape)] * 2, *[whole(small.shape)] * 2],
        out_specs=whole((2 * local * count + 16, width)),
        out_shape=VMEM((2 * local * count + 16, width), BF),
        compiler_params=params(4),
        cost_estimate=cost(1),
        name="merge_attention",
    )(core, mine, theirs, small, small_theirs)


def merge_feed_forward(core, mine, theirs, down):
    _, local, model = mine.shape
    unit = 2 * local
    width = model // 2

    def kernel(core_ref, a_ref, b_ref, d_ref, *outs):
        for f in range(2):
            up = ordered_rows(core_ref[0], a_ref[f], b_ref[f]).astype(BF)
            low = d_ref[f * unit : (f + 1) * unit, :]
            for j, block in enumerate((up[:, :width], up[:, width:], low[:, :width], low[:, width:])):
                outs[f][j * unit : (j + 1) * unit, :] = block

    shape = VMEM((4 * unit, width), BF)
    return pl.pallas_call(
        kernel,
        grid=(1,),
        in_specs=[smem_spec(), *[whole(mine.shape)] * 2, whole(down.shape)],
        out_specs=[whole(shape.shape)] * 2,
        out_shape=[shape] * 2,
        compiler_params=params(4),
        cost_estimate=cost(1),
        name="merge_feed_forward",
    )(core, mine, theirs, down)


def pair_sum(refs):
    parts = [ref[...].astype(F32) for ref in refs]
    while len(parts) > 1:
        half = len(parts) // 2
        parts = [parts[i] + parts[i + half] for i in range(half)]
    return parts[0]


def rows_of(total, first, core_at, local, mine):
    a, b = total[first : first + local], total[first + local : first + 2 * local]
    return jnp.where((core_at == 0) == mine, a, b)


def total_attention(core, parts, local):
    tall, width = parts[0].shape
    tail = tall - 8 * local

    def kernel(core_ref, *refs):
        ins, (mine_ref, sent_ref, tail_ref) = refs[: len(parts)], refs[len(parts) :]
        total = pair_sum(ins)
        for j in range(4):
            mine_ref[j] = rows_of(total, 2 * local * j, core_ref[0], local, True)
            sent_ref[j] = rows_of(total, 2 * local * j, core_ref[0], local, False).astype(BF)
        tail_ref[...] = total[8 * local :].astype(BF)

    shapes = [
        jax.ShapeDtypeStruct((4, local, width), F32),
        jax.ShapeDtypeStruct((4, local, width), BF),
        jax.ShapeDtypeStruct((tail, width), BF),
    ]
    return pl.pallas_call(
        kernel,
        grid=(1,),
        in_specs=[smem_spec(), *[whole(one.shape) for one in parts]],
        out_specs=[whole(one.shape) for one in shapes],
        out_shape=shapes,
        compiler_params=params(6),
        cost_estimate=cost(1),
        name="total_attention",
    )(core, *parts)


def finish_attention(core, mine, theirs, tail, tail_theirs, heads, number):
    _, local, width = mine.shape
    model = 2 * width

    def kernel(core_ref, a_ref, b_ref, s_ref, t_ref, qkv_ref, out_ref, small_ref, table_ref):
        at = core_ref[0]
        for h, ref in enumerate((a_ref, b_ref)):
            for j in range(3):
                cols = pl.ds(pl.multiple_of(j * model + (at ^ h) * width, TILE), width)
                qkv_ref[:, cols] = ref[j].astype(F32)
            out_ref[:, pl.ds(pl.multiple_of((at ^ h) * width, TILE), width)] = ref[3].astype(F32)
        total = s_ref[...].astype(F32) + t_ref[...].astype(F32)
        small = total[:16, :TILE]
        moved = pltpu.roll(small, TILE - local, 1)
        small_ref[:8, :] = jnp.where(at == 0, small[:8], moved[:8])
        small_ref[8:, :] = small[8:]
        table_ref[...] = jnp.concatenate([total[:16, TILE:], total[16:, : 2 * TILE]], 1)[:heads, :number]

    shapes = [
        jax.ShapeDtypeStruct((local, 3 * model), F32),
        jax.ShapeDtypeStruct((local, model), F32),
        jax.ShapeDtypeStruct((16, TILE), F32),
        jax.ShapeDtypeStruct((heads, number), F32),
    ]
    return pl.pallas_call(
        kernel,
        grid=(1,),
        in_specs=[smem_spec(), *[whole(one.shape) for one in (mine, theirs, tail, tail_theirs)]],
        out_specs=[whole(one.shape) for one in shapes],
        out_shape=shapes,
        compiler_params=params(6),
        cost_estimate=cost(1),
        name="finish_attention",
    )(core, mine, theirs, tail, tail_theirs)


def total_feed_forward(core, parts, local):
    _, width = parts[0].shape
    model = 2 * width
    unit = 2 * local

    def kernel(core_ref, *refs):
        ins, (mine_ref, sent_ref, down_ref) = refs[: len(parts)], refs[len(parts) :]
        total = pair_sum(ins)
        for h in range(2):
            cols = slice(h * width, (h + 1) * width)
            mine_ref[:, cols] = rows_of(total, h * unit, core_ref[0], local, True)
            sent_ref[:, cols] = rows_of(total, h * unit, core_ref[0], local, False).astype(BF)
            down_ref[:, cols] = total[(2 + h) * unit : (3 + h) * unit]

    shapes = [
        jax.ShapeDtypeStruct((local, model), F32),
        jax.ShapeDtypeStruct((local, model), BF),
        jax.ShapeDtypeStruct((unit, model), F32),
    ]
    return pl.pallas_call(
        kernel,
        grid=(1,),
        in_specs=[smem_spec(), *[whole(one.shape) for one in parts]],
        out_specs=[whole(one.shape) for one in shapes],
        out_shape=shapes,
        compiler_params=params(6),
        cost_estimate=cost(1),
        name="total_feed_forward",
    )(core, *parts)


def finish_feed_forward(core, mine, theirs, downs):
    local, model = mine[0].shape
    unit = 2 * local
    chips = model // unit

    def kernel(core_ref, m0, m1, t0, t1, d0, d1, up_ref, down_ref):
        first = core_ref[0] == 0
        by = []
        for a, b in ((m0, t0), (m1, t1)):
            a, b = a[...], b[...].astype(F32)
            by.append((jnp.where(first, a, b), jnp.where(first, b, a)))
        up_ref[...] = jnp.concatenate(
            [
                by[f][c][:, chip * unit : (chip + 1) * unit]
                for chip in range(chips)
                for c in range(2)
                for f in range(2)
            ],
            1,
        )
        down_ref[:unit, :] = d0[...]
        down_ref[unit:, :] = d1[...]

    shapes = [jax.ShapeDtypeStruct((local, 4 * model), F32), jax.ShapeDtypeStruct((2 * unit, model), F32)]
    ins = (*mine, *theirs, *downs)
    return pl.pallas_call(
        kernel,
        grid=(1,),
        in_specs=[smem_spec(), *[whole(one.shape) for one in ins]],
        out_specs=[whole(one.shape) for one in shapes],
        out_shape=shapes,
        compiler_params=params(6),
        cost_estimate=cost(1),
        name="finish_feed_forward",
    )(core, *ins)


VECTORS = 8


class Order:
    def __init__(self, token):
        self.token = token

    def go(self, *values):
        out, _ = lax.optimization_barrier((values, self.token))
        return out if len(out) > 1 else out[0]

    def mark(self, *values):
        out, self.token = lax.optimization_barrier((values, self.token))
        return out if len(out) > 1 else out[0]


class GridLinks:
    pair = True

    def __init__(self, sizes, model):
        self.ny, self.nz, self.nx = sizes
        self.chips = self.ny * self.nz * self.nx
        self.rows = model // self.chips
        dp, inner = lax.axis_index("dp"), lax.axis_index("fsdp")
        self.core = inner % 2
        chip = inner // 2
        self.place = (dp, chip // self.nx, chip % self.nx)
        self.gather_offsets = self._offsets(self.core, -1, (range(self.nz),))
        self.early_offsets = self._offsets(self.core, -1, ((0, 1, 3, 2),))
        self.scatter_offsets = self._offsets(self.core, 1, (range(self.nz),))
        self.last_offsets = self._offsets(self.core, 1, (range(1, self.nz), (0,)))
        self.last_counts = (2 * self.nz - 2, 2 * self.nz - 2, 2, 2)

    def _offsets(self, core, sign, parts):
        y, z, x = self.place
        out = []
        for part in parts:
            for r1 in range(2):
                for r2 in range(2):
                    for k in part:
                        fy = jnp.where(core == 0, r1, r2)
                        fx = jnp.where(core == 0, r2, r1)
                        zz = (z + sign * k + self.nz) % self.nz
                        out.append(((y ^ fy) * self.nz + zz) * self.nx + (x ^ fx))
        return (jnp.stack(out) * self.rows).astype(jnp.int32)

    def _send(self, value, move):
        pairs = []
        for y in range(self.ny):
            for z in range(self.nz):
                for x in range(self.nx):
                    for c in range(2):
                        source = ((y * self.nz + z) * self.nx + x) * 2 + c
                        ty, tz, tx, tc = move(y, z, x, c)
                        pairs.append((source, ((ty * self.nz + tz) * self.nx + tx) * 2 + tc))
        return lax.ppermute(value, AXES, pairs)

    def swap(self, value):
        return self._send(value, lambda y, z, x, c: (y, z, x, 1 - c))

    def along_z(self, value, k):
        return self._send(value, lambda y, z, x, c: (y, (z + k) % self.nz, x, c))

    def x_first(self, value):
        return self._send(value, lambda y, z, x, c: (y, z, 1 - x, c) if c == 0 else (1 - y, z, x, c))

    def y_first(self, value):
        return self._send(value, lambda y, z, x, c: (y, z, 1 - x, c) if c == 1 else (1 - y, z, x, c))

    def spread(self, near):
        second = self.x_first(near)
        third = self.y_first(near)
        return [near, second, third, self.y_first(second)]

    def scatter_z(self, sums):
        return [sums[0]] + [self.along_z(sums[k], k) for k in range(1, self.nz)]


def small_kernel(kernel, name, shapes, *ins):
    return pl.pallas_call(
        kernel,
        grid=(1,),
        in_specs=[whole(one.shape) for one in ins],
        out_specs=[whole(shape) for shape in shapes],
        out_shape=[VMEM(shape, BF) for shape in shapes],
        compiler_params=params(4),
        cost_estimate=cost(1),
        name=name,
    )(*ins)


def stack_blocks(*blocks):
    def kernel(*refs):
        for i, ref in enumerate(refs[:-1]):
            refs[-1][i] = ref[...]

    return small_kernel(kernel, "stack_blocks", [(len(blocks), *blocks[0].shape)], *blocks)[0]


def join_blocks(first, last):
    n = first.shape[0]

    def kernel(first_ref, last_ref, out_ref):
        out_ref[:n] = first_ref[...]
        out_ref[n:] = last_ref[...]

    return small_kernel(kernel, "join_blocks", [(n + last.shape[0], *first.shape[1:])], first, last)[0]


def add_low(a, b):
    return (a.astype(F32) + b.astype(F32)).astype(BF)


def fold(keep, moved):
    n = keep.shape[0] // 2

    def kernel(keep_ref, moved_ref, *outs):
        for s in range(2 * n):
            outs[s // n][s % n] = add_low(keep_ref[s], moved_ref[s])

    return small_kernel(kernel, "fold", [(n, *keep.shape[1:])] * 2, keep, moved)


def fold_late(keep, moved, slots):
    half = 8 * slots

    def kernel(keep_ref, moved_ref, *outs):
        total = add_low(keep_ref[...], moved_ref[...])
        for i, out in enumerate(outs):
            out[:half, :] = total[i * half : (i + 1) * half]
            out[half:, :] = total[2 * half :]

    return small_kernel(kernel, "fold_late", [(half + keep.shape[0] - 2 * half, TILE)] * 2, keep, moved)


def fold_last(keep, moved, late=None, first=0):
    n, tall, wide = keep.shape
    tail = 0 if late is None else 32

    def kernel(keep_ref, moved_ref, *refs):
        outs = refs[-n:]
        for s in range(n):
            outs[s][:tall, :] = add_low(keep_ref[s], moved_ref[s])
        if tail:
            total = add_low(refs[0][...], refs[1][...])
            at = total.shape[0] - 64
            blocks = [total[at + 16 * i : at + 16 * i + 16] for i in range(4)]
            for s in range(n):
                small = total[16 * (first + s) : 16 * (first + s) + 16]
                outs[s][tall : tall + 16, :] = jnp.concatenate([small, *blocks[:2]], 1)
                outs[s][tall + 16 :, :] = jnp.concatenate([*blocks[2:], jnp.zeros_like(small)], 1)

    return small_kernel(kernel, "fold_last", [(tall + tail, wide)] * n, keep, moved, *(late or ()))


def on_device(
    links,
    tokens,
    lengths,
    buckets,
    ln1_gain,
    ln1_bias,
    qkv_weight,
    q_bias,
    v_bias,
    out_weight,
    out_bias,
    rel_table,
    ln2_gain,
    ln2_bias,
    up_weight,
    up_bias,
    down_weight,
    down_bias,
    cotangent,
):
    rows, model = tokens.shape
    heads, number = rel_table.shape
    head_size = model // heads
    width = model // 2
    local = qkv_weight.shape[0]
    core, chips = links.core, links.chips
    core_arg = core.astype(jnp.int32).reshape(1)

    order = Order(core_arg)
    vectors = jnp.stack(
        [ln1_gain, ln1_bias, q_bias, v_bias, out_bias, ln2_gain, ln2_bias, down_bias]
        + [up_bias[i * local : (i + 1) * local] for i in range(4)]
    )
    a_mine, a_sent, u_mine, u_sent, line = pack_blocks(
        core_arg, lengths, buckets, qkv_weight, out_weight, up_weight
    )
    small = pack_vectors(core_arg, vectors)
    a_theirs, small_theirs = links.swap(a_sent), links.swap(small)
    line_other, tokens_other, u_theirs = links.swap(line), links.swap(tokens), links.swap(u_sent)
    early_offsets, gather_offsets = links.early_offsets, links.gather_offsets
    scatter_offsets, last_offsets = links.scatter_offsets, links.last_offsets
    a_piece = merge_attention(core_arg, a_mine, a_theirs, small, small_theirs)
    a_piece, line_other, tokens_other, u_theirs, early_offsets, gather_offsets, scatter_offsets, last_offsets = order.mark(
        a_piece, line_other, tokens_other, u_theirs, early_offsets, gather_offsets, scatter_offsets, last_offsets
    )

    z_parts = [links.along_z(a_piece, k) for k in (1, 3, 2)]
    near = a_piece[None]
    second, third = links.x_first(near), links.y_first(near)
    tiles, grad_rows = bias_tiles(core_arg, (line, line_other), rel_table, cotangent, lengths, (0, 0))
    f0, f1 = merge_feed_forward(core_arg, u_mine, order.go(u_theirs), down_weight)
    tiles, grad_rows, f0, f1, z_parts, second, third = order.mark(
        tiles, grad_rows, f0, f1, z_parts, second, third
    )
    near_last = stack_blocks(*z_parts)
    second_last, third_last = links.x_first(near_last), links.y_first(near_last)
    f0_z = [links.along_z(order.go(f0), k) for k in (1, 3, 2)]
    second_last, third_last, f0_z[:2] = order.mark(second_last, third_last, f0_z[:2])
    fourth = links.y_first(join_blocks(second, second_last))
    f1_z = [links.along_z(order.go(f1), k) for k in (1, 3)]
    grad_rows_other = links.swap(grad_rows)
    fourth, grad_rows_other, f0_z[2] = order.mark(fourth, grad_rows_other, f0_z[2])
    parts = [near, near_last, second, second_last, third, third_last, fourth]
    own, own_out, vec = order.mark(*assemble_attention(Pieces(parts, early_offsets, links.rows), model))
    f1_z = order.mark(f1_z)
    f0_near = stack_blocks(f0, f0_z[0], f0_z[2], f0_z[1])
    f0_second, f0_third = links.x_first(f0_near), links.y_first(f0_near)
    f1_z.append(links.along_z(order.go(f1), 2))
    other_out = links.swap(own_out)

    normed_other, joined1, mixed1, probs1 = attention_forward(
        1, 0, core_arg, tokens_other, vec, order.go(own), tiles, line_other, head_size
    )
    mixed1, other_out, f1_z = order.mark(mixed1, other_out, f1_z)
    mixed_rest = links.swap(mixed1)
    f1_near = stack_blocks(f1, f1_z[0], f1_z[2], f1_z[1])
    f1_second = links.x_first(f1_near)
    normed, joined0, mixed0, probs0 = attention_forward(
        0, 0, core_arg, tokens, vec, order.go(own), tiles, line, head_size
    )
    mixed0, mixed_rest, f0_second, f0_third = order.mark(mixed0, mixed_rest, f0_second, f0_third)
    f0_fourth = links.y_first(f0_second)
    mixed_rest_other = links.swap(mixed0)
    residual, normed2 = project_out(core_arg, (order.go(mixed0), mixed_rest), tokens, (own_out, other_out), vec)
    normed2, f0_fourth, f1_second, mixed_rest_other = order.mark(normed2, f0_fourth, f1_second, mixed_rest_other)

    normed2_other = links.swap(normed2)
    f1_third, f1_fourth = links.y_first(f1_near), links.y_first(f1_second)
    normed2_other = order.mark(normed2_other)

    def chunk(bufs):
        return Pieces(bufs, gather_offsets, links.rows)

    (own0, other0), sums_f0, (keep0, send0) = feed_forward(
        lambda c: 8 + c, core_arg,
        [(normed2, grad_rows, residual, None), (normed2_other, grad_rows_other, None, None)],
        vec, chunk([f0_near, f0_second, f0_third, f0_fourth]), scatter_offsets,
    )
    own0, other0, keep0, send0, f1_third, f1_fourth = order.mark(own0, other0, keep0, send0, f1_third, f1_fourth)
    moved0 = links.y_first(send0)
    (own1, other1), sums_f1, (keep1, send1) = feed_forward(
        lambda c: 10 + c, core_arg,
        [(normed2, grad_rows, own0[0], own0[1]), (normed2_other, grad_rows_other, other0[0], other0[1])],
        vec, chunk([f1_near, f1_second, f1_third, f1_fourth]), scatter_offsets,
    )
    own1, other1, keep1, send1, moved0 = order.mark(own1, other1, keep1, send1, moved0)
    keep0, send0 = fold(keep0, moved0)
    moved0 = links.x_first(send0)
    result_rest, grad_rest = links.swap(other1[0]), links.swap(other1[1])
    result_rest, grad_rest = order.mark(result_rest, grad_rest)
    moved1 = links.y_first(order.go(send1))
    output, grad_res, gm0, branch_cols, sent, sums2 = second_norm_back(
        core_arg, residual, (order.go(own1[0]), result_rest), (own1[1], grad_rest), grad_rows,
        (own_out, other_out), vec, lengths,
    )
    sent, moved0 = order.mark(sent, moved0)
    got = links.swap(sent)
    sums0 = fold_last(keep0, moved0)
    parts0 = [sums0[0]] + [links.along_z(sums0[k], k) for k in (1, 3)]
    dj0, diag0 = attention_backward(joined0, probs0, mixed0, order.go(gm0), head_size)
    dj0, got, moved1, parts0 = order.mark(dj0, got, moved1, parts0)
    parts0.insert(2, links.along_z(order.go(sums0[2]), 2))
    keep1, send1 = fold(keep1, moved1)
    moved1 = links.x_first(send1)
    dj1, diag1, part, keep, send, own_keep, own_send = attention_backward(
        joined1, probs1, mixed1, order.go(got), head_size,
        Products(
            core_arg,
            [([(normed, None), (normed_other, None)], [(dj0, j), (None, j)]) for j in range(3)]
            + [([((mixed0, mixed_rest), None), ((mixed1, mixed_rest_other), None)], [(branch_cols, None), (got, 1)])],
            last_offsets,
            links.rows,
            links.last_counts,
        ),
        own,
    )
    part, keep, send, own_keep, own_send, moved1, parts0 = order.mark(
        part, keep, send, own_keep, own_send, moved1, parts0
    )
    part_rest = links.swap(part)
    moved = links.y_first(send)
    sums1 = fold_last(keep1, moved1)
    parts1 = [sums1[0]] + [links.along_z(sums1[k], k) for k in (1, 3)]
    part_rest = order.mark(part_rest)
    input_grad, vec_grads, table_grad = first_norm_back(
        core_arg, (order.go(dj0), dj1), part_rest, tokens, grad_res, vec, own, sums2, ([sums_f0], [sums_f1]),
        (diag0, diag1), (line, line_other), number, False,
    )
    late_keep, late_send, parts1 = order.mark(*late_slots(vec_grads, table_grad, scatter_offsets), parts1)
    late_moved = links.y_first(late_send)
    parts1.insert(2, links.along_z(order.go(sums1[2]), 2))
    moved, late_moved = order.mark(moved, late_moved)
    keep, send = fold(keep, moved)
    moved = links.x_first(send)
    late_keep, late_send = fold_late(late_keep, late_moved, 2 * links.nz)
    late_moved = links.x_first(late_send)
    moved, late_moved, own_send, parts1 = order.mark(moved, late_moved, own_send, parts1)
    sums = fold_last(keep, moved, (late_keep, late_moved), 1)
    parts = [links.along_z(sums[k - 1], k) for k in (1, 2, 3)]
    own_moved = links.y_first(own_send)
    ffn0 = total_feed_forward(core_arg, order.go(parts0), local)
    ffn1 = total_feed_forward(core_arg, order.go(parts1), local)
    ffn0, ffn1, own_moved = order.mark(ffn0, ffn1, own_moved)
    own_keep, own_send = fold(own_keep, own_moved)
    own_moved = links.x_first(own_send)
    ups = [links.swap(ffn0[1]), links.swap(ffn1[1])]
    grad_up, grad_down = finish_feed_forward(
        core_arg, [ffn0[0], ffn1[0]], ups, [ffn0[2], ffn1[2]]
    )
    grad_up, grad_down, parts, own_moved = order.mark(grad_up, grad_down, parts, own_moved)
    parts = [*fold_last(own_keep, own_moved, (late_keep, late_moved)), *parts]
    mine, sent, tail = total_attention(core_arg, parts, local)
    theirs, tail_theirs = links.swap(sent), links.swap(tail)
    grad_qkv, grad_out, small, grad_table = finish_attention(
        core_arg, mine, theirs, tail, tail_theirs, heads, number
    )
    small_grads = [small[i, :local] for i in range(VECTORS)]
    unit = 2 * local
    halves = small[8:12, :].reshape(2, 2, TILE)
    grad_up_bias = lax.dynamic_index_in_dim(halves, core, 1, keepdims=False)[:, :unit].reshape(2 * unit)

    return (
        output,
        input_grad,
        small_grads[0],
        small_grads[1],
        grad_qkv,
        small_grads[2],
        small_grads[3],
        grad_out,
        small_grads[4],
        grad_table,
        small_grads[5],
        small_grads[6],
        grad_up,
        grad_up_bias,
        grad_down,
        small_grads[7],
    )


def on_any_mesh(
    tokens,
    lengths,
    buckets,
    ln1_gain,
    ln1_bias,
    qkv_weight,
    q_bias,
    v_bias,
    out_weight,
    out_bias,
    rel_table,
    ln2_gain,
    ln2_bias,
    up_weight,
    up_bias,
    down_weight,
    down_bias,
    cotangent,
):
    rows, model = tokens.shape
    heads, number = rel_table.shape
    head_size = model // heads
    width = model // 2
    local = qkv_weight.shape[0]
    hidden = up_weight.shape[1]
    core = jnp.zeros((1,), jnp.int32)
    offsets = jnp.zeros((1,), jnp.int32)

    def gathered(x):
        return lax.all_gather(x, AXES, axis=0, tiled=True)

    def scattered(x):
        return lax.psum_scatter(x, AXES, scatter_dimension=0, tiled=True)

    vectors = [ln1_gain, ln1_bias, q_bias, v_bias, out_bias, ln2_gain, ln2_bias, down_bias]
    unit = up_bias.shape[0]
    small = gathered(jnp.concatenate([*vectors, up_bias])[None, :])
    wide = [small[:, i * local : (i + 1) * local].reshape(1, model) for i in range(VECTORS)]
    ub = small[:, VECTORS * local :].reshape(2, 2, model).transpose(1, 0, 2).reshape(4, model)
    del unit
    vec = jnp.concatenate([*wide, ub, jnp.zeros((4, model), BF)], 0).astype(F32)
    attn = gathered(jnp.concatenate([qkv_weight, out_weight], 1))
    up, down = gathered(up_weight), gathered(down_weight)
    a_pieces = tuple(
        jnp.stack([attn[:, j * model + h * width : j * model + (h + 1) * width] for j in range(3)])
        for h in range(2)
    )

    a_out = tuple(attn[:, 3 * model + h * width : 3 * model + (h + 1) * width] for h in range(2))

    def chunk(f, h):
        at = (2 * h + f) * model
        blocks = [one[:, k * width : (k + 1) * width] for one in (up[:, at : at + model], down[at : at + model]) for k in range(2)]
        return Pieces([jnp.concatenate(blocks, 0)[None]], offsets, model)

    ahead = jnp.roll(buckets[0, rows - 1], 1)
    line = jnp.concatenate([ahead, buckets[0, 0]]).astype(F32)
    line = jnp.stack([line, jnp.full_like(line, lengths[0])] + [jnp.zeros_like(line)] * 6)
    tiles, grad_rows = bias_tiles(core, (line, line), rel_table, cotangent, lengths, (0, 1))
    normed, joined0, mixed0, probs0 = attention_forward(0, 0, core, tokens, vec, a_pieces[0], tiles, line, head_size)
    _, joined1, mixed1, probs1 = attention_forward(1, 1, core, tokens, vec, a_pieces[1], tiles, line, head_size)
    residual, normed2 = project_out(core, (mixed0, mixed1), tokens, a_out, vec)
    result, grad_n2 = residual, None
    up_sums, ups, downs = [[], []], [], []
    for f in range(2):
        for h in range(2):
            ((result, grad_n2, active, grad_pre),), sums, _ = feed_forward(
                lambda c, at=8 + 2 * f + h: c + at, core, [(normed2, grad_rows, result, grad_n2)], vec, chunk(f, h)
            )
            up_sums[f].append(sums)
            (both,) = outer_products(
                core,
                [([(normed2, None)], [(grad_pre, k)]) for k in range(2)]
                + [([(active, None)], [(grad_rows, k)]) for k in range(2)],
                offsets,
                model,
            )
            both = both[0].reshape(2, 2, model, width).transpose(0, 2, 1, 3).reshape(2, model, model)
            ups.append(both[0])
            downs.append(both[1])
    output, grad_res, gm0, branch0, sent, sums2 = second_norm_back(
        core, residual, (result,), (grad_n2,), grad_rows, a_out, vec, lengths
    )
    dj0, diag0 = attention_backward(joined0, probs0, mixed0, gm0, head_size)
    dj1, diag1 = attention_backward(joined1, probs1, mixed1, sent, head_size)
    input_grad, vec_grads, table_grad = first_norm_back(
        core, (dj0, dj1), normed_back(dj1, a_pieces[1]), tokens, grad_res, vec, a_pieces[0], sums2, up_sums,
        (diag0, diag1), (line, line), number, True,
    )
    mixed = jnp.concatenate([mixed0, mixed1], 1)
    halves = [
        outer_products(
            core, [([(normed, None)], [(dj, j)]) for j in range(3)] + [([(mixed, None)], [branch])], offsets, model
        )[0][0].reshape(4, model, width)
        for dj, branch in ((dj0, (branch0, None)), (dj1, (sent, 1)))
    ]
    grads = jnp.stack(halves, 2).transpose(1, 0, 2, 3).reshape(model, 4 * model)
    grads = scattered(grads)
    grad_up = scattered(jnp.concatenate([ups[0], ups[2], ups[1], ups[3]], 1))
    grad_down = scattered(jnp.concatenate([downs[0], downs[2], downs[1], downs[3]], 0))
    by_owner = vec_grads[:VECTORS].reshape(VECTORS, model // local, local).transpose(1, 0, 2)
    own_units = vec_grads[VECTORS : VECTORS + 4].reshape(2, 2, model).transpose(1, 0, 2)
    both = jnp.concatenate(
        [by_owner.reshape(model // local, VECTORS * local), own_units.reshape(model // local, hidden * local // model)],
        1,
    )
    both = scattered(both)[0]
    table = jnp.concatenate([table_grad[16 * i : 16 * i + 16] for i in range(4)], 1)[:heads, :number]
    grad_table = lax.psum(table, AXES)
    small_grads = [both[i * local : (i + 1) * local] for i in range(VECTORS)]
    return (
        output,
        input_grad,
        small_grads[0],
        small_grads[1],
        grads[:, : 3 * model].astype(F32),
        small_grads[2],
        small_grads[3],
        grads[:, 3 * model :].astype(F32),
        small_grads[4],
        grad_table,
        small_grads[5],
        small_grads[6],
        grad_up.astype(F32),
        both[VECTORS * local :],
        grad_down.astype(F32),
        small_grads[7],
    )


def solution(mesh):
    both = P(AXES)
    row = P(AXES, None)
    in_specs = (
        row, both, P(AXES, None, None), both, both, row, both, both, row, both, P(), both, both, row, both, row,
        both, row,
    )
    out_specs = (row, row, both, both, row, both, both, row, both, P(), both, both, row, both, row, both)

    if tuple(mesh.shape[name] for name in AXES) == (2, 16):

        def body(*args):
            return on_device(GridLinks((2, 4, 2), args[0].shape[1]), *args)

    else:
        body = on_any_mesh

    return jax.shard_map(body, mesh=mesh, in_specs=in_specs, out_specs=out_specs, check_vma=False)
```

```python
import functools

import jax
import jax.numpy as jnp
from jax import lax
from jax.experimental import pallas as pl
from jax.experimental.pallas import tpu as pltpu
from jax.sharding import PartitionSpec as P

BF = jnp.bfloat16
F32 = jnp.float32
AXES = ("dp", "fsdp")
TILE = 128
CHUNK = 64
EPS = 1e-05
NN = (((1,), (0,)), ((), ()))
NT = (((1,), (1,)), ((), ()))
TN = (((0,), (0,)), ((), ()))
VMEM = pltpu.VMEM


def mm(left, right, dims=NN):
    return lax.dot_general(left, right, dims, preferred_element_type=F32)


def any_spec():
    return pl.BlockSpec(memory_space=pl.ANY)


def hbm_spec():
    return pl.BlockSpec(memory_space=pltpu.HBM)


def in_hbm(x):
    return pltpu.with_memory_space_constraint(x, pltpu.HBM)


def smem_spec():
    return pl.BlockSpec(memory_space=pltpu.SMEM)


def whole(shape):
    return pl.BlockSpec(shape, lambda *_: (0,) * len(shape))


def params(mebibytes):
    return pltpu.CompilerParams(
        dimension_semantics=("arbitrary",), vmem_limit_bytes=mebibytes * 1024 * 1024
    )


def cost(micros):
    return pl.CostEstimate(flops=int(micros * 1e9), bytes_accessed=1, transcendentals=0)


class Pieces:
    def __init__(self, buffers, offsets, rows):
        self.buffers = buffers
        self.offsets = offsets
        self.rows = rows

    @property
    def slots(self):
        return sum(b.shape[0] for b in self.buffers)


def lay_blocks(refs, offs_ref, rows, count, put):
    slot = 0
    for ref in refs:
        for k in range(ref.shape[0]):
            at = pl.multiple_of(offs_ref[slot], 16)
            for j in range(count):
                put(j, at, ref[k, j * rows : (j + 1) * rows, :])
            slot += 1


def row_norm(x):
    centre = x - jnp.mean(x, -1, keepdims=True)
    scale = lax.rsqrt(jnp.mean(centre * centre, -1, keepdims=True) + EPS)
    return centre * scale, scale


def bucket_line(line, number):
    rows = lax.broadcasted_iota(jnp.int32, (number, line.shape[1]), 0)
    return jnp.where(rows == line.astype(jnp.int32), 1.0, 0.0).astype(BF)


def bias_tiles(core, lines, table, cotangent, lengths, halves):
    span = lines[0].shape[1]
    heads, number = table.shape
    count = heads // 2
    tiles = span // TILE - 1
    n = len(lines)
    rows, model = cotangent.shape

    def kernel(core_ref, len_ref, table_ref, cot_ref, *refs):
        line_refs, (out_ref, gr_ref, curve_ref) = refs[:n], refs[n:]
        at = pl.program_id(0)

        @pl.when(at == 0)
        def _():
            for i in range(n):
                curve = mm(table_ref[...], bucket_line(line_refs[i][0:1, :], number))
                curve = jnp.where((core_ref[0] ^ halves[i]) == 0, curve[:count], curve[count:])
                for h in range(count):
                    curve_ref[i * count + h] = jnp.broadcast_to(curve[h : h + 1], (8, span))
            row = lax.broadcasted_iota(jnp.int32, (rows, 1), 0)
            gr_ref[...] = jnp.where(row < len_ref[0], cot_ref[...].astype(F32), 0.0).astype(BF)

        base = pltpu.roll(curve_ref[at], 0, 1, stride=1, stride_axis=0)
        for pair in range(TILE // 16):
            rolled = jnp.concatenate(
                [pltpu.roll(base, 16 * pair + 8 * i, 1) if pair + i else base for i in range(2)], 0
            ).astype(BF)
            for d in range(tiles):
                out_ref[0, 0, d, 16 * pair : 16 * pair + 16, :] = rolled[
                    :, TILE * (d + 1) : TILE * (d + 2)
                ]

    return pl.pallas_call(
        kernel,
        grid=(n * count,),
        in_specs=[
            smem_spec(),
            smem_spec(),
            whole((heads, number)),
            whole((rows, model)),
            *[whole((8, span))] * n,
        ],
        out_specs=[
            pl.BlockSpec((1, 1, tiles, TILE, TILE), lambda h: (h // count, h % count, 0, 0, 0)),
            whole((rows, model)),
        ],
        out_shape=[
            VMEM((n, count, tiles, TILE, TILE), BF),
            VMEM((rows, model), BF),
        ],
        scratch_shapes=[VMEM((n * count, 8, span), F32)],
        compiler_params=params(8),
        cost_estimate=cost(4),
        name="bias_tiles",
    )(core, lengths, table, cotangent, *lines)


def place_rows(block, offset, wide):
    padded = jnp.concatenate([block, jnp.zeros((block.shape[0], wide - TILE), block.dtype)], 1)
    return pltpu.roll(padded, offset, 1)


def assemble_attention(pieces, model):
    width = model // 2
    rows = pieces.rows
    n_buf = len(pieces.buffers)

    def kernel(offs_ref, *refs):
        bufs, (w_ref, o_ref, vec_ref) = refs[:n_buf], refs[n_buf:]

        def put(j, at, block):
            if j < 3:
                w_ref[j, pl.ds(at, rows), :] = block
            else:
                o_ref[pl.ds(at, rows), :] = block

        lay_blocks(bufs, offs_ref, rows, 4, put)
        total, slot = jnp.zeros((16, model), F32), 0
        for ref in bufs:
            for k in range(ref.shape[0]):
                total += place_rows(ref[k, 4 * rows : 4 * rows + 16, :TILE].astype(F32), offs_ref[slot], model)
                slot += 1
        vec_ref[...] = total

    return pl.pallas_call(
        kernel,
        grid=(1,),
        in_specs=[smem_spec(), *[whole(one.shape) for one in pieces.buffers]],
        out_specs=[whole((3, model, width)), whole((model, width)), whole((16, model))],
        out_shape=[
            VMEM((3, model, width), BF),
            VMEM((model, width), BF),
            VMEM((16, model), F32),
        ],
        compiler_params=params(6),
        cost_estimate=cost(2),
        name="assemble_attention",
    )(pieces.offsets, *pieces.buffers)


def attention_forward(item, half, core, tokens, vec, weights, tiles, line, head_size):
    rows, model = tokens.shape
    width = model // 2
    heads = width // head_size
    pairs = width // TILE
    per = TILE // head_size
    scale = head_size**-0.5

    def kernel(core_ref, line_ref, x_ref, vec_ref, tile_ref, w_ref, n1_ref, joined_ref, mixed_ref, p_ref, qs_ref, s_ref):
        pair = pl.program_id(0)

        @pl.when(pair == 0)
        def _():
            for r in range(0, rows, CHUNK):
                xhat, _ = row_norm(x_ref[r : r + CHUNK, :].astype(F32))
                n1_ref[r : r + CHUNK, :] = (xhat * vec_ref[0:1, :] + vec_ref[1:2, :]).astype(BF)
            cols = pl.ds(pl.multiple_of((core_ref[0] ^ half) * width, TILE), width)
            for j in range(3):
                joined = mm(n1_ref[...], w_ref[j])
                if j != 1:
                    joined = joined + vec_ref[2 + j // 2 : 3 + j // 2, cols]
                qs_ref[j] = joined.astype(BF)

        lanes = pl.ds(pl.multiple_of(pair * TILE, TILE), TILE)
        q, k, v = (qs_ref[j, :, lanes] for j in range(3))
        for j, one in enumerate((q, k, v)):
            joined_ref[j] = one
        lane = lax.broadcasted_iota(jnp.int32, (1, TILE), 1)
        column = lax.broadcasted_iota(jnp.int32, (1, rows), 1)
        dead = jnp.where(column < line_ref[1:2, :rows].astype(jnp.int32), 0.0, -1e30).astype(F32)
        scaled = q.astype(F32) * scale
        outs = []
        for e in range(per):
            mine = (lane >= e * head_size) & (lane < (e + 1) * head_size)
            qm = jnp.where(mine, scaled, 0.0).astype(BF)
            s_ref[e] = mm(qm, k, NT)
            for r in range(0, rows, CHUNK):
                block, sub = r // TILE, r % TILE
                rel = jnp.concatenate(
                    [
                        tile_ref[0, e, j - block + rows // TILE - 1, sub : sub + CHUNK, :]
                        for j in range(rows // TILE)
                    ],
                    1,
                ).astype(F32)
                s = s_ref[e, r : r + CHUNK, :] + (rel + dead)
                raised = jnp.exp(s - jnp.max(s, -1, keepdims=True))
                inv = 1.0 / jnp.sum(raised, -1, keepdims=True)
                p_ref[e, r : r + CHUNK, :] = (raised * inv).astype(BF)
            outs.append(jnp.where(mine, mm(p_ref[e], v), 0.0))
        mixed_ref[...] = functools.reduce(lambda a, b: a + b, outs).astype(BF)

    shapes = [
        VMEM((3, rows, width), BF),
        VMEM((rows, width), BF),
        VMEM((heads, rows, rows), BF),
    ]
    outs = [
        pl.BlockSpec((3, rows, TILE), lambda p: (0, 0, p)),
        pl.BlockSpec((rows, TILE), lambda p: (0, p)),
        pl.BlockSpec((per, rows, rows), lambda p: (p, 0, 0)),
    ]
    shapes.insert(0, VMEM((rows, model), BF))
    outs.insert(0, whole((rows, model)))
    return pl.pallas_call(
        kernel,
        grid=(pairs,),
        in_specs=[
            smem_spec(),
            whole((8, 2 * rows)),
            whole((rows, model)),
            whole((16, model)),
            pl.BlockSpec((1, per, tiles.shape[2], TILE, TILE), lambda p: (item, p, 0, 0, 0)),
            whole((3, model, width)),
        ],
        out_specs=outs,
        out_shape=shapes,
        scratch_shapes=[VMEM((3, rows, width), BF), VMEM((per, rows, rows), F32)],
        compiler_params=params(12),
        cost_estimate=cost(6),
        name="attention_forward",
    )(core, line, tokens, vec, tiles, weights)


def project_out(core, mixed, tokens, weights, vec):
    rows, model = tokens.shape
    width = model // 2

    def kernel(core_ref, m0_ref, m1_ref, x_ref, vec_ref, w0_ref, w1_ref, res_ref, n2_ref):
        for h, w_ref in enumerate((w0_ref, w1_ref)):
            cols = pl.ds(pl.multiple_of((core_ref[0] ^ h) * width, TILE), width)
            acc = 0.0
            for g, m_ref in enumerate((m0_ref, m1_ref)):
                feats = pl.ds(pl.multiple_of((core_ref[0] ^ g) * width, TILE), width)
                acc = acc + mm(m_ref[...], w_ref[feats, :])
            res_ref[:, cols] = x_ref[:, cols].astype(F32) + acc + vec_ref[4:5, cols]
        for r in range(0, rows, CHUNK):
            xhat, _ = row_norm(res_ref[r : r + CHUNK, :])
            n2_ref[r : r + CHUNK, :] = (xhat * vec_ref[5:6, :] + vec_ref[6:7, :]).astype(BF)

    return pl.pallas_call(
        kernel,
        grid=(1,),
        in_specs=[
            smem_spec(),
            whole((rows, width)),
            whole((rows, width)),
            whole((rows, model)),
            whole((16, model)),
            whole((model, width)),
            whole((model, width)),
        ],
        out_specs=[whole((rows, model)), whole((rows, model))],
        out_shape=[
            VMEM((rows, model), F32),
            VMEM((rows, model), BF),
        ],
        compiler_params=params(6),
        cost_estimate=cost(2.5),
        name="project_out",
    )(core, mixed[0], mixed[1], tokens, vec, *weights)


def gelu_parts(v):
    bell = jnp.exp(-0.5 * (v * v))
    t = 1.0 / (1.0 + 0.23164189 * jnp.abs(v))
    tail = t * (0.127414796 + t * (-0.142248368 + t * (0.710706871 + t * (-0.726576014 + t * 0.530702714))))
    tail = tail * bell
    return jnp.where(v < 0.0, tail, 1.0 - tail), bell * 0.3989422804014327


def feed_forward(row, core, sets, vec, pieces, offsets=None):
    rows, model = sets[0][0].shape
    hidden = model
    n = len(sets)
    n_buf = len(pieces.buffers)
    per = pieces.rows
    half = rows // 2
    width = model // 2

    def kernel(core_ref, offs_ref, out_offs_ref, vec_ref, *refs):
        ins, refs = refs[: len(flat)], refs[len(flat) :]
        bufs, refs = refs[:n_buf], refs[n_buf:]
        outs, refs = refs[: 4 * n], refs[4 * n :]
        col_ref, slot_refs, (up_ref, down_ref, w_ref) = refs[0], refs[1:-3], refs[-3:]

        def put(j, at, block):
            ref = up_ref if j < 2 else down_ref
            ref[pl.ds(at, per), (j % 2) * width : (j % 2 + 1) * width] = block

        lay_blocks(bufs, offs_ref, per, 4, put)
        up_bias = vec_ref[pl.ds(row(core_ref[0]), 1), :]
        sums = jnp.zeros((1, hidden), F32)
        for i in range(n):
            n_ref, gr_ref, res_ref, gin_ref = (None if at is None else ins[at] for at in where[i])
            out_ref, gn_ref, act_ref, gp_ref = outs[4 * i : 4 * i + 4]
            for r in range(0, rows, half):
                block = slice(r, r + half)
                pre = mm(n_ref[block, :], up_ref[...]) + up_bias
                gact = mm(gr_ref[block, :], down_ref[...], NT)
                cdf, density = gelu_parts(pre)
                act = (pre * cdf).astype(BF)
                gp = gact * (cdf + pre * density)
                low = gp.astype(BF)
                act_ref[block, :] = act
                gp_ref[block, :] = low
                sums += jnp.sum(low.astype(F32), 0, keepdims=True)
                out = mm(act, down_ref[...])
                if res_ref is not None:
                    out = out + res_ref[block, :]
                    if gin_ref is None:
                        out = out + vec_ref[7:8, :]
                out_ref[block, :] = out
                gn = mm(low, up_ref[...], NT)
                gn_ref[block, :] = gn if gin_ref is None else gn + gin_ref[block, :]
        col_ref[...] = sums
        if offsets is None:
            return
        for m in range(4):
            cols = slice((m % 2) * width, (m % 2 + 1) * width)
            total = 0.0
            for i in range(n):
                n_ref, gr_ref = (ins[at] for at in where[i][:2])
                act_ref, gp_ref = outs[4 * i + 2 : 4 * i + 4]
                left, right = (n_ref, gp_ref) if m < 2 else (act_ref, gr_ref)
                total = total + mm(left[...], right[:, cols], TN)
            w_ref[...] = total.astype(BF)
            to_slots(w_ref, out_offs_ref, slot_refs, m, per)

    flat, where = [], []
    for one in sets:
        places = []
        for array in one:
            places.append(None if array is None else len(flat))
            if array is not None:
                flat.append(array)
        where.append(places)
    shapes = [
        VMEM((rows, model), F32),
        VMEM((rows, model), F32),
        VMEM((rows, hidden), BF),
        VMEM((rows, hidden), BF),
    ] * n + [VMEM((1, hidden), F32)]
    if offsets is not None:
        shapes += [VMEM((offsets.shape[0] // 2, 4 * per, width), BF)] * 2
    out = pl.pallas_call(
        kernel,
        grid=(1,),
        in_specs=[
            *[smem_spec()] * 3,
            whole((16, model)),
            *[whole((rows, model))] * len(flat),
            *[whole(one.shape) for one in pieces.buffers],
        ],
        out_specs=[whole(one.shape) for one in shapes],
        out_shape=shapes,
        scratch_shapes=[
            VMEM((model, hidden), BF),
            VMEM((hidden, model), BF),
            VMEM((model, width), BF),
        ],
        compiler_params=params(14),
        cost_estimate=cost(13),
        name="feed_forward",
    )(core, pieces.offsets, pieces.offsets if offsets is None else offsets, vec, *flat, *pieces.buffers)
    return [out[4 * i : 4 * i + 4] for i in range(n)], out[4 * n], out[4 * n + 1 :]


def to_slots(w_ref, offs_ref, outs, matrix, rows):
    slot = 0
    for out in outs:
        for k in range(out.shape[0]):
            at = pl.multiple_of(offs_ref[slot], 16)
            out[k, matrix * rows : (matrix + 1) * rows, :] = w_ref[pl.ds(at, rows), :]
            slot += 1


class Products:
    def __init__(self, core, pairs, offsets, rows, counts):
        self.core, self.offsets, self.rows = core, offsets, rows
        self.tall = pairs[0][0][0][0].shape[-1]
        self.wide = self.tall // 2
        self.flat = []
        self.where = [([self._place(*one) for one in lefts], [self._place(*one) for one in rights]) for lefts, rights in pairs]
        self.shapes = [VMEM((count, len(pairs) * rows, self.wide), BF) for count in counts]
        self.scratch = VMEM((self.tall, self.wide), BF)

    def _place(self, one, part):
        if isinstance(one, tuple):
            return [self._place(each, part) for each in one]
        if one is None:
            return None, part
        match = [i for i, known in enumerate(self.flat) if known is one]
        if not match:
            self.flat.append(one)
            match = [len(self.flat) - 1]
        return match[0], part

    def run(self, core_ref, offs_ref, ins, outs, w_ref, own_ref=None):
        def pick(at, part):
            ref = own_ref if at is None else ins[at]
            if part is None:
                return ref[...]
            if len(ref.shape) == 3:
                return ref[part]
            return ref[:, part * self.wide : (part + 1) * self.wide]

        for m, (lefts, rights) in enumerate(self.where):
            if isinstance(lefts[0], list):
                for h in range(2):
                    total = sum(mm(pick(*left[h]), pick(*right), TN) for left, right in zip(lefts, rights))
                    at = pl.multiple_of((core_ref[0] ^ h) * self.wide, 16)
                    w_ref[pl.ds(at, self.wide), :] = total.astype(BF)
            else:
                total = sum(mm(pick(*left), pick(*right), TN) for left, right in zip(lefts, rights))
                w_ref[...] = total.astype(BF)
            to_slots(w_ref, offs_ref, outs, m, self.rows)


def outer_products(core, pairs, offsets, rows):
    work = Products(core, pairs, offsets, rows, offsets.shape)
    n = len(work.flat)

    def kernel(core_ref, offs_ref, *rest):
        work.run(core_ref, offs_ref, rest[:n], rest[n:-1], rest[-1])

    return pl.pallas_call(
        kernel,
        grid=(1,),
        in_specs=[smem_spec(), smem_spec(), *[whole(one.shape) for one in work.flat]],
        out_specs=[whole(one.shape) for one in work.shapes],
        out_shape=work.shapes,
        scratch_shapes=[work.scratch],
        compiler_params=params(14),
        cost_estimate=cost(5),
        name="outer_products",
    )(core, offsets, *work.flat)


def late_slots(vectors, table, offsets):
    model = vectors.shape[1]
    slots = offsets.shape[0]
    half = slots // 2

    def kernel(offs_ref, vec_ref, table_ref, keep_ref, send_ref):
        for i, ref in enumerate((keep_ref, send_ref)):
            for s in range(half):
                moved = pltpu.roll(vec_ref[...], lax.rem(model - offs_ref[i * half + s], model), 1)
                ref[16 * s : 16 * s + 16, :] = moved[:, :TILE].astype(BF)
            ref[16 * half :, :] = table_ref[...].astype(BF)

    shape = (16 * half + table.shape[0], TILE)
    return pl.pallas_call(
        kernel,
        grid=(1,),
        in_specs=[smem_spec(), whole(vectors.shape), whole(table.shape)],
        out_specs=[whole(shape)] * 2,
        out_shape=[VMEM(shape, BF)] * 2,
        compiler_params=params(4),
        cost_estimate=cost(1),
        name="late_slots",
    )(offsets, vectors, table)


def norm_back(x, up, gain):
    xhat, scale = row_norm(x)
    e = up * gain
    grad = scale * (e - jnp.mean(e, -1, keepdims=True) - xhat * jnp.mean(e * xhat, -1, keepdims=True))
    return grad, up * xhat


def second_norm_back(core, residual, results, grads_normed, grad_rows, weights, vec, lengths):
    rows, model = residual.shape
    width = model // 2
    n, m = len(results), len(grads_normed)

    def kernel(core_ref, len_ref, res_ref, gr_ref, vec_ref, w0_ref, w1_ref, *refs):
        out_refs, gn_refs = refs[:n], refs[n : n + m]
        out_ref, gres_ref, gm_ref, br_ref, sent_ref, sums_ref, gb_ref = refs[n + m :]
        totals = [jnp.zeros((1, model), F32) for _ in range(4)]
        for r in range(0, rows, CHUNK):
            block = slice(r, r + CHUNK)
            row = lax.broadcasted_iota(jnp.int32, (CHUNK, 1), 0) + r
            result = functools.reduce(lambda a, b: a + b, [ref[block, :] for ref in out_refs])
            out_ref[block, :] = jnp.where(row < len_ref[0], result, 0.0).astype(BF)
            up = functools.reduce(lambda a, b: a + b, [ref[block, :] for ref in gn_refs])
            grad, gain_terms = norm_back(res_ref[block, :], up, vec_ref[5:6, :])
            gr = gr_ref[block, :].astype(F32)
            grad = gr + grad
            low = grad.astype(BF)
            gres_ref[block, :] = grad
            gb_ref[block, :] = low
            for i, terms in enumerate((gain_terms, up, low.astype(F32), gr)):
                totals[i] += jnp.sum(terms, 0, keepdims=True)
        sums_ref[...] = jnp.concatenate(totals + [jnp.zeros((4, model), F32)], 0)
        parts = [pl.ds(pl.multiple_of((core_ref[0] ^ h) * width, TILE), width) for h in range(2)]
        for h in range(2):
            acc = 0.0
            for g, w_ref in enumerate((w0_ref, w1_ref)):
                acc = acc + mm(gb_ref[:, parts[g]], w_ref[parts[h], :], NT)
            if h == 0:
                gm_ref[...] = acc.astype(BF)
                br_ref[...] = gb_ref[:, parts[0]]
            else:
                sent_ref[:, :width] = acc.astype(BF)
                sent_ref[:, width:] = gb_ref[:, parts[1]]

    return pl.pallas_call(
        kernel,
        grid=(1,),
        in_specs=[
            *[smem_spec()] * 2,
            *[whole((rows, model))] * 2,
            whole((16, model)),
            whole((model, width)),
            whole((model, width)),
            *[whole((rows, model))] * (n + m),
        ],
        out_specs=[
            *[whole((rows, model))] * 2,
            *[whole((rows, width))] * 2,
            whole((rows, model)),
            whole((8, model)),
        ],
        out_shape=[
            jax.ShapeDtypeStruct((rows, model), BF),
            jax.ShapeDtypeStruct((rows, model), F32),
            jax.ShapeDtypeStruct((rows, width), BF),
            jax.ShapeDtypeStruct((rows, width), BF),
            jax.ShapeDtypeStruct((rows, model), BF),
            jax.ShapeDtypeStruct((8, model), F32),
        ],
        scratch_shapes=[VMEM((rows, model), BF)],
        compiler_params=params(10),
        cost_estimate=cost(4),
        name="second_norm_back",
    )(core, lengths, residual, grad_rows, vec, *weights, *results, *grads_normed)


def attention_backward(joined, probs, mixed, grad_mixed, head_size, products=None, weights=None):
    _, rows, width = joined.shape
    heads = width // head_size
    pairs = width // TILE
    per = TILE // head_size
    tiles = 2 * (rows // TILE) - 1
    span = 2 * rows
    scale = head_size**-0.5
    flat = [] if products is None else products.flat
    n_in = 4 + len(flat) + (2 if products else 0) + (1 if weights is not None else 0)

    def kernel(*refs):
        ins, refs = refs[:n_in], refs[n_in:]
        joined_ref, p_ref, mixed_ref, gm_ref = ins[:4]
        out_ref, diag_ref, refs = refs[0], refs[1], refs[2:]
        gp_ref, ds_ref, acc_ref = refs[-3:]
        lane = lax.broadcasted_iota(jnp.int32, (1, TILE), 1)
        for pair in range(pairs):
            lanes = slice(pair * TILE, (pair + 1) * TILE)
            q, k, v = (joined_ref[j, :, lanes] for j in range(3))
            gm = gm_ref[:, lanes]
            dots = gm.astype(F32) * mixed_ref[:, lanes].astype(F32)
            q_t, gm_t = q.T, gm.T
            dq, dk, dv = [], [], []
            for e in range(per):
                head = pair * per + e
                mine = (lane >= e * head_size) & (lane < (e + 1) * head_size)
                feats = slice(e * head_size, (e + 1) * head_size)
                delta = jnp.sum(jnp.where(mine, dots, 0.0), -1, keepdims=True)
                gp_ref[e] = mm(jnp.where(mine, gm, jnp.zeros_like(gm)), v, NT)
                acc_ref[...] = jnp.zeros_like(acc_ref)
                for r in range(0, rows, CHUNK):
                    block, sub = r // TILE, r % TILE
                    ds = p_ref[head, r : r + CHUNK, :].astype(F32) * (
                        gp_ref[e, r : r + CHUNK, :] - delta[r : r + CHUNK, :]
                    )
                    ds_ref[e, r : r + CHUNK, :] = ds.astype(BF)
                    for j in range(rows // TILE):
                        acc_ref[j - block + rows // TILE - 1, sub : sub + CHUNK, :] += ds[
                            :, j * TILE : (j + 1) * TILE
                        ]
                dq.append(jnp.where(mine, mm(ds_ref[e], k), 0.0))
                dk.append(mm(q_t[feats, :], ds_ref[e]))
                dv.append(mm(gm_t[feats, :], p_ref[head]))
                total = jnp.zeros((8, span), F32)
                for g in range(TILE // 8):
                    strip = jnp.concatenate(
                        [jnp.zeros((8, TILE), F32)]
                        + [acc_ref[d, 8 * g : 8 * g + 8, :] for d in range(tiles)],
                        1,
                    )
                    total += pltpu.roll(strip, (span - 8 * g) % span, 1) if g else strip
                line = total[0:1]
                for i in range(1, 8):
                    line = line + pltpu.roll(total[i : i + 1], span - i, 1)
                diag_ref[head] = line
            out_ref[0, :, lanes] = (functools.reduce(lambda a, b: a + b, dq) * scale).astype(BF)
            out_ref[1, :, lanes] = (jnp.concatenate(dk, 0) * scale).T.astype(BF)
            out_ref[2, :, lanes] = jnp.concatenate(dv, 0).T.astype(BF)
        if weights is not None:
            refs[0][...] = sum(mm(out_ref[j], ins[-1][j], NT) for j in range(3))
        if products is not None:
            slot_refs = refs[1:-4] if weights is not None else refs[:-4]
            products.run(ins[4], ins[5], ins[6 : 6 + len(flat)], slot_refs, refs[-4], out_ref)

    ins = [joined, probs, mixed, grad_mixed]
    specs = [whole(one.shape) for one in ins]
    shapes = [VMEM((3, rows, width), BF), VMEM((heads, 1, span), F32)]
    scratch = [VMEM((per, rows, rows), F32), VMEM((per, rows, rows), BF), VMEM((tiles, TILE, TILE), F32)]
    if products is not None:
        ins += [products.core, products.offsets, *flat]
        specs += [smem_spec(), smem_spec(), *[whole(one.shape) for one in flat]]
    if weights is not None:
        ins.append(weights)
        specs.append(whole(weights.shape))
        shapes.append(VMEM((rows, weights.shape[1]), F32))
    if products is not None:
        shapes += products.shapes
        scratch.insert(0, products.scratch)
    return pl.pallas_call(
        kernel,
        grid=(1,),
        in_specs=specs,
        out_specs=[whole(one.shape) for one in shapes],
        out_shape=shapes,
        scratch_shapes=scratch,
        compiler_params=params(16),
        cost_estimate=cost(4.5),
        name="attention_backward",
    )(*ins)


def normed_back(grads, weights):
    _, rows, width = grads.shape
    model = weights.shape[1]

    def kernel(d_ref, w_ref, out_ref):
        out_ref[...] = sum(mm(d_ref[j], w_ref[j], NT) for j in range(3))

    return pl.pallas_call(
        kernel,
        grid=(1,),
        in_specs=[whole(grads.shape), whole(weights.shape)],
        out_specs=whole((rows, model)),
        out_shape=VMEM((rows, model), F32),
        compiler_params=params(8),
        cost_estimate=cost(1.5),
        name="normed_back",
    )(grads, weights)


def first_norm_back(
    core, grads, part, tokens, grad_residual, vec, weights, sums_second, sums_up, diags, lines, number, apart
):
    rows, model = tokens.shape
    width = model // 2
    count = diags[0].shape[0]
    span = lines[0].shape[1]
    n_up = len(sums_up[0])

    def kernel(core_ref, d0_ref, d1_ref, part_ref, x_ref, gres_ref, vec_ref, w_ref, s2_ref, t0_ref, t1_ref, l0_ref, l1_ref,
               *rest):
        up_refs = rest[: 2 * n_up]
        gx_ref, sums_ref, table_ref, acc_ref = rest[2 * n_up :]
        straight = core_ref[0] == 0

        def ordered(a, b):
            return [jnp.where(straight, a, b), jnp.where(straight, b, a)]

        tables = []
        for t_ref, l_ref in ((t0_ref, l0_ref), (t1_ref, l1_ref)):
            chosen = bucket_line(l_ref[0:1, :], number)
            sums = t_ref[:, 0, :]
            high = sums.astype(BF)
            rest = (sums - high.astype(F32)).astype(BF)
            both = mm(jnp.concatenate([high.astype(F32), rest.astype(F32)], 0).astype(BF), chosen, NT)
            table = both[:count] + both[count:]
            tables.append(table)
        blank = jnp.zeros((count, number), F32)
        tables = tables if apart else ordered(tables[0] + tables[1], blank)
        table = jnp.concatenate([*tables, jnp.zeros((16 - 2 * count, number), F32)], 0)
        table = jnp.concatenate([table, jnp.zeros((16, 4 * TILE - number), F32)], 1)
        table_ref[...] = jnp.concatenate([table[:, i * TILE : (i + 1) * TILE] for i in range(4)], 0)
        columns = []
        for j in (0, 2):
            a, b = (jnp.sum(d_ref[j].astype(F32), 0, keepdims=True) for d_ref in (d0_ref, d1_ref))
            columns.append(jnp.concatenate([a, b] if apart else ordered(a + b, jnp.zeros_like(a)), 1))
        ups = []
        for f in range(2):
            here = [ref[...] for ref in up_refs[f * n_up : (f + 1) * n_up]]
            ups += here if apart else ordered(here[0], jnp.zeros_like(here[0]))
        acc_ref[...] = part_ref[...] + sum(mm(d0_ref[j], w_ref[j], NT) for j in range(3))
        totals = [jnp.zeros((1, model), F32) for _ in range(2)]
        for r in range(0, rows, CHUNK):
            block = slice(r, r + CHUNK)
            up = acc_ref[block, :]
            grad, gain_terms = norm_back(x_ref[block, :].astype(F32), up, vec_ref[0:1, :])
            gx_ref[block, :] = gres_ref[block, :] + grad
            totals[0] += jnp.sum(gain_terms, 0, keepdims=True)
            totals[1] += jnp.sum(up, 0, keepdims=True)
        sums_ref[...] = jnp.concatenate(
            totals
            + columns
            + [s2_ref[2:3, :], s2_ref[0:1, :], s2_ref[1:2, :], s2_ref[3:4, :]]
            + ups
            + [jnp.zeros((4, model), F32)],
            0,
        )

    return pl.pallas_call(
        kernel,
        grid=(1,),
        in_specs=[
            smem_spec(),
            whole((3, rows, width)),
            whole((3, rows, width)),
            whole((rows, model)),
            whole((rows, model)),
            whole((rows, model)),
            whole((16, model)),
            whole((3, model, width)),
            whole((8, model)),
            whole((count, 1, span)),
            whole((count, 1, span)),
            whole((8, span)),
            whole((8, span)),
            *[whole((1, model))] * (2 * n_up),
        ],
        out_specs=[whole((rows, model)), whole((16, model)), whole((64, TILE))],
        out_shape=[
            jax.ShapeDtypeStruct((rows, model), F32),
            jax.ShapeDtypeStruct((16, model), F32),
            jax.ShapeDtypeStruct((64, TILE), F32),
        ],
        scratch_shapes=[VMEM((rows, model), F32)],
        compiler_params=params(14),
        cost_estimate=cost(5),
        name="first_norm_back",
    )(
        core, *grads, part, tokens, grad_residual, vec, weights, sums_second, *diags, *lines, *sums_up[0], *sums_up[1]
    )


def pack_blocks(core, lengths, buckets, qkv, out, up):
    local, model = out.shape
    width = model // 2
    unit = local * 2
    chips = up.shape[1] // (4 * unit)
    rows = buckets.shape[1]

    def kernel(core_ref, len_ref, buckets_hbm, qkv_hbm, out_hbm, up_hbm, a0_ref, a1_ref, u0_ref, u1_ref, line_ref,
               first_ref, last_ref, qkv_ref, out_ref, up_ref, sems):
        copies = [
            pltpu.make_async_copy(source, target, sems.at[i])
            for i, (source, target) in enumerate(
                (
                    (qkv_hbm, qkv_ref),
                    (out_hbm, out_ref),
                    (up_hbm, up_ref),
                    (buckets_hbm.at[pl.ds(0, 1), pl.ds(0, 8)], first_ref),
                    (buckets_hbm.at[pl.ds(0, 1), pl.ds(rows - 8, 8)], last_ref),
                )
            )
        ]
        for c in copies:
            c.start()
        for c in copies:
            c.wait()
        core_at = core_ref[0]
        for h, a_ref in enumerate((a0_ref, a1_ref)):
            at = (core_at ^ h) * width
            for j in range(3):
                a_ref[j] = qkv_ref[:, pl.ds(pl.multiple_of(j * model + at, TILE), width)]
            a_ref[3] = out_ref[:, pl.ds(pl.multiple_of(at, TILE), width)]
        first = core_at == 0
        ahead = pltpu.roll(last_ref[0, 7:8, :].astype(F32), 1, 1)
        line = jnp.concatenate([ahead, first_ref[0, 0:1, :].astype(F32)], 1)
        live = jnp.zeros_like(line) + len_ref[0].astype(F32)
        line_ref[...] = jnp.concatenate([line, live, jnp.zeros((6, 2 * rows), F32)], 0)
        for f in range(2):
            by_core = []
            for c in range(2):
                by_core.append(
                    jnp.concatenate(
                        [
                            up_ref[:, ((2 * chip + c) * 2 + f) * unit : ((2 * chip + c) * 2 + f + 1) * unit]
                            for chip in range(chips)
                        ],
                        1,
                    ).astype(F32)
                )
            u0_ref[f] = jnp.where(first, by_core[0], by_core[1]).astype(BF)
            u1_ref[f] = jnp.where(first, by_core[1], by_core[0]).astype(BF)

    shapes = [
        *[VMEM((4, local, width), BF)] * 2,
        *[VMEM((2, local, model), BF)] * 2,
        VMEM((8, 2 * rows), F32),
    ]
    return pl.pallas_call(
        kernel,
        grid=(1,),
        in_specs=[
            smem_spec(),
            smem_spec(),
            *[hbm_spec()] * 4,
        ],
        out_specs=[whole(one.shape) for one in shapes],
        out_shape=shapes,
        scratch_shapes=[
            VMEM((1, 8, rows), jnp.int32),
            VMEM((1, 8, rows), jnp.int32),
            VMEM(qkv.shape, BF),
            VMEM(out.shape, BF),
            VMEM(up.shape, BF),
            pltpu.SemaphoreType.DMA((5,)),
        ],
        compiler_params=params(6),
        cost_estimate=cost(1.5),
        name="pack_blocks",
    )(core, lengths, in_hbm(buckets), in_hbm(qkv), in_hbm(out), in_hbm(up))


def pack_vectors(core, vectors):
    _, local = vectors.shape

    def kernel(core_ref, vec_ref, small_ref):
        first = core_ref[0] == 0
        values = jnp.concatenate(
            [vec_ref[...].astype(F32), jnp.zeros((VECTORS + 4, TILE - local), F32)], 1
        )
        moved = pltpu.roll(values, local, 1)
        lines = [jnp.where(first, values[:VECTORS], moved[:VECTORS])]
        for f in range(2):
            at = VECTORS + 2 * f
            both = values[at : at + 1] + moved[at + 1 : at + 2]
            blank = jnp.zeros_like(both)
            lines += [jnp.where(first, both, blank), jnp.where(first, blank, both)]
        small_ref[...] = jnp.concatenate(lines + [jnp.zeros((4, TILE), F32)], 0).astype(BF)

    return pl.pallas_call(
        kernel,
        grid=(1,),
        in_specs=[smem_spec(), whole(vectors.shape)],
        out_specs=whole((16, TILE)),
        out_shape=VMEM((16, TILE), BF),
        compiler_params=params(4),
        cost_estimate=cost(1),
        name="pack_vectors",
    )(core, vectors)


def ordered_rows(core_at, mine, theirs):
    first = core_at == 0
    a, b = mine.astype(F32), theirs.astype(F32)
    return jnp.concatenate([jnp.where(first, a, b), jnp.where(first, b, a)], 0)


def merge_attention(core, mine, theirs, small, small_theirs):
    count, local, width = mine.shape

    def kernel(core_ref, a_ref, b_ref, s_ref, t_ref, out_ref):
        for j in range(count):
            out_ref[2 * local * j : 2 * local * (j + 1), :] = ordered_rows(core_ref[0], a_ref[j], b_ref[j]).astype(BF)
        vec = s_ref[...].astype(F32) + t_ref[...].astype(F32)
        out_ref[2 * local * count :, :] = jnp.concatenate([vec, jnp.zeros((16, width - TILE), F32)], 1).astype(BF)

    return pl.pallas_call(
        kernel,
        grid=(1,),
        in_specs=[smem_spec(), *[whole(mine.shape)] * 2, *[whole(small.shape)] * 2],
        out_specs=whole((2 * local * count + 16, width)),
        out_shape=VMEM((2 * local * count + 16, width), BF),
        compiler_params=params(4),
        cost_estimate=cost(1),
        name="merge_attention",
    )(core, mine, theirs, small, small_theirs)


def merge_feed_forward(core, mine, theirs, down):
    _, local, model = mine.shape
    unit = 2 * local
    width = model // 2

    def kernel(core_ref, a_ref, b_ref, d_ref, *outs):
        for f in range(2):
            up = ordered_rows(core_ref[0], a_ref[f], b_ref[f]).astype(BF)
            low = d_ref[f * unit : (f + 1) * unit, :]
            for j, block in enumerate((up[:, :width], up[:, width:], low[:, :width], low[:, width:])):
                outs[f][j * unit : (j + 1) * unit, :] = block

    shape = VMEM((4 * unit, width), BF)
    return pl.pallas_call(
        kernel,
        grid=(1,),
        in_specs=[smem_spec(), *[whole(mine.shape)] * 2, whole(down.shape)],
        out_specs=[whole(shape.shape)] * 2,
        out_shape=[shape] * 2,
        compiler_params=params(4),
        cost_estimate=cost(1),
        name="merge_feed_forward",
    )(core, mine, theirs, down)


def pair_sum(refs):
    parts = [ref[...].astype(F32) for ref in refs]
    while len(parts) > 1:
        half = len(parts) // 2
        parts = [parts[i] + parts[i + half] for i in range(half)]
    return parts[0]


def rows_of(total, first, core_at, local, mine):
    a, b = total[first : first + local], total[first + local : first + 2 * local]
    return jnp.where((core_at == 0) == mine, a, b)


def total_attention(core, parts, local):
    tall, width = parts[0].shape
    tail = tall - 8 * local

    def kernel(core_ref, *refs):
        ins, (mine_ref, sent_ref, tail_ref) = refs[: len(parts)], refs[len(parts) :]
        total = pair_sum(ins)
        for j in range(4):
            mine_ref[j] = rows_of(total, 2 * local * j, core_ref[0], local, True)
            sent_ref[j] = rows_of(total, 2 * local * j, core_ref[0], local, False).astype(BF)
        tail_ref[...] = total[8 * local :].astype(BF)

    shapes = [
        jax.ShapeDtypeStruct((4, local, width), F32),
        jax.ShapeDtypeStruct((4, local, width), BF),
        jax.ShapeDtypeStruct((tail, width), BF),
    ]
    return pl.pallas_call(
        kernel,
        grid=(1,),
        in_specs=[smem_spec(), *[whole(one.shape) for one in parts]],
        out_specs=[whole(one.shape) for one in shapes],
        out_shape=shapes,
        compiler_params=params(6),
        cost_estimate=cost(1),
        name="total_attention",
    )(core, *parts)


def finish_attention(core, mine, theirs, tail, tail_theirs, heads, number):
    _, local, width = mine.shape
    model = 2 * width

    def kernel(core_ref, a_ref, b_ref, s_ref, t_ref, qkv_ref, out_ref, table_ref, *small_refs):
        at = core_ref[0]
        for h, ref in enumerate((a_ref, b_ref)):
            for j in range(3):
                cols = pl.ds(pl.multiple_of(j * model + (at ^ h) * width, TILE), width)
                qkv_ref[:, cols] = ref[j].astype(F32)
            out_ref[:, pl.ds(pl.multiple_of((at ^ h) * width, TILE), width)] = ref[3].astype(F32)
        total = s_ref[...].astype(F32) + t_ref[...].astype(F32)
        small = total[:16, :TILE]
        small = jnp.where(at == 0, small, jnp.concatenate([pltpu.roll(small[:8], TILE - local, 1), small[8:]], 0))
        for i in range(VECTORS):
            small_refs[i][...] = small[i : i + 1, :local]
        ups = [jnp.where(at == 0, small[8 + 2 * f : 9 + 2 * f], small[9 + 2 * f : 10 + 2 * f]) for f in range(2)]
        lane = lax.broadcasted_iota(jnp.int32, (1, TILE), 1)
        both = jnp.where(lane < 2 * local, ups[0], pltpu.roll(ups[1], 2 * local, 1))
        small_refs[VECTORS][...] = both[:, : 4 * local]
        table_ref[...] = jnp.concatenate([total[:16, TILE:], total[16:, : 2 * TILE]], 1)[:heads, :number]

    shapes = [
        jax.ShapeDtypeStruct((local, 3 * model), F32),
        jax.ShapeDtypeStruct((local, model), F32),
        jax.ShapeDtypeStruct((heads, number), F32),
        *[jax.ShapeDtypeStruct((1, local), F32)] * VECTORS,
        jax.ShapeDtypeStruct((1, 4 * local), F32),
    ]
    return pl.pallas_call(
        kernel,
        grid=(1,),
        in_specs=[smem_spec(), *[whole(one.shape) for one in (mine, theirs, tail, tail_theirs)]],
        out_specs=[whole(one.shape) for one in shapes],
        out_shape=shapes,
        compiler_params=params(6),
        cost_estimate=cost(1),
        name="finish_attention",
    )(core, mine, theirs, tail, tail_theirs)


def total_feed_forward(core, parts, local):
    _, width = parts[0].shape
    model = 2 * width
    unit = 2 * local

    def kernel(core_ref, *refs):
        ins, (mine_ref, sent_ref, down_ref) = refs[: len(parts)], refs[len(parts) :]
        total = pair_sum(ins)
        for h in range(2):
            cols = slice(h * width, (h + 1) * width)
            mine_ref[:, cols] = rows_of(total, h * unit, core_ref[0], local, True)
            sent_ref[:, cols] = rows_of(total, h * unit, core_ref[0], local, False).astype(BF)
            down_ref[:, cols] = total[(2 + h) * unit : (3 + h) * unit]

    shapes = [
        jax.ShapeDtypeStruct((local, model), F32),
        jax.ShapeDtypeStruct((local, model), BF),
        jax.ShapeDtypeStruct((unit, model), F32),
    ]
    return pl.pallas_call(
        kernel,
        grid=(1,),
        in_specs=[smem_spec(), *[whole(one.shape) for one in parts]],
        out_specs=[whole(one.shape) for one in shapes],
        out_shape=shapes,
        compiler_params=params(6),
        cost_estimate=cost(1),
        name="total_feed_forward",
    )(core, *parts)


def finish_feed_forward(core, mine, theirs, downs):
    local, model = mine[0].shape
    unit = 2 * local
    chips = model // unit

    def kernel(core_ref, m0, m1, t0, t1, d0, d1, up_ref, down_ref):
        first = core_ref[0] == 0
        by = []
        for a, b in ((m0, t0), (m1, t1)):
            a, b = a[...], b[...].astype(F32)
            by.append((jnp.where(first, a, b), jnp.where(first, b, a)))
        up_ref[...] = jnp.concatenate(
            [
                by[f][c][:, chip * unit : (chip + 1) * unit]
                for chip in range(chips)
                for c in range(2)
                for f in range(2)
            ],
            1,
        )
        down_ref[:unit, :] = d0[...]
        down_ref[unit:, :] = d1[...]

    shapes = [jax.ShapeDtypeStruct((local, 4 * model), F32), jax.ShapeDtypeStruct((2 * unit, model), F32)]
    ins = (*mine, *theirs, *downs)
    return pl.pallas_call(
        kernel,
        grid=(1,),
        in_specs=[smem_spec(), *[whole(one.shape) for one in ins]],
        out_specs=[whole(one.shape) for one in shapes],
        out_shape=shapes,
        compiler_params=params(6),
        cost_estimate=cost(1),
        name="finish_feed_forward",
    )(core, *ins)


VECTORS = 8


class Order:
    def __init__(self, token):
        self.token = token

    def go(self, *values):
        out, _ = lax.optimization_barrier((values, self.token))
        return out if len(out) > 1 else out[0]

    def mark(self, *values):
        out, self.token = lax.optimization_barrier((values, self.token))
        return out if len(out) > 1 else out[0]


class GridLinks:
    pair = True

    def __init__(self, sizes, model):
        self.ny, self.nz, self.nx = sizes
        self.chips = self.ny * self.nz * self.nx
        self.rows = model // self.chips
        dp, inner = lax.axis_index("dp"), lax.axis_index("fsdp")
        self.core = inner % 2
        chip = inner // 2
        self.place = (dp, chip // self.nx, chip % self.nx)
        self.gather_offsets = self._offsets(self.core, -1, (range(self.nz),))
        self.early_offsets = self._offsets(self.core, -1, ((0, 1, 3, 2),))
        self.scatter_offsets = self._offsets(self.core, 1, (range(self.nz),))
        self.last_offsets = self._offsets(self.core, 1, (range(1, self.nz), (0,)))
        self.last_counts = (self.nz - 1,) * 4 + (2, 2)

    def _offsets(self, core, sign, parts):
        y, z, x = self.place
        out = []
        for part in parts:
            for r1 in range(2):
                for r2 in range(2):
                    for k in part:
                        fy = jnp.where(core == 0, r1, r2)
                        fx = jnp.where(core == 0, r2, r1)
                        zz = (z + sign * k + self.nz) % self.nz
                        out.append(((y ^ fy) * self.nz + zz) * self.nx + (x ^ fx))
        return (jnp.stack(out) * self.rows).astype(jnp.int32)

    def _send(self, value, move):
        pairs = []
        for y in range(self.ny):
            for z in range(self.nz):
                for x in range(self.nx):
                    for c in range(2):
                        source = ((y * self.nz + z) * self.nx + x) * 2 + c
                        ty, tz, tx, tc = move(y, z, x, c)
                        pairs.append((source, ((ty * self.nz + tz) * self.nx + tx) * 2 + tc))
        return lax.ppermute(value, AXES, pairs)

    def swap(self, value):
        return self._send(value, lambda y, z, x, c: (y, z, x, 1 - c))

    def along_z(self, value, k):
        return self._send(value, lambda y, z, x, c: (y, (z + k) % self.nz, x, c))

    def x_first(self, value):
        return self._send(value, lambda y, z, x, c: (y, z, 1 - x, c) if c == 0 else (1 - y, z, x, c))

    def y_first(self, value):
        return self._send(value, lambda y, z, x, c: (y, z, 1 - x, c) if c == 1 else (1 - y, z, x, c))

    def spread(self, near):
        second = self.x_first(near)
        third = self.y_first(near)
        return [near, second, third, self.y_first(second)]

    def scatter_z(self, sums):
        return [sums[0]] + [self.along_z(sums[k], k) for k in range(1, self.nz)]


def small_kernel(kernel, name, shapes, *ins):
    return pl.pallas_call(
        kernel,
        grid=(1,),
        in_specs=[whole(one.shape) for one in ins],
        out_specs=[whole(shape) for shape in shapes],
        out_shape=[VMEM(shape, BF) for shape in shapes],
        compiler_params=params(4),
        cost_estimate=cost(1),
        name=name,
    )(*ins)


def stack_blocks(*blocks):
    def kernel(*refs):
        for i, ref in enumerate(refs[:-1]):
            refs[-1][i] = ref[...]

    return small_kernel(kernel, "stack_blocks", [(len(blocks), *blocks[0].shape)], *blocks)[0]


def join_blocks(first, last):
    n = first.shape[0]

    def kernel(first_ref, last_ref, out_ref):
        out_ref[:n] = first_ref[...]
        out_ref[n:] = last_ref[...]

    return small_kernel(kernel, "join_blocks", [(n + last.shape[0], *first.shape[1:])], first, last)[0]


def add_low(a, b):
    return (a.astype(F32) + b.astype(F32)).astype(BF)


def fold(keep, moved):
    n = keep.shape[0] // 2

    def kernel(keep_ref, moved_ref, *outs):
        for s in range(2 * n):
            outs[s // n][s % n] = add_low(keep_ref[s], moved_ref[s])

    return small_kernel(kernel, "fold", [(n, *keep.shape[1:])] * 2, keep, moved)


def add_blocks(a, b):
    def kernel(a_ref, b_ref, out_ref):
        for i in range(a.shape[0]):
            out_ref[i] = add_low(a_ref[i], b_ref[i])

    return small_kernel(kernel, "add_blocks", [a.shape], a, b)[0]


def fold_late(keep, moved, slots):
    half = 8 * slots

    def kernel(keep_ref, moved_ref, *outs):
        total = add_low(keep_ref[...], moved_ref[...])
        for i, out in enumerate(outs):
            out[:half, :] = total[i * half : (i + 1) * half]
            out[half:, :] = total[2 * half :]

    return small_kernel(kernel, "fold_late", [(half + keep.shape[0] - 2 * half, TILE)] * 2, keep, moved)


def fold_last(blocks, late=None, first=0):
    n, tall, wide = blocks[0].shape
    count = len(blocks)
    tail = 0 if late is None else 32

    def kernel(*refs):
        outs = refs[-n:]
        for s in range(n):
            total = sum(ref[s].astype(F32) for ref in refs[:count])
            outs[s][:tall, :] = total.astype(BF)
        if tail:
            total = add_low(refs[count][...], refs[count + 1][...])
            at = total.shape[0] - 64
            blocks = [total[at + 16 * i : at + 16 * i + 16] for i in range(4)]
            for s in range(n):
                small = total[16 * (first + s) : 16 * (first + s) + 16]
                outs[s][tall : tall + 16, :] = jnp.concatenate([small, *blocks[:2]], 1)
                outs[s][tall + 16 :, :] = jnp.concatenate([*blocks[2:], jnp.zeros_like(small)], 1)

    return small_kernel(kernel, "fold_last", [(tall + tail, wide)] * n, *blocks, *(late or ()))


def on_device(
    links,
    tokens,
    lengths,
    buckets,
    ln1_gain,
    ln1_bias,
    qkv_weight,
    q_bias,
    v_bias,
    out_weight,
    out_bias,
    rel_table,
    ln2_gain,
    ln2_bias,
    up_weight,
    up_bias,
    down_weight,
    down_bias,
    cotangent,
):
    rows, model = tokens.shape
    heads, number = rel_table.shape
    head_size = model // heads
    width = model // 2
    local = qkv_weight.shape[0]
    core, chips = links.core, links.chips
    core_arg = core.astype(jnp.int32).reshape(1)

    order = Order(core_arg)
    a_mine, a_sent, u_mine, u_sent, line = pack_blocks(
        core_arg, lengths, buckets, qkv_weight, out_weight, up_weight
    )
    a_mine, a_sent, ln1_gain = order.mark(a_mine, a_sent, ln1_gain)
    vectors = jnp.stack(
        [ln1_gain, ln1_bias, q_bias, v_bias, out_bias, ln2_gain, ln2_bias, down_bias]
        + [up_bias[i * local : (i + 1) * local] for i in range(4)]
    )
    small = pack_vectors(core_arg, vectors)
    a_theirs, small_theirs = links.swap(a_sent), links.swap(small)
    line_other, tokens_other, u_theirs = links.swap(line), links.swap(tokens), links.swap(u_sent)
    early_offsets, gather_offsets = links.early_offsets, links.gather_offsets
    scatter_offsets, last_offsets = links.scatter_offsets, links.last_offsets
    a_piece = merge_attention(core_arg, a_mine, a_theirs, small, small_theirs)
    a_piece, line_other, tokens_other, u_theirs, early_offsets, gather_offsets, scatter_offsets, last_offsets = order.mark(
        a_piece, line_other, tokens_other, u_theirs, early_offsets, gather_offsets, scatter_offsets, last_offsets
    )

    z_parts = [links.along_z(a_piece, k) for k in (1, 3, 2)]
    near = a_piece[None]
    second, third = links.x_first(near), links.y_first(near)
    tiles, grad_rows = bias_tiles(core_arg, (line, line_other), rel_table, cotangent, lengths, (0, 0))
    tiles, grad_rows, z_parts[:2], second, third, a_piece = order.mark(
        tiles, grad_rows, z_parts[:2], second, third, a_piece
    )
    z_parts[2] = links.along_z(a_piece, 2)
    f0, f1 = merge_feed_forward(core_arg, u_mine, order.go(u_theirs), down_weight)
    f_early = [[go(f[None]) for go in (links.x_first, links.y_first)] for f in (f0, f1)]
    f0, f1, z_parts[2], f_early = order.mark(f0, f1, z_parts[2], f_early)
    near_last = stack_blocks(*z_parts)
    second_last, third_last = links.x_first(near_last), links.y_first(near_last)
    f0_z = [links.along_z(order.go(f0), k) for k in (1, 3, 2)]
    second_last, third_last, f0_z[:2] = order.mark(second_last, third_last, f0_z[:2])
    fourth = links.y_first(join_blocks(second, second_last))
    f1_z = [links.along_z(order.go(f1), k) for k in (1, 3)]
    grad_rows_other = links.swap(grad_rows)
    fourth, grad_rows_other, f0_z[2] = order.mark(fourth, grad_rows_other, f0_z[2])
    parts = [near, near_last, second, second_last, third, third_last, fourth]
    own, own_out, vec = order.mark(*assemble_attention(Pieces(parts, early_offsets, links.rows), model))
    f1_z = order.mark(f1_z)
    f0_near = stack_blocks(f0_z[0], f0_z[2], f0_z[1])
    f0_second, f0_third = links.x_first(f0_near), links.y_first(f0_near)
    f1_z.append(links.along_z(order.go(f1), 2))
    other_out = links.swap(own_out)

    normed_other, joined1, mixed1, probs1 = attention_forward(
        1, 0, core_arg, tokens_other, vec, order.go(own), tiles, line_other, head_size
    )
    mixed1, other_out, f1_z = order.mark(mixed1, other_out, f1_z)
    mixed_rest = links.swap(mixed1)
    f0_second, f0_third = order.mark(f0_second, f0_third)
    f0_fourth = links.y_first(join_blocks(f_early[0][0], f0_second))
    f1_near = stack_blocks(f1_z[0], f1_z[2], f1_z[1])
    f1_second = links.x_first(f1_near)
    normed, joined0, mixed0, probs0 = attention_forward(
        0, 0, core_arg, tokens, vec, order.go(own), tiles, line, head_size
    )
    mixed0, mixed_rest = order.mark(mixed0, mixed_rest)
    mixed_rest_other = links.swap(mixed0)
    residual, normed2 = project_out(core_arg, (order.go(mixed0), mixed_rest), tokens, (own_out, other_out), vec)
    normed2, f0_fourth, f1_second, mixed_rest_other = order.mark(normed2, f0_fourth, f1_second, mixed_rest_other)

    normed2_other = links.swap(normed2)
    f1_third, f1_fourth = links.y_first(f1_near), links.y_first(join_blocks(f_early[1][0], f1_second))
    normed2_other = order.mark(normed2_other)

    def chunk(bufs):
        return Pieces(bufs, gather_offsets, links.rows)

    (own0, other0), sums_f0, (keep0, send0) = feed_forward(
        lambda c: 8 + c, core_arg,
        [(normed2, grad_rows, residual, None), (normed2_other, grad_rows_other, None, None)],
        vec, chunk([f0[None], f0_near, f_early[0][0], f0_second, f_early[0][1], f0_third, f0_fourth]), scatter_offsets,
    )
    own0, other0, keep0, send0, f1_third, f1_fourth = order.mark(own0, other0, keep0, send0, f1_third, f1_fourth)
    moved0 = links.y_first(send0)
    (own1, other1), sums_f1, (keep1, send1) = feed_forward(
        lambda c: 10 + c, core_arg,
        [(normed2, grad_rows, own0[0], own0[1]), (normed2_other, grad_rows_other, other0[0], other0[1])],
        vec, chunk([f1[None], f1_near, f_early[1][0], f1_second, f_early[1][1], f1_third, f1_fourth]), scatter_offsets,
    )
    own1, other1, keep1, send1, moved0 = order.mark(own1, other1, keep1, send1, moved0)
    keep0, send0 = fold(keep0, moved0)
    moved0 = links.x_first(send0)
    result_rest, grad_rest = links.swap(other1[0]), links.swap(other1[1])
    result_rest, grad_rest = order.mark(result_rest, grad_rest)
    moved1 = links.y_first(order.go(send1))
    output, grad_res, gm0, branch_cols, sent, sums2 = second_norm_back(
        core_arg, residual, (order.go(own1[0]), result_rest), (own1[1], grad_rest), grad_rows,
        (own_out, other_out), vec, lengths,
    )
    sent, moved0 = order.mark(sent, moved0)
    got = links.swap(sent)
    sums0 = fold_last((keep0, moved0))
    parts0 = [sums0[0]] + [links.along_z(sums0[k], k) for k in (1, 3)]
    dj0, diag0 = attention_backward(joined0, probs0, mixed0, order.go(gm0), head_size)
    dj0, got, moved1, parts0 = order.mark(dj0, got, moved1, parts0)
    parts0.insert(2, links.along_z(order.go(sums0[2]), 2))
    keep1, send1 = fold(keep1, moved1)
    moved1 = links.x_first(send1)
    dj1, diag1, part, keep, keep_next, send, send_next, own_keep, own_send = attention_backward(
        joined1, probs1, mixed1, order.go(got), head_size,
        Products(
            core_arg,
            [([(normed, None), (normed_other, None)], [(dj0, j), (None, j)]) for j in range(3)]
            + [([((mixed0, mixed_rest), None), ((mixed1, mixed_rest_other), None)], [(branch_cols, None), (got, 1)])],
            last_offsets,
            links.rows,
            links.last_counts,
        ),
        own,
    )
    part, keep, keep_next, send, send_next, own_keep, own_send, moved1, parts0 = order.mark(
        part, keep, keep_next, send, send_next, own_keep, own_send, moved1, parts0
    )
    part_rest = links.swap(part)
    next_moved, moved = links.y_first(send_next), links.y_first(send)
    part_rest, keep1, moved1 = order.mark(part_rest, keep1, moved1)
    sums1 = fold_last((keep1, moved1))
    parts1 = [sums1[0]] + [links.along_z(sums1[k], k) for k in (1, 3)]
    input_grad, vec_grads, table_grad = first_norm_back(
        core_arg, (order.go(dj0), dj1), part_rest, tokens, grad_res, vec, own, sums2, ([sums_f0], [sums_f1]),
        (diag0, diag1), (line, line_other), number, False,
    )
    late_keep, late_send, next_moved, parts1 = order.mark(
        *late_slots(vec_grads, table_grad, scatter_offsets), next_moved, parts1
    )
    late_moved = links.y_first(late_send)
    parts1.insert(2, links.along_z(order.go(sums1[2]), 2))
    next_moved = links.x_first(add_blocks(keep_next, next_moved))
    late_moved, moved = order.mark(late_moved, moved)
    late_keep, late_send = fold_late(late_keep, late_moved, 2 * links.nz)
    late_moved = links.x_first(late_send)
    next_moved, late_moved, own_send, parts1 = order.mark(next_moved, late_moved, own_send, parts1)
    sums = fold_last((keep, moved, next_moved), (late_keep, late_moved), 1)
    parts = [links.along_z(sums[k - 1], k) for k in (1, 2, 3)]
    own_moved = links.y_first(own_send)
    ffn0 = total_feed_forward(core_arg, order.go(parts0), local)
    ffn1 = total_feed_forward(core_arg, order.go(parts1), local)
    ffn0, ffn1, own_moved = order.mark(ffn0, ffn1, own_moved)
    own_keep, own_send = fold(own_keep, own_moved)
    own_moved = links.x_first(own_send)
    ups = [links.swap(ffn0[1]), links.swap(ffn1[1])]
    grad_up, grad_down = finish_feed_forward(
        core_arg, [ffn0[0], ffn1[0]], ups, [ffn0[2], ffn1[2]]
    )
    grad_up, grad_down, parts, own_moved = order.mark(grad_up, grad_down, parts, own_moved)
    parts = [*fold_last((own_keep, own_moved), (late_keep, late_moved)), *parts]
    mine, sent, tail = total_attention(core_arg, parts, local)
    theirs, tail_theirs = links.swap(sent), links.swap(tail)
    grad_qkv, grad_out, grad_table, *small_grads = finish_attention(
        core_arg, mine, theirs, tail, tail_theirs, heads, number
    )
    small_grads = [one.reshape(-1) for one in small_grads]
    grad_up_bias = small_grads[VECTORS]

    return (
        output,
        input_grad,
        small_grads[0],
        small_grads[1],
        grad_qkv,
        small_grads[2],
        small_grads[3],
        grad_out,
        small_grads[4],
        grad_table,
        small_grads[5],
        small_grads[6],
        grad_up,
        grad_up_bias,
        grad_down,
        small_grads[7],
    )


def on_any_mesh(
    tokens,
    lengths,
    buckets,
    ln1_gain,
    ln1_bias,
    qkv_weight,
    q_bias,
    v_bias,
    out_weight,
    out_bias,
    rel_table,
    ln2_gain,
    ln2_bias,
    up_weight,
    up_bias,
    down_weight,
    down_bias,
    cotangent,
):
    rows, model = tokens.shape
    heads, number = rel_table.shape
    head_size = model // heads
    width = model // 2
    local = qkv_weight.shape[0]
    hidden = up_weight.shape[1]
    core = jnp.zeros((1,), jnp.int32)
    offsets = jnp.zeros((1,), jnp.int32)

    def gathered(x):
        return lax.all_gather(x, AXES, axis=0, tiled=True)

    def scattered(x):
        return lax.psum_scatter(x, AXES, scatter_dimension=0, tiled=True)

    vectors = [ln1_gain, ln1_bias, q_bias, v_bias, out_bias, ln2_gain, ln2_bias, down_bias]
    unit = up_bias.shape[0]
    small = gathered(jnp.concatenate([*vectors, up_bias])[None, :])
    wide = [small[:, i * local : (i + 1) * local].reshape(1, model) for i in range(VECTORS)]
    ub = small[:, VECTORS * local :].reshape(2, 2, model).transpose(1, 0, 2).reshape(4, model)
    del unit
    vec = jnp.concatenate([*wide, ub, jnp.zeros((4, model), BF)], 0).astype(F32)
    attn = gathered(jnp.concatenate([qkv_weight, out_weight], 1))
    up, down = gathered(up_weight), gathered(down_weight)
    a_pieces = tuple(
        jnp.stack([attn[:, j * model + h * width : j * model + (h + 1) * width] for j in range(3)])
        for h in range(2)
    )

    a_out = tuple(attn[:, 3 * model + h * width : 3 * model + (h + 1) * width] for h in range(2))

    def chunk(f, h):
        at = (2 * h + f) * model
        blocks = [one[:, k * width : (k + 1) * width] for one in (up[:, at : at + model], down[at : at + model]) for k in range(2)]
        return Pieces([jnp.concatenate(blocks, 0)[None]], offsets, model)

    ahead = jnp.roll(buckets[0, rows - 1], 1)
    line = jnp.concatenate([ahead, buckets[0, 0]]).astype(F32)
    line = jnp.stack([line, jnp.full_like(line, lengths[0])] + [jnp.zeros_like(line)] * 6)
    tiles, grad_rows = bias_tiles(core, (line, line), rel_table, cotangent, lengths, (0, 1))
    normed, joined0, mixed0, probs0 = attention_forward(0, 0, core, tokens, vec, a_pieces[0], tiles, line, head_size)
    _, joined1, mixed1, probs1 = attention_forward(1, 1, core, tokens, vec, a_pieces[1], tiles, line, head_size)
    residual, normed2 = project_out(core, (mixed0, mixed1), tokens, a_out, vec)
    result, grad_n2 = residual, None
    up_sums, ups, downs = [[], []], [], []
    for f in range(2):
        for h in range(2):
            ((result, grad_n2, active, grad_pre),), sums, _ = feed_forward(
                lambda c, at=8 + 2 * f + h: c + at, core, [(normed2, grad_rows, result, grad_n2)], vec, chunk(f, h)
            )
            up_sums[f].append(sums)
            (both,) = outer_products(
                core,
                [([(normed2, None)], [(grad_pre, k)]) for k in range(2)]
                + [([(active, None)], [(grad_rows, k)]) for k in range(2)],
                offsets,
                model,
            )
            both = both[0].reshape(2, 2, model, width).transpose(0, 2, 1, 3).reshape(2, model, model)
            ups.append(both[0])
            downs.append(both[1])
    output, grad_res, gm0, branch0, sent, sums2 = second_norm_back(
        core, residual, (result,), (grad_n2,), grad_rows, a_out, vec, lengths
    )
    dj0, diag0 = attention_backward(joined0, probs0, mixed0, gm0, head_size)
    dj1, diag1 = attention_backward(joined1, probs1, mixed1, sent, head_size)
    input_grad, vec_grads, table_grad = first_norm_back(
        core, (dj0, dj1), normed_back(dj1, a_pieces[1]), tokens, grad_res, vec, a_pieces[0], sums2, up_sums,
        (diag0, diag1), (line, line), number, True,
    )
    mixed = jnp.concatenate([mixed0, mixed1], 1)
    halves = [
        outer_products(
            core, [([(normed, None)], [(dj, j)]) for j in range(3)] + [([(mixed, None)], [branch])], offsets, model
        )[0][0].reshape(4, model, width)
        for dj, branch in ((dj0, (branch0, None)), (dj1, (sent, 1)))
    ]
    grads = jnp.stack(halves, 2).transpose(1, 0, 2, 3).reshape(model, 4 * model)
    grads = scattered(grads)
    grad_up = scattered(jnp.concatenate([ups[0], ups[2], ups[1], ups[3]], 1))
    grad_down = scattered(jnp.concatenate([downs[0], downs[2], downs[1], downs[3]], 0))
    by_owner = vec_grads[:VECTORS].reshape(VECTORS, model // local, local).transpose(1, 0, 2)
    own_units = vec_grads[VECTORS : VECTORS + 4].reshape(2, 2, model).transpose(1, 0, 2)
    both = jnp.concatenate(
        [by_owner.reshape(model // local, VECTORS * local), own_units.reshape(model // local, hidden * local // model)],
        1,
    )
    both = scattered(both)[0]
    table = jnp.concatenate([table_grad[16 * i : 16 * i + 16] for i in range(4)], 1)[:heads, :number]
    grad_table = lax.psum(table, AXES)
    small_grads = [both[i * local : (i + 1) * local] for i in range(VECTORS)]
    return (
        output,
        input_grad,
        small_grads[0],
        small_grads[1],
        grads[:, : 3 * model].astype(F32),
        small_grads[2],
        small_grads[3],
        grads[:, 3 * model :].astype(F32),
        small_grads[4],
        grad_table,
        small_grads[5],
        small_grads[6],
        grad_up.astype(F32),
        both[VECTORS * local :],
        grad_down.astype(F32),
        small_grads[7],
    )


def solution(mesh):
    both = P(AXES)
    row = P(AXES, None)
    in_specs = (
        row, both, P(AXES, None, None), both, both, row, both, both, row, both, P(), both, both, row, both, row,
        both, row,
    )
    out_specs = (row, row, both, both, row, both, both, row, both, P(), both, both, row, both, row, both)

    if tuple(mesh.shape[name] for name in AXES) == (2, 16):

        def body(*args):
            return on_device(GridLinks((2, 4, 2), args[0].shape[1]), *args)

    else:
        body = on_any_mesh

    return jax.shard_map(body, mesh=mesh, in_specs=in_specs, out_specs=out_specs, check_vma=False)
```

```python
import functools

import jax
import jax.numpy as jnp
from jax import lax
from jax.experimental import pallas as pl
from jax.experimental.pallas import tpu as pltpu
from jax.sharding import PartitionSpec as P

BF = jnp.bfloat16
F32 = jnp.float32
AXES = ("dp", "fsdp")
TILE = 128
CHUNK = 64
EPS = 1e-05
NN = (((1,), (0,)), ((), ()))
NT = (((1,), (1,)), ((), ()))
TN = (((0,), (0,)), ((), ()))
VMEM = pltpu.VMEM


def mm(left, right, dims=NN):
    return lax.dot_general(left, right, dims, preferred_element_type=F32)


def any_spec():
    return pl.BlockSpec(memory_space=pl.ANY)


def hbm_spec():
    return pl.BlockSpec(memory_space=pltpu.HBM)


def in_hbm(x):
    return pltpu.with_memory_space_constraint(x, pltpu.HBM)


def smem_spec():
    return pl.BlockSpec(memory_space=pltpu.SMEM)


def whole(shape):
    return pl.BlockSpec(shape, lambda *_: (0,) * len(shape))


def params(mebibytes):
    return pltpu.CompilerParams(
        dimension_semantics=("arbitrary",), vmem_limit_bytes=mebibytes * 1024 * 1024
    )


def cost(micros):
    return pl.CostEstimate(flops=int(micros * 1e9), bytes_accessed=1, transcendentals=0)


class Pieces:
    def __init__(self, buffers, offsets, rows):
        self.buffers = buffers
        self.offsets = offsets
        self.rows = rows

    @property
    def slots(self):
        return sum(b.shape[0] for b in self.buffers)


def lay_blocks(refs, offs_ref, rows, count, put):
    slot = 0
    for ref in refs:
        for k in range(ref.shape[0]):
            at = pl.multiple_of(offs_ref[slot], 16)
            for j in range(count):
                put(j, at, ref[k, j * rows : (j + 1) * rows, :])
            slot += 1


def row_norm(x):
    centre = x - jnp.mean(x, -1, keepdims=True)
    scale = lax.rsqrt(jnp.mean(centre * centre, -1, keepdims=True) + EPS)
    return centre * scale, scale


def bucket_line(line, number):
    rows = lax.broadcasted_iota(jnp.int32, (number, line.shape[1]), 0)
    return jnp.where(rows == line.astype(jnp.int32), 1.0, 0.0).astype(BF)


def bias_tiles(core, lines, table, cotangent, lengths, halves):
    span = lines[0].shape[1]
    heads, number = table.shape
    count = heads // 2
    tiles = span // TILE - 1
    n = len(lines)
    rows, model = cotangent.shape

    def kernel(core_ref, len_ref, table_ref, cot_ref, *refs):
        line_refs, (out_ref, gr_ref, curve_ref) = refs[:n], refs[n:]
        at = pl.program_id(0)

        @pl.when(at == 0)
        def _():
            for i in range(n):
                curve = mm(table_ref[...], bucket_line(line_refs[i][0:1, :], number))
                curve = jnp.where((core_ref[0] ^ halves[i]) == 0, curve[:count], curve[count:])
                for h in range(count):
                    curve_ref[i * count + h] = jnp.broadcast_to(curve[h : h + 1], (8, span))
            row = lax.broadcasted_iota(jnp.int32, (rows, 1), 0)
            gr_ref[...] = jnp.where(row < len_ref[0], cot_ref[...].astype(F32), 0.0).astype(BF)

        base = pltpu.roll(curve_ref[at], 0, 1, stride=1, stride_axis=0)
        for pair in range(TILE // 16):
            rolled = jnp.concatenate(
                [pltpu.roll(base, 16 * pair + 8 * i, 1) if pair + i else base for i in range(2)], 0
            ).astype(BF)
            for d in range(tiles):
                out_ref[0, 0, d, 16 * pair : 16 * pair + 16, :] = rolled[
                    :, TILE * (d + 1) : TILE * (d + 2)
                ]

    return pl.pallas_call(
        kernel,
        grid=(n * count,),
        in_specs=[
            smem_spec(),
            smem_spec(),
            whole((heads, number)),
            whole((rows, model)),
            *[whole((8, span))] * n,
        ],
        out_specs=[
            pl.BlockSpec((1, 1, tiles, TILE, TILE), lambda h: (h // count, h % count, 0, 0, 0)),
            whole((rows, model)),
        ],
        out_shape=[
            VMEM((n, count, tiles, TILE, TILE), BF),
            VMEM((rows, model), BF),
        ],
        scratch_shapes=[VMEM((n * count, 8, span), F32)],
        compiler_params=params(8),
        cost_estimate=cost(4),
        name="bias_tiles",
    )(core, lengths, table, cotangent, *lines)


def place_rows(block, offset, wide):
    padded = jnp.concatenate([block, jnp.zeros((block.shape[0], wide - TILE), block.dtype)], 1)
    return pltpu.roll(padded, offset, 1)


def assemble_attention(pieces, model):
    width = model // 2
    rows = pieces.rows
    n_buf = len(pieces.buffers)

    def kernel(offs_ref, *refs):
        bufs, (w_ref, o_ref, vec_ref) = refs[:n_buf], refs[n_buf:]

        def put(j, at, block):
            if j < 3:
                w_ref[j, pl.ds(at, rows), :] = block
            else:
                o_ref[pl.ds(at, rows), :] = block

        lay_blocks(bufs, offs_ref, rows, 4, put)
        total, slot = jnp.zeros((16, model), F32), 0
        for ref in bufs:
            for k in range(ref.shape[0]):
                total += place_rows(ref[k, 4 * rows : 4 * rows + 16, :TILE].astype(F32), offs_ref[slot], model)
                slot += 1
        vec_ref[...] = total

    return pl.pallas_call(
        kernel,
        grid=(1,),
        in_specs=[smem_spec(), *[whole(one.shape) for one in pieces.buffers]],
        out_specs=[whole((3, model, width)), whole((model, width)), whole((16, model))],
        out_shape=[
            VMEM((3, model, width), BF),
            VMEM((model, width), BF),
            VMEM((16, model), F32),
        ],
        compiler_params=params(6),
        cost_estimate=cost(2),
        name="assemble_attention",
    )(pieces.offsets, *pieces.buffers)


def attention_forward(item, half, core, tokens, vec, weights, tiles, line, head_size):
    rows, model = tokens.shape
    width = model // 2
    heads = width // head_size
    pairs = width // TILE
    per = TILE // head_size
    scale = head_size**-0.5

    def kernel(core_ref, line_ref, x_ref, vec_ref, tile_ref, w_ref, n1_ref, joined_ref, mixed_ref, p_ref, qs_ref, s_ref):
        pair = pl.program_id(0)

        @pl.when(pair == 0)
        def _():
            for r in range(0, rows, CHUNK):
                xhat, _ = row_norm(x_ref[r : r + CHUNK, :].astype(F32))
                n1_ref[r : r + CHUNK, :] = (xhat * vec_ref[0:1, :] + vec_ref[1:2, :]).astype(BF)
            cols = pl.ds(pl.multiple_of((core_ref[0] ^ half) * width, TILE), width)
            for j in range(3):
                joined = mm(n1_ref[...], w_ref[j])
                if j != 1:
                    joined = joined + vec_ref[2 + j // 2 : 3 + j // 2, cols]
                qs_ref[j] = joined.astype(BF)

        lanes = pl.ds(pl.multiple_of(pair * TILE, TILE), TILE)
        q, k, v = (qs_ref[j, :, lanes] for j in range(3))
        for j, one in enumerate((q, k, v)):
            joined_ref[j] = one
        lane = lax.broadcasted_iota(jnp.int32, (1, TILE), 1)
        column = lax.broadcasted_iota(jnp.int32, (1, rows), 1)
        dead = jnp.where(column < line_ref[1:2, :rows].astype(jnp.int32), 0.0, -1e30).astype(F32)
        scaled = q.astype(F32) * scale
        outs = []
        for e in range(per):
            mine = (lane >= e * head_size) & (lane < (e + 1) * head_size)
            qm = jnp.where(mine, scaled, 0.0).astype(BF)
            s_ref[e] = mm(qm, k, NT)
            for r in range(0, rows, CHUNK):
                block, sub = r // TILE, r % TILE
                rel = jnp.concatenate(
                    [
                        tile_ref[0, e, j - block + rows // TILE - 1, sub : sub + CHUNK, :]
                        for j in range(rows // TILE)
                    ],
                    1,
                ).astype(F32)
                s = s_ref[e, r : r + CHUNK, :] + (rel + dead)
                raised = jnp.exp(s - jnp.max(s, -1, keepdims=True))
                inv = 1.0 / jnp.sum(raised, -1, keepdims=True)
                p_ref[e, r : r + CHUNK, :] = (raised * inv).astype(BF)
            outs.append(jnp.where(mine, mm(p_ref[e], v), 0.0))
        mixed_ref[...] = functools.reduce(lambda a, b: a + b, outs).astype(BF)

    shapes = [
        VMEM((3, rows, width), BF),
        VMEM((rows, width), BF),
        VMEM((heads, rows, rows), BF),
    ]
    outs = [
        pl.BlockSpec((3, rows, TILE), lambda p: (0, 0, p)),
        pl.BlockSpec((rows, TILE), lambda p: (0, p)),
        pl.BlockSpec((per, rows, rows), lambda p: (p, 0, 0)),
    ]
    shapes.insert(0, VMEM((rows, model), BF))
    outs.insert(0, whole((rows, model)))
    return pl.pallas_call(
        kernel,
        grid=(pairs,),
        in_specs=[
            smem_spec(),
            whole((8, 2 * rows)),
            whole((rows, model)),
            whole((16, model)),
            pl.BlockSpec((1, per, tiles.shape[2], TILE, TILE), lambda p: (item, p, 0, 0, 0)),
            whole((3, model, width)),
        ],
        out_specs=outs,
        out_shape=shapes,
        scratch_shapes=[VMEM((3, rows, width), BF), VMEM((per, rows, rows), F32)],
        compiler_params=params(12),
        cost_estimate=cost(6),
        name="attention_forward",
    )(core, line, tokens, vec, tiles, weights)


def project_out(core, mixed, tokens, weights, vec):
    rows, model = tokens.shape
    width = model // 2

    def kernel(core_ref, m0_ref, m1_ref, x_ref, vec_ref, w0_ref, w1_ref, res_ref, n2_ref):
        for h, w_ref in enumerate((w0_ref, w1_ref)):
            cols = pl.ds(pl.multiple_of((core_ref[0] ^ h) * width, TILE), width)
            acc = 0.0
            for g, m_ref in enumerate((m0_ref, m1_ref)):
                feats = pl.ds(pl.multiple_of((core_ref[0] ^ g) * width, TILE), width)
                acc = acc + mm(m_ref[...], w_ref[feats, :])
            res_ref[:, cols] = x_ref[:, cols].astype(F32) + acc + vec_ref[4:5, cols]
        for r in range(0, rows, CHUNK):
            xhat, _ = row_norm(res_ref[r : r + CHUNK, :])
            n2_ref[r : r + CHUNK, :] = (xhat * vec_ref[5:6, :] + vec_ref[6:7, :]).astype(BF)

    return pl.pallas_call(
        kernel,
        grid=(1,),
        in_specs=[
            smem_spec(),
            whole((rows, width)),
            whole((rows, width)),
            whole((rows, model)),
            whole((16, model)),
            whole((model, width)),
            whole((model, width)),
        ],
        out_specs=[whole((rows, model)), whole((rows, model))],
        out_shape=[
            VMEM((rows, model), F32),
            VMEM((rows, model), BF),
        ],
        compiler_params=params(6),
        cost_estimate=cost(2.5),
        name="project_out",
    )(core, mixed[0], mixed[1], tokens, vec, *weights)


def gelu_parts(v):
    bell = jnp.exp(-0.5 * (v * v))
    t = 1.0 / (1.0 + 0.23164189 * jnp.abs(v))
    tail = t * (0.127414796 + t * (-0.142248368 + t * (0.710706871 + t * (-0.726576014 + t * 0.530702714))))
    tail = tail * bell
    return jnp.where(v < 0.0, tail, 1.0 - tail), bell * 0.3989422804014327


def feed_forward(row, core, sets, vec, pieces, offsets=None):
    rows, model = sets[0][0].shape
    hidden = model
    n = len(sets)
    n_buf = len(pieces.buffers)
    per = pieces.rows
    half = rows // 2
    width = model // 2

    def kernel(core_ref, offs_ref, out_offs_ref, vec_ref, *refs):
        ins, refs = refs[: len(flat)], refs[len(flat) :]
        bufs, refs = refs[:n_buf], refs[n_buf:]
        outs, refs = refs[: 4 * n], refs[4 * n :]
        col_ref, slot_refs, (up_ref, down_ref, w_ref) = refs[0], refs[1:-3], refs[-3:]

        def put(j, at, block):
            ref = up_ref if j < 2 else down_ref
            ref[pl.ds(at, per), (j % 2) * width : (j % 2 + 1) * width] = block

        lay_blocks(bufs, offs_ref, per, 4, put)
        up_bias = vec_ref[pl.ds(row(core_ref[0]), 1), :]
        sums = jnp.zeros((1, hidden), F32)
        for i in range(n):
            n_ref, gr_ref, res_ref, gin_ref = (None if at is None else ins[at] for at in where[i])
            out_ref, gn_ref, act_ref, gp_ref = outs[4 * i : 4 * i + 4]
            for r in range(0, rows, half):
                block = slice(r, r + half)
                pre = mm(n_ref[block, :], up_ref[...]) + up_bias
                gact = mm(gr_ref[block, :], down_ref[...], NT)
                cdf, density = gelu_parts(pre)
                act = (pre * cdf).astype(BF)
                gp = gact * (cdf + pre * density)
                low = gp.astype(BF)
                act_ref[block, :] = act
                gp_ref[block, :] = low
                sums += jnp.sum(low.astype(F32), 0, keepdims=True)
                out = mm(act, down_ref[...])
                if res_ref is not None:
                    out = out + res_ref[block, :]
                    if gin_ref is None:
                        out = out + vec_ref[7:8, :]
                out_ref[block, :] = out
                gn = mm(low, up_ref[...], NT)
                gn_ref[block, :] = gn if gin_ref is None else gn + gin_ref[block, :]
        col_ref[...] = sums
        if offsets is None:
            return
        for m in range(4):
            cols = slice((m % 2) * width, (m % 2 + 1) * width)
            total = 0.0
            for i in range(n):
                n_ref, gr_ref = (ins[at] for at in where[i][:2])
                act_ref, gp_ref = outs[4 * i + 2 : 4 * i + 4]
                left, right = (n_ref, gp_ref) if m < 2 else (act_ref, gr_ref)
                total = total + mm(left[...], right[:, cols], TN)
            w_ref[...] = total.astype(BF)
            to_slots(w_ref, out_offs_ref, slot_refs, m, per)

    flat, where = [], []
    for one in sets:
        places = []
        for array in one:
            places.append(None if array is None else len(flat))
            if array is not None:
                flat.append(array)
        where.append(places)
    shapes = [
        VMEM((rows, model), F32),
        VMEM((rows, model), F32),
        VMEM((rows, hidden), BF),
        VMEM((rows, hidden), BF),
    ] * n + [VMEM((1, hidden), F32)]
    if offsets is not None:
        shapes += [VMEM((offsets.shape[0] // 2, 4 * per, width), BF)] * 2
    out = pl.pallas_call(
        kernel,
        grid=(1,),
        in_specs=[
            *[smem_spec()] * 3,
            whole((16, model)),
            *[whole((rows, model))] * len(flat),
            *[whole(one.shape) for one in pieces.buffers],
        ],
        out_specs=[whole(one.shape) for one in shapes],
        out_shape=shapes,
        scratch_shapes=[
            VMEM((model, hidden), BF),
            VMEM((hidden, model), BF),
            VMEM((model, width), BF),
        ],
        compiler_params=params(14),
        cost_estimate=cost(13),
        name="feed_forward",
    )(core, pieces.offsets, pieces.offsets if offsets is None else offsets, vec, *flat, *pieces.buffers)
    return [out[4 * i : 4 * i + 4] for i in range(n)], out[4 * n], out[4 * n + 1 :]


def to_slots(w_ref, offs_ref, outs, matrix, rows):
    slot = 0
    for out in outs:
        for k in range(out.shape[0]):
            at = pl.multiple_of(offs_ref[slot], 16)
            out[k, matrix * rows : (matrix + 1) * rows, :] = w_ref[pl.ds(at, rows), :]
            slot += 1


class Products:
    def __init__(self, core, pairs, offsets, rows, counts):
        self.core, self.offsets, self.rows = core, offsets, rows
        self.tall = pairs[0][0][0][0].shape[-1]
        self.wide = self.tall // 2
        self.flat = []
        self.where = [([self._place(*one) for one in lefts], [self._place(*one) for one in rights]) for lefts, rights in pairs]
        self.shapes = [VMEM((count, len(pairs) * rows, self.wide), BF) for count in counts]
        self.scratch = VMEM((self.tall, self.wide), BF)

    def _place(self, one, part):
        if isinstance(one, tuple):
            return [self._place(each, part) for each in one]
        if one is None:
            return None, part
        match = [i for i, known in enumerate(self.flat) if known is one]
        if not match:
            self.flat.append(one)
            match = [len(self.flat) - 1]
        return match[0], part

    def run(self, core_ref, offs_ref, ins, outs, w_ref, own_ref=None):
        def pick(at, part):
            ref = own_ref if at is None else ins[at]
            if part is None:
                return ref[...]
            if len(ref.shape) == 3:
                return ref[part]
            return ref[:, part * self.wide : (part + 1) * self.wide]

        for m, (lefts, rights) in enumerate(self.where):
            if isinstance(lefts[0], list):
                for h in range(2):
                    total = sum(mm(pick(*left[h]), pick(*right), TN) for left, right in zip(lefts, rights))
                    at = pl.multiple_of((core_ref[0] ^ h) * self.wide, 16)
                    w_ref[pl.ds(at, self.wide), :] = total.astype(BF)
            else:
                total = sum(mm(pick(*left), pick(*right), TN) for left, right in zip(lefts, rights))
                w_ref[...] = total.astype(BF)
            to_slots(w_ref, offs_ref, outs, m, self.rows)


def outer_products(core, pairs, offsets, rows):
    work = Products(core, pairs, offsets, rows, offsets.shape)
    n = len(work.flat)

    def kernel(core_ref, offs_ref, *rest):
        work.run(core_ref, offs_ref, rest[:n], rest[n:-1], rest[-1])

    return pl.pallas_call(
        kernel,
        grid=(1,),
        in_specs=[smem_spec(), smem_spec(), *[whole(one.shape) for one in work.flat]],
        out_specs=[whole(one.shape) for one in work.shapes],
        out_shape=work.shapes,
        scratch_shapes=[work.scratch],
        compiler_params=params(14),
        cost_estimate=cost(5),
        name="outer_products",
    )(core, offsets, *work.flat)


def norm_back(x, up, gain):
    xhat, scale = row_norm(x)
    e = up * gain
    grad = scale * (e - jnp.mean(e, -1, keepdims=True) - xhat * jnp.mean(e * xhat, -1, keepdims=True))
    return grad, up * xhat


def second_norm_back(core, residual, results, grads_normed, grad_rows, weights, vec, lengths):
    rows, model = residual.shape
    width = model // 2
    n, m = len(results), len(grads_normed)

    def kernel(core_ref, len_ref, res_ref, gr_ref, vec_ref, w0_ref, w1_ref, *refs):
        out_refs, gn_refs = refs[:n], refs[n : n + m]
        out_ref, gres_ref, gm_ref, br_ref, sent_ref, sums_ref, gb_ref = refs[n + m :]
        totals = [jnp.zeros((1, model), F32) for _ in range(4)]
        for r in range(0, rows, CHUNK):
            block = slice(r, r + CHUNK)
            row = lax.broadcasted_iota(jnp.int32, (CHUNK, 1), 0) + r
            result = functools.reduce(lambda a, b: a + b, [ref[block, :] for ref in out_refs])
            out_ref[block, :] = jnp.where(row < len_ref[0], result, 0.0).astype(BF)
            up = functools.reduce(lambda a, b: a + b, [ref[block, :] for ref in gn_refs])
            grad, gain_terms = norm_back(res_ref[block, :], up, vec_ref[5:6, :])
            gr = gr_ref[block, :].astype(F32)
            grad = gr + grad
            low = grad.astype(BF)
            gres_ref[block, :] = grad
            gb_ref[block, :] = low
            for i, terms in enumerate((gain_terms, up, low.astype(F32), gr)):
                totals[i] += jnp.sum(terms, 0, keepdims=True)
        sums_ref[...] = jnp.concatenate(totals + [jnp.zeros((4, model), F32)], 0)
        parts = [pl.ds(pl.multiple_of((core_ref[0] ^ h) * width, TILE), width) for h in range(2)]
        for h in range(2):
            acc = 0.0
            for g, w_ref in enumerate((w0_ref, w1_ref)):
                acc = acc + mm(gb_ref[:, parts[g]], w_ref[parts[h], :], NT)
            if h == 0:
                gm_ref[...] = acc.astype(BF)
                br_ref[...] = gb_ref[:, parts[0]]
            else:
                sent_ref[:, :width] = acc.astype(BF)
                sent_ref[:, width:] = gb_ref[:, parts[1]]

    return pl.pallas_call(
        kernel,
        grid=(1,),
        in_specs=[
            *[smem_spec()] * 2,
            *[whole((rows, model))] * 2,
            whole((16, model)),
            whole((model, width)),
            whole((model, width)),
            *[whole((rows, model))] * (n + m),
        ],
        out_specs=[
            *[whole((rows, model))] * 2,
            *[whole((rows, width))] * 2,
            whole((rows, model)),
            whole((8, model)),
        ],
        out_shape=[
            jax.ShapeDtypeStruct((rows, model), BF),
            jax.ShapeDtypeStruct((rows, model), F32),
            jax.ShapeDtypeStruct((rows, width), BF),
            jax.ShapeDtypeStruct((rows, width), BF),
            jax.ShapeDtypeStruct((rows, model), BF),
            jax.ShapeDtypeStruct((8, model), F32),
        ],
        scratch_shapes=[VMEM((rows, model), BF)],
        compiler_params=params(10),
        cost_estimate=cost(4),
        name="second_norm_back",
    )(core, lengths, residual, grad_rows, vec, *weights, *results, *grads_normed)


def attention_backward(joined, probs, mixed, grad_mixed, head_size, products=None, weights=None):
    _, rows, width = joined.shape
    heads = width // head_size
    pairs = width // TILE
    per = TILE // head_size
    tiles = 2 * (rows // TILE) - 1
    span = 2 * rows
    scale = head_size**-0.5
    flat = [] if products is None else products.flat
    n_in = 4 + len(flat) + (2 if products else 0) + (1 if weights is not None else 0)

    def kernel(*refs):
        ins, refs = refs[:n_in], refs[n_in:]
        joined_ref, p_ref, mixed_ref, gm_ref = ins[:4]
        out_ref, diag_ref, refs = refs[0], refs[1], refs[2:]
        gp_ref, ds_ref, acc_ref = refs[-3:]
        lane = lax.broadcasted_iota(jnp.int32, (1, TILE), 1)
        for pair in range(pairs):
            lanes = slice(pair * TILE, (pair + 1) * TILE)
            q, k, v = (joined_ref[j, :, lanes] for j in range(3))
            gm = gm_ref[:, lanes]
            dots = gm.astype(F32) * mixed_ref[:, lanes].astype(F32)
            q_t, gm_t = q.T, gm.T
            dq, dk, dv = [], [], []
            for e in range(per):
                head = pair * per + e
                mine = (lane >= e * head_size) & (lane < (e + 1) * head_size)
                feats = slice(e * head_size, (e + 1) * head_size)
                delta = jnp.sum(jnp.where(mine, dots, 0.0), -1, keepdims=True)
                gp_ref[e] = mm(jnp.where(mine, gm, jnp.zeros_like(gm)), v, NT)
                acc_ref[...] = jnp.zeros_like(acc_ref)
                for r in range(0, rows, CHUNK):
                    block, sub = r // TILE, r % TILE
                    ds = p_ref[head, r : r + CHUNK, :].astype(F32) * (
                        gp_ref[e, r : r + CHUNK, :] - delta[r : r + CHUNK, :]
                    )
                    ds_ref[e, r : r + CHUNK, :] = ds.astype(BF)
                    for j in range(rows // TILE):
                        acc_ref[j - block + rows // TILE - 1, sub : sub + CHUNK, :] += ds[
                            :, j * TILE : (j + 1) * TILE
                        ]
                dq.append(jnp.where(mine, mm(ds_ref[e], k), 0.0))
                dk.append(mm(q_t[feats, :], ds_ref[e]))
                dv.append(mm(gm_t[feats, :], p_ref[head]))
                total = jnp.zeros((8, span), F32)
                for g in range(TILE // 8):
                    strip = jnp.concatenate(
                        [jnp.zeros((8, TILE), F32)]
                        + [acc_ref[d, 8 * g : 8 * g + 8, :] for d in range(tiles)],
                        1,
                    )
                    total += pltpu.roll(strip, (span - 8 * g) % span, 1) if g else strip
                line = total[0:1]
                for i in range(1, 8):
                    line = line + pltpu.roll(total[i : i + 1], span - i, 1)
                diag_ref[head] = line
            out_ref[0, :, lanes] = (functools.reduce(lambda a, b: a + b, dq) * scale).astype(BF)
            out_ref[1, :, lanes] = (jnp.concatenate(dk, 0) * scale).T.astype(BF)
            out_ref[2, :, lanes] = jnp.concatenate(dv, 0).T.astype(BF)
        if weights is not None:
            refs[0][...] = sum(mm(out_ref[j], ins[-1][j], NT) for j in range(3)).astype(BF)
        if products is not None:
            slot_refs = refs[1:-4] if weights is not None else refs[:-4]
            products.run(ins[4], ins[5], ins[6 : 6 + len(flat)], slot_refs, refs[-4], out_ref)

    ins = [joined, probs, mixed, grad_mixed]
    specs = [whole(one.shape) for one in ins]
    shapes = [VMEM((3, rows, width), BF), VMEM((heads, 1, span), F32)]
    scratch = [VMEM((per, rows, rows), F32), VMEM((per, rows, rows), BF), VMEM((tiles, TILE, TILE), F32)]
    if products is not None:
        ins += [products.core, products.offsets, *flat]
        specs += [smem_spec(), smem_spec(), *[whole(one.shape) for one in flat]]
    if weights is not None:
        ins.append(weights)
        specs.append(whole(weights.shape))
        shapes.append(VMEM((rows, weights.shape[1]), BF))
    if products is not None:
        shapes += products.shapes
        scratch.insert(0, products.scratch)
    return pl.pallas_call(
        kernel,
        grid=(1,),
        in_specs=specs,
        out_specs=[whole(one.shape) for one in shapes],
        out_shape=shapes,
        scratch_shapes=scratch,
        compiler_params=params(16),
        cost_estimate=cost(4.5),
        name="attention_backward",
    )(*ins)


def normed_back(grads, weights):
    _, rows, width = grads.shape
    model = weights.shape[1]

    def kernel(d_ref, w_ref, out_ref):
        out_ref[...] = sum(mm(d_ref[j], w_ref[j], NT) for j in range(3))

    return pl.pallas_call(
        kernel,
        grid=(1,),
        in_specs=[whole(grads.shape), whole(weights.shape)],
        out_specs=whole((rows, model)),
        out_shape=VMEM((rows, model), F32),
        compiler_params=params(8),
        cost_estimate=cost(1.5),
        name="normed_back",
    )(grads, weights)


def first_norm_back(
    core, grads, part, tokens, grad_residual, vec, weights, sums_second, sums_up, diags, lines, number, apart, offsets=None
):
    rows, model = tokens.shape
    width = model // 2
    count = diags[0].shape[0]
    span = lines[0].shape[1]
    n_up = len(sums_up[0])

    def kernel(core_ref, d0_ref, d1_ref, part_ref, x_ref, gres_ref, vec_ref, w_ref, s2_ref, t0_ref, t1_ref, l0_ref, l1_ref,
               *rest):
        up_refs = rest[: 2 * n_up]
        offs_ref, gx_ref, sums_ref, table_ref, acc_ref = rest[2 * n_up :]
        straight = core_ref[0] == 0

        def ordered(a, b):
            return [jnp.where(straight, a, b), jnp.where(straight, b, a)]

        tables = []
        for t_ref, l_ref in ((t0_ref, l0_ref), (t1_ref, l1_ref)):
            chosen = bucket_line(l_ref[0:1, :], number)
            sums = t_ref[:, 0, :]
            high = sums.astype(BF)
            rest = (sums - high.astype(F32)).astype(BF)
            both = mm(jnp.concatenate([high.astype(F32), rest.astype(F32)], 0).astype(BF), chosen, NT)
            table = both[:count] + both[count:]
            tables.append(table)
        blank = jnp.zeros((count, number), F32)
        tables = tables if apart else ordered(tables[0] + tables[1], blank)
        table = jnp.concatenate([*tables, jnp.zeros((16 - 2 * count, number), F32)], 0)
        table = jnp.concatenate([table, jnp.zeros((16, 4 * TILE - number), F32)], 1)
        table = jnp.concatenate([table[:, i * TILE : (i + 1) * TILE] for i in range(4)], 0)
        columns = []
        for j in (0, 2):
            a, b = (jnp.sum(d_ref[j].astype(F32), 0, keepdims=True) for d_ref in (d0_ref, d1_ref))
            columns.append(jnp.concatenate([a, b] if apart else ordered(a + b, jnp.zeros_like(a)), 1))
        ups = []
        for f in range(2):
            here = [ref[...] for ref in up_refs[f * n_up : (f + 1) * n_up]]
            ups += here if apart else ordered(here[0], jnp.zeros_like(here[0]))
        acc_ref[...] = part_ref[...].astype(F32) + sum(mm(d0_ref[j], w_ref[j], NT) for j in range(3))
        totals = [jnp.zeros((1, model), F32) for _ in range(2)]
        for r in range(0, rows, CHUNK):
            block = slice(r, r + CHUNK)
            up = acc_ref[block, :]
            grad, gain_terms = norm_back(x_ref[block, :].astype(F32), up, vec_ref[0:1, :])
            gx_ref[block, :] = gres_ref[block, :] + grad
            totals[0] += jnp.sum(gain_terms, 0, keepdims=True)
            totals[1] += jnp.sum(up, 0, keepdims=True)
        sums = jnp.concatenate(
            totals
            + columns
            + [s2_ref[2:3, :], s2_ref[0:1, :], s2_ref[1:2, :], s2_ref[3:4, :]]
            + ups
            + [jnp.zeros((4, model), F32)],
            0,
        )
        if offsets is None:
            sums_ref[...] = sums
            table_ref[...] = table
            return
        for i, ref in enumerate((sums_ref, table_ref)):
            for s in range(half):
                moved = pltpu.roll(sums, lax.rem(model - offs_ref[i * half + s], model), 1)
                ref[16 * s : 16 * s + 16, :] = moved[:, :TILE].astype(BF)
            ref[16 * half :, :] = table.astype(BF)

    half = 0 if offsets is None else offsets.shape[0] // 2
    late = [VMEM((16 * half + 64, TILE), BF)] * 2
    plain = [jax.ShapeDtypeStruct((16, model), F32), jax.ShapeDtypeStruct((64, TILE), F32)]
    shapes = [jax.ShapeDtypeStruct((rows, model), F32), *(plain if offsets is None else late)]
    return pl.pallas_call(
        kernel,
        grid=(1,),
        in_specs=[
            smem_spec(),
            whole((3, rows, width)),
            whole((3, rows, width)),
            whole((rows, model)),
            whole((rows, model)),
            whole((rows, model)),
            whole((16, model)),
            whole((3, model, width)),
            whole((8, model)),
            whole((count, 1, span)),
            whole((count, 1, span)),
            whole((8, span)),
            whole((8, span)),
            *[whole((1, model))] * (2 * n_up),
            smem_spec(),
        ],
        out_specs=[whole(one.shape) for one in shapes],
        out_shape=shapes,
        scratch_shapes=[VMEM((rows, model), F32)],
        compiler_params=params(14),
        cost_estimate=cost(5),
        name="first_norm_back",
    )(
        core, *grads, part, tokens, grad_residual, vec, weights, sums_second, *diags, *lines, *sums_up[0], *sums_up[1],
        core if offsets is None else offsets,
    )


def pack_blocks(core, lengths, buckets, qkv, out, up):
    local, model = out.shape
    width = model // 2
    unit = local * 2
    chips = up.shape[1] // (4 * unit)
    rows = buckets.shape[1]

    def kernel(core_ref, len_ref, buckets_hbm, qkv_hbm, out_hbm, up_hbm, a0_ref, a1_ref, u0_ref, u1_ref, line_ref,
               first_ref, last_ref, qkv_ref, out_ref, up_ref, sems):
        copies = [
            pltpu.make_async_copy(source, target, sems.at[i])
            for i, (source, target) in enumerate(
                (
                    (qkv_hbm, qkv_ref),
                    (out_hbm, out_ref),
                    (up_hbm, up_ref),
                    (buckets_hbm.at[pl.ds(0, 1), pl.ds(0, 8)], first_ref),
                    (buckets_hbm.at[pl.ds(0, 1), pl.ds(rows - 8, 8)], last_ref),
                )
            )
        ]
        for c in copies:
            c.start()
        for c in copies:
            c.wait()
        core_at = core_ref[0]
        for h, a_ref in enumerate((a0_ref, a1_ref)):
            at = (core_at ^ h) * width
            for j in range(3):
                a_ref[j] = qkv_ref[:, pl.ds(pl.multiple_of(j * model + at, TILE), width)]
            a_ref[3] = out_ref[:, pl.ds(pl.multiple_of(at, TILE), width)]
        first = core_at == 0
        ahead = pltpu.roll(last_ref[0, 7:8, :].astype(F32), 1, 1)
        line = jnp.concatenate([ahead, first_ref[0, 0:1, :].astype(F32)], 1)
        live = jnp.zeros_like(line) + len_ref[0].astype(F32)
        line_ref[...] = jnp.concatenate([line, live, jnp.zeros((6, 2 * rows), F32)], 0)
        for f in range(2):
            by_core = []
            for c in range(2):
                by_core.append(
                    jnp.concatenate(
                        [
                            up_ref[:, ((2 * chip + c) * 2 + f) * unit : ((2 * chip + c) * 2 + f + 1) * unit]
                            for chip in range(chips)
                        ],
                        1,
                    ).astype(F32)
                )
            u0_ref[f] = jnp.where(first, by_core[0], by_core[1]).astype(BF)
            u1_ref[f] = jnp.where(first, by_core[1], by_core[0]).astype(BF)

    shapes = [
        *[VMEM((4, local, width), BF)] * 2,
        *[VMEM((2, local, model), BF)] * 2,
        VMEM((8, 2 * rows), F32),
    ]
    return pl.pallas_call(
        kernel,
        grid=(1,),
        in_specs=[
            smem_spec(),
            smem_spec(),
            *[hbm_spec()] * 4,
        ],
        out_specs=[whole(one.shape) for one in shapes],
        out_shape=shapes,
        scratch_shapes=[
            VMEM((1, 8, rows), jnp.int32),
            VMEM((1, 8, rows), jnp.int32),
            VMEM(qkv.shape, BF),
            VMEM(out.shape, BF),
            VMEM(up.shape, BF),
            pltpu.SemaphoreType.DMA((5,)),
        ],
        compiler_params=params(6),
        cost_estimate=cost(1.5),
        name="pack_blocks",
    )(core, lengths, in_hbm(buckets), in_hbm(qkv), in_hbm(out), in_hbm(up))


def pack_vectors(core, vectors):
    _, local = vectors.shape

    def kernel(core_ref, vec_ref, small_ref):
        first = core_ref[0] == 0
        values = jnp.concatenate(
            [vec_ref[...].astype(F32), jnp.zeros((VECTORS + 4, TILE - local), F32)], 1
        )
        moved = pltpu.roll(values, local, 1)
        lines = [jnp.where(first, values[:VECTORS], moved[:VECTORS])]
        for f in range(2):
            at = VECTORS + 2 * f
            both = values[at : at + 1] + moved[at + 1 : at + 2]
            blank = jnp.zeros_like(both)
            lines += [jnp.where(first, both, blank), jnp.where(first, blank, both)]
        small_ref[...] = jnp.concatenate(lines + [jnp.zeros((4, TILE), F32)], 0).astype(BF)

    return pl.pallas_call(
        kernel,
        grid=(1,),
        in_specs=[smem_spec(), whole(vectors.shape)],
        out_specs=whole((16, TILE)),
        out_shape=VMEM((16, TILE), BF),
        compiler_params=params(4),
        cost_estimate=cost(1),
        name="pack_vectors",
    )(core, vectors)


def ordered_rows(core_at, mine, theirs):
    first = core_at == 0
    a, b = mine.astype(F32), theirs.astype(F32)
    return jnp.concatenate([jnp.where(first, a, b), jnp.where(first, b, a)], 0)


def merge_attention(core, mine, theirs, small, small_theirs):
    count, local, width = mine.shape

    def kernel(core_ref, a_ref, b_ref, s_ref, t_ref, out_ref):
        for j in range(count):
            out_ref[2 * local * j : 2 * local * (j + 1), :] = ordered_rows(core_ref[0], a_ref[j], b_ref[j]).astype(BF)
        vec = s_ref[...].astype(F32) + t_ref[...].astype(F32)
        out_ref[2 * local * count :, :] = jnp.concatenate([vec, jnp.zeros((16, width - TILE), F32)], 1).astype(BF)

    return pl.pallas_call(
        kernel,
        grid=(1,),
        in_specs=[smem_spec(), *[whole(mine.shape)] * 2, *[whole(small.shape)] * 2],
        out_specs=whole((2 * local * count + 16, width)),
        out_shape=VMEM((2 * local * count + 16, width), BF),
        compiler_params=params(4),
        cost_estimate=cost(1),
        name="merge_attention",
    )(core, mine, theirs, small, small_theirs)


def merge_feed_forward(core, mine, theirs, down):
    _, local, model = mine.shape
    unit = 2 * local
    width = model // 2

    def kernel(core_ref, a_ref, b_ref, d_ref, *outs):
        for f in range(2):
            up = ordered_rows(core_ref[0], a_ref[f], b_ref[f]).astype(BF)
            low = d_ref[f * unit : (f + 1) * unit, :]
            for j, block in enumerate((up[:, :width], up[:, width:], low[:, :width], low[:, width:])):
                outs[f][j * unit : (j + 1) * unit, :] = block

    shape = VMEM((4 * unit, width), BF)
    return pl.pallas_call(
        kernel,
        grid=(1,),
        in_specs=[smem_spec(), *[whole(mine.shape)] * 2, whole(down.shape)],
        out_specs=[whole(shape.shape)] * 2,
        out_shape=[shape] * 2,
        compiler_params=params(4),
        cost_estimate=cost(1),
        name="merge_feed_forward",
    )(core, mine, theirs, down)


def pair_sum(refs):
    parts = [ref[...].astype(F32) for ref in refs]
    while len(parts) > 1:
        half = len(parts) // 2
        parts = [parts[i] + parts[i + half] for i in range(half)]
    return parts[0]


def rows_of(total, first, core_at, local, mine):
    a, b = total[first : first + local], total[first + local : first + 2 * local]
    return jnp.where((core_at == 0) == mine, a, b)


def total_attention(core, parts, local):
    tall, width = parts[0].shape
    tail = tall - 8 * local

    def kernel(core_ref, *refs):
        ins, (mine_ref, sent_ref, tail_ref) = refs[: len(parts)], refs[len(parts) :]
        total = pair_sum(ins)
        for j in range(4):
            mine_ref[j] = rows_of(total, 2 * local * j, core_ref[0], local, True)
            sent_ref[j] = rows_of(total, 2 * local * j, core_ref[0], local, False).astype(BF)
        tail_ref[...] = total[8 * local :].astype(BF)

    shapes = [
        jax.ShapeDtypeStruct((4, local, width), F32),
        jax.ShapeDtypeStruct((4, local, width), BF),
        jax.ShapeDtypeStruct((tail, width), BF),
    ]
    return pl.pallas_call(
        kernel,
        grid=(1,),
        in_specs=[smem_spec(), *[whole(one.shape) for one in parts]],
        out_specs=[whole(one.shape) for one in shapes],
        out_shape=shapes,
        compiler_params=params(6),
        cost_estimate=cost(1),
        name="total_attention",
    )(core, *parts)


def finish_attention(core, mine, theirs, tail, tail_theirs, heads, number):
    _, local, width = mine.shape
    model = 2 * width

    def kernel(core_ref, a_ref, b_ref, s_ref, t_ref, qkv_ref, out_ref, table_ref, *small_refs):
        at = core_ref[0]
        for h, ref in enumerate((a_ref, b_ref)):
            for j in range(3):
                cols = pl.ds(pl.multiple_of(j * model + (at ^ h) * width, TILE), width)
                qkv_ref[:, cols] = ref[j].astype(F32)
            out_ref[:, pl.ds(pl.multiple_of((at ^ h) * width, TILE), width)] = ref[3].astype(F32)
        total = s_ref[...].astype(F32) + t_ref[...].astype(F32)
        small = total[:16, :TILE]
        small = jnp.where(at == 0, small, jnp.concatenate([pltpu.roll(small[:8], TILE - local, 1), small[8:]], 0))
        for i in range(VECTORS):
            small_refs[i][...] = small[i : i + 1, :local]
        ups = [jnp.where(at == 0, small[8 + 2 * f : 9 + 2 * f], small[9 + 2 * f : 10 + 2 * f]) for f in range(2)]
        lane = lax.broadcasted_iota(jnp.int32, (1, TILE), 1)
        both = jnp.where(lane < 2 * local, ups[0], pltpu.roll(ups[1], 2 * local, 1))
        small_refs[VECTORS][...] = both[:, : 4 * local]
        table_ref[...] = jnp.concatenate([total[:16, TILE:], total[16:, : 2 * TILE]], 1)[:heads, :number]

    shapes = [
        jax.ShapeDtypeStruct((local, 3 * model), F32),
        jax.ShapeDtypeStruct((local, model), F32),
        jax.ShapeDtypeStruct((heads, number), F32),
        *[jax.ShapeDtypeStruct((1, local), F32)] * VECTORS,
        jax.ShapeDtypeStruct((1, 4 * local), F32),
    ]
    return pl.pallas_call(
        kernel,
        grid=(1,),
        in_specs=[smem_spec(), *[whole(one.shape) for one in (mine, theirs, tail, tail_theirs)]],
        out_specs=[whole(one.shape) for one in shapes],
        out_shape=shapes,
        compiler_params=params(6),
        cost_estimate=cost(1),
        name="finish_attention",
    )(core, mine, theirs, tail, tail_theirs)


def total_feed_forward(core, parts, local):
    _, width = parts[0].shape
    model = 2 * width
    unit = 2 * local

    def kernel(core_ref, *refs):
        ins, (mine_ref, sent_ref, down_ref) = refs[: len(parts)], refs[len(parts) :]
        total = pair_sum(ins)
        for h in range(2):
            cols = slice(h * width, (h + 1) * width)
            mine_ref[:, cols] = rows_of(total, h * unit, core_ref[0], local, True)
            sent_ref[:, cols] = rows_of(total, h * unit, core_ref[0], local, False).astype(BF)
            down_ref[:, cols] = total[(2 + h) * unit : (3 + h) * unit]

    shapes = [
        jax.ShapeDtypeStruct((local, model), F32),
        jax.ShapeDtypeStruct((local, model), BF),
        jax.ShapeDtypeStruct((unit, model), F32),
    ]
    return pl.pallas_call(
        kernel,
        grid=(1,),
        in_specs=[smem_spec(), *[whole(one.shape) for one in parts]],
        out_specs=[whole(one.shape) for one in shapes],
        out_shape=shapes,
        compiler_params=params(6),
        cost_estimate=cost(1),
        name="total_feed_forward",
    )(core, *parts)


def finish_feed_forward(core, mine, theirs, downs):
    local, model = mine[0].shape
    unit = 2 * local
    chips = model // unit

    def kernel(core_ref, m0, m1, t0, t1, d0, d1, up_ref, down_ref):
        first = core_ref[0] == 0
        by = []
        for a, b in ((m0, t0), (m1, t1)):
            a, b = a[...], b[...].astype(F32)
            by.append((jnp.where(first, a, b), jnp.where(first, b, a)))
        up_ref[...] = jnp.concatenate(
            [
                by[f][c][:, chip * unit : (chip + 1) * unit]
                for chip in range(chips)
                for c in range(2)
                for f in range(2)
            ],
            1,
        )
        down_ref[:unit, :] = d0[...]
        down_ref[unit:, :] = d1[...]

    shapes = [jax.ShapeDtypeStruct((local, 4 * model), F32), jax.ShapeDtypeStruct((2 * unit, model), F32)]
    ins = (*mine, *theirs, *downs)
    return pl.pallas_call(
        kernel,
        grid=(1,),
        in_specs=[smem_spec(), *[whole(one.shape) for one in ins]],
        out_specs=[whole(one.shape) for one in shapes],
        out_shape=shapes,
        compiler_params=params(6),
        cost_estimate=cost(1),
        name="finish_feed_forward",
    )(core, *ins)


VECTORS = 8


class Order:
    def __init__(self, token):
        self.token = token

    def go(self, *values):
        out, _ = lax.optimization_barrier((values, self.token))
        return out if len(out) > 1 else out[0]

    def mark(self, *values):
        out, self.token = lax.optimization_barrier((values, self.token))
        return out if len(out) > 1 else out[0]


class GridLinks:
    pair = True

    def __init__(self, sizes, model):
        self.ny, self.nz, self.nx = sizes
        self.chips = self.ny * self.nz * self.nx
        self.rows = model // self.chips
        dp, inner = lax.axis_index("dp"), lax.axis_index("fsdp")
        self.core = inner % 2
        chip = inner // 2
        self.place = (dp, chip // self.nx, chip % self.nx)
        self.gather_offsets = self._offsets(self.core, -1, (range(self.nz),))
        self.early_offsets = self._offsets(self.core, -1, ((0, 1, 3, 2),))
        self.scatter_offsets = self._offsets(self.core, 1, (range(self.nz),))
        self.last_offsets = self._offsets(self.core, 1, (range(1, self.nz), (0,)))
        self.last_counts = (self.nz - 1,) * 4 + (2, 2)

    def _offsets(self, core, sign, parts):
        y, z, x = self.place
        out = []
        for part in parts:
            for r1 in range(2):
                for r2 in range(2):
                    for k in part:
                        fy = jnp.where(core == 0, r1, r2)
                        fx = jnp.where(core == 0, r2, r1)
                        zz = (z + sign * k + self.nz) % self.nz
                        out.append(((y ^ fy) * self.nz + zz) * self.nx + (x ^ fx))
        return (jnp.stack(out) * self.rows).astype(jnp.int32)

    def _send(self, value, move):
        pairs = []
        for y in range(self.ny):
            for z in range(self.nz):
                for x in range(self.nx):
                    for c in range(2):
                        source = ((y * self.nz + z) * self.nx + x) * 2 + c
                        ty, tz, tx, tc = move(y, z, x, c)
                        pairs.append((source, ((ty * self.nz + tz) * self.nx + tx) * 2 + tc))
        return lax.ppermute(value, AXES, pairs)

    def swap(self, value):
        return self._send(value, lambda y, z, x, c: (y, z, x, 1 - c))

    def along_z(self, value, k):
        return self._send(value, lambda y, z, x, c: (y, (z + k) % self.nz, x, c))

    def x_first(self, value):
        return self._send(value, lambda y, z, x, c: (y, z, 1 - x, c) if c == 0 else (1 - y, z, x, c))

    def y_first(self, value):
        return self._send(value, lambda y, z, x, c: (y, z, 1 - x, c) if c == 1 else (1 - y, z, x, c))

    def spread(self, near):
        second = self.x_first(near)
        third = self.y_first(near)
        return [near, second, third, self.y_first(second)]

    def scatter_z(self, sums):
        return [sums[0]] + [self.along_z(sums[k], k) for k in range(1, self.nz)]


def small_kernel(kernel, name, shapes, *ins):
    return pl.pallas_call(
        kernel,
        grid=(1,),
        in_specs=[whole(one.shape) for one in ins],
        out_specs=[whole(shape) for shape in shapes],
        out_shape=[VMEM(shape, BF) for shape in shapes],
        compiler_params=params(4),
        cost_estimate=cost(1),
        name=name,
    )(*ins)


def stack_blocks(*blocks):
    def kernel(*refs):
        for i, ref in enumerate(refs[:-1]):
            refs[-1][i] = ref[...]

    return small_kernel(kernel, "stack_blocks", [(len(blocks), *blocks[0].shape)], *blocks)[0]


def join_blocks(first, last):
    n = first.shape[0]

    def kernel(first_ref, last_ref, out_ref):
        out_ref[:n] = first_ref[...]
        out_ref[n:] = last_ref[...]

    return small_kernel(kernel, "join_blocks", [(n + last.shape[0], *first.shape[1:])], first, last)[0]


def add_low(a, b):
    return (a.astype(F32) + b.astype(F32)).astype(BF)


def fold(keep, moved):
    n = keep.shape[0] // 2

    def kernel(keep_ref, moved_ref, *outs):
        for s in range(2 * n):
            outs[s // n][s % n] = add_low(keep_ref[s], moved_ref[s])

    return small_kernel(kernel, "fold", [(n, *keep.shape[1:])] * 2, keep, moved)


def add_blocks(a, b):
    def kernel(a_ref, b_ref, out_ref):
        for i in range(a.shape[0]):
            out_ref[i] = add_low(a_ref[i], b_ref[i])

    return small_kernel(kernel, "add_blocks", [a.shape], a, b)[0]


def fold_late(keep, moved, slots):
    half = 8 * slots

    def kernel(keep_ref, moved_ref, *outs):
        total = add_low(keep_ref[...], moved_ref[...])
        for i, out in enumerate(outs):
            out[:half, :] = total[i * half : (i + 1) * half]
            out[half:, :] = total[2 * half :]

    return small_kernel(kernel, "fold_late", [(half + keep.shape[0] - 2 * half, TILE)] * 2, keep, moved)


def fold_last(blocks, late=None, first=0):
    n, tall, wide = blocks[0].shape
    count = len(blocks)
    tail = 0 if late is None else 32

    def kernel(*refs):
        outs = refs[-n:]
        for s in range(n):
            total = sum(ref[s].astype(F32) for ref in refs[:count])
            outs[s][:tall, :] = total.astype(BF)
        if tail:
            total = add_low(refs[count][...], refs[count + 1][...])
            at = total.shape[0] - 64
            blocks = [total[at + 16 * i : at + 16 * i + 16] for i in range(4)]
            for s in range(n):
                small = total[16 * (first + s) : 16 * (first + s) + 16]
                outs[s][tall : tall + 16, :] = jnp.concatenate([small, *blocks[:2]], 1)
                outs[s][tall + 16 :, :] = jnp.concatenate([*blocks[2:], jnp.zeros_like(small)], 1)

    return small_kernel(kernel, "fold_last", [(tall + tail, wide)] * n, *blocks, *(late or ()))


def on_device(
    links,
    tokens,
    lengths,
    buckets,
    ln1_gain,
    ln1_bias,
    qkv_weight,
    q_bias,
    v_bias,
    out_weight,
    out_bias,
    rel_table,
    ln2_gain,
    ln2_bias,
    up_weight,
    up_bias,
    down_weight,
    down_bias,
    cotangent,
):
    rows, model = tokens.shape
    heads, number = rel_table.shape
    head_size = model // heads
    width = model // 2
    local = qkv_weight.shape[0]
    core, chips = links.core, links.chips
    core_arg = core.astype(jnp.int32).reshape(1)

    order = Order(core_arg)
    a_mine, a_sent, u_mine, u_sent, line = pack_blocks(
        core_arg, lengths, buckets, qkv_weight, out_weight, up_weight
    )
    a_mine, a_sent, ln1_gain = order.mark(a_mine, a_sent, ln1_gain)
    vectors = jnp.stack(
        [ln1_gain, ln1_bias, q_bias, v_bias, out_bias, ln2_gain, ln2_bias, down_bias]
        + [up_bias[i * local : (i + 1) * local] for i in range(4)]
    )
    small = pack_vectors(core_arg, vectors)
    a_theirs, small_theirs = links.swap(a_sent), links.swap(small)
    line_other, tokens_other, u_theirs = links.swap(line), links.swap(tokens), links.swap(u_sent)
    early_offsets, gather_offsets = links.early_offsets, links.gather_offsets
    scatter_offsets, last_offsets = links.scatter_offsets, links.last_offsets
    a_piece = merge_attention(core_arg, a_mine, a_theirs, small, small_theirs)
    a_piece, line_other, tokens_other, u_theirs, early_offsets, gather_offsets, scatter_offsets, last_offsets = order.mark(
        a_piece, line_other, tokens_other, u_theirs, early_offsets, gather_offsets, scatter_offsets, last_offsets
    )

    z_parts = [links.along_z(a_piece, k) for k in (1, 3, 2)]
    near = a_piece[None]
    second, third = links.x_first(near), links.y_first(near)
    tiles, grad_rows = bias_tiles(core_arg, (line, line_other), rel_table, cotangent, lengths, (0, 0))
    tiles, grad_rows, z_parts[:2], second, third, a_piece = order.mark(
        tiles, grad_rows, z_parts[:2], second, third, a_piece
    )
    z_parts[2] = links.along_z(a_piece, 2)
    f0, f1 = merge_feed_forward(core_arg, u_mine, order.go(u_theirs), down_weight)
    f_early = [[go(f[None]) for go in (links.x_first, links.y_first)] for f in (f0, f1)]
    f0, f1, z_parts[2], f_early = order.mark(f0, f1, z_parts[2], f_early)
    near_last = stack_blocks(*z_parts)
    second_last, third_last = links.x_first(near_last), links.y_first(near_last)
    f0_z = [links.along_z(order.go(f0), k) for k in (1, 3, 2)]
    second_last, third_last, f0_z[:2] = order.mark(second_last, third_last, f0_z[:2])
    fourth = links.y_first(join_blocks(second, second_last))
    f1_z = [links.along_z(order.go(f1), k) for k in (1, 3)]
    grad_rows_other = links.swap(grad_rows)
    fourth, grad_rows_other, f0_z[2] = order.mark(fourth, grad_rows_other, f0_z[2])
    parts = [near, near_last, second, second_last, third, third_last, fourth]
    own, own_out, vec = order.mark(*assemble_attention(Pieces(parts, early_offsets, links.rows), model))
    f1_z = order.mark(f1_z)
    f0_near = stack_blocks(f0_z[0], f0_z[2], f0_z[1])
    f0_second, f0_third = links.x_first(f0_near), links.y_first(f0_near)
    f1_z.append(links.along_z(order.go(f1), 2))
    other_out = links.swap(own_out)

    normed_other, joined1, mixed1, probs1 = attention_forward(
        1, 0, core_arg, tokens_other, vec, order.go(own), tiles, line_other, head_size
    )
    mixed1, other_out, f1_z = order.mark(mixed1, other_out, f1_z)
    mixed_rest = links.swap(mixed1)
    f0_second, f0_third = order.mark(f0_second, f0_third)
    f0_fourth = links.y_first(join_blocks(f_early[0][0], f0_second))
    f1_near = stack_blocks(f1_z[0], f1_z[2], f1_z[1])
    f1_second = links.x_first(f1_near)
    normed, joined0, mixed0, probs0 = attention_forward(
        0, 0, core_arg, tokens, vec, order.go(own), tiles, line, head_size
    )
    mixed0, mixed_rest = order.mark(mixed0, mixed_rest)
    mixed_rest_other = links.swap(mixed0)
    residual, normed2 = project_out(core_arg, (order.go(mixed0), mixed_rest), tokens, (own_out, other_out), vec)
    normed2, f0_fourth, f1_second, mixed_rest_other = order.mark(normed2, f0_fourth, f1_second, mixed_rest_other)

    normed2_other = links.swap(normed2)
    f1_third, f1_fourth = links.y_first(f1_near), links.y_first(join_blocks(f_early[1][0], f1_second))
    normed2_other = order.mark(normed2_other)

    def chunk(bufs):
        return Pieces(bufs, gather_offsets, links.rows)

    (own0, other0), sums_f0, (keep0, send0) = feed_forward(
        lambda c: 8 + c, core_arg,
        [(normed2, grad_rows, residual, None), (normed2_other, grad_rows_other, None, None)],
        vec, chunk([f0[None], f0_near, f_early[0][0], f0_second, f_early[0][1], f0_third, f0_fourth]), scatter_offsets,
    )
    own0, other0, keep0, send0, f1_third, f1_fourth = order.mark(own0, other0, keep0, send0, f1_third, f1_fourth)
    moved0 = links.y_first(send0)
    (own1, other1), sums_f1, (keep1, send1) = feed_forward(
        lambda c: 10 + c, core_arg,
        [(normed2, grad_rows, own0[0], own0[1]), (normed2_other, grad_rows_other, other0[0], other0[1])],
        vec, chunk([f1[None], f1_near, f_early[1][0], f1_second, f_early[1][1], f1_third, f1_fourth]), scatter_offsets,
    )
    own1, other1, keep1, send1, moved0 = order.mark(own1, other1, keep1, send1, moved0)
    keep0, send0 = fold(keep0, moved0)
    moved0 = links.x_first(send0)
    result_rest, grad_rest = links.swap(other1[0]), links.swap(other1[1])
    result_rest, grad_rest = order.mark(result_rest, grad_rest)
    moved1 = links.y_first(order.go(send1))
    output, grad_res, gm0, branch_cols, sent, sums2 = second_norm_back(
        core_arg, residual, (order.go(own1[0]), result_rest), (own1[1], grad_rest), grad_rows,
        (own_out, other_out), vec, lengths,
    )
    sent, moved0 = order.mark(sent, moved0)
    got = links.swap(sent)
    sums0 = fold_last((keep0, moved0))
    parts0 = [sums0[0]] + [links.along_z(sums0[k], k) for k in (1, 3)]
    dj0, diag0 = attention_backward(joined0, probs0, mixed0, order.go(gm0), head_size)
    dj0, got, moved1, parts0 = order.mark(dj0, got, moved1, parts0)
    parts0.insert(2, links.along_z(order.go(sums0[2]), 2))
    keep1, send1 = fold(keep1, moved1)
    moved1 = links.x_first(send1)
    dj1, diag1, part, keep, keep_next, send, send_next, own_keep, own_send = attention_backward(
        joined1, probs1, mixed1, order.go(got), head_size,
        Products(
            core_arg,
            [([(normed, None), (normed_other, None)], [(dj0, j), (None, j)]) for j in range(3)]
            + [([((mixed0, mixed_rest), None), ((mixed1, mixed_rest_other), None)], [(branch_cols, None), (got, 1)])],
            last_offsets,
            links.rows,
            links.last_counts,
        ),
        own,
    )
    part, keep, keep_next, send, send_next, own_keep, own_send, moved1, parts0 = order.mark(
        part, keep, keep_next, send, send_next, own_keep, own_send, moved1, parts0
    )
    part_rest = links.swap(part)
    next_moved, moved = links.y_first(send_next), links.y_first(send)
    part_rest, keep1, moved1 = order.mark(part_rest, keep1, moved1)
    sums1 = fold_last((keep1, moved1))
    parts1 = [sums1[0]] + [links.along_z(sums1[k], k) for k in (1, 3)]
    input_grad, late_keep, late_send = first_norm_back(
        core_arg, (order.go(dj0), dj1), part_rest, tokens, grad_res, vec, own, sums2, ([sums_f0], [sums_f1]),
        (diag0, diag1), (line, line_other), number, False, scatter_offsets,
    )
    late_keep, late_send, next_moved, parts1 = order.mark(late_keep, late_send, next_moved, parts1)
    late_moved = links.y_first(late_send)
    parts1.insert(2, links.along_z(order.go(sums1[2]), 2))
    next_moved = links.x_first(add_blocks(keep_next, next_moved))
    late_moved, moved = order.mark(late_moved, moved)
    late_keep, late_send = fold_late(late_keep, late_moved, 2 * links.nz)
    late_moved = links.x_first(late_send)
    next_moved, late_moved, own_send, parts1 = order.mark(next_moved, late_moved, own_send, parts1)
    sums = fold_last((keep, moved, next_moved), (late_keep, late_moved), 1)
    parts = [links.along_z(sums[k - 1], k) for k in (1, 2, 3)]
    own_moved = links.y_first(own_send)
    ffn0 = total_feed_forward(core_arg, order.go(parts0), local)
    ffn1 = total_feed_forward(core_arg, order.go(parts1), local)
    ffn0, ffn1, own_moved = order.mark(ffn0, ffn1, own_moved)
    own_keep, own_send = fold(own_keep, own_moved)
    own_moved = links.x_first(own_send)
    ups = [links.swap(ffn0[1]), links.swap(ffn1[1])]
    grad_up, grad_down = finish_feed_forward(
        core_arg, [ffn0[0], ffn1[0]], ups, [ffn0[2], ffn1[2]]
    )
    grad_up, grad_down, parts, own_moved = order.mark(grad_up, grad_down, parts, own_moved)
    parts = [*fold_last((own_keep, own_moved), (late_keep, late_moved)), *parts]
    mine, sent, tail = total_attention(core_arg, parts, local)
    theirs, tail_theirs = links.swap(sent), links.swap(tail)
    grad_qkv, grad_out, grad_table, *small_grads = finish_attention(
        core_arg, mine, theirs, tail, tail_theirs, heads, number
    )
    small_grads = [one.reshape(-1) for one in small_grads]
    grad_up_bias = small_grads[VECTORS]

    return (
        output,
        input_grad,
        small_grads[0],
        small_grads[1],
        grad_qkv,
        small_grads[2],
        small_grads[3],
        grad_out,
        small_grads[4],
        grad_table,
        small_grads[5],
        small_grads[6],
        grad_up,
        grad_up_bias,
        grad_down,
        small_grads[7],
    )


def on_any_mesh(
    tokens,
    lengths,
    buckets,
    ln1_gain,
    ln1_bias,
    qkv_weight,
    q_bias,
    v_bias,
    out_weight,
    out_bias,
    rel_table,
    ln2_gain,
    ln2_bias,
    up_weight,
    up_bias,
    down_weight,
    down_bias,
    cotangent,
):
    rows, model = tokens.shape
    heads, number = rel_table.shape
    head_size = model // heads
    width = model // 2
    local = qkv_weight.shape[0]
    hidden = up_weight.shape[1]
    core = jnp.zeros((1,), jnp.int32)
    offsets = jnp.zeros((1,), jnp.int32)

    def gathered(x):
        return lax.all_gather(x, AXES, axis=0, tiled=True)

    def scattered(x):
        return lax.psum_scatter(x, AXES, scatter_dimension=0, tiled=True)

    vectors = [ln1_gain, ln1_bias, q_bias, v_bias, out_bias, ln2_gain, ln2_bias, down_bias]
    unit = up_bias.shape[0]
    small = gathered(jnp.concatenate([*vectors, up_bias])[None, :])
    wide = [small[:, i * local : (i + 1) * local].reshape(1, model) for i in range(VECTORS)]
    ub = small[:, VECTORS * local :].reshape(2, 2, model).transpose(1, 0, 2).reshape(4, model)
    del unit
    vec = jnp.concatenate([*wide, ub, jnp.zeros((4, model), BF)], 0).astype(F32)
    attn = gathered(jnp.concatenate([qkv_weight, out_weight], 1))
    up, down = gathered(up_weight), gathered(down_weight)
    a_pieces = tuple(
        jnp.stack([attn[:, j * model + h * width : j * model + (h + 1) * width] for j in range(3)])
        for h in range(2)
    )

    a_out = tuple(attn[:, 3 * model + h * width : 3 * model + (h + 1) * width] for h in range(2))

    def chunk(f, h):
        at = (2 * h + f) * model
        blocks = [one[:, k * width : (k + 1) * width] for one in (up[:, at : at + model], down[at : at + model]) for k in range(2)]
        return Pieces([jnp.concatenate(blocks, 0)[None]], offsets, model)

    ahead = jnp.roll(buckets[0, rows - 1], 1)
    line = jnp.concatenate([ahead, buckets[0, 0]]).astype(F32)
    line = jnp.stack([line, jnp.full_like(line, lengths[0])] + [jnp.zeros_like(line)] * 6)
    tiles, grad_rows = bias_tiles(core, (line, line), rel_table, cotangent, lengths, (0, 1))
    normed, joined0, mixed0, probs0 = attention_forward(0, 0, core, tokens, vec, a_pieces[0], tiles, line, head_size)
    _, joined1, mixed1, probs1 = attention_forward(1, 1, core, tokens, vec, a_pieces[1], tiles, line, head_size)
    residual, normed2 = project_out(core, (mixed0, mixed1), tokens, a_out, vec)
    result, grad_n2 = residual, None
    up_sums, ups, downs = [[], []], [], []
    for f in range(2):
        for h in range(2):
            ((result, grad_n2, active, grad_pre),), sums, _ = feed_forward(
                lambda c, at=8 + 2 * f + h: c + at, core, [(normed2, grad_rows, result, grad_n2)], vec, chunk(f, h)
            )
            up_sums[f].append(sums)
            (both,) = outer_products(
                core,
                [([(normed2, None)], [(grad_pre, k)]) for k in range(2)]
                + [([(active, None)], [(grad_rows, k)]) for k in range(2)],
                offsets,
                model,
            )
            both = both[0].reshape(2, 2, model, width).transpose(0, 2, 1, 3).reshape(2, model, model)
            ups.append(both[0])
            downs.append(both[1])
    output, grad_res, gm0, branch0, sent, sums2 = second_norm_back(
        core, residual, (result,), (grad_n2,), grad_rows, a_out, vec, lengths
    )
    dj0, diag0 = attention_backward(joined0, probs0, mixed0, gm0, head_size)
    dj1, diag1 = attention_backward(joined1, probs1, mixed1, sent, head_size)
    input_grad, vec_grads, table_grad = first_norm_back(
        core, (dj0, dj1), normed_back(dj1, a_pieces[1]), tokens, grad_res, vec, a_pieces[0], sums2, up_sums,
        (diag0, diag1), (line, line), number, True,
    )
    mixed = jnp.concatenate([mixed0, mixed1], 1)
    halves = [
        outer_products(
            core, [([(normed, None)], [(dj, j)]) for j in range(3)] + [([(mixed, None)], [branch])], offsets, model
        )[0][0].reshape(4, model, width)
        for dj, branch in ((dj0, (branch0, None)), (dj1, (sent, 1)))
    ]
    grads = jnp.stack(halves, 2).transpose(1, 0, 2, 3).reshape(model, 4 * model)
    grads = scattered(grads)
    grad_up = scattered(jnp.concatenate([ups[0], ups[2], ups[1], ups[3]], 1))
    grad_down = scattered(jnp.concatenate([downs[0], downs[2], downs[1], downs[3]], 0))
    by_owner = vec_grads[:VECTORS].reshape(VECTORS, model // local, local).transpose(1, 0, 2)
    own_units = vec_grads[VECTORS : VECTORS + 4].reshape(2, 2, model).transpose(1, 0, 2)
    both = jnp.concatenate(
        [by_owner.reshape(model // local, VECTORS * local), own_units.reshape(model // local, hidden * local // model)],
        1,
    )
    both = scattered(both)[0]
    table = jnp.concatenate([table_grad[16 * i : 16 * i + 16] for i in range(4)], 1)[:heads, :number]
    grad_table = lax.psum(table, AXES)
    small_grads = [both[i * local : (i + 1) * local] for i in range(VECTORS)]
    return (
        output,
        input_grad,
        small_grads[0],
        small_grads[1],
        grads[:, : 3 * model].astype(F32),
        small_grads[2],
        small_grads[3],
        grads[:, 3 * model :].astype(F32),
        small_grads[4],
        grad_table,
        small_grads[5],
        small_grads[6],
        grad_up.astype(F32),
        both[VECTORS * local :],
        grad_down.astype(F32),
        small_grads[7],
    )


def solution(mesh):
    both = P(AXES)
    row = P(AXES, None)
    in_specs = (
        row, both, P(AXES, None, None), both, both, row, both, both, row, both, P(), both, both, row, both, row,
        both, row,
    )
    out_specs = (row, row, both, both, row, both, both, row, both, P(), both, both, row, both, row, both)

    if tuple(mesh.shape[name] for name in AXES) == (2, 16):

        def body(*args):
            return on_device(GridLinks((2, 4, 2), args[0].shape[1]), *args)

    else:
        body = on_any_mesh

    return jax.shard_map(body, mesh=mesh, in_specs=in_specs, out_specs=out_specs, check_vma=False)
```

```python
import functools

import jax
import jax.numpy as jnp
from jax import lax
from jax.experimental import pallas as pl
from jax.experimental.pallas import tpu as pltpu
from jax.sharding import PartitionSpec as P

BF = jnp.bfloat16
F32 = jnp.float32
AXES = ("dp", "fsdp")
TILE = 128
CHUNK = 64
EPS = 1e-05
NN = (((1,), (0,)), ((), ()))
NT = (((1,), (1,)), ((), ()))
TN = (((0,), (0,)), ((), ()))
VMEM = pltpu.VMEM


def mm(left, right, dims=NN):
    return lax.dot_general(left, right, dims, preferred_element_type=F32)


def hbm_spec():
    return pl.BlockSpec(memory_space=pltpu.HBM)


def in_hbm(x):
    return pltpu.with_memory_space_constraint(x, pltpu.HBM)


def smem_spec():
    return pl.BlockSpec(memory_space=pltpu.SMEM)


def whole(shape):
    return pl.BlockSpec(shape, lambda *_: (0,) * len(shape))


def params(mebibytes):
    return pltpu.CompilerParams(
        dimension_semantics=("arbitrary",), vmem_limit_bytes=mebibytes * 1024 * 1024
    )


def cost(micros):
    return pl.CostEstimate(flops=int(micros * 1e9), bytes_accessed=1, transcendentals=0)


class Pieces:
    def __init__(self, buffers, offsets, rows):
        self.buffers = buffers
        self.offsets = offsets
        self.rows = rows

    @property
    def slots(self):
        return sum(b.shape[0] for b in self.buffers)


def lay_blocks(refs, offs_ref, rows, count, put):
    slot = 0
    for ref in refs:
        for k in range(ref.shape[0]):
            at = pl.multiple_of(offs_ref[slot], 16)
            for j in range(count):
                put(j, at, ref[k, j * rows : (j + 1) * rows, :])
            slot += 1


def row_norm(x):
    centre = x - jnp.mean(x, -1, keepdims=True)
    scale = lax.rsqrt(jnp.mean(centre * centre, -1, keepdims=True) + EPS)
    return centre * scale, scale


def bucket_line(line, number):
    rows = lax.broadcasted_iota(jnp.int32, (number, line.shape[1]), 0)
    return jnp.where(rows == line.astype(jnp.int32), 1.0, 0.0).astype(BF)


def bias_tiles(core, lines, table, cotangent, lengths, halves):
    span = lines[0].shape[1]
    heads, number = table.shape
    count = heads // 2
    tiles = span // TILE - 1
    n = len(lines)
    rows, model = cotangent.shape

    def kernel(core_ref, len_ref, table_ref, cot_ref, *refs):
        line_refs, (out_ref, gr_ref, curve_ref) = refs[:n], refs[n:]
        at = pl.program_id(0)

        @pl.when(at == 0)
        def _():
            for i in range(n):
                curve = mm(table_ref[...], bucket_line(line_refs[i][0:1, :], number))
                curve = jnp.where((core_ref[0] ^ halves[i]) == 0, curve[:count], curve[count:])
                for h in range(count):
                    curve_ref[i * count + h] = jnp.broadcast_to(curve[h : h + 1], (8, span))
            row = lax.broadcasted_iota(jnp.int32, (rows, 1), 0)
            gr_ref[...] = jnp.where(row < len_ref[0], cot_ref[...].astype(F32), 0.0).astype(BF)

        base = pltpu.roll(curve_ref[at], 0, 1, stride=1, stride_axis=0)
        for pair in range(TILE // 16):
            rolled = jnp.concatenate(
                [pltpu.roll(base, 16 * pair + 8 * i, 1) if pair + i else base for i in range(2)], 0
            ).astype(BF)
            for d in range(tiles):
                out_ref[0, 0, d, 16 * pair : 16 * pair + 16, :] = rolled[
                    :, TILE * (d + 1) : TILE * (d + 2)
                ]

    return pl.pallas_call(
        kernel,
        grid=(n * count,),
        in_specs=[
            smem_spec(),
            smem_spec(),
            whole((heads, number)),
            whole((rows, model)),
            *[whole((8, span))] * n,
        ],
        out_specs=[
            pl.BlockSpec((1, 1, tiles, TILE, TILE), lambda h: (h // count, h % count, 0, 0, 0)),
            whole((rows, model)),
        ],
        out_shape=[
            VMEM((n, count, tiles, TILE, TILE), BF),
            VMEM((rows, model), BF),
        ],
        scratch_shapes=[VMEM((n * count, 8, span), F32)],
        compiler_params=params(8),
        cost_estimate=cost(4),
        name="bias_tiles",
    )(core, lengths, table, cotangent, *lines)


def place_rows(block, offset, wide):
    padded = jnp.concatenate([block, jnp.zeros((block.shape[0], wide - TILE), block.dtype)], 1)
    return pltpu.roll(padded, offset, 1)


def assemble_attention(pieces, model):
    width = model // 2
    rows = pieces.rows
    n_buf = len(pieces.buffers)

    def kernel(offs_ref, *refs):
        bufs, (w_ref, o_ref, vec_ref) = refs[:n_buf], refs[n_buf:]

        def put(j, at, block):
            if j < 3:
                w_ref[j, pl.ds(at, rows), :] = block
            else:
                o_ref[pl.ds(at, rows), :] = block

        lay_blocks(bufs, offs_ref, rows, 4, put)
        total, slot = jnp.zeros((16, model), F32), 0
        for ref in bufs:
            for k in range(ref.shape[0]):
                total += place_rows(ref[k, 4 * rows : 4 * rows + 16, :TILE].astype(F32), offs_ref[slot], model)
                slot += 1
        vec_ref[...] = total

    return pl.pallas_call(
        kernel,
        grid=(1,),
        in_specs=[smem_spec(), *[whole(one.shape) for one in pieces.buffers]],
        out_specs=[whole((3, model, width)), whole((model, width)), whole((16, model))],
        out_shape=[
            VMEM((3, model, width), BF),
            VMEM((model, width), BF),
            VMEM((16, model), F32),
        ],
        compiler_params=params(6),
        cost_estimate=cost(2),
        name="assemble_attention",
    )(pieces.offsets, *pieces.buffers)


def attention_forward(item, half, core, tokens, vec, weights, tiles, line, head_size):
    rows, model = tokens.shape
    width = model // 2
    heads = width // head_size
    pairs = width // TILE
    per = TILE // head_size
    scale = head_size**-0.5

    def kernel(core_ref, line_ref, x_ref, vec_ref, tile_ref, w_ref, n1_ref, joined_ref, mixed_ref, p_ref, sums_ref, qs_ref, s_ref):
        pair = pl.program_id(0)

        @pl.when(pair == 0)
        def _():
            for r in range(0, rows, CHUNK):
                xhat, _ = row_norm(x_ref[r : r + CHUNK, :].astype(F32))
                n1_ref[r : r + CHUNK, :] = (xhat * vec_ref[0:1, :] + vec_ref[1:2, :]).astype(BF)
            cols = pl.ds(pl.multiple_of((core_ref[0] ^ half) * width, TILE), width)
            for j in range(3):
                joined = mm(n1_ref[...], w_ref[j])
                if j != 1:
                    joined = joined + vec_ref[2 + j // 2 : 3 + j // 2, cols]
                qs_ref[j] = joined.astype(BF)

        lanes = pl.ds(pl.multiple_of(pair * TILE, TILE), TILE)
        q, k, v = (qs_ref[j, :, lanes] for j in range(3))
        for j, one in enumerate((q, k, v)):
            joined_ref[j] = one
        lane = lax.broadcasted_iota(jnp.int32, (1, TILE), 1)
        column = lax.broadcasted_iota(jnp.int32, (1, rows), 1)
        dead = jnp.where(column < line_ref[1:2, :rows].astype(jnp.int32), 0.0, -1e30).astype(F32)
        scaled = q.astype(F32) * scale
        outs = []
        for e in range(per):
            mine = (lane >= e * head_size) & (lane < (e + 1) * head_size)
            qm = jnp.where(mine, scaled, 0.0).astype(BF)
            s_ref[e] = mm(qm, k, NT)
            for r in range(0, rows, CHUNK):
                block, sub = r // TILE, r % TILE
                rel = jnp.concatenate(
                    [
                        tile_ref[0, e, j - block + rows // TILE - 1, sub : sub + CHUNK, :]
                        for j in range(rows // TILE)
                    ],
                    1,
                ).astype(F32)
                s = s_ref[e, r : r + CHUNK, :] + (rel + dead)
                raised = jnp.exp(s - jnp.max(s, -1, keepdims=True))
                inv = 1.0 / jnp.sum(raised, -1, keepdims=True)
                p_ref[e, r : r + CHUNK, :] = (raised * inv).astype(BF)
            outs.append(jnp.where(mine, mm(p_ref[e], v), 0.0))
        mixed = functools.reduce(lambda a, b: a + b, outs)
        sums_ref[...] = mixed
        mixed_ref[...] = mixed.astype(BF)

    shapes = [
        VMEM((3, rows, width), BF),
        VMEM((rows, width), BF),
        VMEM((heads, rows, rows), BF),
        VMEM((rows, width), F32),
    ]
    outs = [
        pl.BlockSpec((3, rows, TILE), lambda p: (0, 0, p)),
        pl.BlockSpec((rows, TILE), lambda p: (0, p)),
        pl.BlockSpec((per, rows, rows), lambda p: (p, 0, 0)),
        pl.BlockSpec((rows, TILE), lambda p: (0, p)),
    ]
    shapes.insert(0, VMEM((rows, model), BF))
    outs.insert(0, whole((rows, model)))
    return pl.pallas_call(
        kernel,
        grid=(pairs,),
        in_specs=[
            smem_spec(),
            whole((8, 2 * rows)),
            whole((rows, model)),
            whole((16, model)),
            pl.BlockSpec((1, per, tiles.shape[2], TILE, TILE), lambda p: (item, p, 0, 0, 0)),
            whole((3, model, width)),
        ],
        out_specs=outs,
        out_shape=shapes,
        scratch_shapes=[VMEM((3, rows, width), BF), VMEM((per, rows, rows), F32)],
        compiler_params=params(12),
        cost_estimate=cost(6),
        name="attention_forward",
    )(core, line, tokens, vec, tiles, weights)


def project_out(core, mixed, tokens, weights, vec):
    rows, model = tokens.shape
    width = model // 2

    def kernel(core_ref, m0_ref, m1_ref, x_ref, vec_ref, w0_ref, w1_ref, res_ref, n2_ref):
        for h, w_ref in enumerate((w0_ref, w1_ref)):
            cols = pl.ds(pl.multiple_of((core_ref[0] ^ h) * width, TILE), width)
            acc = 0.0
            for g, m_ref in enumerate((m0_ref, m1_ref)):
                feats = pl.ds(pl.multiple_of((core_ref[0] ^ g) * width, TILE), width)
                acc = acc + mm(m_ref[...], w_ref[feats, :])
            res_ref[:, cols] = x_ref[:, cols].astype(F32) + acc + vec_ref[4:5, cols]
        for r in range(0, rows, CHUNK):
            xhat, _ = row_norm(res_ref[r : r + CHUNK, :])
            n2_ref[r : r + CHUNK, :] = (xhat * vec_ref[5:6, :] + vec_ref[6:7, :]).astype(BF)

    return pl.pallas_call(
        kernel,
        grid=(1,),
        in_specs=[
            smem_spec(),
            whole((rows, width)),
            whole((rows, width)),
            whole((rows, model)),
            whole((16, model)),
            whole((model, width)),
            whole((model, width)),
        ],
        out_specs=[whole((rows, model)), whole((rows, model))],
        out_shape=[
            VMEM((rows, model), F32),
            VMEM((rows, model), BF),
        ],
        compiler_params=params(6),
        cost_estimate=cost(2.5),
        name="project_out",
    )(core, mixed[0], mixed[1], tokens, vec, *weights)


def gelu_parts(v):
    bell = jnp.exp(-0.5 * (v * v))
    t = 1.0 / (1.0 + 0.23164189 * jnp.abs(v))
    tail = t * (0.127414796 + t * (-0.142248368 + t * (0.710706871 + t * (-0.726576014 + t * 0.530702714))))
    tail = tail * bell
    return jnp.where(v < 0.0, tail, 1.0 - tail), bell * 0.3989422804014327


def feed_forward(row, core, sets, vec, pieces, offsets=None):
    rows, model = sets[0][0].shape
    hidden = model
    n = len(sets)
    n_buf = len(pieces.buffers)
    per = pieces.rows
    half = rows // 2
    width = model // 2

    def kernel(core_ref, offs_ref, out_offs_ref, vec_ref, *refs):
        ins, refs = refs[: len(flat)], refs[len(flat) :]
        bufs, refs = refs[:n_buf], refs[n_buf:]
        outs, refs = refs[: 4 * n], refs[4 * n :]
        col_ref, slot_refs, (up_ref, down_ref, w_ref) = refs[0], refs[1:-3], refs[-3:]

        def put(j, at, block):
            ref = up_ref if j < 2 else down_ref
            ref[pl.ds(at, per), (j % 2) * width : (j % 2 + 1) * width] = block

        lay_blocks(bufs, offs_ref, per, 4, put)
        up_bias = vec_ref[pl.ds(row(core_ref[0]), 1), :]
        sums = jnp.zeros((1, hidden), F32)
        for i in range(n):
            n_ref, gr_ref, res_ref, gin_ref = (None if at is None else ins[at] for at in where[i])
            out_ref, gn_ref, act_ref, gp_ref = outs[4 * i : 4 * i + 4]
            for r in range(0, rows, half):
                block = slice(r, r + half)
                pre = mm(n_ref[block, :], up_ref[...]) + up_bias
                gact = mm(gr_ref[block, :], down_ref[...], NT)
                cdf, density = gelu_parts(pre)
                act = (pre * cdf).astype(BF)
                gp = gact * (cdf + pre * density)
                low = gp.astype(BF)
                act_ref[block, :] = act
                gp_ref[block, :] = low
                sums += jnp.sum(low.astype(F32), 0, keepdims=True)
                out = mm(act, down_ref[...])
                if res_ref is not None:
                    out = out + res_ref[block, :]
                    if gin_ref is None:
                        out = out + vec_ref[7:8, :]
                out_ref[block, :] = out
                gn = mm(low, up_ref[...], NT)
                gn_ref[block, :] = gn if gin_ref is None else gn + gin_ref[block, :]
        col_ref[...] = sums
        if offsets is None:
            return
        for m in range(4):
            cols = slice((m % 2) * width, (m % 2 + 1) * width)
            total = 0.0
            for i in range(n):
                n_ref, gr_ref = (ins[at] for at in where[i][:2])
                act_ref, gp_ref = outs[4 * i + 2 : 4 * i + 4]
                left, right = (n_ref, gp_ref) if m < 2 else (act_ref, gr_ref)
                total = total + mm(left[...], right[:, cols], TN)
            w_ref[...] = total.astype(BF)
            to_slots(w_ref, out_offs_ref, slot_refs, m, per)

    flat, where = [], []
    for one in sets:
        places = []
        for array in one:
            places.append(None if array is None else len(flat))
            if array is not None:
                flat.append(array)
        where.append(places)
    shapes = [
        VMEM((rows, model), F32),
        VMEM((rows, model), F32),
        VMEM((rows, hidden), BF),
        VMEM((rows, hidden), BF),
    ] * n + [VMEM((1, hidden), F32)]
    if offsets is not None:
        shapes += [VMEM((offsets.shape[0] // 2, 4 * per, width), BF)] * 2
    out = pl.pallas_call(
        kernel,
        grid=(1,),
        in_specs=[
            *[smem_spec()] * 3,
            whole((16, model)),
            *[whole((rows, model))] * len(flat),
            *[whole(one.shape) for one in pieces.buffers],
        ],
        out_specs=[whole(one.shape) for one in shapes],
        out_shape=shapes,
        scratch_shapes=[
            VMEM((model, hidden), BF),
            VMEM((hidden, model), BF),
            VMEM((model, width), BF),
        ],
        compiler_params=params(14),
        cost_estimate=cost(13),
        name="feed_forward",
    )(core, pieces.offsets, pieces.offsets if offsets is None else offsets, vec, *flat, *pieces.buffers)
    return [out[4 * i : 4 * i + 4] for i in range(n)], out[4 * n], out[4 * n + 1 :]


def to_slots(w_ref, offs_ref, outs, matrix, rows):
    slot = 0
    for out in outs:
        for k in range(out.shape[0]):
            at = pl.multiple_of(offs_ref[slot], 16)
            out[k, matrix * rows : (matrix + 1) * rows, :] = w_ref[pl.ds(at, rows), :]
            slot += 1


class Products:
    def __init__(self, core, pairs, offsets, rows, counts):
        self.core, self.offsets, self.rows = core, offsets, rows
        self.tall = pairs[0][0][0][0].shape[-1]
        self.wide = self.tall // 2
        self.flat = []
        self.where = [([self._place(*one) for one in lefts], [self._place(*one) for one in rights]) for lefts, rights in pairs]
        self.shapes = [VMEM((count, len(pairs) * rows, self.wide), BF) for count in counts]
        self.scratch = VMEM((self.tall, self.wide), BF)

    def _place(self, one, part):
        if isinstance(one, tuple):
            return [self._place(each, part) for each in one]
        if one is None:
            return None, part
        match = [i for i, known in enumerate(self.flat) if known is one]
        if not match:
            self.flat.append(one)
            match = [len(self.flat) - 1]
        return match[0], part

    def run(self, core_ref, offs_ref, ins, outs, w_ref, own_ref=None):
        def pick(at, part):
            ref = own_ref if at is None else ins[at]
            if part is None:
                return ref[...]
            if len(ref.shape) == 3:
                return ref[part]
            return ref[:, part * self.wide : (part + 1) * self.wide]

        for m, (lefts, rights) in enumerate(self.where):
            if isinstance(lefts[0], list):
                for h in range(2):
                    total = sum(mm(pick(*left[h]), pick(*right), TN) for left, right in zip(lefts, rights))
                    at = pl.multiple_of((core_ref[0] ^ h) * self.wide, 16)
                    w_ref[pl.ds(at, self.wide), :] = total.astype(BF)
            else:
                total = sum(mm(pick(*left), pick(*right), TN) for left, right in zip(lefts, rights))
                w_ref[...] = total.astype(BF)
            to_slots(w_ref, offs_ref, outs, m, self.rows)


def outer_products(core, pairs, offsets, rows):
    work = Products(core, pairs, offsets, rows, offsets.shape)
    n = len(work.flat)

    def kernel(core_ref, offs_ref, *rest):
        work.run(core_ref, offs_ref, rest[:n], rest[n:-1], rest[-1])

    return pl.pallas_call(
        kernel,
        grid=(1,),
        in_specs=[smem_spec(), smem_spec(), *[whole(one.shape) for one in work.flat]],
        out_specs=[whole(one.shape) for one in work.shapes],
        out_shape=work.shapes,
        scratch_shapes=[work.scratch],
        compiler_params=params(14),
        cost_estimate=cost(5),
        name="outer_products",
    )(core, offsets, *work.flat)


def norm_back(x, up, gain):
    xhat, scale = row_norm(x)
    e = up * gain
    grad = scale * (e - jnp.mean(e, -1, keepdims=True) - xhat * jnp.mean(e * xhat, -1, keepdims=True))
    return grad, up * xhat


def second_norm_back(core, residual, results, grads_normed, grad_rows, weights, vec, lengths):
    rows, model = residual.shape
    width = model // 2
    n, m = len(results), len(grads_normed)

    def kernel(core_ref, len_ref, res_ref, gr_ref, vec_ref, w0_ref, w1_ref, *refs):
        out_refs, gn_refs = refs[:n], refs[n : n + m]
        out_ref, gres_ref, gm_ref, br_ref, sent_ref, sums_ref, gb_ref = refs[n + m :]
        totals = [jnp.zeros((1, model), F32) for _ in range(4)]
        for r in range(0, rows, CHUNK):
            block = slice(r, r + CHUNK)
            row = lax.broadcasted_iota(jnp.int32, (CHUNK, 1), 0) + r
            result = functools.reduce(lambda a, b: a + b, [ref[block, :] for ref in out_refs])
            out_ref[block, :] = jnp.where(row < len_ref[0], result, 0.0).astype(BF)
            up = functools.reduce(lambda a, b: a + b, [ref[block, :] for ref in gn_refs])
            grad, gain_terms = norm_back(res_ref[block, :], up, vec_ref[5:6, :])
            gr = gr_ref[block, :].astype(F32)
            grad = gr + grad
            low = grad.astype(BF)
            gres_ref[block, :] = grad
            gb_ref[block, :] = low
            for i, terms in enumerate((gain_terms, up, low.astype(F32), gr)):
                totals[i] += jnp.sum(terms, 0, keepdims=True)
        sums_ref[...] = jnp.concatenate(totals + [jnp.zeros((4, model), F32)], 0)
        parts = [pl.ds(pl.multiple_of((core_ref[0] ^ h) * width, TILE), width) for h in range(2)]
        for h in range(2):
            acc = 0.0
            for g, w_ref in enumerate((w0_ref, w1_ref)):
                acc = acc + mm(gb_ref[:, parts[g]], w_ref[parts[h], :], NT)
            if h == 0:
                gm_ref[...] = acc.astype(BF)
                br_ref[...] = gb_ref[:, parts[0]]
            else:
                sent_ref[:, :width] = acc.astype(BF)
                sent_ref[:, width:] = gb_ref[:, parts[1]]

    return pl.pallas_call(
        kernel,
        grid=(1,),
        in_specs=[
            *[smem_spec()] * 2,
            *[whole((rows, model))] * 2,
            whole((16, model)),
            whole((model, width)),
            whole((model, width)),
            *[whole((rows, model))] * (n + m),
        ],
        out_specs=[
            *[whole((rows, model))] * 2,
            *[whole((rows, width))] * 2,
            whole((rows, model)),
            whole((8, model)),
        ],
        out_shape=[
            jax.ShapeDtypeStruct((rows, model), BF),
            jax.ShapeDtypeStruct((rows, model), F32),
            jax.ShapeDtypeStruct((rows, width), BF),
            jax.ShapeDtypeStruct((rows, width), BF),
            jax.ShapeDtypeStruct((rows, model), BF),
            jax.ShapeDtypeStruct((8, model), F32),
        ],
        scratch_shapes=[VMEM((rows, model), BF)],
        compiler_params=params(10),
        cost_estimate=cost(4),
        name="second_norm_back",
    )(core, lengths, residual, grad_rows, vec, *weights, *results, *grads_normed)


def attention_backward(joined, probs, mixed, grad_mixed, head_size, products=None, weights=None):
    _, rows, width = joined.shape
    heads = width // head_size
    pairs = width // TILE
    per = TILE // head_size
    tiles = 2 * (rows // TILE) - 1
    span = 2 * rows
    scale = head_size**-0.5
    flat = [] if products is None else products.flat
    n_in = 4 + len(flat) + (2 if products else 0) + (1 if weights is not None else 0)

    def kernel(*refs):
        ins, refs = refs[:n_in], refs[n_in:]
        joined_ref, p_ref, mixed_ref, gm_ref = ins[:4]
        out_ref, diag_ref, refs = refs[0], refs[1], refs[2:]
        gp_ref, ds_ref, acc_ref = refs[-3:]
        lane = lax.broadcasted_iota(jnp.int32, (1, TILE), 1)
        for pair in range(pairs):
            lanes = slice(pair * TILE, (pair + 1) * TILE)
            q, k, v = (joined_ref[j, :, lanes] for j in range(3))
            gm = gm_ref[:, lanes]
            dots = gm.astype(F32) * mixed_ref[:, lanes]
            q_t, gm_t = q.T, gm.T
            dq, dk, dv = [], [], []
            for e in range(per):
                head = pair * per + e
                mine = (lane >= e * head_size) & (lane < (e + 1) * head_size)
                feats = slice(e * head_size, (e + 1) * head_size)
                delta = jnp.sum(jnp.where(mine, dots, 0.0), -1, keepdims=True)
                gp_ref[e] = mm(jnp.where(mine, gm, jnp.zeros_like(gm)), v, NT)
                acc_ref[...] = jnp.zeros_like(acc_ref)
                for r in range(0, rows, CHUNK):
                    block, sub = r // TILE, r % TILE
                    ds = p_ref[head, r : r + CHUNK, :].astype(F32) * (
                        gp_ref[e, r : r + CHUNK, :] - delta[r : r + CHUNK, :]
                    )
                    ds_ref[e, r : r + CHUNK, :] = ds.astype(BF)
                    for j in range(rows // TILE):
                        acc_ref[j - block + rows // TILE - 1, sub : sub + CHUNK, :] += ds[
                            :, j * TILE : (j + 1) * TILE
                        ]
                dq.append(jnp.where(mine, mm(ds_ref[e], k), 0.0))
                dk.append(mm(q_t[feats, :], ds_ref[e]))
                dv.append(mm(gm_t[feats, :], p_ref[head]))
                total = jnp.zeros((8, span), F32)
                for g in range(TILE // 8):
                    strip = jnp.concatenate(
                        [jnp.zeros((8, TILE), F32)]
                        + [acc_ref[d, 8 * g : 8 * g + 8, :] for d in range(tiles)],
                        1,
                    )
                    total += pltpu.roll(strip, (span - 8 * g) % span, 1) if g else strip
                line = total[0:1]
                for i in range(1, 8):
                    line = line + pltpu.roll(total[i : i + 1], span - i, 1)
                diag_ref[head] = line
            out_ref[0, :, lanes] = (functools.reduce(lambda a, b: a + b, dq) * scale).astype(BF)
            out_ref[1, :, lanes] = (jnp.concatenate(dk, 0) * scale).T.astype(BF)
            out_ref[2, :, lanes] = jnp.concatenate(dv, 0).T.astype(BF)
        if weights is not None:
            refs[0][...] = sum(mm(out_ref[j], ins[-1][j], NT) for j in range(3)).astype(BF)
        if products is not None:
            slot_refs = refs[1:-4] if weights is not None else refs[:-4]
            products.run(ins[4], ins[5], ins[6 : 6 + len(flat)], slot_refs, refs[-4], out_ref)

    ins = [joined, probs, mixed, grad_mixed]
    specs = [whole(one.shape) for one in ins]
    shapes = [VMEM((3, rows, width), BF), VMEM((heads, 1, span), F32)]
    scratch = [VMEM((per, rows, rows), F32), VMEM((per, rows, rows), BF), VMEM((tiles, TILE, TILE), F32)]
    if products is not None:
        ins += [products.core, products.offsets, *flat]
        specs += [smem_spec(), smem_spec(), *[whole(one.shape) for one in flat]]
    if weights is not None:
        ins.append(weights)
        specs.append(whole(weights.shape))
        shapes.append(VMEM((rows, weights.shape[1]), BF))
    if products is not None:
        shapes += products.shapes
        scratch.insert(0, products.scratch)
    return pl.pallas_call(
        kernel,
        grid=(1,),
        in_specs=specs,
        out_specs=[whole(one.shape) for one in shapes],
        out_shape=shapes,
        scratch_shapes=scratch,
        compiler_params=params(16),
        cost_estimate=cost(4.5),
        name="attention_backward",
    )(*ins)


def normed_back(grads, weights):
    _, rows, width = grads.shape
    model = weights.shape[1]

    def kernel(d_ref, w_ref, out_ref):
        out_ref[...] = sum(mm(d_ref[j], w_ref[j], NT) for j in range(3))

    return pl.pallas_call(
        kernel,
        grid=(1,),
        in_specs=[whole(grads.shape), whole(weights.shape)],
        out_specs=whole((rows, model)),
        out_shape=VMEM((rows, model), F32),
        compiler_params=params(8),
        cost_estimate=cost(1.5),
        name="normed_back",
    )(grads, weights)


def first_norm_back(
    core, grads, part, tokens, grad_residual, vec, weights, sums_second, sums_up, diags, lines, number, apart, offsets=None
):
    rows, model = tokens.shape
    width = model // 2
    count = diags[0].shape[0]
    span = lines[0].shape[1]
    n_up = len(sums_up[0])

    def kernel(core_ref, d0_ref, d1_ref, part_ref, x_ref, gres_ref, vec_ref, w_ref, s2_ref, t0_ref, t1_ref, l0_ref, l1_ref,
               *rest):
        up_refs = rest[: 2 * n_up]
        offs_ref, gx_ref, sums_ref, table_ref, acc_ref = rest[2 * n_up :]
        straight = core_ref[0] == 0

        def ordered(a, b):
            return [jnp.where(straight, a, b), jnp.where(straight, b, a)]

        tables = []
        for t_ref, l_ref in ((t0_ref, l0_ref), (t1_ref, l1_ref)):
            chosen = bucket_line(l_ref[0:1, :], number)
            sums = t_ref[:, 0, :]
            high = sums.astype(BF)
            rest = (sums - high.astype(F32)).astype(BF)
            both = mm(jnp.concatenate([high.astype(F32), rest.astype(F32)], 0).astype(BF), chosen, NT)
            table = both[:count] + both[count:]
            tables.append(table)
        blank = jnp.zeros((count, number), F32)
        tables = tables if apart else ordered(tables[0] + tables[1], blank)
        table = jnp.concatenate([*tables, jnp.zeros((16 - 2 * count, number), F32)], 0)
        table = jnp.concatenate([table, jnp.zeros((16, 4 * TILE - number), F32)], 1)
        table = jnp.concatenate([table[:, i * TILE : (i + 1) * TILE] for i in range(4)], 0)
        columns = []
        for j in (0, 2):
            a, b = (jnp.sum(d_ref[j].astype(F32), 0, keepdims=True) for d_ref in (d0_ref, d1_ref))
            columns.append(jnp.concatenate([a, b] if apart else ordered(a + b, jnp.zeros_like(a)), 1))
        ups = []
        for f in range(2):
            here = [ref[...] for ref in up_refs[f * n_up : (f + 1) * n_up]]
            ups += here if apart else ordered(here[0], jnp.zeros_like(here[0]))
        acc_ref[...] = part_ref[...].astype(F32) + sum(mm(d0_ref[j], w_ref[j], NT) for j in range(3))
        totals = [jnp.zeros((1, model), F32) for _ in range(2)]
        for r in range(0, rows, CHUNK):
            block = slice(r, r + CHUNK)
            up = acc_ref[block, :]
            grad, gain_terms = norm_back(x_ref[block, :].astype(F32), up, vec_ref[0:1, :])
            gx_ref[block, :] = gres_ref[block, :] + grad
            totals[0] += jnp.sum(gain_terms, 0, keepdims=True)
            totals[1] += jnp.sum(up, 0, keepdims=True)
        sums = jnp.concatenate(
            totals
            + columns
            + [s2_ref[2:3, :], s2_ref[0:1, :], s2_ref[1:2, :], s2_ref[3:4, :]]
            + ups
            + [jnp.zeros((4, model), F32)],
            0,
        )
        if offsets is None:
            sums_ref[...] = sums
            table_ref[...] = table
            return
        for i, ref in enumerate((sums_ref, table_ref)):
            for s in range(half):
                moved = pltpu.roll(sums, lax.rem(model - offs_ref[i * half + s], model), 1)
                ref[16 * s : 16 * s + 16, :] = moved[:, :TILE].astype(BF)
            ref[16 * half :, :] = table.astype(BF)

    half = 0 if offsets is None else offsets.shape[0] // 2
    late = [VMEM((16 * half + 64, TILE), BF)] * 2
    plain = [jax.ShapeDtypeStruct((16, model), F32), jax.ShapeDtypeStruct((64, TILE), F32)]
    shapes = [jax.ShapeDtypeStruct((rows, model), F32), *(plain if offsets is None else late)]
    return pl.pallas_call(
        kernel,
        grid=(1,),
        in_specs=[
            smem_spec(),
            whole((3, rows, width)),
            whole((3, rows, width)),
            whole((rows, model)),
            whole((rows, model)),
            whole((rows, model)),
            whole((16, model)),
            whole((3, model, width)),
            whole((8, model)),
            whole((count, 1, span)),
            whole((count, 1, span)),
            whole((8, span)),
            whole((8, span)),
            *[whole((1, model))] * (2 * n_up),
            smem_spec(),
        ],
        out_specs=[whole(one.shape) for one in shapes],
        out_shape=shapes,
        scratch_shapes=[VMEM((rows, model), F32)],
        compiler_params=params(14),
        cost_estimate=cost(5),
        name="first_norm_back",
    )(
        core, *grads, part, tokens, grad_residual, vec, weights, sums_second, *diags, *lines, *sums_up[0], *sums_up[1],
        core if offsets is None else offsets,
    )


def pack_blocks(core, lengths, buckets, qkv, out, up):
    local, model = out.shape
    width = model // 2
    unit = local * 2
    chips = up.shape[1] // (4 * unit)
    rows = buckets.shape[1]

    def kernel(core_ref, len_ref, buckets_hbm, qkv_hbm, out_hbm, up_hbm, a0_ref, a1_ref, u0_ref, u1_ref, line_ref,
               first_ref, last_ref, qkv_ref, out_ref, up_ref, sems):
        copies = [
            pltpu.make_async_copy(source, target, sems.at[i])
            for i, (source, target) in enumerate(
                (
                    (qkv_hbm, qkv_ref),
                    (out_hbm, out_ref),
                    (up_hbm, up_ref),
                    (buckets_hbm.at[pl.ds(0, 1), pl.ds(0, 8)], first_ref),
                    (buckets_hbm.at[pl.ds(0, 1), pl.ds(rows - 8, 8)], last_ref),
                )
            )
        ]
        for c in copies:
            c.start()
        for c in copies:
            c.wait()
        core_at = core_ref[0]
        for h, a_ref in enumerate((a0_ref, a1_ref)):
            at = (core_at ^ h) * width
            for j in range(3):
                a_ref[j] = qkv_ref[:, pl.ds(pl.multiple_of(j * model + at, TILE), width)]
            a_ref[3] = out_ref[:, pl.ds(pl.multiple_of(at, TILE), width)]
        first = core_at == 0
        ahead = pltpu.roll(last_ref[0, 7:8, :].astype(F32), 1, 1)
        line = jnp.concatenate([ahead, first_ref[0, 0:1, :].astype(F32)], 1)
        live = jnp.zeros_like(line) + len_ref[0].astype(F32)
        line_ref[...] = jnp.concatenate([line, live, jnp.zeros((6, 2 * rows), F32)], 0)
        for f in range(2):
            by_core = []
            for c in range(2):
                by_core.append(
                    jnp.concatenate(
                        [
                            up_ref[:, ((2 * chip + c) * 2 + f) * unit : ((2 * chip + c) * 2 + f + 1) * unit]
                            for chip in range(chips)
                        ],
                        1,
                    ).astype(F32)
                )
            u0_ref[f] = jnp.where(first, by_core[0], by_core[1]).astype(BF)
            u1_ref[f] = jnp.where(first, by_core[1], by_core[0]).astype(BF)

    shapes = [
        *[VMEM((4, local, width), BF)] * 2,
        *[VMEM((2, local, model), BF)] * 2,
        VMEM((8, 2 * rows), F32),
    ]
    return pl.pallas_call(
        kernel,
        grid=(1,),
        in_specs=[
            smem_spec(),
            smem_spec(),
            *[hbm_spec()] * 4,
        ],
        out_specs=[whole(one.shape) for one in shapes],
        out_shape=shapes,
        scratch_shapes=[
            VMEM((1, 8, rows), jnp.int32),
            VMEM((1, 8, rows), jnp.int32),
            VMEM(qkv.shape, BF),
            VMEM(out.shape, BF),
            VMEM(up.shape, BF),
            pltpu.SemaphoreType.DMA((5,)),
        ],
        compiler_params=params(6),
        cost_estimate=cost(1.5),
        name="pack_blocks",
    )(core, lengths, in_hbm(buckets), in_hbm(qkv), in_hbm(out), in_hbm(up))


def pack_vectors(core, vectors):
    _, local = vectors.shape

    def kernel(core_ref, vec_ref, small_ref):
        first = core_ref[0] == 0
        values = jnp.concatenate(
            [vec_ref[...].astype(F32), jnp.zeros((VECTORS + 4, TILE - local), F32)], 1
        )
        moved = pltpu.roll(values, local, 1)
        lines = [jnp.where(first, values[:VECTORS], moved[:VECTORS])]
        for f in range(2):
            at = VECTORS + 2 * f
            both = values[at : at + 1] + moved[at + 1 : at + 2]
            blank = jnp.zeros_like(both)
            lines += [jnp.where(first, both, blank), jnp.where(first, blank, both)]
        small_ref[...] = jnp.concatenate(lines + [jnp.zeros((4, TILE), F32)], 0).astype(BF)

    return pl.pallas_call(
        kernel,
        grid=(1,),
        in_specs=[smem_spec(), whole(vectors.shape)],
        out_specs=whole((16, TILE)),
        out_shape=VMEM((16, TILE), BF),
        compiler_params=params(4),
        cost_estimate=cost(1),
        name="pack_vectors",
    )(core, vectors)


def ordered_rows(core_at, mine, theirs):
    first = core_at == 0
    a, b = mine.astype(F32), theirs.astype(F32)
    return jnp.concatenate([jnp.where(first, a, b), jnp.where(first, b, a)], 0)


def merge_attention(core, mine, theirs, small, small_theirs):
    count, local, width = mine.shape

    def kernel(core_ref, a_ref, b_ref, s_ref, t_ref, out_ref):
        for j in range(count):
            out_ref[2 * local * j : 2 * local * (j + 1), :] = ordered_rows(core_ref[0], a_ref[j], b_ref[j]).astype(BF)
        vec = s_ref[...].astype(F32) + t_ref[...].astype(F32)
        out_ref[2 * local * count :, :] = jnp.concatenate([vec, jnp.zeros((16, width - TILE), F32)], 1).astype(BF)

    return pl.pallas_call(
        kernel,
        grid=(1,),
        in_specs=[smem_spec(), *[whole(mine.shape)] * 2, *[whole(small.shape)] * 2],
        out_specs=whole((2 * local * count + 16, width)),
        out_shape=VMEM((2 * local * count + 16, width), BF),
        compiler_params=params(4),
        cost_estimate=cost(1),
        name="merge_attention",
    )(core, mine, theirs, small, small_theirs)


def merge_feed_forward(core, mine, theirs, down):
    _, local, model = mine.shape
    unit = 2 * local
    width = model // 2

    def kernel(core_ref, a_ref, b_ref, d_ref, *outs):
        for f in range(2):
            up = ordered_rows(core_ref[0], a_ref[f], b_ref[f]).astype(BF)
            low = d_ref[f * unit : (f + 1) * unit, :]
            for j, block in enumerate((up[:, :width], up[:, width:], low[:, :width], low[:, width:])):
                outs[f][j * unit : (j + 1) * unit, :] = block

    shape = VMEM((4 * unit, width), BF)
    return pl.pallas_call(
        kernel,
        grid=(1,),
        in_specs=[smem_spec(), *[whole(mine.shape)] * 2, whole(down.shape)],
        out_specs=[whole(shape.shape)] * 2,
        out_shape=[shape] * 2,
        compiler_params=params(4),
        cost_estimate=cost(1),
        name="merge_feed_forward",
    )(core, mine, theirs, down)


def pair_sum(refs):
    parts = [ref[...].astype(F32) for ref in refs]
    while len(parts) > 1:
        half = len(parts) // 2
        parts = [parts[i] + parts[i + half] for i in range(half)]
    return parts[0]


def rows_of(total, first, core_at, local, mine):
    a, b = total[first : first + local], total[first + local : first + 2 * local]
    return jnp.where((core_at == 0) == mine, a, b)


def total_attention(core, parts, local):
    tall, width = parts[0].shape
    tail = tall - 8 * local

    def kernel(core_ref, *refs):
        ins, (mine_ref, sent_ref) = refs[: len(parts)], refs[len(parts) :]
        total = pair_sum(ins)
        for j in range(4):
            mine_ref[j] = rows_of(total, 2 * local * j, core_ref[0], local, True)
            theirs = rows_of(total, 2 * local * j, core_ref[0], local, False)
            sent_ref[j] = jnp.concatenate([theirs, jnp.zeros((tail - local, width), F32)], 0).astype(BF)
        sent_ref[4] = total[8 * local :].astype(BF)

    shapes = [
        VMEM((4, local, width), F32),
        VMEM((5, tail, width), BF),
    ]
    return pl.pallas_call(
        kernel,
        grid=(1,),
        in_specs=[smem_spec(), *[whole(one.shape) for one in parts]],
        out_specs=[whole(one.shape) for one in shapes],
        out_shape=shapes,
        compiler_params=params(6),
        cost_estimate=cost(1),
        name="total_attention",
    )(core, *parts)


def finish_attention(core, mine, sent, theirs, heads, number):
    _, local, width = mine.shape
    model = 2 * width

    def kernel(core_ref, a_ref, s_ref, b_ref, qkv_ref, out_ref, table_ref, *small_refs):
        at = core_ref[0]
        for h, ref in enumerate((a_ref, b_ref)):
            for j in range(3):
                cols = pl.ds(pl.multiple_of(j * model + (at ^ h) * width, TILE), width)
                qkv_ref[:, cols] = ref[j, :local, :].astype(F32)
            out_ref[:, pl.ds(pl.multiple_of((at ^ h) * width, TILE), width)] = ref[3, :local, :].astype(F32)
        total = s_ref[4].astype(F32) + b_ref[4].astype(F32)
        small = total[:16, :TILE]
        small = jnp.where(at == 0, small, jnp.concatenate([pltpu.roll(small[:8], TILE - local, 1), small[8:]], 0))
        for i in range(VECTORS):
            small_refs[i][...] = small[i : i + 1, :local]
        ups = [jnp.where(at == 0, small[8 + 2 * f : 9 + 2 * f], small[9 + 2 * f : 10 + 2 * f]) for f in range(2)]
        lane = lax.broadcasted_iota(jnp.int32, (1, TILE), 1)
        both = jnp.where(lane < 2 * local, ups[0], pltpu.roll(ups[1], 2 * local, 1))
        small_refs[VECTORS][...] = both[:, : 4 * local]
        table_ref[...] = jnp.concatenate([total[:16, TILE:], total[16:, : 2 * TILE]], 1)[:heads, :number]

    shapes = [
        jax.ShapeDtypeStruct((local, 3 * model), F32),
        jax.ShapeDtypeStruct((local, model), F32),
        jax.ShapeDtypeStruct((heads, number), F32),
        *[jax.ShapeDtypeStruct((1, local), F32)] * VECTORS,
        jax.ShapeDtypeStruct((1, 4 * local), F32),
    ]
    return pl.pallas_call(
        kernel,
        grid=(1,),
        in_specs=[smem_spec(), *[whole(one.shape) for one in (mine, sent, theirs)]],
        out_specs=[whole(one.shape) for one in shapes],
        out_shape=shapes,
        compiler_params=params(6),
        cost_estimate=cost(1),
        name="finish_attention",
    )(core, mine, sent, theirs)


def total_feed_forward(core, parts, local):
    _, width = parts[0].shape
    model = 2 * width
    unit = 2 * local

    def kernel(core_ref, *refs):
        ins, (mine_ref, sent_ref, down_ref) = refs[: len(parts)], refs[len(parts) :]
        total = pair_sum(ins)
        for h in range(2):
            cols = slice(h * width, (h + 1) * width)
            mine_ref[:, cols] = rows_of(total, h * unit, core_ref[0], local, True)
            sent_ref[:, cols] = rows_of(total, h * unit, core_ref[0], local, False).astype(BF)
            down_ref[:, cols] = total[(2 + h) * unit : (3 + h) * unit]

    shapes = [
        jax.ShapeDtypeStruct((local, model), F32),
        jax.ShapeDtypeStruct((local, model), BF),
        jax.ShapeDtypeStruct((unit, model), F32),
    ]
    return pl.pallas_call(
        kernel,
        grid=(1,),
        in_specs=[smem_spec(), *[whole(one.shape) for one in parts]],
        out_specs=[whole(one.shape) for one in shapes],
        out_shape=shapes,
        compiler_params=params(6),
        cost_estimate=cost(1),
        name="total_feed_forward",
    )(core, *parts)


def finish_feed_forward(core, mine, theirs, downs):
    local, model = mine[0].shape
    unit = 2 * local
    chips = model // unit

    def kernel(core_ref, m0, m1, t0, t1, d0, d1, up_ref, down_ref):
        first = core_ref[0] == 0
        by = []
        for a, b in ((m0, t0), (m1, t1)):
            a, b = a[...], b[...].astype(F32)
            by.append((jnp.where(first, a, b), jnp.where(first, b, a)))
        up_ref[...] = jnp.concatenate(
            [
                by[f][c][:, chip * unit : (chip + 1) * unit]
                for chip in range(chips)
                for c in range(2)
                for f in range(2)
            ],
            1,
        )
        down_ref[:unit, :] = d0[...]
        down_ref[unit:, :] = d1[...]

    shapes = [jax.ShapeDtypeStruct((local, 4 * model), F32), jax.ShapeDtypeStruct((2 * unit, model), F32)]
    ins = (*mine, *theirs, *downs)
    return pl.pallas_call(
        kernel,
        grid=(1,),
        in_specs=[smem_spec(), *[whole(one.shape) for one in ins]],
        out_specs=[whole(one.shape) for one in shapes],
        out_shape=shapes,
        compiler_params=params(6),
        cost_estimate=cost(1),
        name="finish_feed_forward",
    )(core, *ins)


VECTORS = 8


class Order:
    def __init__(self, token):
        self.token = token

    def go(self, *values):
        out, _ = lax.optimization_barrier((values, self.token))
        return out if len(out) > 1 else out[0]

    def mark(self, *values):
        out, self.token = lax.optimization_barrier((values, self.token))
        return out if len(out) > 1 else out[0]


class GridLinks:
    pair = True

    def __init__(self, sizes, model):
        self.ny, self.nz, self.nx = sizes
        self.chips = self.ny * self.nz * self.nx
        self.rows = model // self.chips
        dp, inner = lax.axis_index("dp"), lax.axis_index("fsdp")
        self.core = inner % 2
        chip = inner // 2
        self.place = (dp, chip // self.nx, chip % self.nx)
        self.gather_offsets = self._offsets(self.core, -1, (range(self.nz),))
        self.early_offsets = self._offsets(self.core, -1, ((0, 1, 3, 2),))
        self.scatter_offsets = self._offsets(self.core, 1, (range(self.nz),))
        self.last_offsets = self._offsets(self.core, 1, (range(1, self.nz), (0,)))
        self.last_counts = (self.nz - 1,) * 4 + (2, 2)

    def _offsets(self, core, sign, parts):
        y, z, x = self.place
        out = []
        for part in parts:
            for r1 in range(2):
                for r2 in range(2):
                    for k in part:
                        fy = jnp.where(core == 0, r1, r2)
                        fx = jnp.where(core == 0, r2, r1)
                        zz = (z + sign * k + self.nz) % self.nz
                        out.append(((y ^ fy) * self.nz + zz) * self.nx + (x ^ fx))
        return (jnp.stack(out) * self.rows).astype(jnp.int32)

    def _send(self, value, move):
        pairs = []
        for y in range(self.ny):
            for z in range(self.nz):
                for x in range(self.nx):
                    for c in range(2):
                        source = ((y * self.nz + z) * self.nx + x) * 2 + c
                        ty, tz, tx, tc = move(y, z, x, c)
                        pairs.append((source, ((ty * self.nz + tz) * self.nx + tx) * 2 + tc))
        return lax.ppermute(value, AXES, pairs)

    def swap(self, value):
        return self._send(value, lambda y, z, x, c: (y, z, x, 1 - c))

    def along_z(self, value, k):
        return self._send(value, lambda y, z, x, c: (y, (z + k) % self.nz, x, c))

    def x_first(self, value):
        return self._send(value, lambda y, z, x, c: (y, z, 1 - x, c) if c == 0 else (1 - y, z, x, c))

    def y_first(self, value):
        return self._send(value, lambda y, z, x, c: (y, z, 1 - x, c) if c == 1 else (1 - y, z, x, c))


def small_kernel(kernel, name, shapes, *ins):
    return pl.pallas_call(
        kernel,
        grid=(1,),
        in_specs=[whole(one.shape) for one in ins],
        out_specs=[whole(shape) for shape in shapes],
        out_shape=[VMEM(shape, BF) for shape in shapes],
        compiler_params=params(4),
        cost_estimate=cost(1),
        name=name,
    )(*ins)


def stack_blocks(*blocks):
    def kernel(*refs):
        for i, ref in enumerate(refs[:-1]):
            refs[-1][i] = ref[...]

    return small_kernel(kernel, "stack_blocks", [(len(blocks), *blocks[0].shape)], *blocks)[0]


def join_blocks(first, last):
    n = first.shape[0]

    def kernel(first_ref, last_ref, out_ref):
        out_ref[:n] = first_ref[...]
        out_ref[n:] = last_ref[...]

    return small_kernel(kernel, "join_blocks", [(n + last.shape[0], *first.shape[1:])], first, last)[0]


def add_low(a, b):
    return (a.astype(F32) + b.astype(F32)).astype(BF)


def fold(keep, moved):
    n = keep.shape[0] // 2

    def kernel(keep_ref, moved_ref, *outs):
        for s in range(2 * n):
            outs[s // n][s % n] = add_low(keep_ref[s], moved_ref[s])

    return small_kernel(kernel, "fold", [(n, *keep.shape[1:])] * 2, keep, moved)


def add_blocks(a, b):
    def kernel(a_ref, b_ref, out_ref):
        for i in range(a.shape[0]):
            out_ref[i] = add_low(a_ref[i], b_ref[i])

    return small_kernel(kernel, "add_blocks", [a.shape], a, b)[0]


def fold_late(keep, moved, slots):
    half = 8 * slots

    def kernel(keep_ref, moved_ref, *outs):
        total = add_low(keep_ref[...], moved_ref[...])
        for i, out in enumerate(outs):
            out[:half, :] = total[i * half : (i + 1) * half]
            out[half:, :] = total[2 * half :]

    return small_kernel(kernel, "fold_late", [(half + keep.shape[0] - 2 * half, TILE)] * 2, keep, moved)


def fold_last(blocks, late=None, first=0):
    n, tall, wide = blocks[0].shape
    count = len(blocks)
    tail = 0 if late is None else 32

    def kernel(*refs):
        outs = refs[-n:]
        for s in range(n):
            total = sum(ref[s].astype(F32) for ref in refs[:count])
            outs[s][:tall, :] = total.astype(BF)
        if tail:
            total = add_low(refs[count][...], refs[count + 1][...])
            at = total.shape[0] - 64
            blocks = [total[at + 16 * i : at + 16 * i + 16] for i in range(4)]
            for s in range(n):
                small = total[16 * (first + s) : 16 * (first + s) + 16]
                outs[s][tall : tall + 16, :] = jnp.concatenate([small, *blocks[:2]], 1)
                outs[s][tall + 16 :, :] = jnp.concatenate([*blocks[2:], jnp.zeros_like(small)], 1)

    return small_kernel(kernel, "fold_last", [(tall + tail, wide)] * n, *blocks, *(late or ()))


def on_device(
    links,
    tokens,
    lengths,
    buckets,
    ln1_gain,
    ln1_bias,
    qkv_weight,
    q_bias,
    v_bias,
    out_weight,
    out_bias,
    rel_table,
    ln2_gain,
    ln2_bias,
    up_weight,
    up_bias,
    down_weight,
    down_bias,
    cotangent,
):
    rows, model = tokens.shape
    heads, number = rel_table.shape
    head_size = model // heads
    width = model // 2
    local = qkv_weight.shape[0]
    core, chips = links.core, links.chips
    core_arg = core.astype(jnp.int32).reshape(1)

    order = Order(core_arg)
    a_mine, a_sent, u_mine, u_sent, line = pack_blocks(
        core_arg, lengths, buckets, qkv_weight, out_weight, up_weight
    )
    a_mine, a_sent, ln1_gain = order.mark(a_mine, a_sent, ln1_gain)
    vectors = jnp.stack(
        [ln1_gain, ln1_bias, q_bias, v_bias, out_bias, ln2_gain, ln2_bias, down_bias]
        + [up_bias[i * local : (i + 1) * local] for i in range(4)]
    )
    small = pack_vectors(core_arg, vectors)
    a_theirs, small_theirs = links.swap(a_sent), links.swap(small)
    line_other, tokens_other, u_theirs = links.swap(line), links.swap(tokens), links.swap(u_sent)
    early_offsets, gather_offsets = links.early_offsets, links.gather_offsets
    scatter_offsets, last_offsets = links.scatter_offsets, links.last_offsets
    a_piece = merge_attention(core_arg, a_mine, a_theirs, small, small_theirs)
    a_piece, line_other, tokens_other, u_theirs, early_offsets, gather_offsets, scatter_offsets, last_offsets = order.mark(
        a_piece, line_other, tokens_other, u_theirs, early_offsets, gather_offsets, scatter_offsets, last_offsets
    )

    z_parts = [links.along_z(a_piece, k) for k in (1, 3, 2)]
    near = a_piece[None]
    second, third = links.x_first(near), links.y_first(near)
    tiles, grad_rows = bias_tiles(core_arg, (line, line_other), rel_table, cotangent, lengths, (0, 0))
    tiles, grad_rows, z_parts[:2], second, third, a_piece = order.mark(
        tiles, grad_rows, z_parts[:2], second, third, a_piece
    )
    z_parts[2] = links.along_z(a_piece, 2)
    f0, f1 = merge_feed_forward(core_arg, u_mine, order.go(u_theirs), down_weight)
    f_early = [[go(f[None]) for go in (links.x_first, links.y_first)] for f in (f0, f1)]
    f0, f1, z_parts[2], f_early = order.mark(f0, f1, z_parts[2], f_early)
    near_last = stack_blocks(*z_parts)
    second_last, third_last = links.x_first(near_last), links.y_first(near_last)
    f0_z = [links.along_z(order.go(f0), k) for k in (1, 3, 2)]
    second_last, third_last, f0_z[:2] = order.mark(second_last, third_last, f0_z[:2])
    fourth = links.y_first(join_blocks(second, second_last))
    f1_z = [links.along_z(order.go(f1), k) for k in (1, 3)]
    grad_rows_other = links.swap(grad_rows)
    fourth, grad_rows_other, f0_z[2] = order.mark(fourth, grad_rows_other, f0_z[2])
    parts = [near, near_last, second, second_last, third, third_last, fourth]
    own, own_out, vec = order.mark(*assemble_attention(Pieces(parts, early_offsets, links.rows), model))
    f1_z = order.mark(f1_z)
    f0_near = stack_blocks(f0_z[0], f0_z[2], f0_z[1])
    f0_second, f0_third = links.x_first(f0_near), links.y_first(f0_near)
    f1_z.append(links.along_z(order.go(f1), 2))
    other_out = links.swap(own_out)

    normed_other, joined1, mixed1, probs1, full1 = attention_forward(
        1, 0, core_arg, tokens_other, vec, order.go(own), tiles, line_other, head_size
    )
    mixed1, other_out, f1_z = order.mark(mixed1, other_out, f1_z)
    mixed_rest = links.swap(mixed1)
    f0_second, f0_third = order.mark(f0_second, f0_third)
    f0_fourth = links.y_first(join_blocks(f_early[0][0], f0_second))
    f1_near = stack_blocks(f1_z[0], f1_z[2], f1_z[1])
    f1_second = links.x_first(f1_near)
    normed, joined0, mixed0, probs0, full0 = attention_forward(
        0, 0, core_arg, tokens, vec, order.go(own), tiles, line, head_size
    )
    mixed0, mixed_rest = order.mark(mixed0, mixed_rest)
    mixed_rest_other = links.swap(mixed0)
    residual, normed2 = project_out(core_arg, (order.go(mixed0), mixed_rest), tokens, (own_out, other_out), vec)
    normed2, f0_fourth, f1_second, mixed_rest_other = order.mark(normed2, f0_fourth, f1_second, mixed_rest_other)

    normed2_other = links.swap(normed2)
    f1_third, f1_fourth = links.y_first(f1_near), links.y_first(join_blocks(f_early[1][0], f1_second))
    normed2_other = order.mark(normed2_other)

    def chunk(bufs):
        return Pieces(bufs, gather_offsets, links.rows)

    (own0, other0), sums_f0, (keep0, send0) = feed_forward(
        lambda c: 8 + c, core_arg,
        [(normed2, grad_rows, residual, None), (normed2_other, grad_rows_other, None, None)],
        vec, chunk([f0[None], f0_near, f_early[0][0], f0_second, f_early[0][1], f0_third, f0_fourth]), scatter_offsets,
    )
    own0, other0, keep0, send0, f1_third, f1_fourth = order.mark(own0, other0, keep0, send0, f1_third, f1_fourth)
    moved0 = links.y_first(send0)
    (own1, other1), sums_f1, (keep1, send1) = feed_forward(
        lambda c: 10 + c, core_arg,
        [(normed2, grad_rows, own0[0], own0[1]), (normed2_other, grad_rows_other, other0[0], other0[1])],
        vec, chunk([f1[None], f1_near, f_early[1][0], f1_second, f_early[1][1], f1_third, f1_fourth]), scatter_offsets,
    )
    own1, other1, keep1, send1, moved0 = order.mark(own1, other1, keep1, send1, moved0)
    keep0, send0 = fold(keep0, moved0)
    moved0 = links.x_first(send0)
    result_rest, grad_rest = links.swap(other1[0]), links.swap(other1[1])
    result_rest, grad_rest = order.mark(result_rest, grad_rest)
    moved1 = links.y_first(order.go(send1))
    output, grad_res, gm0, branch_cols, sent, sums2 = second_norm_back(
        core_arg, residual, (order.go(own1[0]), result_rest), (own1[1], grad_rest), grad_rows,
        (own_out, other_out), vec, lengths,
    )
    sent, moved0 = order.mark(sent, moved0)
    got = links.swap(sent)
    sums0 = fold_last((keep0, moved0))
    parts0 = [sums0[0]] + [links.along_z(sums0[k], k) for k in (1, 3)]
    dj0, diag0 = attention_backward(joined0, probs0, full0, order.go(gm0), head_size)
    dj0, got, moved1, parts0 = order.mark(dj0, got, moved1, parts0)
    parts0.insert(2, links.along_z(order.go(sums0[2]), 2))
    keep1, send1 = fold(keep1, moved1)
    moved1 = links.x_first(send1)
    dj1, diag1, part, keep, keep_next, send, send_next, own_keep, own_send = attention_backward(
        joined1, probs1, full1, order.go(got), head_size,
        Products(
            core_arg,
            [([(normed, None), (normed_other, None)], [(dj0, j), (None, j)]) for j in range(3)]
            + [([((mixed0, mixed_rest), None), ((mixed1, mixed_rest_other), None)], [(branch_cols, None), (got, 1)])],
            last_offsets,
            links.rows,
            links.last_counts,
        ),
        own,
    )
    part, keep, keep_next, send, send_next, own_keep, own_send, moved1, parts0 = order.mark(
        part, keep, keep_next, send, send_next, own_keep, own_send, moved1, parts0
    )
    part_rest = links.swap(part)
    next_moved, moved = links.y_first(send_next), links.y_first(send)
    part_rest, keep1, moved1 = order.mark(part_rest, keep1, moved1)
    sums1 = fold_last((keep1, moved1))
    parts1 = [sums1[0]] + [links.along_z(sums1[k], k) for k in (1, 3)]
    input_grad, late_keep, late_send = first_norm_back(
        core_arg, (order.go(dj0), dj1), part_rest, tokens, grad_res, vec, own, sums2, ([sums_f0], [sums_f1]),
        (diag0, diag1), (line, line_other), number, False, scatter_offsets,
    )
    late_keep, late_send, next_moved, parts1 = order.mark(late_keep, late_send, next_moved, parts1)
    late_moved = links.y_first(late_send)
    parts1.insert(2, links.along_z(order.go(sums1[2]), 2))
    next_moved = links.x_first(add_blocks(keep_next, next_moved))
    late_moved, moved = order.mark(late_moved, moved)
    late_keep, late_send = fold_late(late_keep, late_moved, 2 * links.nz)
    late_moved = links.x_first(late_send)
    next_moved, late_moved, own_send, parts1 = order.mark(next_moved, late_moved, own_send, parts1)
    sums = fold_last((keep, moved, next_moved), (late_keep, late_moved), 1)
    parts = [links.along_z(sums[k - 1], k) for k in (1, 2, 3)]
    own_moved = links.y_first(own_send)
    ffn0 = total_feed_forward(core_arg, order.go(parts0), local)
    ffn1 = total_feed_forward(core_arg, order.go(parts1), local)
    ffn0, ffn1, own_moved = order.mark(ffn0, ffn1, own_moved)
    own_keep, own_send = fold(own_keep, own_moved)
    own_moved = links.x_first(own_send)
    ups = [links.swap(ffn0[1]), links.swap(ffn1[1])]
    grad_up, grad_down = finish_feed_forward(
        core_arg, [ffn0[0], ffn1[0]], ups, [ffn0[2], ffn1[2]]
    )
    grad_up, grad_down, parts, own_moved = order.mark(grad_up, grad_down, parts, own_moved)
    parts = [*fold_last((own_keep, own_moved), (late_keep, late_moved)), *parts]
    mine, sent = total_attention(core_arg, parts, local)
    theirs = links.swap(sent)
    grad_qkv, grad_out, grad_table, *small_grads = finish_attention(
        core_arg, mine, sent, theirs, heads, number
    )
    small_grads = [one.reshape(-1) for one in small_grads]
    grad_up_bias = small_grads[VECTORS]

    return (
        output,
        input_grad,
        small_grads[0],
        small_grads[1],
        grad_qkv,
        small_grads[2],
        small_grads[3],
        grad_out,
        small_grads[4],
        grad_table,
        small_grads[5],
        small_grads[6],
        grad_up,
        grad_up_bias,
        grad_down,
        small_grads[7],
    )


def on_any_mesh(
    tokens,
    lengths,
    buckets,
    ln1_gain,
    ln1_bias,
    qkv_weight,
    q_bias,
    v_bias,
    out_weight,
    out_bias,
    rel_table,
    ln2_gain,
    ln2_bias,
    up_weight,
    up_bias,
    down_weight,
    down_bias,
    cotangent,
):
    rows, model = tokens.shape
    heads, number = rel_table.shape
    head_size = model // heads
    width = model // 2
    local = qkv_weight.shape[0]
    hidden = up_weight.shape[1]
    core = jnp.zeros((1,), jnp.int32)
    offsets = jnp.zeros((1,), jnp.int32)

    def gathered(x):
        return lax.all_gather(x, AXES, axis=0, tiled=True)

    def scattered(x):
        return lax.psum_scatter(x, AXES, scatter_dimension=0, tiled=True)

    vectors = [ln1_gain, ln1_bias, q_bias, v_bias, out_bias, ln2_gain, ln2_bias, down_bias]
    unit = up_bias.shape[0]
    small = gathered(jnp.concatenate([*vectors, up_bias])[None, :])
    wide = [small[:, i * local : (i + 1) * local].reshape(1, model) for i in range(VECTORS)]
    ub = small[:, VECTORS * local :].reshape(2, 2, model).transpose(1, 0, 2).reshape(4, model)
    del unit
    vec = jnp.concatenate([*wide, ub, jnp.zeros((4, model), BF)], 0).astype(F32)
    attn = gathered(jnp.concatenate([qkv_weight, out_weight], 1))
    up, down = gathered(up_weight), gathered(down_weight)
    a_pieces = tuple(
        jnp.stack([attn[:, j * model + h * width : j * model + (h + 1) * width] for j in range(3)])
        for h in range(2)
    )

    a_out = tuple(attn[:, 3 * model + h * width : 3 * model + (h + 1) * width] for h in range(2))

    def chunk(f, h):
        at = (2 * h + f) * model
        blocks = [one[:, k * width : (k + 1) * width] for one in (up[:, at : at + model], down[at : at + model]) for k in range(2)]
        return Pieces([jnp.concatenate(blocks, 0)[None]], offsets, model)

    ahead = jnp.roll(buckets[0, rows - 1], 1)
    line = jnp.concatenate([ahead, buckets[0, 0]]).astype(F32)
    line = jnp.stack([line, jnp.full_like(line, lengths[0])] + [jnp.zeros_like(line)] * 6)
    tiles, grad_rows = bias_tiles(core, (line, line), rel_table, cotangent, lengths, (0, 1))
    normed, joined0, mixed0, probs0, full0 = attention_forward(0, 0, core, tokens, vec, a_pieces[0], tiles, line, head_size)
    _, joined1, mixed1, probs1, full1 = attention_forward(1, 1, core, tokens, vec, a_pieces[1], tiles, line, head_size)
    residual, normed2 = project_out(core, (mixed0, mixed1), tokens, a_out, vec)
    result, grad_n2 = residual, None
    up_sums, ups, downs = [[], []], [], []
    for f in range(2):
        for h in range(2):
            ((result, grad_n2, active, grad_pre),), sums, _ = feed_forward(
                lambda c, at=8 + 2 * f + h: c + at, core, [(normed2, grad_rows, result, grad_n2)], vec, chunk(f, h)
            )
            up_sums[f].append(sums)
            (both,) = outer_products(
                core,
                [([(normed2, None)], [(grad_pre, k)]) for k in range(2)]
                + [([(active, None)], [(grad_rows, k)]) for k in range(2)],
                offsets,
                model,
            )
            both = both[0].reshape(2, 2, model, width).transpose(0, 2, 1, 3).reshape(2, model, model)
            ups.append(both[0])
            downs.append(both[1])
    output, grad_res, gm0, branch0, sent, sums2 = second_norm_back(
        core, residual, (result,), (grad_n2,), grad_rows, a_out, vec, lengths
    )
    dj0, diag0 = attention_backward(joined0, probs0, full0, gm0, head_size)
    dj1, diag1 = attention_backward(joined1, probs1, full1, sent, head_size)
    input_grad, vec_grads, table_grad = first_norm_back(
        core, (dj0, dj1), normed_back(dj1, a_pieces[1]), tokens, grad_res, vec, a_pieces[0], sums2, up_sums,
        (diag0, diag1), (line, line), number, True,
    )
    mixed = jnp.concatenate([mixed0, mixed1], 1)
    halves = [
        outer_products(
            core, [([(normed, None)], [(dj, j)]) for j in range(3)] + [([(mixed, None)], [branch])], offsets, model
        )[0][0].reshape(4, model, width)
        for dj, branch in ((dj0, (branch0, None)), (dj1, (sent, 1)))
    ]
    grads = jnp.stack(halves, 2).transpose(1, 0, 2, 3).reshape(model, 4 * model)
    grads = scattered(grads)
    grad_up = scattered(jnp.concatenate([ups[0], ups[2], ups[1], ups[3]], 1))
    grad_down = scattered(jnp.concatenate([downs[0], downs[2], downs[1], downs[3]], 0))
    by_owner = vec_grads[:VECTORS].reshape(VECTORS, model // local, local).transpose(1, 0, 2)
    own_units = vec_grads[VECTORS : VECTORS + 4].reshape(2, 2, model).transpose(1, 0, 2)
    both = jnp.concatenate(
        [by_owner.reshape(model // local, VECTORS * local), own_units.reshape(model // local, hidden * local // model)],
        1,
    )
    both = scattered(both)[0]
    table = jnp.concatenate([table_grad[16 * i : 16 * i + 16] for i in range(4)], 1)[:heads, :number]
    grad_table = lax.psum(table, AXES)
    small_grads = [both[i * local : (i + 1) * local] for i in range(VECTORS)]
    return (
        output,
        input_grad,
        small_grads[0],
        small_grads[1],
        grads[:, : 3 * model].astype(F32),
        small_grads[2],
        small_grads[3],
        grads[:, 3 * model :].astype(F32),
        small_grads[4],
        grad_table,
        small_grads[5],
        small_grads[6],
        grad_up.astype(F32),
        both[VECTORS * local :],
        grad_down.astype(F32),
        small_grads[7],
    )


def solution(mesh):
    both = P(AXES)
    row = P(AXES, None)
    in_specs = (
        row, both, P(AXES, None, None), both, both, row, both, both, row, both, P(), both, both, row, both, row,
        both, row,
    )
    out_specs = (row, row, both, both, row, both, both, row, both, P(), both, both, row, both, row, both)

    if tuple(mesh.shape[name] for name in AXES) == (2, 16):

        def body(*args):
            return on_device(GridLinks((2, 4, 2), args[0].shape[1]), *args)

    else:
        body = on_any_mesh

    return jax.shard_map(body, mesh=mesh, in_specs=in_specs, out_specs=out_specs, check_vma=False)
```

```python
import functools

import jax
import jax.numpy as jnp
from jax import lax
from jax.experimental import pallas as pl
from jax.experimental.pallas import tpu as pltpu
from jax.sharding import PartitionSpec as P

BF = jnp.bfloat16
F32 = jnp.float32
AXES = ("dp", "fsdp")
TILE = 128
CHUNK = 64
EPS = 1e-05
NN = (((1,), (0,)), ((), ()))
NT = (((1,), (1,)), ((), ()))
TN = (((0,), (0,)), ((), ()))
VMEM = pltpu.VMEM


def mm(left, right, dims=NN):
    return lax.dot_general(left, right, dims, preferred_element_type=F32)


def hbm_spec():
    return pl.BlockSpec(memory_space=pltpu.HBM)


def in_hbm(x):
    return pltpu.with_memory_space_constraint(x, pltpu.HBM)


def smem_spec():
    return pl.BlockSpec(memory_space=pltpu.SMEM)


def whole(shape):
    return pl.BlockSpec(shape, lambda *_: (0,) * len(shape))


def params(mebibytes):
    return pltpu.CompilerParams(
        dimension_semantics=("arbitrary",), vmem_limit_bytes=mebibytes * 1024 * 1024
    )


def cost(micros):
    return pl.CostEstimate(flops=int(micros * 1e9), bytes_accessed=1, transcendentals=0)


class Pieces:
    def __init__(self, buffers, offsets, rows):
        self.buffers = buffers
        self.offsets = offsets
        self.rows = rows

    @property
    def slots(self):
        return sum(b.shape[0] for b in self.buffers)


def lay_blocks(refs, offs_ref, rows, count, put):
    slot = 0
    for ref in refs:
        for k in range(ref.shape[0]):
            at = pl.multiple_of(offs_ref[slot], 16)
            for j in range(count):
                put(j, at, ref[k, j * rows : (j + 1) * rows, :])
            slot += 1


def row_norm(x):
    centre = x - jnp.mean(x, -1, keepdims=True)
    scale = lax.rsqrt(jnp.mean(centre * centre, -1, keepdims=True) + EPS)
    return centre * scale, scale


def bucket_line(line, number):
    rows = lax.broadcasted_iota(jnp.int32, (number, line.shape[1]), 0)
    return jnp.where(rows == line.astype(jnp.int32), 1.0, 0.0).astype(BF)


def bias_tiles(core, lines, table, cotangent, lengths, halves):
    span = lines[0].shape[1]
    heads, number = table.shape
    count = heads // 2
    tiles = span // TILE - 1
    n = len(lines)
    rows, model = cotangent.shape

    def kernel(core_ref, len_ref, table_ref, cot_ref, *refs):
        line_refs, (out_ref, gr_ref, curve_ref) = refs[:n], refs[n:]
        at = pl.program_id(0)

        @pl.when(at == 0)
        def _():
            for i in range(n):
                curve = mm(table_ref[...], bucket_line(line_refs[i][0:1, :], number))
                curve = jnp.where((core_ref[0] ^ halves[i]) == 0, curve[:count], curve[count:])
                for h in range(count):
                    curve_ref[i * count + h] = jnp.broadcast_to(curve[h : h + 1], (8, span))
            row = lax.broadcasted_iota(jnp.int32, (rows, 1), 0)
            gr_ref[...] = jnp.where(row < len_ref[0], cot_ref[...].astype(F32), 0.0).astype(BF)

        base = pltpu.roll(curve_ref[at], 0, 1, stride=1, stride_axis=0)
        for pair in range(TILE // 16):
            rolled = jnp.concatenate(
                [pltpu.roll(base, 16 * pair + 8 * i, 1) if pair + i else base for i in range(2)], 0
            ).astype(BF)
            for d in range(tiles):
                out_ref[0, 0, d, 16 * pair : 16 * pair + 16, :] = rolled[
                    :, TILE * (d + 1) : TILE * (d + 2)
                ]

    return pl.pallas_call(
        kernel,
        grid=(n * count,),
        in_specs=[
            smem_spec(),
            smem_spec(),
            whole((heads, number)),
            whole((rows, model)),
            *[whole((8, span))] * n,
        ],
        out_specs=[
            pl.BlockSpec((1, 1, tiles, TILE, TILE), lambda h: (h // count, h % count, 0, 0, 0)),
            whole((rows, model)),
        ],
        out_shape=[
            VMEM((n, count, tiles, TILE, TILE), BF),
            VMEM((rows, model), BF),
        ],
        scratch_shapes=[VMEM((n * count, 8, span), F32)],
        compiler_params=params(8),
        cost_estimate=cost(4),
        name="bias_tiles",
    )(core, lengths, table, cotangent, *lines)


def place_rows(block, offset, wide):
    padded = jnp.concatenate([block, jnp.zeros((block.shape[0], wide - TILE), block.dtype)], 1)
    return pltpu.roll(padded, offset, 1)


def assemble_attention(pieces, model):
    width = model // 2
    rows = pieces.rows
    n_buf = len(pieces.buffers)

    def kernel(offs_ref, *refs):
        bufs, (w_ref, o_ref, vec_ref) = refs[:n_buf], refs[n_buf:]

        def put(j, at, block):
            if j < 3:
                w_ref[j, pl.ds(at, rows), :] = block
            else:
                o_ref[pl.ds(at, rows), :] = block

        lay_blocks(bufs, offs_ref, rows, 4, put)
        total, slot = jnp.zeros((16, model), F32), 0
        for ref in bufs:
            for k in range(ref.shape[0]):
                total += place_rows(ref[k, 4 * rows : 4 * rows + 16, :TILE].astype(F32), offs_ref[slot], model)
                slot += 1
        vec_ref[...] = total

    return pl.pallas_call(
        kernel,
        grid=(1,),
        in_specs=[smem_spec(), *[whole(one.shape) for one in pieces.buffers]],
        out_specs=[whole((3, model, width)), whole((model, width)), whole((16, model))],
        out_shape=[
            VMEM((3, model, width), BF),
            VMEM((model, width), BF),
            VMEM((16, model), F32),
        ],
        compiler_params=params(6),
        cost_estimate=cost(2),
        name="assemble_attention",
    )(pieces.offsets, *pieces.buffers)


def attention_forward(item, half, core, tokens, vec, weights, tiles, line, head_size):
    rows, model = tokens.shape
    width = model // 2
    heads = width // head_size
    pairs = width // TILE
    per = TILE // head_size
    scale = head_size**-0.5

    def kernel(core_ref, line_ref, x_ref, vec_ref, tile_ref, w_ref, n1_ref, joined_ref, mixed_ref, p_ref, sums_ref, qs_ref, s_ref):
        pair = pl.program_id(0)

        @pl.when(pair == 0)
        def _():
            for r in range(0, rows, CHUNK):
                xhat, _ = row_norm(x_ref[r : r + CHUNK, :].astype(F32))
                n1_ref[r : r + CHUNK, :] = (xhat * vec_ref[0:1, :] + vec_ref[1:2, :]).astype(BF)
            cols = pl.ds(pl.multiple_of((core_ref[0] ^ half) * width, TILE), width)
            for j in range(3):
                joined = mm(n1_ref[...], w_ref[j])
                if j != 1:
                    joined = joined + vec_ref[2 + j // 2 : 3 + j // 2, cols]
                qs_ref[j] = joined.astype(BF)

        lanes = pl.ds(pl.multiple_of(pair * TILE, TILE), TILE)
        q, k, v = (qs_ref[j, :, lanes] for j in range(3))
        for j, one in enumerate((q, k, v)):
            joined_ref[j] = one
        lane = lax.broadcasted_iota(jnp.int32, (1, TILE), 1)
        column = lax.broadcasted_iota(jnp.int32, (1, rows), 1)
        dead = jnp.where(column < line_ref[1:2, :rows].astype(jnp.int32), 0.0, -1e30).astype(F32)
        scaled = q.astype(F32) * scale
        outs = []
        for e in range(per):
            mine = (lane >= e * head_size) & (lane < (e + 1) * head_size)
            qm = jnp.where(mine, scaled, 0.0).astype(BF)
            s_ref[e] = mm(qm, k, NT)
            for r in range(0, rows, CHUNK):
                block, sub = r // TILE, r % TILE
                rel = jnp.concatenate(
                    [
                        tile_ref[0, e, j - block + rows // TILE - 1, sub : sub + CHUNK, :]
                        for j in range(rows // TILE)
                    ],
                    1,
                ).astype(F32)
                s = s_ref[e, r : r + CHUNK, :] + (rel + dead)
                raised = jnp.exp(s - jnp.max(s, -1, keepdims=True))
                inv = 1.0 / jnp.sum(raised, -1, keepdims=True)
                p_ref[e, r : r + CHUNK, :] = (raised * inv).astype(BF)
            outs.append(jnp.where(mine, mm(p_ref[e], v), 0.0))
        mixed = functools.reduce(lambda a, b: a + b, outs)
        sums_ref[...] = mixed
        mixed_ref[...] = mixed.astype(BF)

    shapes = [
        VMEM((3, rows, width), BF),
        VMEM((rows, width), BF),
        VMEM((heads, rows, rows), BF),
        VMEM((rows, width), F32),
    ]
    outs = [
        pl.BlockSpec((3, rows, TILE), lambda p: (0, 0, p)),
        pl.BlockSpec((rows, TILE), lambda p: (0, p)),
        pl.BlockSpec((per, rows, rows), lambda p: (p, 0, 0)),
        pl.BlockSpec((rows, TILE), lambda p: (0, p)),
    ]
    shapes.insert(0, VMEM((rows, model), BF))
    outs.insert(0, whole((rows, model)))
    return pl.pallas_call(
        kernel,
        grid=(pairs,),
        in_specs=[
            smem_spec(),
            whole((8, 2 * rows)),
            whole((rows, model)),
            whole((16, model)),
            pl.BlockSpec((1, per, tiles.shape[2], TILE, TILE), lambda p: (item, p, 0, 0, 0)),
            whole((3, model, width)),
        ],
        out_specs=outs,
        out_shape=shapes,
        scratch_shapes=[VMEM((3, rows, width), BF), VMEM((per, rows, rows), F32)],
        compiler_params=params(12),
        cost_estimate=cost(6),
        name="attention_forward",
    )(core, line, tokens, vec, tiles, weights)


def project_out(core, mixed, tokens, weights, vec):
    rows, model = tokens.shape
    width = model // 2

    def kernel(core_ref, m0_ref, m1_ref, x_ref, vec_ref, w0_ref, w1_ref, res_ref, n2_ref):
        for h, w_ref in enumerate((w0_ref, w1_ref)):
            cols = pl.ds(pl.multiple_of((core_ref[0] ^ h) * width, TILE), width)
            acc = 0.0
            for g, m_ref in enumerate((m0_ref, m1_ref)):
                feats = pl.ds(pl.multiple_of((core_ref[0] ^ g) * width, TILE), width)
                acc = acc + mm(m_ref[...], w_ref[feats, :])
            res_ref[:, cols] = x_ref[:, cols].astype(F32) + acc + vec_ref[4:5, cols]
        for r in range(0, rows, CHUNK):
            xhat, _ = row_norm(res_ref[r : r + CHUNK, :])
            n2_ref[r : r + CHUNK, :] = (xhat * vec_ref[5:6, :] + vec_ref[6:7, :]).astype(BF)

    return pl.pallas_call(
        kernel,
        grid=(1,),
        in_specs=[
            smem_spec(),
            whole((rows, width)),
            whole((rows, width)),
            whole((rows, model)),
            whole((16, model)),
            whole((model, width)),
            whole((model, width)),
        ],
        out_specs=[whole((rows, model)), whole((rows, model))],
        out_shape=[
            VMEM((rows, model), F32),
            VMEM((rows, model), BF),
        ],
        compiler_params=params(6),
        cost_estimate=cost(2.5),
        name="project_out",
    )(core, mixed[0], mixed[1], tokens, vec, *weights)


def gelu_parts(v):
    bell = jnp.exp(-0.5 * (v * v))
    t = 1.0 / (1.0 + 0.23164189 * jnp.abs(v))
    tail = t * (0.127414796 + t * (-0.142248368 + t * (0.710706871 + t * (-0.726576014 + t * 0.530702714))))
    tail = tail * bell
    return jnp.where(v < 0.0, tail, 1.0 - tail), bell * 0.3989422804014327


def feed_forward(row, core, sets, vec, pieces, offsets=None):
    rows, model = sets[0][0].shape
    hidden = model
    n = len(sets)
    n_buf = len(pieces.buffers)
    per = pieces.rows
    half = rows // 2
    width = model // 2

    def kernel(core_ref, offs_ref, out_offs_ref, vec_ref, *refs):
        ins, refs = refs[: len(flat)], refs[len(flat) :]
        bufs, refs = refs[:n_buf], refs[n_buf:]
        outs, refs = refs[: 4 * n], refs[4 * n :]
        col_ref, slot_refs, (up_ref, down_ref, w_ref) = refs[0], refs[1:-3], refs[-3:]

        def put(j, at, block):
            ref = up_ref if j < 2 else down_ref
            ref[pl.ds(at, per), (j % 2) * width : (j % 2 + 1) * width] = block

        lay_blocks(bufs, offs_ref, per, 4, put)
        up_bias = vec_ref[pl.ds(row(core_ref[0]), 1), :]
        sums = jnp.zeros((1, hidden), F32)
        for i in range(n):
            n_ref, gr_ref, res_ref, gin_ref = (None if at is None else ins[at] for at in where[i])
            out_ref, gn_ref, act_ref, gp_ref = outs[4 * i : 4 * i + 4]
            for r in range(0, rows, half):
                block = slice(r, r + half)
                pre = mm(n_ref[block, :], up_ref[...]) + up_bias
                gact = mm(gr_ref[block, :], down_ref[...], NT)
                cdf, density = gelu_parts(pre)
                act = (pre * cdf).astype(BF)
                gp = gact * (cdf + pre * density)
                low = gp.astype(BF)
                act_ref[block, :] = act
                gp_ref[block, :] = low
                sums += jnp.sum(low.astype(F32), 0, keepdims=True)
                out = mm(act, down_ref[...])
                if res_ref is not None:
                    out = out + res_ref[block, :]
                    if gin_ref is None:
                        out = out + vec_ref[7:8, :]
                out_ref[block, :] = out
                gn = mm(low, up_ref[...], NT)
                gn_ref[block, :] = gn if gin_ref is None else gn + gin_ref[block, :]
        col_ref[...] = sums
        if offsets is None:
            return
        for m in range(4):
            cols = slice((m % 2) * width, (m % 2 + 1) * width)
            total = 0.0
            for i in range(n):
                n_ref, gr_ref = (ins[at] for at in where[i][:2])
                act_ref, gp_ref = outs[4 * i + 2 : 4 * i + 4]
                left, right = (n_ref, gp_ref) if m < 2 else (act_ref, gr_ref)
                total = total + mm(left[...], right[:, cols], TN)
            w_ref[...] = total.astype(BF)
            to_slots(w_ref, out_offs_ref, slot_refs, m, per)

    flat, where = [], []
    for one in sets:
        places = []
        for array in one:
            places.append(None if array is None else len(flat))
            if array is not None:
                flat.append(array)
        where.append(places)
    shapes = [
        VMEM((rows, model), F32),
        VMEM((rows, model), F32),
        VMEM((rows, hidden), BF),
        VMEM((rows, hidden), BF),
    ] * n + [VMEM((1, hidden), F32)]
    if offsets is not None:
        shapes += [VMEM((offsets.shape[0] // 2, 4 * per, width), BF)] * 2
    out = pl.pallas_call(
        kernel,
        grid=(1,),
        in_specs=[
            *[smem_spec()] * 3,
            whole((16, model)),
            *[whole((rows, model))] * len(flat),
            *[whole(one.shape) for one in pieces.buffers],
        ],
        out_specs=[whole(one.shape) for one in shapes],
        out_shape=shapes,
        scratch_shapes=[
            VMEM((model, hidden), BF),
            VMEM((hidden, model), BF),
            VMEM((model, width), BF),
        ],
        compiler_params=params(14),
        cost_estimate=cost(13),
        name="feed_forward",
    )(core, pieces.offsets, pieces.offsets if offsets is None else offsets, vec, *flat, *pieces.buffers)
    return [out[4 * i : 4 * i + 4] for i in range(n)], out[4 * n], out[4 * n + 1 :]


def to_slots(w_ref, offs_ref, outs, matrix, rows):
    slot = 0
    for out in outs:
        for k in range(out.shape[0]):
            at = pl.multiple_of(offs_ref[slot], 16)
            out[k, matrix * rows : (matrix + 1) * rows, :] = w_ref[pl.ds(at, rows), :]
            slot += 1


class Products:
    def __init__(self, core, pairs, offsets, rows, counts):
        self.core, self.offsets, self.rows = core, offsets, rows
        self.tall = pairs[0][0][0][0].shape[-1]
        self.wide = self.tall // 2
        self.flat = []
        self.where = [([self._place(*one) for one in lefts], [self._place(*one) for one in rights]) for lefts, rights in pairs]
        self.shapes = [VMEM((count, len(pairs) * rows, self.wide), BF) for count in counts]
        self.scratch = VMEM((self.tall, self.wide), BF)

    def _place(self, one, part):
        if isinstance(one, tuple):
            return [self._place(each, part) for each in one]
        if one is None:
            return None, part
        match = [i for i, known in enumerate(self.flat) if known is one]
        if not match:
            self.flat.append(one)
            match = [len(self.flat) - 1]
        return match[0], part

    def run(self, core_ref, offs_ref, ins, outs, w_ref, own_ref=None):
        def pick(at, part):
            ref = own_ref if at is None else ins[at]
            if part is None:
                return ref[...]
            if len(ref.shape) == 3:
                return ref[part]
            return ref[:, part * self.wide : (part + 1) * self.wide]

        for m, (lefts, rights) in enumerate(self.where):
            if isinstance(lefts[0], list):
                for h in range(2):
                    total = sum(mm(pick(*left[h]), pick(*right), TN) for left, right in zip(lefts, rights))
                    at = pl.multiple_of((core_ref[0] ^ h) * self.wide, 16)
                    w_ref[pl.ds(at, self.wide), :] = total.astype(BF)
            else:
                total = sum(mm(pick(*left), pick(*right), TN) for left, right in zip(lefts, rights))
                w_ref[...] = total.astype(BF)
            to_slots(w_ref, offs_ref, outs, m, self.rows)


def outer_products(core, pairs, offsets, rows):
    work = Products(core, pairs, offsets, rows, offsets.shape)
    n = len(work.flat)

    def kernel(core_ref, offs_ref, *rest):
        work.run(core_ref, offs_ref, rest[:n], rest[n:-1], rest[-1])

    return pl.pallas_call(
        kernel,
        grid=(1,),
        in_specs=[smem_spec(), smem_spec(), *[whole(one.shape) for one in work.flat]],
        out_specs=[whole(one.shape) for one in work.shapes],
        out_shape=work.shapes,
        scratch_shapes=[work.scratch],
        compiler_params=params(14),
        cost_estimate=cost(5),
        name="outer_products",
    )(core, offsets, *work.flat)


def norm_back(x, up, gain):
    xhat, scale = row_norm(x)
    e = up * gain
    grad = scale * (e - jnp.mean(e, -1, keepdims=True) - xhat * jnp.mean(e * xhat, -1, keepdims=True))
    return grad, up * xhat


def second_norm_back(core, residual, results, grads_normed, grad_rows, weights, vec, lengths):
    rows, model = residual.shape
    width = model // 2
    n, m = len(results), len(grads_normed)

    def kernel(core_ref, len_ref, res_ref, gr_ref, vec_ref, w0_ref, w1_ref, *refs):
        out_refs, gn_refs = refs[:n], refs[n : n + m]
        out_ref, gres_ref, gm_ref, br_ref, sent_ref, sums_ref, gb_ref = refs[n + m :]
        totals = [jnp.zeros((1, model), F32) for _ in range(4)]
        for r in range(0, rows, CHUNK):
            block = slice(r, r + CHUNK)
            row = lax.broadcasted_iota(jnp.int32, (CHUNK, 1), 0) + r
            result = functools.reduce(lambda a, b: a + b, [ref[block, :] for ref in out_refs])
            out_ref[block, :] = jnp.where(row < len_ref[0], result, 0.0).astype(BF)
            up = functools.reduce(lambda a, b: a + b, [ref[block, :] for ref in gn_refs])
            grad, gain_terms = norm_back(res_ref[block, :], up, vec_ref[5:6, :])
            gr = gr_ref[block, :].astype(F32)
            grad = gr + grad
            low = grad.astype(BF)
            gres_ref[block, :] = grad
            gb_ref[block, :] = low
            for i, terms in enumerate((gain_terms, up, low.astype(F32), gr)):
                totals[i] += jnp.sum(terms, 0, keepdims=True)
        sums_ref[...] = jnp.concatenate(totals + [jnp.zeros((4, model), F32)], 0)
        parts = [pl.ds(pl.multiple_of((core_ref[0] ^ h) * width, TILE), width) for h in range(2)]
        for h in range(2):
            acc = 0.0
            for g, w_ref in enumerate((w0_ref, w1_ref)):
                acc = acc + mm(gb_ref[:, parts[g]], w_ref[parts[h], :], NT)
            if h == 0:
                gm_ref[...] = acc.astype(BF)
                br_ref[...] = gb_ref[:, parts[0]]
            else:
                sent_ref[:, :width] = acc.astype(BF)
                sent_ref[:, width:] = gb_ref[:, parts[1]]

    return pl.pallas_call(
        kernel,
        grid=(1,),
        in_specs=[
            *[smem_spec()] * 2,
            *[whole((rows, model))] * 2,
            whole((16, model)),
            whole((model, width)),
            whole((model, width)),
            *[whole((rows, model))] * (n + m),
        ],
        out_specs=[
            *[whole((rows, model))] * 2,
            *[whole((rows, width))] * 2,
            whole((rows, model)),
            whole((8, model)),
        ],
        out_shape=[
            jax.ShapeDtypeStruct((rows, model), BF),
            jax.ShapeDtypeStruct((rows, model), F32),
            jax.ShapeDtypeStruct((rows, width), BF),
            jax.ShapeDtypeStruct((rows, width), BF),
            jax.ShapeDtypeStruct((rows, model), BF),
            jax.ShapeDtypeStruct((8, model), F32),
        ],
        scratch_shapes=[VMEM((rows, model), BF)],
        compiler_params=params(10),
        cost_estimate=cost(4),
        name="second_norm_back",
    )(core, lengths, residual, grad_rows, vec, *weights, *results, *grads_normed)


def attention_backward(joined, probs, mixed, grad_mixed, head_size, products=None, weights=None):
    _, rows, width = joined.shape
    heads = width // head_size
    pairs = width // TILE
    per = TILE // head_size
    tiles = 2 * (rows // TILE) - 1
    span = 2 * rows
    scale = head_size**-0.5
    flat = [] if products is None else products.flat
    n_in = 4 + len(flat) + (2 if products else 0) + (1 if weights is not None else 0)

    def kernel(*refs):
        ins, refs = refs[:n_in], refs[n_in:]
        joined_ref, p_ref, mixed_ref, gm_ref = ins[:4]
        out_ref, diag_ref, refs = refs[0], refs[1], refs[2:]
        gp_ref, ds_ref, acc_ref = refs[-3:]
        lane = lax.broadcasted_iota(jnp.int32, (1, TILE), 1)
        for pair in range(pairs):
            lanes = slice(pair * TILE, (pair + 1) * TILE)
            q, k, v = (joined_ref[j, :, lanes] for j in range(3))
            gm = gm_ref[:, lanes]
            dots = gm.astype(F32) * mixed_ref[:, lanes]
            q_t, gm_t = q.T, gm.T
            dq, dk, dv = [], [], []
            for e in range(per):
                head = pair * per + e
                mine = (lane >= e * head_size) & (lane < (e + 1) * head_size)
                feats = slice(e * head_size, (e + 1) * head_size)
                delta = jnp.sum(jnp.where(mine, dots, 0.0), -1, keepdims=True)
                gp_ref[e] = mm(jnp.where(mine, gm, jnp.zeros_like(gm)), v, NT)
                acc_ref[...] = jnp.zeros_like(acc_ref)
                for r in range(0, rows, CHUNK):
                    block, sub = r // TILE, r % TILE
                    ds = p_ref[head, r : r + CHUNK, :].astype(F32) * (
                        gp_ref[e, r : r + CHUNK, :] - delta[r : r + CHUNK, :]
                    )
                    ds_ref[e, r : r + CHUNK, :] = ds.astype(BF)
                    for j in range(rows // TILE):
                        acc_ref[j - block + rows // TILE - 1, sub : sub + CHUNK, :] += ds[
                            :, j * TILE : (j + 1) * TILE
                        ]
                dq.append(jnp.where(mine, mm(ds_ref[e], k), 0.0))
                dk.append(mm(q_t[feats, :], ds_ref[e]))
                dv.append(mm(gm_t[feats, :], p_ref[head]))
                total = jnp.zeros((8, span), F32)
                for g in range(TILE // 8):
                    strip = jnp.concatenate(
                        [jnp.zeros((8, TILE), F32)]
                        + [acc_ref[d, 8 * g : 8 * g + 8, :] for d in range(tiles)],
                        1,
                    )
                    total += pltpu.roll(strip, (span - 8 * g) % span, 1) if g else strip
                line = total[0:1]
                for i in range(1, 8):
                    line = line + pltpu.roll(total[i : i + 1], span - i, 1)
                diag_ref[head] = line
            out_ref[0, :, lanes] = (functools.reduce(lambda a, b: a + b, dq) * scale).astype(BF)
            out_ref[1, :, lanes] = (jnp.concatenate(dk, 0) * scale).T.astype(BF)
            out_ref[2, :, lanes] = jnp.concatenate(dv, 0).T.astype(BF)
        if weights is not None:
            refs[0][...] = sum(mm(out_ref[j], ins[-1][j], NT) for j in range(3)).astype(BF)
        if products is not None:
            slot_refs = refs[1:-4] if weights is not None else refs[:-4]
            products.run(ins[4], ins[5], ins[6 : 6 + len(flat)], slot_refs, refs[-4], out_ref)

    ins = [joined, probs, mixed, grad_mixed]
    specs = [whole(one.shape) for one in ins]
    shapes = [VMEM((3, rows, width), BF), VMEM((heads, 1, span), F32)]
    scratch = [VMEM((per, rows, rows), F32), VMEM((per, rows, rows), BF), VMEM((tiles, TILE, TILE), F32)]
    if products is not None:
        ins += [products.core, products.offsets, *flat]
        specs += [smem_spec(), smem_spec(), *[whole(one.shape) for one in flat]]
    if weights is not None:
        ins.append(weights)
        specs.append(whole(weights.shape))
        shapes.append(VMEM((rows, weights.shape[1]), BF))
    if products is not None:
        shapes += products.shapes
        scratch.insert(0, products.scratch)
    return pl.pallas_call(
        kernel,
        grid=(1,),
        in_specs=specs,
        out_specs=[whole(one.shape) for one in shapes],
        out_shape=shapes,
        scratch_shapes=scratch,
        compiler_params=params(16),
        cost_estimate=cost(4.5),
        name="attention_backward",
    )(*ins)


def normed_back(grads, weights):
    _, rows, width = grads.shape
    model = weights.shape[1]

    def kernel(d_ref, w_ref, out_ref):
        out_ref[...] = sum(mm(d_ref[j], w_ref[j], NT) for j in range(3))

    return pl.pallas_call(
        kernel,
        grid=(1,),
        in_specs=[whole(grads.shape), whole(weights.shape)],
        out_specs=whole((rows, model)),
        out_shape=VMEM((rows, model), F32),
        compiler_params=params(8),
        cost_estimate=cost(1.5),
        name="normed_back",
    )(grads, weights)


def first_norm_back(
    core, grads, part, tokens, grad_residual, vec, weights, sums_second, sums_up, diags, lines, number, apart, offsets=None
):
    rows, model = tokens.shape
    width = model // 2
    count = diags[0].shape[0]
    span = lines[0].shape[1]
    n_up = len(sums_up[0])

    def kernel(core_ref, d0_ref, d1_ref, part_ref, x_ref, gres_ref, vec_ref, w_ref, s2_ref, t0_ref, t1_ref, l0_ref, l1_ref,
               *rest):
        up_refs = rest[: 2 * n_up]
        offs_ref, gx_ref, sums_ref, table_ref, acc_ref = rest[2 * n_up :]
        straight = core_ref[0] == 0

        def ordered(a, b):
            return [jnp.where(straight, a, b), jnp.where(straight, b, a)]

        tables = []
        for t_ref, l_ref in ((t0_ref, l0_ref), (t1_ref, l1_ref)):
            chosen = bucket_line(l_ref[0:1, :], number)
            sums = t_ref[:, 0, :]
            high = sums.astype(BF)
            rest = (sums - high.astype(F32)).astype(BF)
            both = mm(jnp.concatenate([high.astype(F32), rest.astype(F32)], 0).astype(BF), chosen, NT)
            table = both[:count] + both[count:]
            tables.append(table)
        blank = jnp.zeros((count, number), F32)
        tables = tables if apart else ordered(tables[0] + tables[1], blank)
        table = jnp.concatenate([*tables, jnp.zeros((16 - 2 * count, number), F32)], 0)
        table = jnp.concatenate([table, jnp.zeros((16, 4 * TILE - number), F32)], 1)
        table = jnp.concatenate([table[:, i * TILE : (i + 1) * TILE] for i in range(4)], 0)
        columns = []
        for j in (0, 2):
            a, b = (jnp.sum(d_ref[j].astype(F32), 0, keepdims=True) for d_ref in (d0_ref, d1_ref))
            columns.append(jnp.concatenate([a, b] if apart else ordered(a + b, jnp.zeros_like(a)), 1))
        ups = []
        for f in range(2):
            here = [ref[...] for ref in up_refs[f * n_up : (f + 1) * n_up]]
            ups += here if apart else ordered(here[0], jnp.zeros_like(here[0]))
        acc_ref[...] = part_ref[...].astype(F32) + sum(mm(d0_ref[j], w_ref[j], NT) for j in range(3))
        totals = [jnp.zeros((1, model), F32) for _ in range(2)]
        for r in range(0, rows, CHUNK):
            block = slice(r, r + CHUNK)
            up = acc_ref[block, :]
            grad, gain_terms = norm_back(x_ref[block, :].astype(F32), up, vec_ref[0:1, :])
            gx_ref[block, :] = gres_ref[block, :] + grad
            totals[0] += jnp.sum(gain_terms, 0, keepdims=True)
            totals[1] += jnp.sum(up, 0, keepdims=True)
        sums = jnp.concatenate(
            totals
            + columns
            + [s2_ref[2:3, :], s2_ref[0:1, :], s2_ref[1:2, :], s2_ref[3:4, :]]
            + ups
            + [jnp.zeros((4, model), F32)],
            0,
        )
        if offsets is None:
            sums_ref[...] = sums
            table_ref[...] = table
            return
        for i, ref in enumerate((sums_ref, table_ref)):
            for s in range(half):
                moved = pltpu.roll(sums, lax.rem(model - offs_ref[i * half + s], model), 1)
                ref[16 * s : 16 * s + 16, :] = moved[:, :TILE].astype(BF)
            ref[16 * half :, :] = table.astype(BF)

    half = 0 if offsets is None else offsets.shape[0] // 2
    late = [VMEM((16 * half + 64, TILE), BF)] * 2
    plain = [jax.ShapeDtypeStruct((16, model), F32), jax.ShapeDtypeStruct((64, TILE), F32)]
    grad_shape = (jax.ShapeDtypeStruct if offsets is None else VMEM)((rows, model), F32)
    shapes = [grad_shape, *(plain if offsets is None else late)]
    return pl.pallas_call(
        kernel,
        grid=(1,),
        in_specs=[
            smem_spec(),
            whole((3, rows, width)),
            whole((3, rows, width)),
            whole((rows, model)),
            whole((rows, model)),
            whole((rows, model)),
            whole((16, model)),
            whole((3, model, width)),
            whole((8, model)),
            whole((count, 1, span)),
            whole((count, 1, span)),
            whole((8, span)),
            whole((8, span)),
            *[whole((1, model))] * (2 * n_up),
            smem_spec(),
        ],
        out_specs=[whole(one.shape) for one in shapes],
        out_shape=shapes,
        scratch_shapes=[VMEM((rows, model), F32)],
        compiler_params=params(14),
        cost_estimate=cost(5),
        name="first_norm_back",
    )(
        core, *grads, part, tokens, grad_residual, vec, weights, sums_second, *diags, *lines, *sums_up[0], *sums_up[1],
        core if offsets is None else offsets,
    )


def pack_blocks(core, lengths, buckets, qkv, out, up):
    local, model = out.shape
    width = model // 2
    unit = local * 2
    chips = up.shape[1] // (4 * unit)
    rows = buckets.shape[1]

    def kernel(core_ref, len_ref, buckets_hbm, qkv_hbm, out_hbm, up_hbm, a0_ref, a1_ref, u0_ref, u1_ref, line_ref,
               first_ref, last_ref, qkv_ref, out_ref, up_ref, sems):
        copies = [
            pltpu.make_async_copy(source, target, sems.at[i])
            for i, (source, target) in enumerate(
                (
                    (qkv_hbm, qkv_ref),
                    (out_hbm, out_ref),
                    (up_hbm, up_ref),
                    (buckets_hbm.at[pl.ds(0, 1), pl.ds(0, 8)], first_ref),
                    (buckets_hbm.at[pl.ds(0, 1), pl.ds(rows - 8, 8)], last_ref),
                )
            )
        ]
        for c in copies:
            c.start()
        for c in copies:
            c.wait()
        core_at = core_ref[0]
        for h, a_ref in enumerate((a0_ref, a1_ref)):
            at = (core_at ^ h) * width
            for j in range(3):
                a_ref[j] = qkv_ref[:, pl.ds(pl.multiple_of(j * model + at, TILE), width)]
            a_ref[3] = out_ref[:, pl.ds(pl.multiple_of(at, TILE), width)]
        first = core_at == 0
        ahead = pltpu.roll(last_ref[0, 7:8, :].astype(F32), 1, 1)
        line = jnp.concatenate([ahead, first_ref[0, 0:1, :].astype(F32)], 1)
        live = jnp.zeros_like(line) + len_ref[0].astype(F32)
        line_ref[...] = jnp.concatenate([line, live, jnp.zeros((6, 2 * rows), F32)], 0)
        for f in range(2):
            by_core = []
            for c in range(2):
                by_core.append(
                    jnp.concatenate(
                        [
                            up_ref[:, ((2 * chip + c) * 2 + f) * unit : ((2 * chip + c) * 2 + f + 1) * unit]
                            for chip in range(chips)
                        ],
                        1,
                    ).astype(F32)
                )
            u0_ref[f] = jnp.where(first, by_core[0], by_core[1]).astype(BF)
            u1_ref[f] = jnp.where(first, by_core[1], by_core[0]).astype(BF)

    shapes = [
        *[VMEM((4, local, width), BF)] * 2,
        *[VMEM((2, local, model), BF)] * 2,
        VMEM((8, 2 * rows), F32),
    ]
    return pl.pallas_call(
        kernel,
        grid=(1,),
        in_specs=[
            smem_spec(),
            smem_spec(),
            *[hbm_spec()] * 4,
        ],
        out_specs=[whole(one.shape) for one in shapes],
        out_shape=shapes,
        scratch_shapes=[
            VMEM((1, 8, rows), jnp.int32),
            VMEM((1, 8, rows), jnp.int32),
            VMEM(qkv.shape, BF),
            VMEM(out.shape, BF),
            VMEM(up.shape, BF),
            pltpu.SemaphoreType.DMA((5,)),
        ],
        compiler_params=params(6),
        cost_estimate=cost(1.5),
        name="pack_blocks",
    )(core, lengths, in_hbm(buckets), in_hbm(qkv), in_hbm(out), in_hbm(up))


def pack_vectors(core, vectors):
    _, local = vectors.shape

    def kernel(core_ref, vec_ref, small_ref):
        first = core_ref[0] == 0
        values = jnp.concatenate(
            [vec_ref[...].astype(F32), jnp.zeros((VECTORS + 4, TILE - local), F32)], 1
        )
        moved = pltpu.roll(values, local, 1)
        lines = [jnp.where(first, values[:VECTORS], moved[:VECTORS])]
        for f in range(2):
            at = VECTORS + 2 * f
            both = values[at : at + 1] + moved[at + 1 : at + 2]
            blank = jnp.zeros_like(both)
            lines += [jnp.where(first, both, blank), jnp.where(first, blank, both)]
        small_ref[...] = jnp.concatenate(lines + [jnp.zeros((4, TILE), F32)], 0).astype(BF)

    return pl.pallas_call(
        kernel,
        grid=(1,),
        in_specs=[smem_spec(), whole(vectors.shape)],
        out_specs=whole((16, TILE)),
        out_shape=VMEM((16, TILE), BF),
        compiler_params=params(4),
        cost_estimate=cost(1),
        name="pack_vectors",
    )(core, vectors)


def ordered_rows(core_at, mine, theirs):
    first = core_at == 0
    a, b = mine.astype(F32), theirs.astype(F32)
    return jnp.concatenate([jnp.where(first, a, b), jnp.where(first, b, a)], 0)


def merge_attention(core, mine, theirs, small, small_theirs):
    count, local, width = mine.shape

    def kernel(core_ref, a_ref, b_ref, s_ref, t_ref, out_ref):
        for j in range(count):
            out_ref[2 * local * j : 2 * local * (j + 1), :] = ordered_rows(core_ref[0], a_ref[j], b_ref[j]).astype(BF)
        vec = s_ref[...].astype(F32) + t_ref[...].astype(F32)
        out_ref[2 * local * count :, :] = jnp.concatenate([vec, jnp.zeros((16, width - TILE), F32)], 1).astype(BF)

    return pl.pallas_call(
        kernel,
        grid=(1,),
        in_specs=[smem_spec(), *[whole(mine.shape)] * 2, *[whole(small.shape)] * 2],
        out_specs=whole((2 * local * count + 16, width)),
        out_shape=VMEM((2 * local * count + 16, width), BF),
        compiler_params=params(4),
        cost_estimate=cost(1),
        name="merge_attention",
    )(core, mine, theirs, small, small_theirs)


def merge_feed_forward(core, mine, theirs, down):
    _, local, model = mine.shape
    unit = 2 * local
    width = model // 2

    def kernel(core_ref, a_ref, b_ref, d_ref, *outs):
        for f in range(2):
            up = ordered_rows(core_ref[0], a_ref[f], b_ref[f]).astype(BF)
            low = d_ref[f * unit : (f + 1) * unit, :]
            for j, block in enumerate((up[:, :width], up[:, width:], low[:, :width], low[:, width:])):
                outs[f][j * unit : (j + 1) * unit, :] = block

    shape = VMEM((4 * unit, width), BF)
    return pl.pallas_call(
        kernel,
        grid=(1,),
        in_specs=[smem_spec(), *[whole(mine.shape)] * 2, whole(down.shape)],
        out_specs=[whole(shape.shape)] * 2,
        out_shape=[shape] * 2,
        compiler_params=params(4),
        cost_estimate=cost(1),
        name="merge_feed_forward",
    )(core, mine, theirs, down)


def pair_sum(refs):
    parts = [ref[...].astype(F32) for ref in refs]
    while len(parts) > 1:
        half = len(parts) // 2
        parts = [parts[i] + parts[i + half] for i in range(half)]
    return parts[0]


def rows_of(total, first, core_at, local, mine):
    a, b = total[first : first + local], total[first + local : first + 2 * local]
    return jnp.where((core_at == 0) == mine, a, b)


def total_attention(core, parts, local):
    tall, width = parts[0].shape
    tail = tall - 8 * local

    def kernel(core_ref, *refs):
        ins, (mine_ref, sent_ref) = refs[: len(parts)], refs[len(parts) :]
        total = pair_sum(ins)
        for j in range(4):
            mine_ref[j] = rows_of(total, 2 * local * j, core_ref[0], local, True)
            theirs = rows_of(total, 2 * local * j, core_ref[0], local, False)
            sent_ref[j] = jnp.concatenate([theirs, jnp.zeros((tail - local, width), F32)], 0).astype(BF)
        sent_ref[4] = total[8 * local :].astype(BF)

    shapes = [
        VMEM((4, local, width), F32),
        VMEM((5, tail, width), BF),
    ]
    return pl.pallas_call(
        kernel,
        grid=(1,),
        in_specs=[smem_spec(), *[whole(one.shape) for one in parts]],
        out_specs=[whole(one.shape) for one in shapes],
        out_shape=shapes,
        compiler_params=params(6),
        cost_estimate=cost(1),
        name="total_attention",
    )(core, *parts)


def finish_attention(core, mine, sent, theirs, heads, number):
    _, local, width = mine.shape
    model = 2 * width

    def kernel(core_ref, a_ref, s_ref, b_ref, qkv_ref, out_ref, table_ref, *small_refs):
        at = core_ref[0]
        for h, ref in enumerate((a_ref, b_ref)):
            for j in range(3):
                cols = pl.ds(pl.multiple_of(j * model + (at ^ h) * width, TILE), width)
                qkv_ref[:, cols] = ref[j, :local, :].astype(F32)
            out_ref[:, pl.ds(pl.multiple_of((at ^ h) * width, TILE), width)] = ref[3, :local, :].astype(F32)
        total = s_ref[4].astype(F32) + b_ref[4].astype(F32)
        small = total[:16, :TILE]
        small = jnp.where(at == 0, small, jnp.concatenate([pltpu.roll(small[:8], TILE - local, 1), small[8:]], 0))
        for i in range(VECTORS):
            small_refs[i][...] = small[i : i + 1, :local]
        ups = [jnp.where(at == 0, small[8 + 2 * f : 9 + 2 * f], small[9 + 2 * f : 10 + 2 * f]) for f in range(2)]
        lane = lax.broadcasted_iota(jnp.int32, (1, TILE), 1)
        both = jnp.where(lane < 2 * local, ups[0], pltpu.roll(ups[1], 2 * local, 1))
        small_refs[VECTORS][...] = both[:, : 4 * local]
        table_ref[...] = jnp.concatenate([total[:16, TILE:], total[16:, : 2 * TILE]], 1)[:heads, :number]

    shapes = [
        jax.ShapeDtypeStruct((local, 3 * model), F32),
        jax.ShapeDtypeStruct((local, model), F32),
        jax.ShapeDtypeStruct((heads, number), F32),
        *[jax.ShapeDtypeStruct((1, local), F32)] * VECTORS,
        jax.ShapeDtypeStruct((1, 4 * local), F32),
    ]
    return pl.pallas_call(
        kernel,
        grid=(1,),
        in_specs=[smem_spec(), *[whole(one.shape) for one in (mine, sent, theirs)]],
        out_specs=[whole(one.shape) for one in shapes],
        out_shape=shapes,
        compiler_params=params(6),
        cost_estimate=cost(1),
        name="finish_attention",
    )(core, mine, sent, theirs)


def total_feed_forward(core, parts, local):
    _, width = parts[0].shape
    model = 2 * width
    unit = 2 * local

    def kernel(core_ref, *refs):
        ins, (mine_ref, sent_ref, down_ref) = refs[: len(parts)], refs[len(parts) :]
        total = pair_sum(ins)
        for h in range(2):
            cols = slice(h * width, (h + 1) * width)
            mine_ref[:, cols] = rows_of(total, h * unit, core_ref[0], local, True)
            sent_ref[:, cols] = rows_of(total, h * unit, core_ref[0], local, False).astype(BF)
            down_ref[:, cols] = total[(2 + h) * unit : (3 + h) * unit]

    shapes = [
        jax.ShapeDtypeStruct((local, model), F32),
        jax.ShapeDtypeStruct((local, model), BF),
        jax.ShapeDtypeStruct((unit, model), F32),
    ]
    return pl.pallas_call(
        kernel,
        grid=(1,),
        in_specs=[smem_spec(), *[whole(one.shape) for one in parts]],
        out_specs=[whole(one.shape) for one in shapes],
        out_shape=shapes,
        compiler_params=params(6),
        cost_estimate=cost(1),
        name="total_feed_forward",
    )(core, *parts)


def finish_feed_forward(core, mine, theirs, downs):
    local, model = mine[0].shape
    unit = 2 * local
    chips = model // unit

    def kernel(core_ref, m0, m1, t0, t1, d0, d1, up_ref, down_ref):
        first = core_ref[0] == 0
        by = []
        for a, b in ((m0, t0), (m1, t1)):
            a, b = a[...], b[...].astype(F32)
            by.append((jnp.where(first, a, b), jnp.where(first, b, a)))
        up_ref[...] = jnp.concatenate(
            [
                by[f][c][:, chip * unit : (chip + 1) * unit]
                for chip in range(chips)
                for c in range(2)
                for f in range(2)
            ],
            1,
        )
        down_ref[:unit, :] = d0[...]
        down_ref[unit:, :] = d1[...]

    shapes = [jax.ShapeDtypeStruct((local, 4 * model), F32), jax.ShapeDtypeStruct((2 * unit, model), F32)]
    ins = (*mine, *theirs, *downs)
    return pl.pallas_call(
        kernel,
        grid=(1,),
        in_specs=[smem_spec(), *[whole(one.shape) for one in ins]],
        out_specs=[whole(one.shape) for one in shapes],
        out_shape=shapes,
        compiler_params=params(6),
        cost_estimate=cost(1),
        name="finish_feed_forward",
    )(core, *ins)


VECTORS = 8


class Order:
    def __init__(self, token):
        self.token = token

    def go(self, *values):
        out, _ = lax.optimization_barrier((values, self.token))
        return out if len(out) > 1 else out[0]

    def mark(self, *values):
        out, self.token = lax.optimization_barrier((values, self.token))
        return out if len(out) > 1 else out[0]


class GridLinks:
    pair = True

    def __init__(self, sizes, model):
        self.ny, self.nz, self.nx = sizes
        self.chips = self.ny * self.nz * self.nx
        self.rows = model // self.chips
        dp, inner = lax.axis_index("dp"), lax.axis_index("fsdp")
        self.core = inner % 2
        chip = inner // 2
        self.place = (dp, chip // self.nx, chip % self.nx)
        self.gather_offsets = self._offsets(self.core, -1, (range(self.nz),))
        self.early_offsets = self._offsets(self.core, -1, ((0, 1, 3, 2),))
        self.scatter_offsets = self._offsets(self.core, 1, (range(self.nz),))
        self.last_offsets = self._offsets(self.core, 1, (range(1, self.nz), (0,)))
        self.last_counts = (self.nz - 1,) * 4 + (2, 2)

    def _offsets(self, core, sign, parts):
        y, z, x = self.place
        out = []
        for part in parts:
            for r1 in range(2):
                for r2 in range(2):
                    for k in part:
                        fy = jnp.where(core == 0, r1, r2)
                        fx = jnp.where(core == 0, r2, r1)
                        zz = (z + sign * k + self.nz) % self.nz
                        out.append(((y ^ fy) * self.nz + zz) * self.nx + (x ^ fx))
        return (jnp.stack(out) * self.rows).astype(jnp.int32)

    def _send(self, value, move):
        pairs = []
        for y in range(self.ny):
            for z in range(self.nz):
                for x in range(self.nx):
                    for c in range(2):
                        source = ((y * self.nz + z) * self.nx + x) * 2 + c
                        ty, tz, tx, tc = move(y, z, x, c)
                        pairs.append((source, ((ty * self.nz + tz) * self.nx + tx) * 2 + tc))
        return lax.ppermute(value, AXES, pairs)

    def swap(self, value):
        return self._send(value, lambda y, z, x, c: (y, z, x, 1 - c))

    def along_z(self, value, k):
        return self._send(value, lambda y, z, x, c: (y, (z + k) % self.nz, x, c))

    def x_first(self, value):
        return self._send(value, lambda y, z, x, c: (y, z, 1 - x, c) if c == 0 else (1 - y, z, x, c))

    def y_first(self, value):
        return self._send(value, lambda y, z, x, c: (y, z, 1 - x, c) if c == 1 else (1 - y, z, x, c))


def small_kernel(kernel, name, shapes, *ins):
    return pl.pallas_call(
        kernel,
        grid=(1,),
        in_specs=[whole(one.shape) for one in ins],
        out_specs=[whole(shape) for shape in shapes],
        out_shape=[VMEM(shape, BF) for shape in shapes],
        compiler_params=params(4),
        cost_estimate=cost(1),
        name=name,
    )(*ins)


def stack_blocks(*blocks):
    def kernel(*refs):
        for i, ref in enumerate(refs[:-1]):
            refs[-1][i] = ref[...]

    return small_kernel(kernel, "stack_blocks", [(len(blocks), *blocks[0].shape)], *blocks)[0]


def join_blocks(first, last):
    n = first.shape[0]

    def kernel(first_ref, last_ref, out_ref):
        out_ref[:n] = first_ref[...]
        out_ref[n:] = last_ref[...]

    return small_kernel(kernel, "join_blocks", [(n + last.shape[0], *first.shape[1:])], first, last)[0]


def add_low(a, b):
    return (a.astype(F32) + b.astype(F32)).astype(BF)


def fold(keep, moved):
    n = keep.shape[0] // 2

    def kernel(keep_ref, moved_ref, *outs):
        for s in range(2 * n):
            outs[s // n][s % n] = add_low(keep_ref[s], moved_ref[s])

    return small_kernel(kernel, "fold", [(n, *keep.shape[1:])] * 2, keep, moved)


def add_blocks(a, b):
    def kernel(a_ref, b_ref, out_ref):
        for i in range(a.shape[0]):
            out_ref[i] = add_low(a_ref[i], b_ref[i])

    return small_kernel(kernel, "add_blocks", [a.shape], a, b)[0]


def fold_late(keep, moved, slots):
    half = 8 * slots

    def kernel(keep_ref, moved_ref, *outs):
        total = add_low(keep_ref[...], moved_ref[...])
        for i, out in enumerate(outs):
            out[:half, :] = total[i * half : (i + 1) * half]
            out[half:, :] = total[2 * half :]

    return small_kernel(kernel, "fold_late", [(half + keep.shape[0] - 2 * half, TILE)] * 2, keep, moved)


def fold_last(blocks, late=None, first=0):
    n, tall, wide = blocks[0].shape
    count = len(blocks)
    tail = 0 if late is None else 32

    def kernel(*refs):
        outs = refs[-n:]
        for s in range(n):
            total = sum(ref[s].astype(F32) for ref in refs[:count])
            outs[s][:tall, :] = total.astype(BF)
        if tail:
            total = add_low(refs[count][...], refs[count + 1][...])
            at = total.shape[0] - 64
            blocks = [total[at + 16 * i : at + 16 * i + 16] for i in range(4)]
            for s in range(n):
                small = total[16 * (first + s) : 16 * (first + s) + 16]
                outs[s][tall : tall + 16, :] = jnp.concatenate([small, *blocks[:2]], 1)
                outs[s][tall + 16 :, :] = jnp.concatenate([*blocks[2:], jnp.zeros_like(small)], 1)

    return small_kernel(kernel, "fold_last", [(tall + tail, wide)] * n, *blocks, *(late or ()))


def on_device(
    links,
    tokens,
    lengths,
    buckets,
    ln1_gain,
    ln1_bias,
    qkv_weight,
    q_bias,
    v_bias,
    out_weight,
    out_bias,
    rel_table,
    ln2_gain,
    ln2_bias,
    up_weight,
    up_bias,
    down_weight,
    down_bias,
    cotangent,
):
    rows, model = tokens.shape
    heads, number = rel_table.shape
    head_size = model // heads
    width = model // 2
    local = qkv_weight.shape[0]
    core, chips = links.core, links.chips
    core_arg = core.astype(jnp.int32).reshape(1)

    order = Order(core_arg)
    a_mine, a_sent, u_mine, u_sent, line = pack_blocks(
        core_arg, lengths, buckets, qkv_weight, out_weight, up_weight
    )
    a_mine, a_sent, ln1_gain = order.mark(a_mine, a_sent, ln1_gain)
    vectors = jnp.stack(
        [ln1_gain, ln1_bias, q_bias, v_bias, out_bias, ln2_gain, ln2_bias, down_bias]
        + [up_bias[i * local : (i + 1) * local] for i in range(4)]
    )
    small = pack_vectors(core_arg, vectors)
    a_theirs, small_theirs = links.swap(a_sent), links.swap(small)
    line_other, tokens_other, u_theirs = links.swap(line), links.swap(tokens), links.swap(u_sent)
    early_offsets, gather_offsets = links.early_offsets, links.gather_offsets
    scatter_offsets, last_offsets = links.scatter_offsets, links.last_offsets
    a_piece = merge_attention(core_arg, a_mine, a_theirs, small, small_theirs)
    a_piece, line_other, tokens_other, u_theirs, early_offsets, gather_offsets, scatter_offsets, last_offsets = order.mark(
        a_piece, line_other, tokens_other, u_theirs, early_offsets, gather_offsets, scatter_offsets, last_offsets
    )

    z_parts = [links.along_z(a_piece, k) for k in (1, 3, 2)]
    near = a_piece[None]
    second, third = links.x_first(near), links.y_first(near)
    tiles, grad_rows = bias_tiles(core_arg, (line, line_other), rel_table, cotangent, lengths, (0, 0))
    tiles, grad_rows, z_parts[:2], second, third, a_piece = order.mark(
        tiles, grad_rows, z_parts[:2], second, third, a_piece
    )
    z_parts[2] = links.along_z(a_piece, 2)
    f0, f1 = merge_feed_forward(core_arg, u_mine, order.go(u_theirs), down_weight)
    f_early = [[go(f[None]) for go in (links.x_first, links.y_first)] for f in (f0, f1)]
    f0, f1, z_parts[2], f_early = order.mark(f0, f1, z_parts[2], f_early)
    near_last = stack_blocks(*z_parts)
    second_last, third_last = links.x_first(near_last), links.y_first(near_last)
    f0_z = [links.along_z(order.go(f0), k) for k in (1, 3, 2)]
    second_last, third_last, f0_z[:2] = order.mark(second_last, third_last, f0_z[:2])
    fourth = links.y_first(join_blocks(second, second_last))
    f1_z = [links.along_z(order.go(f1), k) for k in (1, 3)]
    grad_rows_other = links.swap(grad_rows)
    fourth, grad_rows_other, f0_z[2] = order.mark(fourth, grad_rows_other, f0_z[2])
    parts = [near, near_last, second, second_last, third, third_last, fourth]
    own, own_out, vec = order.mark(*assemble_attention(Pieces(parts, early_offsets, links.rows), model))
    f1_z = order.mark(f1_z)
    f0_near = stack_blocks(f0_z[0], f0_z[2], f0_z[1])
    f0_second, f0_third = links.x_first(f0_near), links.y_first(f0_near)
    f1_z.append(links.along_z(order.go(f1), 2))
    other_out = links.swap(own_out)

    normed_other, joined1, mixed1, probs1, full1 = attention_forward(
        1, 0, core_arg, tokens_other, vec, order.go(own), tiles, line_other, head_size
    )
    mixed1, other_out, f1_z = order.mark(mixed1, other_out, f1_z)
    mixed_rest = links.swap(mixed1)
    f0_second, f0_third = order.mark(f0_second, f0_third)
    f0_fourth = links.y_first(join_blocks(f_early[0][0], f0_second))
    f1_near = stack_blocks(f1_z[0], f1_z[2], f1_z[1])
    f1_second = links.x_first(f1_near)
    normed, joined0, mixed0, probs0, full0 = attention_forward(
        0, 0, core_arg, tokens, vec, order.go(own), tiles, line, head_size
    )
    mixed0, mixed_rest = order.mark(mixed0, mixed_rest)
    mixed_rest_other = links.swap(mixed0)
    residual, normed2 = project_out(core_arg, (order.go(mixed0), mixed_rest), tokens, (own_out, other_out), vec)
    normed2, f0_fourth, f1_second, mixed_rest_other = order.mark(normed2, f0_fourth, f1_second, mixed_rest_other)

    normed2_other = links.swap(normed2)
    f1_third, f1_fourth = links.y_first(f1_near), links.y_first(join_blocks(f_early[1][0], f1_second))
    normed2_other = order.mark(normed2_other)

    def chunk(bufs):
        return Pieces(bufs, gather_offsets, links.rows)

    (own0, other0), sums_f0, (keep0, send0) = feed_forward(
        lambda c: 8 + c, core_arg,
        [(normed2, grad_rows, residual, None), (normed2_other, grad_rows_other, None, None)],
        vec, chunk([f0[None], f0_near, f_early[0][0], f0_second, f_early[0][1], f0_third, f0_fourth]), scatter_offsets,
    )
    own0, other0, keep0, send0, f1_third, f1_fourth = order.mark(own0, other0, keep0, send0, f1_third, f1_fourth)
    moved0 = links.y_first(send0)
    (own1, other1), sums_f1, (keep1, send1) = feed_forward(
        lambda c: 10 + c, core_arg,
        [(normed2, grad_rows, own0[0], own0[1]), (normed2_other, grad_rows_other, other0[0], other0[1])],
        vec, chunk([f1[None], f1_near, f_early[1][0], f1_second, f_early[1][1], f1_third, f1_fourth]), scatter_offsets,
    )
    own1, other1, keep1, send1, moved0 = order.mark(own1, other1, keep1, send1, moved0)
    keep0, send0 = fold(keep0, moved0)
    moved0 = links.x_first(send0)
    result_rest, grad_rest = links.swap(other1[0]), links.swap(other1[1])
    result_rest, grad_rest = order.mark(result_rest, grad_rest)
    moved1 = links.y_first(order.go(send1))
    output, grad_res, gm0, branch_cols, sent, sums2 = second_norm_back(
        core_arg, residual, (order.go(own1[0]), result_rest), (own1[1], grad_rest), grad_rows,
        (own_out, other_out), vec, lengths,
    )
    sent, moved0 = order.mark(sent, moved0)
    got = links.swap(sent)
    sums0 = fold_last((keep0, moved0))
    parts0 = [sums0[0]] + [links.along_z(sums0[k], k) for k in (1, 3)]
    dj0, diag0 = attention_backward(joined0, probs0, full0, order.go(gm0), head_size)
    dj0, got, moved1, parts0 = order.mark(dj0, got, moved1, parts0)
    parts0.insert(2, links.along_z(order.go(sums0[2]), 2))
    keep1, send1 = fold(keep1, moved1)
    moved1 = links.x_first(send1)
    dj1, diag1, part, keep, keep_next, send, send_next, own_keep, own_send = attention_backward(
        joined1, probs1, full1, order.go(got), head_size,
        Products(
            core_arg,
            [([(normed, None), (normed_other, None)], [(dj0, j), (None, j)]) for j in range(3)]
            + [([((mixed0, mixed_rest), None), ((mixed1, mixed_rest_other), None)], [(branch_cols, None), (got, 1)])],
            last_offsets,
            links.rows,
            links.last_counts,
        ),
        own,
    )
    part, keep, keep_next, send, send_next, own_keep, own_send, moved1, parts0 = order.mark(
        part, keep, keep_next, send, send_next, own_keep, own_send, moved1, parts0
    )
    part_rest = links.swap(part)
    next_moved, moved = links.y_first(send_next), links.y_first(send)
    part_rest, keep1, moved1 = order.mark(part_rest, keep1, moved1)
    sums1 = fold_last((keep1, moved1))
    parts1 = [sums1[0]] + [links.along_z(sums1[k], k) for k in (1, 3)]
    input_grad, late_keep, late_send = first_norm_back(
        core_arg, (order.go(dj0), dj1), part_rest, tokens, grad_res, vec, own, sums2, ([sums_f0], [sums_f1]),
        (diag0, diag1), (line, line_other), number, False, scatter_offsets,
    )
    late_keep, late_send, next_moved, parts1 = order.mark(late_keep, late_send, next_moved, parts1)
    late_moved = links.y_first(late_send)
    parts1.insert(2, links.along_z(order.go(sums1[2]), 2))
    next_moved = links.x_first(add_blocks(keep_next, next_moved))
    late_moved, moved = order.mark(late_moved, moved)
    late_keep, late_send = fold_late(late_keep, late_moved, 2 * links.nz)
    late_moved = links.x_first(late_send)
    next_moved, late_moved, own_send, parts1 = order.mark(next_moved, late_moved, own_send, parts1)
    sums = fold_last((keep, moved, next_moved), (late_keep, late_moved), 1)
    parts = [links.along_z(sums[k - 1], k) for k in (1, 2, 3)]
    own_moved = links.y_first(own_send)
    ffn0 = total_feed_forward(core_arg, order.go(parts0), local)
    ffn1 = total_feed_forward(core_arg, order.go(parts1), local)
    ffn0, ffn1, own_moved = order.mark(ffn0, ffn1, own_moved)
    own_keep, own_send = fold(own_keep, own_moved)
    own_moved = links.x_first(own_send)
    ups = [links.swap(ffn0[1]), links.swap(ffn1[1])]
    grad_up, grad_down = finish_feed_forward(
        core_arg, [ffn0[0], ffn1[0]], ups, [ffn0[2], ffn1[2]]
    )
    grad_up, grad_down, parts, own_moved = order.mark(grad_up, grad_down, parts, own_moved)
    parts = [*fold_last((own_keep, own_moved), (late_keep, late_moved)), *parts]
    mine, sent = total_attention(core_arg, parts, local)
    theirs = links.swap(sent)
    grad_qkv, grad_out, grad_table, *small_grads = finish_attention(
        core_arg, mine, sent, theirs, heads, number
    )
    small_grads = [one.reshape(-1) for one in small_grads]
    grad_up_bias = small_grads[VECTORS]

    return (
        output,
        input_grad,
        small_grads[0],
        small_grads[1],
        grad_qkv,
        small_grads[2],
        small_grads[3],
        grad_out,
        small_grads[4],
        grad_table,
        small_grads[5],
        small_grads[6],
        grad_up,
        grad_up_bias,
        grad_down,
        small_grads[7],
    )


def on_any_mesh(
    tokens,
    lengths,
    buckets,
    ln1_gain,
    ln1_bias,
    qkv_weight,
    q_bias,
    v_bias,
    out_weight,
    out_bias,
    rel_table,
    ln2_gain,
    ln2_bias,
    up_weight,
    up_bias,
    down_weight,
    down_bias,
    cotangent,
):
    rows, model = tokens.shape
    heads, number = rel_table.shape
    head_size = model // heads
    width = model // 2
    local = qkv_weight.shape[0]
    hidden = up_weight.shape[1]
    core = jnp.zeros((1,), jnp.int32)
    offsets = jnp.zeros((1,), jnp.int32)

    def gathered(x):
        return lax.all_gather(x, AXES, axis=0, tiled=True)

    def scattered(x):
        return lax.psum_scatter(x, AXES, scatter_dimension=0, tiled=True)

    vectors = [ln1_gain, ln1_bias, q_bias, v_bias, out_bias, ln2_gain, ln2_bias, down_bias]
    unit = up_bias.shape[0]
    small = gathered(jnp.concatenate([*vectors, up_bias])[None, :])
    wide = [small[:, i * local : (i + 1) * local].reshape(1, model) for i in range(VECTORS)]
    ub = small[:, VECTORS * local :].reshape(2, 2, model).transpose(1, 0, 2).reshape(4, model)
    del unit
    vec = jnp.concatenate([*wide, ub, jnp.zeros((4, model), BF)], 0).astype(F32)
    attn = gathered(jnp.concatenate([qkv_weight, out_weight], 1))
    up, down = gathered(up_weight), gathered(down_weight)
    a_pieces = tuple(
        jnp.stack([attn[:, j * model + h * width : j * model + (h + 1) * width] for j in range(3)])
        for h in range(2)
    )

    a_out = tuple(attn[:, 3 * model + h * width : 3 * model + (h + 1) * width] for h in range(2))

    def chunk(f, h):
        at = (2 * h + f) * model
        blocks = [one[:, k * width : (k + 1) * width] for one in (up[:, at : at + model], down[at : at + model]) for k in range(2)]
        return Pieces([jnp.concatenate(blocks, 0)[None]], offsets, model)

    ahead = jnp.roll(buckets[0, rows - 1], 1)
    line = jnp.concatenate([ahead, buckets[0, 0]]).astype(F32)
    line = jnp.stack([line, jnp.full_like(line, lengths[0])] + [jnp.zeros_like(line)] * 6)
    tiles, grad_rows = bias_tiles(core, (line, line), rel_table, cotangent, lengths, (0, 1))
    normed, joined0, mixed0, probs0, full0 = attention_forward(0, 0, core, tokens, vec, a_pieces[0], tiles, line, head_size)
    _, joined1, mixed1, probs1, full1 = attention_forward(1, 1, core, tokens, vec, a_pieces[1], tiles, line, head_size)
    residual, normed2 = project_out(core, (mixed0, mixed1), tokens, a_out, vec)
    result, grad_n2 = residual, None
    up_sums, ups, downs = [[], []], [], []
    for f in range(2):
        for h in range(2):
            ((result, grad_n2, active, grad_pre),), sums, _ = feed_forward(
                lambda c, at=8 + 2 * f + h: c + at, core, [(normed2, grad_rows, result, grad_n2)], vec, chunk(f, h)
            )
            up_sums[f].append(sums)
            (both,) = outer_products(
                core,
                [([(normed2, None)], [(grad_pre, k)]) for k in range(2)]
                + [([(active, None)], [(grad_rows, k)]) for k in range(2)],
                offsets,
                model,
            )
            both = both[0].reshape(2, 2, model, width).transpose(0, 2, 1, 3).reshape(2, model, model)
            ups.append(both[0])
            downs.append(both[1])
    output, grad_res, gm0, branch0, sent, sums2 = second_norm_back(
        core, residual, (result,), (grad_n2,), grad_rows, a_out, vec, lengths
    )
    dj0, diag0 = attention_backward(joined0, probs0, full0, gm0, head_size)
    dj1, diag1 = attention_backward(joined1, probs1, full1, sent, head_size)
    input_grad, vec_grads, table_grad = first_norm_back(
        core, (dj0, dj1), normed_back(dj1, a_pieces[1]), tokens, grad_res, vec, a_pieces[0], sums2, up_sums,
        (diag0, diag1), (line, line), number, True,
    )
    mixed = jnp.concatenate([mixed0, mixed1], 1)
    halves = [
        outer_products(
            core, [([(normed, None)], [(dj, j)]) for j in range(3)] + [([(mixed, None)], [branch])], offsets, model
        )[0][0].reshape(4, model, width)
        for dj, branch in ((dj0, (branch0, None)), (dj1, (sent, 1)))
    ]
    grads = jnp.stack(halves, 2).transpose(1, 0, 2, 3).reshape(model, 4 * model)
    grads = scattered(grads)
    grad_up = scattered(jnp.concatenate([ups[0], ups[2], ups[1], ups[3]], 1))
    grad_down = scattered(jnp.concatenate([downs[0], downs[2], downs[1], downs[3]], 0))
    by_owner = vec_grads[:VECTORS].reshape(VECTORS, model // local, local).transpose(1, 0, 2)
    own_units = vec_grads[VECTORS : VECTORS + 4].reshape(2, 2, model).transpose(1, 0, 2)
    both = jnp.concatenate(
        [by_owner.reshape(model // local, VECTORS * local), own_units.reshape(model // local, hidden * local // model)],
        1,
    )
    both = scattered(both)[0]
    table = jnp.concatenate([table_grad[16 * i : 16 * i + 16] for i in range(4)], 1)[:heads, :number]
    grad_table = lax.psum(table, AXES)
    small_grads = [both[i * local : (i + 1) * local] for i in range(VECTORS)]
    return (
        output,
        input_grad,
        small_grads[0],
        small_grads[1],
        grads[:, : 3 * model].astype(F32),
        small_grads[2],
        small_grads[3],
        grads[:, 3 * model :].astype(F32),
        small_grads[4],
        grad_table,
        small_grads[5],
        small_grads[6],
        grad_up.astype(F32),
        both[VECTORS * local :],
        grad_down.astype(F32),
        small_grads[7],
    )


def solution(mesh):
    both = P(AXES)
    row = P(AXES, None)
    in_specs = (
        row, both, P(AXES, None, None), both, both, row, both, both, row, both, P(), both, both, row, both, row,
        both, row,
    )
    out_specs = (row, row, both, both, row, both, both, row, both, P(), both, both, row, both, row, both)

    if tuple(mesh.shape[name] for name in AXES) == (2, 16):

        def body(*args):
            return on_device(GridLinks((2, 4, 2), args[0].shape[1]), *args)

    else:
        body = on_any_mesh

    return jax.shard_map(body, mesh=mesh, in_specs=in_specs, out_specs=out_specs, check_vma=False)
```
